32 devices in a mesh: dp: 8 (over y, x, core), fsdp: 4 (over z).
Axes of the slice: x: 2, y: 2, z: 4, core: 2. Of those that a mesh axis runs over, the one named last changes fastest.
Arguments:
- tokens: bfloat16 [64, 160, 1280], P(('dp', 'fsdp')), may hold values from -6 to 6
- cotangent: bfloat16 [64, 160, 1280], P(('dp', 'fsdp')), may hold values from -15 to 15
- segment_ids: int32 [64, 160], P(('dp', 'fsdp')), may hold values from 0 to 3, never falling along the last dimension, each value on 1 to 80 neighbouring positions
- w_query: float32 [1280, 1024], P(('dp', 'fsdp')), may hold values from -0.15625 to 0.15625
- w_key: float32 [1280, 256], P(('dp', 'fsdp')), may hold values from -0.15625 to 0.15625
- w_value: float32 [1280, 256], P(('dp', 'fsdp')), may hold values from -0.15625 to 0.15625
- w_out: float32 [1024, 1280], P(('dp', 'fsdp')), may hold values from -0.5 to 0.5
- w_gate: float32 [1280, 3072], P(('dp', 'fsdp')), may hold values from -0.15625 to 0.15625
- w_up: float32 [1280, 3072], P(('dp', 'fsdp')), may hold values from -0.15625 to 0.15625
- w_down: float32 [3072, 1280], P(('dp', 'fsdp')), may hold values from -0.109375 to 0.109375
- m_query: float32 [1280, 1024], P(('dp', 'fsdp')), may hold values from -0.00024414062 to 0.00024414062
- m_key: float32 [1280, 256], P(('dp', 'fsdp')), may hold values from -0.00048828125 to 0.00048828125
- m_value: float32 [1280, 256], P(('dp', 'fsdp')), may hold values from -0.00048828125 to 0.00048828125
- m_out: float32 [1024, 1280], P(('dp', 'fsdp')), may hold values from -9.1552734e-05 to 9.1552734e-05
- m_gate: float32 [1280, 3072], P(('dp', 'fsdp')), may hold values from -0.00010681152 to 0.00010681152
- m_up: float32 [1280, 3072], P(('dp', 'fsdp')), may hold values from -0.00010681152 to 0.00010681152
- m_down: float32 [3072, 1280], P(('dp', 'fsdp')), may hold values from -0.00015258789 to 0.00015258789
- v_query: float32 [1280, 1024], P(('dp', 'fsdp')), may hold values from 7.3703874e-09 to 2.9412345e-08
- v_key: float32 [1280, 256], P(('dp', 'fsdp')), may hold values from 2.6298096e-08 to 1.05192385e-07
- v_value: float32 [1280, 256], P(('dp', 'fsdp')), may hold values from 3.287262e-08 to 1.3149048e-07
- v_out: float32 [1024, 1280], P(('dp', 'fsdp')), may hold values from 9.91369e-10 to 3.9620156e-09
- v_gate: float32 [1280, 3072], P(('dp', 'fsdp')), may hold values from 1.179954e-09 to 4.7232764e-09
- v_up: float32 [1280, 3072], P(('dp', 'fsdp')), may hold values from 1.179954e-09 to 4.7232764e-09
- v_down: float32 [3072, 1280], P(('dp', 'fsdp')), may hold values from 3.2699607e-09 to 1.3097144e-08
- gains: float32 [2688], replicated, may hold values from 0.4 to 2.6
- gain_first: float32 [2688], replicated, may hold values from -0.00048828125 to 0.00048828125
- gain_second: float32 [2688], replicated, may hold values from 3.6332896e-08 to 1.4533158e-07
Outputs:
- output: bfloat16 [64, 160, 1280], P(('dp', 'fsdp'))
- input_grad: bfloat16 [64, 160, 1280], P(('dp', 'fsdp'))
- grad_query: float32 [1280, 1024], P(('dp', 'fsdp'))
- grad_key: float32 [1280, 256], P(('dp', 'fsdp'))
- grad_value: float32 [1280, 256], P(('dp', 'fsdp'))
- grad_out: float32 [1024, 1280], P(('dp', 'fsdp'))
- grad_gate: float32 [1280, 3072], P(('dp', 'fsdp'))
- grad_up: float32 [1280, 3072], P(('dp', 'fsdp'))
- grad_down: float32 [3072, 1280], P(('dp', 'fsdp'))
- grad_gains: float32 [2688], replicated
- grad_norm: float32 [], replicated
- new_query: float32 [1280, 1024], P(('dp', 'fsdp'))
- new_key: float32 [1280, 256], P(('dp', 'fsdp'))
- new_value: float32 [1280, 256], P(('dp', 'fsdp'))
- new_out: float32 [1024, 1280], P(('dp', 'fsdp'))
- new_gate: float32 [1280, 3072], P(('dp', 'fsdp'))
- new_up: float32 [1280, 3072], P(('dp', 'fsdp'))
- new_down: float32 [3072, 1280], P(('dp', 'fsdp'))
- new_gains: float32 [2688], replicated
- copy_query: bfloat16 [1280, 1024], P(('dp', 'fsdp'))
- copy_key: bfloat16 [1280, 256], P(('dp', 'fsdp'))
- copy_value: bfloat16 [1280, 256], P(('dp', 'fsdp'))
- copy_out: bfloat16 [1024, 1280], P(('dp', 'fsdp'))
- copy_gate: bfloat16 [1280, 3072], P(('dp', 'fsdp'))
- copy_up: bfloat16 [1280, 3072], P(('dp', 'fsdp'))
- copy_down: bfloat16 [3072, 1280], P(('dp', 'fsdp'))
- second_query: float32 [1280, 1024], P(('dp', 'fsdp'))
- second_key: float32 [1280, 256], P(('dp', 'fsdp'))
- second_value: float32 [1280, 256], P(('dp', 'fsdp'))
- second_out: float32 [1024, 1280], P(('dp', 'fsdp'))
- second_gate: float32 [1280, 3072], P(('dp', 'fsdp'))
- second_up: float32 [1280, 3072], P(('dp', 'fsdp'))
- second_down: float32 [3072, 1280], P(('dp', 'fsdp'))
- second_gains: float32 [2688], replicated
The draws below stay inside these ranges and needn't reach their ends.
Inputs may be any that keep to these rules, and one draw needn't show every extreme that they name: `segment_ids`: along each row the ids never fall, so that each document is one run of positions.
All inputs are finite; a program needn't handle non-finite values.
Results may differ from the reference program's by a relative error of at most 0.014.
Values may be sent and summed in bfloat16 or wider, within the bound.
A program may use at most 256 MiB of HBM per device.

```python
import math
import jax
import jax.numpy as jnp
import numpy as np
from jax import lax

D = 1280
HQ = 16
KV = 4
HD = 64
FF = 3072
ROW = 160
DOCS = 4
STEP = 10
ROWS = 64
GAINS = 2688


def draw_cotangent(key, part):
    noise_key, jitter_key = jax.random.split(jax.random.fold_in(key, 11))
    place = (jnp.arange(ROWS, dtype=jnp.float32) + 0.5) / ROWS
    base = jnp.clip(jax.random.normal(noise_key, (ROWS, ROW, D), jnp.float32), -4.0, 4.0)
    profile = 3.0 ** place
    jitter = jax.random.uniform(jitter_key, (ROWS, 1, 1), jnp.float32, 0.8, 1.25)
    return (base * profile[:, None, None] * jitter).astype(jnp.bfloat16)


def draw_gains(key, part):
    first_key, second_key = jax.random.split(jax.random.fold_in(key, 23))
    place = (jnp.arange(D, dtype=jnp.float32) + 0.5) / D
    profile = 0.6 * 3.0 ** place
    spread = jax.random.uniform(first_key, (2, D), jnp.float32, 0.85, 1.15)
    heads = jax.random.uniform(second_key, (2 * HD,), jnp.float32, 0.8, 1.25)
    return jnp.concatenate([(profile[None, :] * spread).reshape(2 * D), heads])


def with_spikes(values, rng, source, target, parts, factor):
    def block_of(position):
        return (jnp.arange(values.shape[position]) // (values.shape[position] // parts)).reshape((-1,) + (1,) * (values.ndim - 1 - position))

    near = jax.random.permutation(rng, parts)[block_of(target)]
    other_side = (block_of(target) + parts // 2) % parts
    return jnp.where((block_of(source) == near) | (block_of(source) == other_side), factor * values, values)


def block_levels(stream_key, shape, cuts, low, top_value):
    def one(position, parts):
        steps = jax.random.uniform(jax.random.fold_in(jax.random.fold_in(stream_key, 6), position), (parts,), jnp.float32, low / len(cuts), top_value / len(cuts))
        return jnp.repeat(jnp.exp(steps), shape[position] // parts).reshape((-1,) + (1,) * (len(shape) - position - 1))

    loudness = one(*cuts[0])
    for cut in cuts[1:]:
        loudness = loudness * one(*cut)
    return loudness


def length_profile(number_of, total, most, lean):
    loads = [(1 << 20) // math.isqrt(standing ** lean) + 1 for standing in range(2, number_of + 1)]
    surplus, holding = total - most - (number_of - 1), [1] * (number_of - 1)
    while surplus > 0:
        movable = [i for i in range(number_of - 1) if holding[i] < most]
        pool, left = sum([loads[i] for i in movable]), surplus
        for i in movable:
            more = min(most - holding[i], max(1, left * loads[i] // pool), surplus)
            holding[i] = holding[i] + more
            surplus = surplus - more
    return np.array([most] + holding)


def uneven(stream_key, count, total, limit, skew):
    if count == 2:
        one = jax.random.randint(stream_key, (), max(1, total - limit), min(limit, total - 1) + 1)
        return jnp.stack([one, total - one])
    lengths = jnp.asarray(length_profile(count, total, limit, skew), jnp.int32)
    couples = (count - 1) // 2
    donor, sink = lengths[1:1 + 2 * couples:2], lengths[2:2 + 2 * couples:2]
    room = jnp.minimum(donor - 1, limit - sink)
    passed = jax.random.randint(jax.random.fold_in(stream_key, 1), (couples,), 0, 1 << 20) % (room + 1)
    lengths = lengths.at[1:1 + 2 * couples:2].set(donor - passed).at[2:2 + 2 * couples:2].set(sink + passed)
    return lengths[jax.random.permutation(jax.random.fold_in(stream_key, 2), count)]


def noise(rng, shape, deviation, limit, shards=(), kind=jnp.bfloat16):
    drawn = deviation * jax.random.normal(rng, shape, jnp.float32)
    if shards:
        drawn = drawn * block_levels(rng, shape, shards, -0.22, 0.18)
    return jnp.clip(drawn, -limit, limit).astype(kind)


def bell_draw_with(stream_key, extent, width, limit, pieces, heavy, kind=jnp.bfloat16):
    values = width * jax.random.normal(stream_key, extent, jnp.float32)
    if pieces:
        values = values * block_levels(stream_key, extent, pieces, -0.22, 0.18)
    return jnp.clip(with_spikes(values, jax.random.fold_in(stream_key, 3), *heavy), -limit, limit).astype(kind)


def setup_inputs(seed: int = 0) -> dict:
    splits = jax.random.split(jax.random.key(seed), 28)
    return {
        "tokens": bell_draw_with(splits[0], (ROWS, ROW, D), 1.0, 6.0, ((0, 32),), (0, 2, 32, 2.75)),
        "cotangent": draw_cotangent(jax.random.fold_in(splits[27], 71), 0),
        "segment_ids": jax.vmap(lambda own: jnp.searchsorted(jnp.cumsum(uneven(own, DOCS, ROW, ROW // 2, 2)), jnp.arange(ROW), side="right"))(jax.random.split(splits[2], ROWS)).reshape((ROWS, ROW)).astype(jnp.int32),
        "w_query": noise(splits[3], (D, HQ * HD), D ** -0.5, 0.15625, ((0, 32),), jnp.float32),
        "w_key": noise(splits[4], (D, KV * HD), D ** -0.5, 0.15625, ((0, 32),), jnp.float32),
        "w_value": noise(splits[5], (D, KV * HD), D ** -0.5, 0.15625, ((0, 32),), jnp.float32),
        "w_out": noise(splits[6], (HQ * HD, D), (HQ * HD // 8) ** -0.5, 0.5, ((0, 32),), jnp.float32),
        "w_gate": noise(splits[7], (D, FF), D ** -0.5, 0.15625, ((0, 32),), jnp.float32),
        "w_up": noise(splits[8], (D, FF), D ** -0.5, 0.15625, ((0, 32),), jnp.float32),
        "w_down": noise(splits[9], (FF, D), FF ** -0.5, 0.109375, ((0, 32),), jnp.float32),
        "m_query": noise(splits[10], (D, HQ * HD), (0.1 * (D * HQ * HD * 0.9189 + D * KV * HD * 6.5 + D * FF * 0.6192 + (2 * D + 2 * HD) * 4.0) ** -0.5), 0.00024414062, ((0, 32),), jnp.float32),
        "m_key": noise(splits[11], (D, KV * HD), (0.189 * (D * HQ * HD * 0.9189 + D * KV * HD * 6.5 + D * FF * 0.6192 + (2 * D + 2 * HD) * 4.0) ** -0.5), 0.00048828125, ((0, 32),), jnp.float32),
        "m_value": noise(splits[12], (D, KV * HD), (0.211 * (D * HQ * HD * 0.9189 + D * KV * HD * 6.5 + D * FF * 0.6192 + (2 * D + 2 * HD) * 4.0) ** -0.5), 0.00048828125, ((0, 32),), jnp.float32),
        "m_out": noise(splits[13], (HQ * HD, D), (0.0366 * (D * HQ * HD * 0.9189 + D * KV * HD * 6.5 + D * FF * 0.6192 + (2 * D + 2 * HD) * 4.0) ** -0.5), 9.1552734375e-05, ((0, 32),), jnp.float32),
        "m_gate": noise(splits[14], (D, FF), (0.04 * (D * HQ * HD * 0.9189 + D * KV * HD * 6.5 + D * FF * 0.6192 + (2 * D + 2 * HD) * 4.0) ** -0.5), 0.00010681152, ((0, 32),), jnp.float32),
        "m_up": noise(splits[15], (D, FF), (0.04 * (D * HQ * HD * 0.9189 + D * KV * HD * 6.5 + D * FF * 0.6192 + (2 * D + 2 * HD) * 4.0) ** -0.5), 0.00010681152, ((0, 32),), jnp.float32),
        "m_down": noise(splits[16], (FF, D), (0.0667 * (D * HQ * HD * 0.9189 + D * KV * HD * 6.5 + D * FF * 0.6192 + (2 * D + 2 * HD) * 4.0) ** -0.5), 0.00015258789, ((0, 32),), jnp.float32),
        "v_query": jnp.clip(jnp.exp(math.log(2.941234455988706e-08) - 1.3839442 * jax.random.uniform(splits[17], (D, HQ * HD), jnp.float32) ** block_levels(splits[17], (D, HQ * HD), ((0, 32),), -0.2, 0.2)), 7.370387411498314e-09, 2.941234455988706e-08),
        "v_key": jnp.clip(jnp.exp(math.log(1.0519238458073232e-07) - 1.3862944 * jax.random.uniform(splits[18], (D, KV * HD), jnp.float32) ** block_levels(splits[18], (D, KV * HD), ((0, 32),), -0.2, 0.2)), 2.629809614518308e-08, 1.0519238458073232e-07),
        "v_value": jnp.clip(jnp.exp(math.log(1.314904807259154e-07) - 1.3862944 * jax.random.uniform(splits[19], (D, KV * HD), jnp.float32) ** block_levels(splits[19], (D, KV * HD), ((0, 32),), -0.2, 0.2)), 3.287262018147885e-08, 1.314904807259154e-07),
        "v_out": jnp.clip(jnp.exp(math.log(3.962015604486169e-09) - 1.3854214 * jax.random.uniform(splits[20], (HQ * HD, D), jnp.float32) ** block_levels(splits[20], (HQ * HD, D), ((0, 32),), -0.2, 0.2)), 9.913689869023301e-10, 3.962015604486169e-09),
        "v_gate": jnp.clip(jnp.exp(math.log(4.723276436635615e-09) - 1.38702724 * jax.random.uniform(splits[21], (D, FF), jnp.float32) ** block_levels(splits[21], (D, FF), ((0, 32),), -0.2, 0.2)), 1.1799540233781158e-09, 4.723276436635615e-09),
        "v_up": jnp.clip(jnp.exp(math.log(4.723276436635615e-09) - 1.38702724 * jax.random.uniform(splits[22], (D, FF), jnp.float32) ** block_levels(splits[22], (D, FF), ((0, 32),), -0.2, 0.2)), 1.1799540233781158e-09, 4.723276436635615e-09),
        "v_down": jnp.clip(jnp.exp(math.log(1.3097143813922685e-08) - 1.3876162 * jax.random.uniform(splits[23], (FF, D), jnp.float32) ** block_levels(splits[23], (FF, D), ((0, 32),), -0.2, 0.2)), 3.2699607466213365e-09, 1.3097143813922685e-08),
        "gains": draw_gains(jax.random.fold_in(splits[27], 71), 0),
        "gain_first": noise(splits[25], (GAINS,), (0.222 * (D * HQ * HD * 0.9189 + D * KV * HD * 6.5 + D * FF * 0.6192 + (2 * D + 2 * HD) * 4.0) ** -0.5), 0.00048828125, (), jnp.float32),
        "gain_second": jnp.clip(jnp.exp(jax.random.uniform(splits[26], (GAINS,), jnp.float32, math.log(3.633289580307064e-08), math.log(1.4533158321228257e-07))), 3.633289580307064e-08, 1.4533158321228257e-07),
    }


norm_eps = 1e-05
rope_base = 10000.0
beta_one = 0.9
beta_two = 0.95
adam_eps = 1e-08
decay_rate = 0.1
clip_limit = 1.0
gain_rate = 0.4
masked_score = -1e+30

@jax.custom_vjp
def low(v):
    return lax.optimization_barrier(v.astype(jnp.bfloat16)).astype(jnp.float32)

@jax.custom_vjp
def low_back(v):
    return v

def low_keep(v):
    return (low(v), None)

def low_pass(kept, grad):
    return (grad,)

def back_keep(v):
    return (v, None)

def back_low(kept, grad):
    return (low(grad),)
low.defvjp(low_keep, low_pass)
low_back.defvjp(back_keep, back_low)

def rms_scale(values, gain):
    return values * lax.rsqrt(lax.optimization_barrier(jnp.mean(values * values, -1, keepdims=True)) + norm_eps) * gain

def rotary_tables(length, size):
    half = size // 2
    frequency = rope_base ** (-jnp.arange(half, dtype=jnp.float32) * 2.0 / size)
    angles = jnp.arange(length, dtype=jnp.float32)[:, None] * frequency[None, :]
    return (jnp.cos(angles), jnp.sin(angles))

def rotate(vectors, cosine, sine):
    half = vectors.shape[-1] // 2
    first = vectors[..., :half]
    second = vectors[..., half:]
    cosine = cosine[:, None, :]
    sine = sine[:, None, :]
    return jnp.concatenate([first * cosine - second * sine, second * cosine + first * sine], -1)

def head_norm(raw, gain, cosine, sine):
    size = gain.shape[0]
    shaped = raw.reshape(raw.shape[:-1] + (raw.shape[-1] // size, size))
    return rotate(rms_scale(shaped, gain), cosine, sine)

def product(left, right):
    return jnp.matmul(left, right, precision=lax.Precision.HIGHEST)

def block_rows(rounded, gains, rows_in, segment_rows, cosine, sine):
    w_query, w_key, w_value, w_out, w_gate, w_up, w_down = rounded
    gain_attn = gains[:D]
    gain_ffn = gains[D:2 * D]
    gain_query = gains[2 * D:2 * D + HD]
    gain_key = gains[2 * D + HD:]
    groups = rows_in.shape[0]
    length = rows_in.shape[1]
    normed = low(rms_scale(rows_in, gain_attn))
    query_raw = low_back(product(normed, w_query))
    key_raw = low_back(product(normed, w_key))
    value_all = low(low_back(product(normed, w_value)))
    queries = low(head_norm(query_raw, gain_query, cosine, sine))
    keys = low(head_norm(key_raw, gain_key, cosine, sine))
    queries = queries.reshape(groups, length, KV, HQ // KV, HD)
    values = value_all.reshape(groups, length, KV, HD)
    scores = jnp.einsum('glkrd,gmkd->gkrlm', queries, keys, precision=lax.Precision.HIGHEST) * HD ** (-0.5)
    scores = low_back(scores)
    positions = jnp.arange(length)
    causal = positions[None, :] <= positions[:, None]
    allowed = causal[None] & (segment_rows[:, :, None] == segment_rows[:, None, :])
    scores = jnp.where(allowed[:, None, None], scores, masked_score)
    attention = low(jax.nn.softmax(scores, axis=-1))
    mixed = jnp.einsum('gkrlm,gmkd->glkrd', attention, values, precision=lax.Precision.HIGHEST)
    mixed = low(low_back(mixed.reshape(groups, length, HQ * HD)))
    hidden_in = rows_in + low_back(product(mixed, w_out))
    ffn_in = low(rms_scale(hidden_in, gain_ffn))
    gate = low_back(product(ffn_in, w_gate))
    upper = low_back(product(ffn_in, w_up))
    hidden = low(jax.nn.silu(gate) * upper)
    return hidden_in + low_back(product(hidden, w_down))

def adam_update(master, first, second, grad, rate, decay):
    first_new = beta_one * first + (1.0 - beta_one) * grad
    second_new = beta_two * second + (1.0 - beta_two) * grad * grad
    first_hat = first_new / (1.0 - beta_one ** STEP)
    second_hat = second_new / (1.0 - beta_two ** STEP)
    master_new = master - rate * (first_hat / (jnp.sqrt(second_hat) + adam_eps) + decay * master)
    return (master_new, second_new)

def reference(tokens, cotangent, segment_ids, w_query, w_key, w_value, w_out, w_gate, w_up, w_down, m_query, m_key, m_value, m_out, m_gate, m_up, m_down, v_query, v_key, v_value, v_out, v_gate, v_up, v_down, gains, gain_first, gain_second):
    masters = (w_query, w_key, w_value, w_out, w_gate, w_up, w_down)
    firsts = (m_query, m_key, m_value, m_out, m_gate, m_up, m_down)
    seconds = (v_query, v_key, v_value, v_out, v_gate, v_up, v_down)
    cosine, sine = rotary_tables(ROW, HD)
    group = math.gcd(ROWS, 16)

    def layer(weights, gain_values, inputs):
        rounded = tuple((low(weight) for weight in weights))
        blocked_in = inputs.reshape(ROWS // group, group, ROW, D)
        blocked_ids = segment_ids.reshape(ROWS // group, group, ROW)

        def one_block(pair):
            return block_rows(rounded, gain_values, pair[0], pair[1], cosine, sine)
        results = lax.map(jax.checkpoint(one_block), (blocked_in, blocked_ids))
        return results.reshape(ROWS, ROW, D)
    output, pullback = jax.vjp(layer, masters, gains, tokens.astype(jnp.float32))
    weight_grads, gain_grad, input_grad = pullback(cotangent.astype(jnp.float32))
    squares = sum((jnp.sum(grad * grad) for grad in weight_grads)) + jnp.sum(gain_grad * gain_grad)
    total_norm = jnp.sqrt(squares)
    factor = jnp.minimum(1.0, clip_limit / (total_norm + 1e-06))
    clipped = tuple((grad * factor for grad in weight_grads))
    gain_clipped = gain_grad * factor
    weight_rate = 2.0 * D ** (-0.5)
    updates = [adam_update(masters[index], firsts[index], seconds[index], clipped[index], weight_rate, decay_rate) for index in range(7)]
    new_masters = tuple((item[0] for item in updates))
    new_seconds = tuple((item[1] for item in updates))
    new_gains, gain_seconds = adam_update(gains, gain_first, gain_second, gain_clipped, gain_rate, 0.0)
    copies = tuple((item.astype(jnp.bfloat16) for item in new_masters))
    return (output.astype(jnp.bfloat16), input_grad.astype(jnp.bfloat16)) + clipped + (gain_clipped, total_norm) + new_masters + (new_gains,) + copies + new_seconds + (gain_seconds,)
```

```python
import functools

import jax
import jax.numpy as jnp
from jax import lax
from jax.sharding import PartitionSpec as P

D = 1280
HQ = 16
KV = 4
HD = 64
STEP = 10
MEMBERS = 4

norm_eps = 1e-05
rope_base = 10000.0
beta_one = 0.9
beta_two = 0.95
adam_eps = 1e-08
decay_rate = 0.1
clip_limit = 1.0
gain_rate = 0.4
masked_score = -1e30

AXES = ("dp", "fsdp")


def rms_scale(values, gain):
    return values * lax.rsqrt(jnp.mean(values * values, -1, keepdims=True) + norm_eps) * gain


def rotary_tables(length, size):
    half = size // 2
    frequency = rope_base ** (-jnp.arange(half, dtype=jnp.float32) * 2.0 / size)
    angles = jnp.arange(length, dtype=jnp.float32)[:, None] * frequency[None, :]
    return (jnp.cos(angles), jnp.sin(angles))


def rotate(vectors, cosine, sine):
    half = vectors.shape[-1] // 2
    first = vectors[..., :half]
    second = vectors[..., half:]
    cosine = cosine[:, None, :]
    sine = sine[:, None, :]
    return jnp.concatenate([first * cosine - second * sine, second * cosine + first * sine], -1)


def head_norm(raw, gain, cosine, sine):
    size = gain.shape[0]
    shaped = raw.reshape(raw.shape[:-1] + (raw.shape[-1] // size, size))
    return rotate(rms_scale(shaped, gain), cosine, sine)


def swiglu(gate, upper):
    return jax.nn.silu(gate) * upper


def forward_product(left, right):
    return jnp.dot(left, right, preferred_element_type=jnp.float32)


def weight_product(left, right):
    return lax.dot_general(
        left, right, (((0,), (0,)), ((), ())), preferred_element_type=jnp.float32
    )


def back_product(left, right):
    return lax.dot_general(
        left, right, (((1,), (1,)), ((), ())), preferred_element_type=jnp.float32
    )


def adam_update(master, first, second, grad, rate, decay):
    first_new = beta_one * first + (1.0 - beta_one) * grad
    second_new = beta_two * second + (1.0 - beta_two) * grad * grad
    first_hat = first_new / (1.0 - beta_one**STEP)
    second_hat = second_new / (1.0 - beta_two**STEP)
    master_new = master - rate * (first_hat / (jnp.sqrt(second_hat) + adam_eps) + decay * master)
    return (master_new, second_new)


def put(buffer, block, axis, index):
    return lax.dynamic_update_index_in_dim(buffer, block, index, axis)


def pick(array, axis, index):
    return lax.dynamic_index_in_dim(array, index, axis, keepdims=False)


class Ring:
    def __init__(self, extent, place, target, nd, nf):
        self.extent = extent
        self.place = place
        self.target = target
        self.nd = nd
        self.nf = nf

    def move(self, block, step):
        pairs = []
        for d in range(self.nd):
            for f in range(self.nf):
                d2, f2 = self.target(d, f, step)
                pairs.append((d * self.nf + f, d2 * self.nf + f2))
        return lax.ppermute(block, AXES, pairs)

    def source(self, step):
        return lax.rem(self.place - step + self.extent, self.extent)

    def dest(self, step):
        return lax.rem(self.place + step, self.extent)

    def gather(self, block, axis):
        shape = block.shape[:axis] + (self.extent,) + block.shape[axis:]
        full = put(jnp.zeros(shape, block.dtype), block, axis, self.place)
        for step in range(1, self.extent):
            full = put(full, self.move(block, step), axis, self.source(step))
        return full

    def reduce(self, terms, axis):
        total = pick(terms, axis, self.place).astype(jnp.float32)
        for step in range(1, self.extent):
            got = self.move(pick(terms, axis, self.dest(step)), step)
            total = total + got.astype(jnp.float32)
        return total


def after(value, *others):
    return lax.optimization_barrier((value,) + others)[0]


def low(value):
    return value.astype(jnp.bfloat16)


def shards(
    nd,
    nf,
    tokens,
    cotangent,
    segment_ids,
    w_query,
    w_key,
    w_value,
    w_out,
    w_gate,
    w_up,
    w_down,
    m_query,
    m_key,
    m_value,
    m_out,
    m_gate,
    m_up,
    m_down,
    v_query,
    v_key,
    v_value,
    v_out,
    v_gate,
    v_up,
    v_down,
    gains,
    gain_first,
    gain_second,
):
    masters = (w_query, w_key, w_value, w_out, w_gate, w_up, w_down)
    firsts = (m_query, m_key, m_value, m_out, m_gate, m_up, m_down)
    seconds = (v_query, v_key, v_value, v_out, v_gate, v_up, v_down)
    outer = nd // MEMBERS
    dp = lax.axis_index("dp")
    ring_z = Ring(nf, lax.axis_index("fsdp"), lambda d, f, s: (d, (f + s) % nf), nd, nf)
    ring_y = Ring(
        outer,
        dp // MEMBERS,
        lambda d, f, s: ((d // MEMBERS + s) % outer * MEMBERS + d % MEMBERS, f),
        nd,
        nf,
    )
    ring_x = Ring(2, dp // 2 % 2, lambda d, f, s: (d ^ 2, f), nd, nf)
    ring_core = Ring(2, dp % 2, lambda d, f, s: (d ^ 1, f), nd, nf)
    member = dp % MEMBERS

    def trade(block, mask):
        return Ring(2, dp % 2, lambda d, f, s: (d ^ mask, f), nd, nf).move(block, 1)

    def swap(blocks):
        full = put(jnp.zeros_like(blocks), pick(blocks, 0, member), 0, member)
        for mask in range(1, MEMBERS):
            full = put(full, trade(pick(blocks, 0, member ^ mask), mask), 0, member ^ mask)
        return full

    def spread(rows):
        return ring_core.gather(ring_x.gather(rows, 0), 1)

    def collapse(terms):
        half = low(ring_core.reduce(terms, 1))
        return ring_x.reduce(half, 0)

    batch, length, width = tokens.shape
    count = batch * length
    hidden_rows = w_down.shape[0]
    hidden_all = w_gate.shape[1]
    span = nf * hidden_rows
    mine = outer * span
    in_rows = w_query.shape[0]
    out_rows = w_out.shape[0]
    attn_cols = (HQ + 2 * KV) * HD

    shard_in = jnp.concatenate([low(w_query), low(w_key), low(w_value)], 1)
    shard_out = low(w_out)
    in_z = ring_z.gather(shard_in, 0)
    out_z = ring_z.gather(shard_out, 0)
    in_xy = ring_x.gather(ring_y.gather(in_z, 0), 1)
    out_xy = ring_y.gather(ring_x.gather(out_z, 0), 0)
    in_w = ring_core.gather(in_xy, 2).reshape(D, attn_cols)
    out_w = ring_core.gather(out_xy, 2).reshape(HQ * HD, D)

    def member_columns(weight):
        return low(weight).reshape(in_rows, outer, MEMBERS, span).transpose(2, 0, 1, 3)

    columns = jnp.concatenate(
        [
            member_columns(w_gate).reshape(MEMBERS, in_rows, mine),
            member_columns(w_up).reshape(MEMBERS, in_rows, mine),
        ],
        2,
    )
    inner = swap(columns)
    inner = after(inner, in_z, out_z)
    inner_z = ring_z.gather(inner, 1)
    inner_w = ring_y.gather(inner_z, 0).reshape(D, 2 * mine)
    shard_down = after(low(w_down), inner_z)
    down_z = ring_z.gather(shard_down, 0)
    down_w = ring_y.gather(down_z, 0).reshape(mine, D)

    back_in = cotangent.reshape(count, width)
    back_all = spread(after(back_in, in_xy)).reshape(MEMBERS * count, width)

    cosine, sine = rotary_tables(length, HD)
    scale = HD ** (-0.5)
    group_size = HQ // KV
    gain_attn = gains[:D]
    gain_ffn = gains[D : 2 * D]
    gain_query = gains[2 * D : 2 * D + HD]
    gain_key = gains[2 * D + HD :]
    positions = jnp.arange(length)
    causal = positions[None, :] <= positions[:, None]
    allowed = causal[None] & (segment_ids[:, :, None] == segment_ids[:, None, :])
    allowed = allowed[:, None, None]

    def piece(raw, gain):
        return head_norm(raw.reshape(batch, length, -1), gain, cosine, sine)

    inputs = tokens.reshape(count, width).astype(jnp.float32)
    normed = low(rms_scale(inputs, gain_attn))
    raw = forward_product(normed, in_w)
    query_raw = raw[:, : HQ * HD]
    key_raw = raw[:, HQ * HD : (HQ + KV) * HD]
    values = low(raw[:, (HQ + KV) * HD :]).reshape(batch, length, KV, HD)
    queries = low(piece(query_raw, gain_query)).reshape(batch, length, KV, group_size, HD)
    keys = low(piece(key_raw, gain_key))
    scores = (
        jnp.einsum("blkrd,bmkd->bkrlm", queries, keys, preferred_element_type=jnp.float32) * scale
    )
    scores = jnp.where(allowed, scores, masked_score)
    top = jnp.max(scores, -1, keepdims=True)
    weights = jnp.exp(scores - top)
    attention_full = weights / jnp.sum(weights, -1, keepdims=True)
    attention = low(attention_full)
    mixed = jnp.einsum("bkrlm,bmkd->blkrd", attention, values, preferred_element_type=jnp.float32)
    mixed = low(mixed.reshape(count, HQ * HD))
    hidden_in = inputs + forward_product(mixed, out_w)

    ffn_all = spread(low(rms_scale(hidden_in, gain_ffn))).reshape(MEMBERS * count, width)
    inner_out = forward_product(ffn_all, inner_w)
    gate = inner_out[:, :mine]
    upper = inner_out[:, mine:]
    hidden = low(swiglu(gate, upper))
    down_terms = low(weight_product(hidden, back_all)).reshape(outer, nf, hidden_rows, width)
    down_sum = ring_z.reduce(low(ring_y.reduce(down_terms, 0)), 0)
    grad_hidden = back_product(back_all, down_w)
    _, swiglu_pull = jax.vjp(swiglu, gate, upper)
    grad_gate, grad_upper = swiglu_pull(grad_hidden)
    grad_inner = jnp.concatenate([low(grad_gate), low(grad_upper)], 1)
    grad_ffn_terms = low(back_product(grad_inner, inner_w)).reshape(2, 2, count, width)
    grad_ffn = collapse(grad_ffn_terms)
    inner_terms = low(weight_product(ffn_all, grad_inner)).reshape(
        outer, MEMBERS, nf, in_rows, 2 * mine
    )
    inner_sum = ring_z.reduce(low(ring_y.reduce(inner_terms, 0)), 1)
    inner_sum = swap(low(inner_sum)).astype(jnp.float32)
    inner_sum = inner_sum.reshape(MEMBERS, in_rows, 2, outer, span).transpose(2, 1, 3, 0, 4)
    inner_sum = inner_sum.reshape(2, in_rows, hidden_all)
    down_out = low(forward_product(hidden, down_w)).reshape(2, 2, count, width)
    output = low(hidden_in + collapse(down_out))

    _, ffn_pull = jax.vjp(rms_scale, hidden_in, gain_ffn)
    grad_hidden_in, grad_gain_ffn = ffn_pull(grad_ffn)
    grad_hidden_in = grad_hidden_in + back_in.astype(jnp.float32)
    grad_branch = low(grad_hidden_in)
    out_terms = low(weight_product(mixed, grad_branch)).reshape(
        outer, 2, 2, nf, out_rows, width
    )
    out_sum = low(ring_core.reduce(out_terms, 2))
    out_sum = low(ring_x.reduce(low(ring_y.reduce(out_sum, 0)), 0))
    out_sum = ring_z.reduce(out_sum, 0)
    grad_mixed = low(back_product(grad_branch, out_w)).reshape(batch, length, KV, group_size, HD)
    grad_attention = jnp.einsum(
        "blkrd,bmkd->bkrlm", grad_mixed, values, preferred_element_type=jnp.float32
    )
    grad_scores = low(
        attention_full
        * (grad_attention - jnp.sum(attention_full * grad_attention, -1, keepdims=True))
    )
    grad_values = jnp.einsum(
        "bkrlm,blkrd->bmkd", attention, grad_mixed, preferred_element_type=jnp.float32
    )
    grad_values = low(grad_values.reshape(count, KV * HD))
    grad_queries = (
        jnp.einsum("bkrlm,bmkd->blkrd", grad_scores, keys, preferred_element_type=jnp.float32)
        * scale
    )
    grad_keys = (
        jnp.einsum("bkrlm,blkrd->bmkd", grad_scores, queries, preferred_element_type=jnp.float32)
        * scale
    )
    _, query_pull = jax.vjp(piece, query_raw, gain_query)
    grad_query_raw, grad_gain_query = query_pull(grad_queries.reshape(batch, length, HQ, HD))
    _, key_pull = jax.vjp(piece, key_raw, gain_key)
    grad_key_raw, grad_gain_key = key_pull(grad_keys)
    grad_raw = jnp.concatenate([low(grad_query_raw), low(grad_key_raw), grad_values], 1)
    in_terms = low(weight_product(normed, grad_raw)).reshape(
        outer, 2, 2, nf, in_rows, attn_cols
    )
    in_sum = low(ring_core.reduce(in_terms, 2))
    in_sum = low(ring_y.reduce(low(ring_x.reduce(in_sum, 1)), 0))
    in_sum = ring_z.reduce(in_sum, 0)
    grad_normed = back_product(grad_raw, in_w)
    _, attn_pull = jax.vjp(rms_scale, inputs, gain_attn)
    grad_inputs, grad_gain_attn = attn_pull(grad_normed)
    input_grad = low(grad_inputs + grad_hidden_in)
    gain_terms = jnp.concatenate([grad_gain_attn, grad_gain_ffn, grad_gain_query, grad_gain_key])

    reduced = (
        in_sum[:, : HQ * HD],
        in_sum[:, HQ * HD : (HQ + KV) * HD],
        in_sum[:, (HQ + KV) * HD :],
        out_sum,
        inner_sum[0],
        inner_sum[1],
        down_sum,
    )
    local_squares = (
        jnp.sum(in_sum * in_sum)
        + jnp.sum(out_sum * out_sum)
        + jnp.sum(inner_sum * inner_sum)
        + jnp.sum(down_sum * down_sum)
    )
    gain_total = lax.psum(gain_terms, AXES)
    square_total = lax.psum(local_squares, AXES)
    total_norm = jnp.sqrt(square_total + jnp.sum(gain_total * gain_total))
    factor = jnp.minimum(1.0, clip_limit / (total_norm + 1e-06))
    clipped = tuple((share * factor for share in reduced))
    gain_clipped = gain_total * factor
    weight_rate = 2.0 * D ** (-0.5)
    updates = [
        adam_update(
            masters[index], firsts[index], seconds[index], clipped[index], weight_rate, decay_rate
        )
        for index in range(7)
    ]
    new_masters = tuple((item[0] for item in updates))
    new_seconds = tuple((item[1] for item in updates))
    new_gains, gain_seconds = adam_update(
        gains, gain_first, gain_second, gain_clipped, gain_rate, 0.0
    )
    copies = tuple((low(item) for item in new_masters))
    return (
        (output.reshape(tokens.shape), input_grad.reshape(tokens.shape))
        + clipped
        + (gain_clipped, total_norm)
        + new_masters
        + (new_gains,)
        + copies
        + new_seconds
        + (gain_seconds,)
    )


def solution(mesh):
    rows3 = P(AXES, None, None)
    rows2 = P(AXES, None)
    whole = P()
    return jax.shard_map(
        functools.partial(shards, mesh.shape["dp"], mesh.shape["fsdp"]),
        mesh=mesh,
        in_specs=(rows3, rows3) + (rows2,) * 22 + (whole,) * 3,
        out_specs=(rows3, rows3)
        + (rows2,) * 7
        + (whole, whole)
        + (rows2,) * 7
        + (whole,)
        + (rows2,) * 14
        + (whole,),
        check_vma=False,
    )
```

```python
import functools

import jax
import jax.numpy as jnp
from jax import lax
from jax.experimental import pallas as pl
from jax.experimental.pallas import tpu as pltpu
from jax.sharding import PartitionSpec as P

D = 1280
HQ = 16
KV = 4
HD = 64
STEP = 10
MEMBERS = 4

norm_eps = 1e-05
rope_base = 10000.0
beta_one = 0.9
beta_two = 0.95
adam_eps = 1e-08
decay_rate = 0.1
clip_limit = 1.0
gain_rate = 0.4
masked_score = -1e30

AXES = ("dp", "fsdp")
LANES = 128
MESH = pl.DeviceIdType.MESH
ANYWHERE = pl.BlockSpec(memory_space=pl.ANY)
ON_CHIP = pl.BlockSpec(memory_space=pltpu.VMEM)


def rms_scale(values, gain):
    return values * lax.rsqrt(jnp.mean(values * values, -1, keepdims=True) + norm_eps) * gain


def rotary_tables(length, size):
    half = size // 2
    frequency = rope_base ** (-jnp.arange(half, dtype=jnp.float32) * 2.0 / size)
    angles = jnp.arange(length, dtype=jnp.float32)[:, None] * frequency[None, :]
    return (jnp.cos(angles), jnp.sin(angles))


def rotate(vectors, cosine, sine):
    half = vectors.shape[-1] // 2
    first = vectors[..., :half]
    second = vectors[..., half:]
    cosine = cosine[:, None, :]
    sine = sine[:, None, :]
    return jnp.concatenate([first * cosine - second * sine, second * cosine + first * sine], -1)


def head_norm(raw, gain, cosine, sine):
    size = gain.shape[0]
    shaped = raw.reshape(raw.shape[:-1] + (raw.shape[-1] // size, size))
    return rotate(rms_scale(shaped, gain), cosine, sine)


def swiglu(gate, upper):
    return jax.nn.silu(gate) * upper


def forward_product(left, right):
    return jnp.dot(left, right, preferred_element_type=jnp.float32)


def weight_product(left, right):
    return lax.dot_general(
        left, right, (((0,), (0,)), ((), ())), preferred_element_type=jnp.float32
    )


def back_product(left, right):
    return lax.dot_general(
        left, right, (((1,), (1,)), ((), ())), preferred_element_type=jnp.float32
    )


def adam_update(master, first, second, grad, rate, decay):
    first_new = beta_one * first + (1.0 - beta_one) * grad
    second_new = beta_two * second + (1.0 - beta_two) * grad * grad
    first_hat = first_new / (1.0 - beta_one**STEP)
    second_hat = second_new / (1.0 - beta_two**STEP)
    master_new = master - rate * (first_hat / (jnp.sqrt(second_hat) + adam_eps) + decay * master)
    return (master_new, second_new)


def put(buffer, block, axis, index):
    return lax.dynamic_update_index_in_dim(buffer, block, index, axis)


def pick(array, axis, index):
    return lax.dynamic_index_in_dim(array, index, axis, keepdims=False)


class Ring:
    def __init__(self, extent, place, target, nd, nf):
        self.extent = extent
        self.place = place
        self.target = target
        self.nd = nd
        self.nf = nf

    def move(self, block, step):
        pairs = []
        for d in range(self.nd):
            for f in range(self.nf):
                d2, f2 = self.target(d, f, step)
                pairs.append((d * self.nf + f, d2 * self.nf + f2))
        return lax.ppermute(block, AXES, pairs)

    def source(self, step):
        return lax.rem(self.place - step + self.extent, self.extent)

    def dest(self, step):
        return lax.rem(self.place + step, self.extent)

    def gather(self, block, axis):
        shape = block.shape[:axis] + (self.extent,) + block.shape[axis:]
        full = put(jnp.zeros(shape, block.dtype), block, axis, self.place)
        for step in range(1, self.extent):
            full = put(full, self.move(block, step), axis, self.source(step))
        return full

    def reduce(self, terms, axis):
        total = pick(terms, axis, self.place).astype(jnp.float32)
        for step in range(1, self.extent):
            got = self.move(pick(terms, axis, self.dest(step)), step)
            total = total + got.astype(jnp.float32)
        return total


def start_all(copies):
    for copy in copies:
        copy.start()
    return copies


def weights_kernel(
    nd,
    nf,
    in_ref,
    out_ref,
    inner_ref,
    in_w,
    out_w,
    gate_w,
    upper_x,
    z_send,
    z_recv,
    y_send,
    y_recv,
    x_send,
    x_recv,
    hop_send,
    hop_recv,
    core_send,
    core_recv,
    swap_send,
    swap_recv,
    gate_send,
    gate_recv,
    over_send,
    over_recv,
    local_sem,
):
    outer = nd // MEMBERS
    dp = lax.axis_index("dp")
    z = lax.axis_index("fsdp")
    y = dp // MEMBERS
    member = dp % MEMBERS
    x = member // 2
    c = member % 2

    def z_peer(step):
        return (dp, lax.rem(z + step, nf))

    def y_peer(step):
        return (lax.rem(y + step, outer) * MEMBERS + member, z)

    def in_group(k):
        return (y * MEMBERS + k, z)

    def from_z(step):
        return lax.rem(z - step + nf, nf)

    def from_y(step):
        return lax.rem(y - step + outer, outer)

    x_peer = in_group((1 - x) * 2 + c)
    core_peer = in_group(x * 2 + 1 - c)
    barrier = pltpu.get_barrier_semaphore()
    peers = [z_peer(step) for step in range(1, nf)] + [y_peer(step) for step in range(1, outer)]
    peers += [x_peer, core_peer, in_group(MEMBERS - 1 - member)]
    for peer in peers:
        pl.semaphore_signal(barrier, inc=1, device_id=peer, device_id_type=MESH)
    pl.semaphore_wait(barrier, len(peers))

    def remote(source, target, send, recv, device):
        return pltpu.make_async_remote_copy(
            src_ref=source,
            dst_ref=target,
            send_sem=send,
            recv_sem=recv,
            device_id=device,
            device_id_type=MESH,
        )

    shards_here = (in_ref, out_ref)
    wholes = (in_w, out_w)
    sent = []

    def send(copy):
        copy.start()
        sent.append(copy)
        return copy

    local = [
        pltpu.make_async_copy(shards_here[a], wholes[a].at[y, x, c, z], local_sem.at[a])
        for a in range(2)
    ]
    start_all(local)
    z_copies = {}
    for a in range(2):
        for step in range(1, nf):
            z_copies[a, step] = send(
                remote(
                    shards_here[a],
                    wholes[a].at[y, x, c, z],
                    z_send.at[a, step],
                    z_recv.at[a, step],
                    z_peer(step),
                )
            )
    masks = (2, 1, 3)
    trades = {}
    for half, target in ((0, gate_w.at[y, :, z]), (1, upper_x)):
        for mask in masks:
            other = member ^ mask
            trades[half, mask] = send(
                remote(
                    inner_ref.at[half, other],
                    target.at[member],
                    swap_send.at[half, mask],
                    swap_recv.at[half, mask],
                    in_group(other),
                )
            )
        kept = pltpu.make_async_copy(
            inner_ref.at[half, member], target.at[member], local_sem.at[2 + half]
        )
        kept.start()
        local.append(kept)

    def block(a, step, oy=None, ox=None):
        return wholes[a].at[y if oy is None else oy, x if ox is None else ox, c, from_z(step)]

    y_copies = {}
    x_copies = {}
    for a in range(2):
        for step in range(nf):
            if step:
                z_copies[a, step].wait_recv()
            source = shards_here[a] if step == 0 else block(a, step)
            for hop in range(1, outer):
                y_copies[a, hop, step] = send(
                    remote(
                        source,
                        block(a, step),
                        y_send.at[a, hop, step],
                        y_recv.at[a, hop, step],
                        y_peer(hop),
                    )
                )
            x_copies[a, step] = send(
                remote(
                    source, block(a, step), x_send.at[a, step], x_recv.at[a, step], x_peer
                )
            )
    for mask in masks:
        trades[0, mask].wait_recv()
    local[2].wait()
    gates = {}
    gate_own = gate_w.at[y, :, z]
    for step in range(1, nf):
        gates[step] = send(
            remote(gate_own, gate_own, gate_send.at[step], gate_recv.at[step], z_peer(step))
        )
    for hop in range(1, outer):
        gates[-hop] = send(
            remote(gate_own, gate_own, over_send.at[hop], over_recv.at[hop], y_peer(hop))
        )
    hops = {}
    for step in range(nf):
        x_copies[0, step].wait_recv()
        for hop in range(1, outer):
            hops[0, hop, step] = send(
                remote(
                    block(0, step, ox=1 - x),
                    block(0, step, ox=1 - x),
                    hop_send.at[0, hop, step],
                    hop_recv.at[0, hop, step],
                    y_peer(hop),
                )
            )
    for step in range(nf):
        for hop in range(1, outer):
            y_copies[1, hop, step].wait_recv()
            hops[1, hop, step] = send(
                remote(
                    block(1, step, oy=from_y(hop)),
                    block(1, step, oy=from_y(hop)),
                    hop_send.at[1, hop, step],
                    hop_recv.at[1, hop, step],
                    x_peer,
                )
            )
    cores = {}

    def to_core(a, hop, far):
        place = wholes[a].at[y if hop == 0 else from_y(hop), 1 - x if far else x, c]
        cores[a, hop, far] = send(
            remote(
                place,
                place,
                core_send.at[a, hop, far],
                core_recv.at[a, hop, far],
                core_peer,
            )
        )

    local[0].wait()
    local[1].wait()
    for a in range(2):
        to_core(a, 0, 0)
    to_core(0, 0, 1)
    for hop in range(1, outer):
        for step in range(nf):
            y_copies[0, hop, step].wait_recv()
        to_core(0, hop, 0)
        to_core(1, hop, 0)
    for step in range(nf):
        x_copies[1, step].wait_recv()
    to_core(1, 0, 1)
    for a in range(2):
        for hop in range(1, outer):
            for step in range(nf):
                hops[a, hop, step].wait_recv()
            to_core(a, hop, 1)
    for mask in masks:
        trades[1, mask].wait_recv()
    local[3].wait()
    for key in gates:
        gates[key].wait_recv()
    for key in cores:
        cores[key].wait_recv()
    for copy in sent:
        copy.wait_send()


def gather_weights(nd, nf, shard_in, shard_out, inner):
    outer = nd // MEMBERS
    dma = pltpu.SemaphoreType.DMA
    lead = (outer, 2, 2, nf)
    low_type = jnp.bfloat16
    pairs = [(2, nf), (2, outer, nf), (2, nf), (2, outer, nf), (2, outer, 2), (2, 4), (nf,), (outer,)]
    moved = 2 * nd * nf * (shard_in.size + shard_out.size)
    return pl.pallas_call(
        functools.partial(weights_kernel, nd, nf),
        name="gather_weights",
        out_shape=(
            jax.ShapeDtypeStruct(lead + shard_in.shape, low_type),
            jax.ShapeDtypeStruct(lead + shard_out.shape, low_type),
            jax.ShapeDtypeStruct((outer, MEMBERS, nf) + inner.shape[2:], low_type),
            jax.ShapeDtypeStruct((MEMBERS,) + inner.shape[2:], low_type),
        ),
        in_specs=[ANYWHERE] * 3,
        out_specs=(ANYWHERE,) * 4,
        scratch_shapes=[dma(shape) for shape in pairs for _ in range(2)] + [dma((4,))],
        cost_estimate=pl.CostEstimate(flops=0, bytes_accessed=16 * moved, transcendentals=0),
        compiler_params=pltpu.CompilerParams(collective_id=0, has_side_effects=True),
    )(shard_in, shard_out, inner)


def totals_kernel(nd, nf, part_ref, square_ref, all_ref, pieces, own, p_send, p_recv, q_send, q_recv):
    total = nd * nf
    dp = lax.axis_index("dp")
    z = lax.axis_index("fsdp")
    me = dp * nf + z

    def device(step):
        index = lax.rem(me + step, total)
        return index, (index // nf, lax.rem(index, nf))

    barrier = pltpu.get_barrier_semaphore()

    def greet(step, carry):
        pl.semaphore_signal(barrier, inc=1, device_id=device(step)[1], device_id_type=MESH)
        return carry

    lax.fori_loop(1, total, greet, 0)
    pl.semaphore_wait(barrier, total - 1)

    def part(step):
        index, there = device(step)
        return pltpu.make_async_remote_copy(
            src_ref=part_ref.at[index],
            dst_ref=pieces.at[me],
            send_sem=p_send.at[step],
            recv_sem=p_recv.at[step],
            device_id=there,
            device_id_type=MESH,
        )

    def share(step):
        _, there = device(step)
        return pltpu.make_async_remote_copy(
            src_ref=own,
            dst_ref=all_ref.at[me],
            send_sem=q_send.at[step],
            recv_sem=q_recv.at[step],
            device_id=there,
            device_id_type=MESH,
        )

    def begin(make):
        def step_once(step, carry):
            make(step).start()
            return carry

        lax.fori_loop(1, total, step_once, 0)

    def finish(make):
        def step_once(step, carry):
            make(step).wait()
            return carry

        lax.fori_loop(1, total, step_once, 0)

    begin(part)
    pieces[me] = part_ref[me]
    finish(part)
    summed = jnp.sum(pieces[...], 0)
    own[...] = jnp.concatenate([summed[:1], square_ref[...]], 0)
    begin(share)
    all_ref[me] = own[...]
    finish(share)


def all_totals(nd, nf, parts, square):
    total = nd * nf
    parts = jnp.pad(parts[:, None, :], ((0, 0), (0, 7), (0, 0)))
    square = jnp.broadcast_to(square, (7, LANES))
    dma = pltpu.SemaphoreType.DMA
    result = pl.pallas_call(
        functools.partial(totals_kernel, nd, nf),
        name="all_totals",
        out_shape=jax.ShapeDtypeStruct((total, 8, LANES), jnp.float32),
        in_specs=[ON_CHIP] * 2,
        out_specs=ON_CHIP,
        scratch_shapes=[
            pltpu.VMEM((total, 8, LANES), jnp.float32),
            pltpu.VMEM((8, LANES), jnp.float32),
        ]
        + [dma((total,))] * 4,
        compiler_params=pltpu.CompilerParams(collective_id=1, has_side_effects=True),
    )(parts, square)
    return result[:, 0], jnp.sum(result[:, 1, 0])


def block_mean():
    row = lax.broadcasted_iota(jnp.int32, (LANES, LANES), 0) // HD
    column = lax.broadcasted_iota(jnp.int32, (LANES, LANES), 1) // HD
    return jnp.where(row == column, 1.0 / HD, 0.0)


def head_mean(values, averages):
    return jnp.dot(
        values, averages, preferred_element_type=jnp.float32, precision=lax.Precision.HIGHEST
    )


def swap_halves(values):
    lane = lax.broadcasted_iota(jnp.int32, values.shape, 1) // (HD // 2)
    ahead = pltpu.roll(values, LANES - HD // 2, 1)
    behind = pltpu.roll(values, HD // 2, 1)
    return jnp.where(lane % 2 == 0, ahead, behind)


def in_half(values, source, target):
    lane = lax.broadcasted_iota(jnp.int32, values.shape, 1) // HD
    wide = values.astype(jnp.float32)
    if source != target:
        wide = pltpu.roll(wide, HD, 1)
    return jnp.where(lane == target, wide, 0.0).astype(values.dtype)


def tile_of(index, width=LANES):
    return pl.ds(pl.multiple_of(index * width, LANES), width)


def rows_of(index, size):
    return pl.ds(pl.multiple_of(index * size, 16), size)


def dot_last(left, right):
    return lax.dot_general(
        left, right, (((1,), (1,)), ((), ())), preferred_element_type=jnp.float32
    )


def probabilities(query, key, keep):
    scores = dot_last(query, key) * HD**-0.5
    scores = jnp.where(keep, scores, masked_score)
    weights = jnp.exp(scores - jnp.max(scores, -1, keepdims=True))
    return weights / jnp.sum(weights, -1, keepdims=True)


def attend_kernel(
    nd,
    nf,
    length,
    tokens,
    in_w,
    out_w,
    gain_attn,
    gain_ffn,
    gain_heads,
    cosine,
    sine,
    mask,
    cot,
    gate_in,
    upper_x,
    down_x,
    gate_w,
    upper_w,
    down_w,
    back_all,
    ffn_all,
    raw,
    heads,
    values,
    mixed,
    hidden_in,
    normed,
    ffn_in,
    gate_send,
    gate_recv,
    uz_send,
    uz_recv,
    uy_send,
    uy_recv,
    dz_send,
    dz_recv,
    dy_send,
    dy_recv,
    row_send,
    row_recv,
    local_sem,
):
    outer = nd // MEMBERS
    dp = lax.axis_index("dp")
    z = lax.axis_index("fsdp")
    y = dp // MEMBERS
    member = dp % MEMBERS
    x = member // 2
    c = member % 2

    def z_peer(step):
        return (dp, lax.rem(z + step, nf))

    def y_peer(step):
        return (lax.rem(y + step, outer) * MEMBERS + member, z)

    def from_z(step):
        return lax.rem(z - step + nf, nf)

    x_peer = (y * MEMBERS + (1 - x) * 2 + c, z)
    core_peer = (y * MEMBERS + x * 2 + 1 - c, z)
    barrier = pltpu.get_barrier_semaphore()
    peers = [z_peer(step) for step in range(1, nf)] + [y_peer(step) for step in range(1, outer)]
    peers += [x_peer, core_peer]
    for peer in peers:
        pl.semaphore_signal(barrier, inc=1, device_id=peer, device_id_type=MESH)
    pl.semaphore_wait(barrier, len(peers))
    sent = []

    def remote(source, target, send, recv, device):
        copy = pltpu.make_async_remote_copy(
            src_ref=source,
            dst_ref=target,
            send_sem=send,
            recv_sem=recv,
            device_id=device,
            device_id_type=MESH,
        )
        copy.start()
        sent.append(copy)
        return copy

    def keep(index, source, target):
        copy = pltpu.make_async_copy(source, target, local_sem.at[index])
        copy.start()
        return copy

    arrivals = []
    for step in range(1, nf):
        piece = gate_w.at[y, :, from_z(step)]
        for hop in range(1, outer):
            arrivals.append(
                remote(piece, piece, gate_send.at[hop, step], gate_recv.at[hop, step], y_peer(hop))
            )
    upper_own = upper_w.at[y, :, z]
    down_own = down_w.at[y, z]
    upper_z = [
        remote(upper_x, upper_own, uz_send.at[step], uz_recv.at[step], z_peer(step))
        for step in range(1, nf)
    ]
    for hop in range(1, outer):
        arrivals.append(
            remote(upper_x, upper_own, uy_send.at[hop, 0], uy_recv.at[hop, 0], y_peer(hop))
        )
    kept = [keep(0, upper_x, upper_own), keep(1, down_x, down_own), keep(2, cot, back_all.at[0])]
    cot_near = remote(cot, back_all.at[1], row_send.at[0], row_recv.at[0], core_peer)
    cot_far = remote(cot, back_all.at[2], row_send.at[1], row_recv.at[1], x_peer)

    count = tokens.shape[0]
    width = tokens.shape[1]
    chunk = 32

    def norm_rows(index, carry):
        rows = rows_of(index, chunk)
        part = tokens[rows, :].astype(jnp.float32)
        scale = lax.rsqrt(jnp.mean(part * part, -1, keepdims=True) + norm_eps)
        normed[rows, :] = (part * scale * gain_attn[...]).astype(jnp.bfloat16)
        return carry

    lax.fori_loop(0, count // chunk, norm_rows, 0)
    head_tiles = (HQ + KV) * HD // LANES

    def project(index, carry):
        columns = tile_of(index, 2 * LANES)
        raw[:, columns] = jnp.dot(
            normed[...], in_w[:, columns], preferred_element_type=jnp.float32
        )
        return carry

    lax.fori_loop(0, head_tiles // 2, project, 0)
    values[...] = jnp.dot(
        normed[...], in_w[:, pl.ds(head_tiles * LANES, KV * HD)], preferred_element_type=jnp.float32
    ).astype(jnp.bfloat16)
    averages = block_mean()

    def turn(index, carry):
        columns = tile_of(index)
        for row in range(count // length):
            rows = pl.ds(row * length, length)
            part = raw[rows, columns]
            scale = lax.rsqrt(head_mean(part * part, averages) + norm_eps)
            part = part * scale * gain_heads[:, columns]
            part = part * cosine[...] + swap_halves(part) * sine[...]
            heads[rows, columns] = part.astype(jnp.bfloat16)
        return carry

    lax.fori_loop(0, head_tiles, turn, 0)

    def attend(row):
        rows = pl.ds(row * length, length)
        allowed = mask[row] > 0.5

        def pair(tile, carry):
            key_tile = heads[rows, tile_of(HQ * HD // LANES + tile)]
            value_tile = values[rows, tile_of(tile)]
            for own in range(2):
                key = [in_half(key_tile, own, half) for half in range(2)]
                value = [in_half(value_tile, own, half) for half in range(2)]
                for quarter in range(2):
                    columns = tile_of(tile * 4 + own * 2 + quarter)
                    query = heads[rows, columns]
                    total = None
                    for half in range(2):
                        weights = probabilities(query, key[half], allowed).astype(jnp.bfloat16)
                        term = jnp.dot(weights, value[half], preferred_element_type=jnp.float32)
                        total = term if total is None else total + term
                    mixed[rows, columns] = total.astype(jnp.bfloat16)
            return carry

        lax.fori_loop(0, KV * HD // LANES, pair, 0)

    for row in range(count // length):
        attend(row)

    def project_out(index, carry):
        columns = tile_of(index, 2 * LANES)
        hidden_in[:, columns] = tokens[:, columns].astype(jnp.float32) + jnp.dot(
            mixed[...], out_w[:, columns], preferred_element_type=jnp.float32
        )
        return carry

    lax.fori_loop(0, width // (2 * LANES), project_out, 0)

    def norm_hidden(index, carry):
        rows = rows_of(index, chunk)
        part = hidden_in[rows, :]
        scale = lax.rsqrt(jnp.mean(part * part, -1, keepdims=True) + norm_eps)
        ffn_in[rows, :] = (part * scale * gain_ffn[...]).astype(jnp.bfloat16)
        return carry

    lax.fori_loop(0, count // chunk, norm_hidden, 0)
    ffn_far = remote(ffn_in, ffn_all.at[2], row_send.at[3], row_recv.at[3], x_peer)
    ffn_near = remote(ffn_in, ffn_all.at[1], row_send.at[4], row_recv.at[4], core_peer)
    kept.append(keep(3, ffn_in, ffn_all.at[0]))

    cot_far.wait_recv()
    cot_cross = remote(back_all.at[2], back_all.at[3], row_send.at[2], row_recv.at[2], core_peer)
    for step in range(1, nf):
        upper_z[step - 1].wait_recv()
        piece = upper_w.at[y, :, from_z(step)]
        for hop in range(1, outer):
            arrivals.append(
                remote(piece, piece, uy_send.at[hop, step], uy_recv.at[hop, step], y_peer(hop))
            )
    down_z = [
        remote(down_x, down_own, dz_send.at[step], dz_recv.at[step], z_peer(step))
        for step in range(1, nf)
    ]
    for hop in range(1, outer):
        arrivals.append(
            remote(down_x, down_own, dy_send.at[hop, 0], dy_recv.at[hop, 0], y_peer(hop))
        )
    ffn_far.wait_recv()
    ffn_cross = remote(ffn_all.at[2], ffn_all.at[3], row_send.at[5], row_recv.at[5], core_peer)
    for step in range(1, nf):
        down_z[step - 1].wait_recv()
        piece = down_w.at[y, from_z(step)]
        for hop in range(1, outer):
            arrivals.append(
                remote(piece, piece, dy_send.at[hop, step], dy_recv.at[hop, step], y_peer(hop))
            )
    for copy in arrivals + [cot_near, cot_cross, ffn_near, ffn_cross]:
        copy.wait_recv()
    for copy in sent:
        copy.wait_send()
    for copy in kept:
        copy.wait()


def attend(nd, nf, length, tokens, in_w, out_w, small, cot, gate_w, upper_x, down_x):
    outer = nd // MEMBERS
    count, width = tokens.shape
    lo, hi = jnp.bfloat16, jnp.float32
    dma = pltpu.SemaphoreType.DMA
    moves = [(outer, nf), (nf,), (outer, nf), (nf,), (outer, nf), (6,)]
    shapes = [
        (gate_w.shape, lo),
        (gate_w.shape, lo),
        ((outer, nf) + down_x.shape, lo),
        ((MEMBERS, count, width), lo),
        ((MEMBERS, count, width), lo),
        ((count, (HQ + KV) * HD), hi),
        ((count, (HQ + KV) * HD), lo),
        ((count, KV * HD), lo),
        ((count, HQ * HD), lo),
        ((count, width), hi),
    ]
    return pl.pallas_call(
        functools.partial(attend_kernel, nd, nf, length),
        name="attend",
        out_shape=tuple(jax.ShapeDtypeStruct(*item) for item in shapes),
        in_specs=[ON_CHIP] * 9 + [ANYWHERE] * 4,
        out_specs=(ANYWHERE,) * 5 + (ON_CHIP,) * 5,
        input_output_aliases={10: 0},
        scratch_shapes=[pltpu.VMEM((count, width), lo), pltpu.VMEM((count, width), lo)]
        + [dma(shape) for shape in moves for _ in range(2)]
        + [dma((4,))],
        compiler_params=pltpu.CompilerParams(
            collective_id=2, has_side_effects=True, vmem_limit_bytes=40 * 2**20
        ),
    )(tokens, in_w, out_w, *small, cot, gate_w, upper_x, down_x)


def after(value, *others):
    return lax.optimization_barrier((value,) + others)[0]


def low(value):
    return value.astype(jnp.bfloat16)


def shards(
    nd,
    nf,
    tokens,
    cotangent,
    segment_ids,
    w_query,
    w_key,
    w_value,
    w_out,
    w_gate,
    w_up,
    w_down,
    m_query,
    m_key,
    m_value,
    m_out,
    m_gate,
    m_up,
    m_down,
    v_query,
    v_key,
    v_value,
    v_out,
    v_gate,
    v_up,
    v_down,
    gains,
    gain_first,
    gain_second,
):
    masters = (w_query, w_key, w_value, w_out, w_gate, w_up, w_down)
    firsts = (m_query, m_key, m_value, m_out, m_gate, m_up, m_down)
    seconds = (v_query, v_key, v_value, v_out, v_gate, v_up, v_down)
    outer = nd // MEMBERS
    dp = lax.axis_index("dp")
    ring_z = Ring(nf, lax.axis_index("fsdp"), lambda d, f, s: (d, (f + s) % nf), nd, nf)
    ring_y = Ring(
        outer,
        dp // MEMBERS,
        lambda d, f, s: ((d // MEMBERS + s) % outer * MEMBERS + d % MEMBERS, f),
        nd,
        nf,
    )
    ring_x = Ring(2, dp // 2 % 2, lambda d, f, s: (d ^ 2, f), nd, nf)
    ring_core = Ring(2, dp % 2, lambda d, f, s: (d ^ 1, f), nd, nf)
    member = dp % MEMBERS

    def trade(block, mask):
        return Ring(2, dp % 2, lambda d, f, s: (d ^ mask, f), nd, nf).move(block, 1)

    def swap(blocks):
        full = put(jnp.zeros_like(blocks), pick(blocks, 0, member), 0, member)
        for mask in range(1, MEMBERS):
            full = put(full, trade(pick(blocks, 0, member ^ mask), mask), 0, member ^ mask)
        return full

    def spread(rows):
        far = ring_x.move(rows, 1)
        near = jnp.concatenate([rows, ring_core.move(rows, 1)], 0)
        return near, jnp.concatenate([far, ring_core.move(far, 1)], 0)

    def collapse(near, far):
        rows = near.shape[0] // 2
        got = ring_core.move(far[rows:], 1).astype(jnp.float32)
        got = ring_x.move(low(far[:rows].astype(jnp.float32) + got), 1)
        total = near[:rows].astype(jnp.float32)
        total = total + ring_core.move(near[rows:], 1).astype(jnp.float32)
        return total + got.astype(jnp.float32)

    batch, length, width = tokens.shape
    count = batch * length
    hidden_rows = w_down.shape[0]
    hidden_all = w_gate.shape[1]
    span = nf * hidden_rows
    mine = outer * span
    in_rows = w_query.shape[0]
    out_rows = w_out.shape[0]
    attn_cols = (HQ + 2 * KV) * HD

    shard_in = jnp.concatenate([low(w_query), low(w_key), low(w_value)], 1)
    shard_out = low(w_out)

    def member_columns(weight):
        cut = low(weight).reshape(in_rows, outer, MEMBERS, span).transpose(2, 0, 1, 3)
        return cut.reshape(MEMBERS, in_rows, mine)

    columns = jnp.stack([member_columns(w_gate), member_columns(w_up)])
    in_w, out_w, gate_w, upper_x = gather_weights(nd, nf, shard_in, shard_out, columns)
    in_w = in_w.reshape(D, attn_cols)
    out_w = out_w.reshape(HQ * HD, D)

    gain_attn = gains[:D]
    gain_ffn = gains[D : 2 * D]
    gain_query = gains[2 * D : 2 * D + HD]
    gain_key = gains[2 * D + HD :]
    positions = jnp.arange(length)
    causal = positions[None, :] <= positions[:, None]
    allowed = causal[None] & (segment_ids[:, :, None] == segment_ids[:, None, :])
    cosine, sine = rotary_tables(length, HD)
    scale = HD ** (-0.5)
    group_size = HQ // KV
    small = (
        gain_attn[None],
        gain_ffn[None],
        jnp.concatenate([jnp.tile(gain_query, HQ), jnp.tile(gain_key, KV)])[None],
        jnp.tile(cosine, (1, 2 * LANES // HD)),
        jnp.tile(jnp.concatenate([-sine, sine], 1), (1, LANES // HD)),
        allowed.astype(jnp.float32),
    )
    back_in = cotangent.reshape(count, width)
    token_rows = tokens.reshape(count, width)
    (
        gate_w,
        upper_w,
        down_w,
        back_all,
        ffn_all,
        raw,
        heads,
        values,
        mixed,
        hidden_in,
    ) = attend(
        nd, nf, length, token_rows, in_w, out_w, small, back_in, gate_w, upper_x, low(w_down)
    )
    gate_w = gate_w.reshape(D, mine)
    upper_w = upper_w.reshape(D, mine)
    down_w = down_w.reshape(mine, D)
    back_all = back_all.reshape(MEMBERS * count, width)
    ffn_all = ffn_all.reshape(MEMBERS * count, width)
    back_halves = (back_all[: 2 * count], back_all[2 * count :])
    ffn_halves = (ffn_all[: 2 * count], ffn_all[2 * count :])
    query_raw = raw[:, : HQ * HD]
    key_raw = raw[:, HQ * HD :]
    queries = heads[:, : HQ * HD].reshape(batch, length, KV, group_size, HD)
    keys = heads[:, HQ * HD :].reshape(batch, length, KV, HD)
    values = values.reshape(batch, length, KV, HD)

    def piece(raw, gain):
        return head_norm(raw.reshape(batch, length, -1), gain, cosine, sine)

    gates = [forward_product(half, gate_w) for half in ffn_halves]
    uppers = [forward_product(half, upper_w) for half in ffn_halves]
    hiddens = [low(swiglu(gate, upper)) for gate, upper in zip(gates, uppers)]
    down_terms = low(weight_product(jnp.concatenate(hiddens, 0), back_all))
    down_terms = down_terms.reshape(outer, nf, hidden_rows, width)
    down_sum = ring_z.reduce(low(ring_y.reduce(down_terms, 0)), 0)

    def inner_grads(half):
        grad_hidden = back_product(back_halves[half], down_w)
        _, pull = jax.vjp(swiglu, gates[half], uppers[half])
        grad_gate, grad_upper = pull(grad_hidden)
        grad_gate, grad_upper = low(grad_gate), low(grad_upper)
        back = back_product(grad_gate, gate_w) + back_product(grad_upper, upper_w)
        return grad_gate, grad_upper, low(back)

    far_gate, far_upper, far_ffn = inner_grads(1)
    near_gate, near_upper, near_ffn = inner_grads(0)
    grad_ffn = collapse(near_ffn, far_ffn)

    def inner_reduce(near, far):
        terms = low(weight_product(ffn_all, jnp.concatenate([near, far], 0)))
        terms = terms.reshape(outer, MEMBERS, nf, in_rows, mine)
        total = ring_z.reduce(low(ring_y.reduce(terms, 0)), 1)
        total = swap(low(total)).astype(jnp.float32)
        total = total.reshape(MEMBERS, in_rows, outer, span).transpose(1, 2, 0, 3)
        return total.reshape(in_rows, hidden_all)

    gate_sum = inner_reduce(near_gate, far_gate)
    upper_sum = inner_reduce(near_upper, far_upper)
    down_out = [low(forward_product(after(half, grad_ffn), down_w)) for half in hiddens]
    output = low(hidden_in + collapse(*down_out))

    inputs = token_rows.astype(jnp.float32)
    normed = low(rms_scale(inputs, gain_attn))
    scores = (
        jnp.einsum("blkrd,bmkd->bkrlm", queries, keys, preferred_element_type=jnp.float32) * scale
    )
    scores = jnp.where(allowed[:, None, None], scores, masked_score)
    weights = jnp.exp(scores - jnp.max(scores, -1, keepdims=True))
    attention_full = weights / jnp.sum(weights, -1, keepdims=True)
    attention = low(attention_full)
    _, ffn_pull = jax.vjp(rms_scale, hidden_in, gain_ffn)
    grad_hidden_in, grad_gain_ffn = ffn_pull(grad_ffn)
    grad_hidden_in = grad_hidden_in + back_in.astype(jnp.float32)
    grad_branch = low(grad_hidden_in)
    out_terms = low(weight_product(mixed, grad_branch)).reshape(
        outer, 2, 2, nf, out_rows, width
    )
    out_sum = low(ring_core.reduce(out_terms, 2))
    out_sum = low(ring_x.reduce(low(ring_y.reduce(out_sum, 0)), 0))
    out_sum = ring_z.reduce(out_sum, 0)
    grad_mixed = low(back_product(grad_branch, out_w)).reshape(batch, length, KV, group_size, HD)
    grad_attention = jnp.einsum(
        "blkrd,bmkd->bkrlm", grad_mixed, values, preferred_element_type=jnp.float32
    )
    grad_scores = low(
        attention_full
        * (grad_attention - jnp.sum(attention_full * grad_attention, -1, keepdims=True))
    )
    grad_values = jnp.einsum(
        "bkrlm,blkrd->bmkd", attention, grad_mixed, preferred_element_type=jnp.float32
    )
    grad_values = low(grad_values.reshape(count, KV * HD))
    grad_queries = (
        jnp.einsum("bkrlm,bmkd->blkrd", grad_scores, keys, preferred_element_type=jnp.float32)
        * scale
    )
    grad_keys = (
        jnp.einsum("bkrlm,blkrd->bmkd", grad_scores, queries, preferred_element_type=jnp.float32)
        * scale
    )
    _, query_pull = jax.vjp(piece, query_raw, gain_query)
    grad_query_raw, grad_gain_query = query_pull(grad_queries.reshape(batch, length, HQ, HD))
    _, key_pull = jax.vjp(piece, key_raw, gain_key)
    grad_key_raw, grad_gain_key = key_pull(grad_keys)
    grad_raw = jnp.concatenate([low(grad_query_raw), low(grad_key_raw), grad_values], 1)
    in_terms = low(weight_product(normed, grad_raw)).reshape(
        outer, 2, 2, nf, in_rows, attn_cols
    )
    in_sum = low(ring_core.reduce(in_terms, 2))
    in_sum = low(ring_y.reduce(low(ring_x.reduce(in_sum, 1)), 0))
    in_sum = ring_z.reduce(in_sum, 0)
    grad_normed = back_product(grad_raw, in_w)
    _, attn_pull = jax.vjp(rms_scale, inputs, gain_attn)
    grad_inputs, grad_gain_attn = attn_pull(grad_normed)
    input_grad = low(grad_inputs + grad_hidden_in)
    gain_terms = jnp.concatenate([grad_gain_attn, grad_gain_ffn, grad_gain_query, grad_gain_key])

    reduced = (
        in_sum[:, : HQ * HD],
        in_sum[:, HQ * HD : (HQ + KV) * HD],
        in_sum[:, (HQ + KV) * HD :],
        out_sum,
        gate_sum,
        upper_sum,
        down_sum,
    )
    local_squares = (
        jnp.sum(in_sum * in_sum)
        + jnp.sum(out_sum * out_sum)
        + jnp.sum(gate_sum * gate_sum)
        + jnp.sum(upper_sum * upper_sum)
        + jnp.sum(down_sum * down_sum)
    )
    gain_size = gains.shape[0]
    share = -(-gain_size // (nd * nf))
    gain_terms = jnp.pad(gain_terms, (0, share * nd * nf - gain_size)).reshape(nd * nf, share)
    gain_terms = jnp.pad(gain_terms, ((0, 0), (0, LANES - share)))
    gain_total, square_total = all_totals(nd, nf, gain_terms, local_squares)
    gain_total = gain_total[:, :share].reshape(-1)[:gain_size]
    total_norm = jnp.sqrt(square_total + jnp.sum(gain_total * gain_total))
    factor = jnp.minimum(1.0, clip_limit / (total_norm + 1e-06))
    clipped = tuple((share * factor for share in reduced))
    gain_clipped = gain_total * factor
    weight_rate = 2.0 * D ** (-0.5)
    updates = [
        adam_update(
            masters[index], firsts[index], seconds[index], clipped[index], weight_rate, decay_rate
        )
        for index in range(7)
    ]
    new_masters = tuple((item[0] for item in updates))
    new_seconds = tuple((item[1] for item in updates))
    new_gains, gain_seconds = adam_update(
        gains, gain_first, gain_second, gain_clipped, gain_rate, 0.0
    )
    copies = tuple((low(item) for item in new_masters))
    return (
        (output.reshape(tokens.shape), input_grad.reshape(tokens.shape))
        + clipped
        + (gain_clipped, total_norm)
        + new_masters
        + (new_gains,)
        + copies
        + new_seconds
        + (gain_seconds,)
    )


def solution(mesh):
    rows3 = P(AXES, None, None)
    rows2 = P(AXES, None)
    whole = P()
    return jax.shard_map(
        functools.partial(shards, mesh.shape["dp"], mesh.shape["fsdp"]),
        mesh=mesh,
        in_specs=(rows3, rows3) + (rows2,) * 22 + (whole,) * 3,
        out_specs=(rows3, rows3)
        + (rows2,) * 7
        + (whole, whole)
        + (rows2,) * 7
        + (whole,)
        + (rows2,) * 14
        + (whole,),
        check_vma=False,
    )
```

```python
import functools
import math

import jax
import jax.numpy as jnp
from jax import lax
from jax.experimental import pallas as pl
from jax.experimental.pallas import tpu as pltpu
from jax.sharding import PartitionSpec as P

D = 1280
HQ = 16
KV = 4
HD = 64
STEP = 10
MEMBERS = 4

norm_eps = 1e-05
rope_base = 10000.0
beta_one = 0.9
beta_two = 0.95
adam_eps = 1e-08
decay_rate = 0.1
clip_limit = 1.0
gain_rate = 0.4
masked_score = -1e30

AXES = ("dp", "fsdp")
LANES = 128
MESH = pl.DeviceIdType.MESH
ANYWHERE = pl.BlockSpec(memory_space=pl.ANY)
ON_CHIP = pl.BlockSpec(memory_space=pltpu.VMEM)


def rms_scale(values, gain):
    return values * lax.rsqrt(jnp.mean(values * values, -1, keepdims=True) + norm_eps) * gain


def rotary_tables(length, size):
    half = size // 2
    frequency = rope_base ** (-jnp.arange(half, dtype=jnp.float32) * 2.0 / size)
    angles = jnp.arange(length, dtype=jnp.float32)[:, None] * frequency[None, :]
    return (jnp.cos(angles), jnp.sin(angles))


def rotate(vectors, cosine, sine):
    half = vectors.shape[-1] // 2
    first = vectors[..., :half]
    second = vectors[..., half:]
    cosine = cosine[:, None, :]
    sine = sine[:, None, :]
    return jnp.concatenate([first * cosine - second * sine, second * cosine + first * sine], -1)


def head_norm(raw, gain, cosine, sine):
    size = gain.shape[0]
    shaped = raw.reshape(raw.shape[:-1] + (raw.shape[-1] // size, size))
    return rotate(rms_scale(shaped, gain), cosine, sine)


def swiglu(gate, upper):
    return jax.nn.silu(gate) * upper


def forward_product(left, right):
    return jnp.dot(left, right, preferred_element_type=jnp.float32)


def weight_product(left, right):
    return lax.dot_general(
        left, right, (((0,), (0,)), ((), ())), preferred_element_type=jnp.float32
    )


def back_product(left, right):
    return lax.dot_general(
        left, right, (((1,), (1,)), ((), ())), preferred_element_type=jnp.float32
    )


def adam_update(master, first, second, grad, rate, decay):
    first_new = beta_one * first + (1.0 - beta_one) * grad
    second_new = beta_two * second + (1.0 - beta_two) * grad * grad
    first_hat = first_new / (1.0 - beta_one**STEP)
    second_hat = second_new / (1.0 - beta_two**STEP)
    master_new = master - rate * (first_hat / (jnp.sqrt(second_hat) + adam_eps) + decay * master)
    return (master_new, second_new)


def put(buffer, block, axis, index):
    return lax.dynamic_update_index_in_dim(buffer, block, index, axis)


def pick(array, axis, index):
    return lax.dynamic_index_in_dim(array, index, axis, keepdims=False)


class Ring:
    def __init__(self, extent, place, target, nd, nf):
        self.extent = extent
        self.place = place
        self.target = target
        self.nd = nd
        self.nf = nf

    def move(self, block, step):
        pairs = []
        for d in range(self.nd):
            for f in range(self.nf):
                d2, f2 = self.target(d, f, step)
                pairs.append((d * self.nf + f, d2 * self.nf + f2))
        return lax.ppermute(block, AXES, pairs)

    def source(self, step):
        return lax.rem(self.place - step + self.extent, self.extent)

    def dest(self, step):
        return lax.rem(self.place + step, self.extent)

    def gather(self, block, axis):
        shape = block.shape[:axis] + (self.extent,) + block.shape[axis:]
        full = put(jnp.zeros(shape, block.dtype), block, axis, self.place)
        for step in range(1, self.extent):
            full = put(full, self.move(block, step), axis, self.source(step))
        return full

    def reduce(self, terms, axis):
        total = pick(terms, axis, self.place).astype(jnp.float32)
        for step in range(1, self.extent):
            got = self.move(pick(terms, axis, self.dest(step)), step)
            total = total + got.astype(jnp.float32)
        return total


def start_all(copies):
    for copy in copies:
        copy.start()
    return copies


def weights_kernel(
    nd,
    nf,
    in_ref,
    out_ref,
    inner_ref,
    in_w,
    out_w,
    gate_w,
    upper_x,
    z_send,
    z_recv,
    y_send,
    y_recv,
    x_send,
    x_recv,
    hop_send,
    hop_recv,
    core_send,
    core_recv,
    swap_send,
    swap_recv,
    gate_send,
    gate_recv,
    over_send,
    over_recv,
    local_sem,
):
    outer = nd // MEMBERS
    dp = lax.axis_index("dp")
    z = lax.axis_index("fsdp")
    y = dp // MEMBERS
    member = dp % MEMBERS
    x = member // 2
    c = member % 2

    def z_peer(step):
        return (dp, lax.rem(z + step, nf))

    def y_peer(step):
        return (lax.rem(y + step, outer) * MEMBERS + member, z)

    def in_group(k):
        return (y * MEMBERS + k, z)

    def from_z(step):
        return lax.rem(z - step + nf, nf)

    def from_y(step):
        return lax.rem(y - step + outer, outer)

    x_peer = in_group((1 - x) * 2 + c)
    core_peer = in_group(x * 2 + 1 - c)
    barrier = pltpu.get_barrier_semaphore()
    peers = [z_peer(step) for step in range(1, nf)] + [y_peer(step) for step in range(1, outer)]
    peers += [x_peer, core_peer, in_group(MEMBERS - 1 - member)]
    for peer in peers:
        pl.semaphore_signal(barrier, inc=1, device_id=peer, device_id_type=MESH)
    pl.semaphore_wait(barrier, len(peers))

    def remote(source, target, send, recv, device):
        return pltpu.make_async_remote_copy(
            src_ref=source,
            dst_ref=target,
            send_sem=send,
            recv_sem=recv,
            device_id=device,
            device_id_type=MESH,
        )

    shards_here = (in_ref, out_ref)
    wholes = (in_w, out_w)
    sent = []

    def send(copy):
        copy.start()
        sent.append(copy)
        return copy

    local = [
        pltpu.make_async_copy(shards_here[a], wholes[a].at[y, x, c, z], local_sem.at[a])
        for a in range(2)
    ]
    start_all(local)
    z_copies = {}
    for a in range(2):
        for step in range(1, nf):
            z_copies[a, step] = send(
                remote(
                    shards_here[a],
                    wholes[a].at[y, x, c, z],
                    z_send.at[a, step],
                    z_recv.at[a, step],
                    z_peer(step),
                )
            )
    masks = (2, 1, 3)
    trades = {}
    for half, target in ((0, gate_w.at[y, :, z]), (1, upper_x)):
        for mask in masks:
            other = member ^ mask
            trades[half, mask] = send(
                remote(
                    inner_ref.at[half, other],
                    target.at[member],
                    swap_send.at[half, mask],
                    swap_recv.at[half, mask],
                    in_group(other),
                )
            )
        kept = pltpu.make_async_copy(
            inner_ref.at[half, member], target.at[member], local_sem.at[2 + half]
        )
        kept.start()
        local.append(kept)

    def block(a, step, oy=None, ox=None):
        return wholes[a].at[y if oy is None else oy, x if ox is None else ox, c, from_z(step)]

    y_copies = {}
    x_copies = {}
    for a in range(2):
        for step in range(nf):
            if step:
                z_copies[a, step].wait_recv()
            source = shards_here[a] if step == 0 else block(a, step)
            for hop in range(1, outer):
                y_copies[a, hop, step] = send(
                    remote(
                        source,
                        block(a, step),
                        y_send.at[a, hop, step],
                        y_recv.at[a, hop, step],
                        y_peer(hop),
                    )
                )
            x_copies[a, step] = send(
                remote(
                    source, block(a, step), x_send.at[a, step], x_recv.at[a, step], x_peer
                )
            )
    for mask in masks:
        trades[0, mask].wait_recv()
    local[2].wait()
    gates = {}
    gate_own = gate_w.at[y, :, z]
    for step in range(1, nf):
        gates[step] = send(
            remote(gate_own, gate_own, gate_send.at[step], gate_recv.at[step], z_peer(step))
        )
    for hop in range(1, outer):
        gates[-hop] = send(
            remote(gate_own, gate_own, over_send.at[hop], over_recv.at[hop], y_peer(hop))
        )
    hops = {}
    for step in range(nf):
        x_copies[0, step].wait_recv()
        for hop in range(1, outer):
            hops[0, hop, step] = send(
                remote(
                    block(0, step, ox=1 - x),
                    block(0, step, ox=1 - x),
                    hop_send.at[0, hop, step],
                    hop_recv.at[0, hop, step],
                    y_peer(hop),
                )
            )
    for step in range(nf):
        for hop in range(1, outer):
            y_copies[1, hop, step].wait_recv()
            hops[1, hop, step] = send(
                remote(
                    block(1, step, oy=from_y(hop)),
                    block(1, step, oy=from_y(hop)),
                    hop_send.at[1, hop, step],
                    hop_recv.at[1, hop, step],
                    x_peer,
                )
            )
    cores = {}

    def to_core(a, hop, far):
        place = wholes[a].at[y if hop == 0 else from_y(hop), 1 - x if far else x, c]
        cores[a, hop, far] = send(
            remote(
                place,
                place,
                core_send.at[a, hop, far],
                core_recv.at[a, hop, far],
                core_peer,
            )
        )

    local[0].wait()
    local[1].wait()
    for a in range(2):
        to_core(a, 0, 0)
    to_core(0, 0, 1)
    for hop in range(1, outer):
        for step in range(nf):
            y_copies[0, hop, step].wait_recv()
        to_core(0, hop, 0)
        to_core(1, hop, 0)
    for step in range(nf):
        x_copies[1, step].wait_recv()
    to_core(1, 0, 1)
    for a in range(2):
        for hop in range(1, outer):
            for step in range(nf):
                hops[a, hop, step].wait_recv()
            to_core(a, hop, 1)
    for mask in masks:
        trades[1, mask].wait_recv()
    local[3].wait()
    for key in gates:
        gates[key].wait_recv()
    for key in cores:
        cores[key].wait_recv()
    for copy in sent:
        copy.wait_send()


def gather_weights(nd, nf, shard_in, shard_out, inner):
    outer = nd // MEMBERS
    dma = pltpu.SemaphoreType.DMA
    lead = (outer, 2, 2, nf)
    low_type = jnp.bfloat16
    pairs = [(2, nf), (2, outer, nf), (2, nf), (2, outer, nf), (2, outer, 2), (2, 4), (nf,), (outer,)]
    moved = 2 * nd * nf * (shard_in.size + shard_out.size)
    return pl.pallas_call(
        functools.partial(weights_kernel, nd, nf),
        name="gather_weights",
        out_shape=(
            jax.ShapeDtypeStruct(lead + shard_in.shape, low_type),
            jax.ShapeDtypeStruct(lead + shard_out.shape, low_type),
            jax.ShapeDtypeStruct((outer, MEMBERS, nf) + inner.shape[2:], low_type),
            jax.ShapeDtypeStruct((MEMBERS,) + inner.shape[2:], low_type),
        ),
        in_specs=[ANYWHERE] * 3,
        out_specs=(ANYWHERE,) * 4,
        scratch_shapes=[dma(shape) for shape in pairs for _ in range(2)] + [dma((4,))],
        cost_estimate=pl.CostEstimate(flops=0, bytes_accessed=16 * moved, transcendentals=0),
        compiler_params=pltpu.CompilerParams(collective_id=0, has_side_effects=True),
    )(shard_in, shard_out, inner)


def totals_kernel(nd, nf, part_ref, square_ref, all_ref, pieces, own, p_send, p_recv, q_send, q_recv):
    total = nd * nf
    dp = lax.axis_index("dp")
    z = lax.axis_index("fsdp")
    me = dp * nf + z

    def device(step):
        index = lax.rem(me + step, total)
        return index, (index // nf, lax.rem(index, nf))

    barrier = pltpu.get_barrier_semaphore()

    def greet(step, carry):
        pl.semaphore_signal(barrier, inc=1, device_id=device(step)[1], device_id_type=MESH)
        return carry

    lax.fori_loop(1, total, greet, 0)
    pl.semaphore_wait(barrier, total - 1)

    def part(step):
        index, there = device(step)
        return pltpu.make_async_remote_copy(
            src_ref=part_ref.at[index],
            dst_ref=pieces.at[me],
            send_sem=p_send.at[step],
            recv_sem=p_recv.at[step],
            device_id=there,
            device_id_type=MESH,
        )

    def share(step):
        _, there = device(step)
        return pltpu.make_async_remote_copy(
            src_ref=own,
            dst_ref=all_ref.at[me],
            send_sem=q_send.at[step],
            recv_sem=q_recv.at[step],
            device_id=there,
            device_id_type=MESH,
        )

    def begin(make):
        def step_once(step, carry):
            make(step).start()
            return carry

        lax.fori_loop(1, total, step_once, 0)

    def finish(make):
        def step_once(step, carry):
            make(step).wait()
            return carry

        lax.fori_loop(1, total, step_once, 0)

    begin(part)
    pieces[me] = part_ref[me]
    finish(part)
    summed = jnp.sum(pieces[...], 0)
    own[...] = jnp.concatenate([summed[:1], square_ref[...]], 0)
    begin(share)
    all_ref[me] = own[...]
    finish(share)


def all_totals(nd, nf, parts, square):
    total = nd * nf
    parts = jnp.pad(parts[:, None, :], ((0, 0), (0, 7), (0, 0)))
    square = jnp.broadcast_to(square, (7, LANES))
    dma = pltpu.SemaphoreType.DMA
    result = pl.pallas_call(
        functools.partial(totals_kernel, nd, nf),
        name="all_totals",
        out_shape=jax.ShapeDtypeStruct((total, 8, LANES), jnp.float32),
        in_specs=[ON_CHIP] * 2,
        out_specs=ON_CHIP,
        scratch_shapes=[
            pltpu.VMEM((total, 8, LANES), jnp.float32),
            pltpu.VMEM((8, LANES), jnp.float32),
        ]
        + [dma((total,))] * 4,
        compiler_params=pltpu.CompilerParams(collective_id=1, has_side_effects=True),
    )(parts, square)
    return result[:, 0], jnp.sum(result[:, 1, 0])


def block_mean():
    row = lax.broadcasted_iota(jnp.int32, (LANES, LANES), 0) // HD
    column = lax.broadcasted_iota(jnp.int32, (LANES, LANES), 1) // HD
    return jnp.where(row == column, 1.0 / HD, 0.0)


def head_mean(values, averages):
    return jnp.dot(
        values, averages, preferred_element_type=jnp.float32, precision=lax.Precision.HIGHEST
    )


def swap_halves(values):
    lane = lax.broadcasted_iota(jnp.int32, values.shape, 1) // (HD // 2)
    ahead = pltpu.roll(values, LANES - HD // 2, 1)
    behind = pltpu.roll(values, HD // 2, 1)
    return jnp.where(lane % 2 == 0, ahead, behind)


def in_half(values, source, target):
    lane = lax.broadcasted_iota(jnp.int32, values.shape, 1) // HD
    wide = values.astype(jnp.float32)
    if source != target:
        wide = pltpu.roll(wide, HD, 1)
    return jnp.where(lane == target, wide, 0.0).astype(values.dtype)


def tile_of(index, width=LANES):
    return pl.ds(pl.multiple_of(index * width, LANES), width)


def rows_of(index, size):
    return pl.ds(pl.multiple_of(index * size, 16), size)


def dot_last(left, right):
    return lax.dot_general(
        left, right, (((1,), (1,)), ((), ())), preferred_element_type=jnp.float32
    )


def probabilities(query, key, keep):
    scores = dot_last(query, key) * HD**-0.5
    scores = jnp.where(keep, scores, masked_score)
    weights = jnp.exp(scores - jnp.max(scores, -1, keepdims=True))
    return weights / jnp.sum(weights, -1, keepdims=True)


def attend_kernel(
    nd,
    nf,
    length,
    tokens,
    in_w,
    out_w,
    gain_attn,
    gain_ffn,
    gain_heads,
    cosine,
    sine,
    mask,
    cot,
    gate_in,
    upper_x,
    down_x,
    gate_w,
    upper_w,
    down_w,
    back_all,
    ffn_all,
    raw,
    heads,
    values,
    mixed,
    hidden_in,
    normed,
    ffn_in,
    gate_send,
    gate_recv,
    uz_send,
    uz_recv,
    uy_send,
    uy_recv,
    dz_send,
    dz_recv,
    dy_send,
    dy_recv,
    row_send,
    row_recv,
    local_sem,
):
    outer = nd // MEMBERS
    dp = lax.axis_index("dp")
    z = lax.axis_index("fsdp")
    y = dp // MEMBERS
    member = dp % MEMBERS
    x = member // 2
    c = member % 2

    def z_peer(step):
        return (dp, lax.rem(z + step, nf))

    def y_peer(step):
        return (lax.rem(y + step, outer) * MEMBERS + member, z)

    def from_z(step):
        return lax.rem(z - step + nf, nf)

    x_peer = (y * MEMBERS + (1 - x) * 2 + c, z)
    core_peer = (y * MEMBERS + x * 2 + 1 - c, z)
    barrier = pltpu.get_barrier_semaphore()
    peers = [z_peer(step) for step in range(1, nf)] + [y_peer(step) for step in range(1, outer)]
    peers += [x_peer, core_peer]
    for peer in peers:
        pl.semaphore_signal(barrier, inc=1, device_id=peer, device_id_type=MESH)
    pl.semaphore_wait(barrier, len(peers))
    sent = []

    def remote(source, target, send, recv, device):
        copy = pltpu.make_async_remote_copy(
            src_ref=source,
            dst_ref=target,
            send_sem=send,
            recv_sem=recv,
            device_id=device,
            device_id_type=MESH,
        )
        copy.start()
        sent.append(copy)
        return copy

    def keep(index, source, target):
        copy = pltpu.make_async_copy(source, target, local_sem.at[index])
        copy.start()
        return copy

    arrivals = []
    for step in range(1, nf):
        piece = gate_w.at[y, :, from_z(step)]
        for hop in range(1, outer):
            arrivals.append(
                remote(piece, piece, gate_send.at[hop, step], gate_recv.at[hop, step], y_peer(hop))
            )
    upper_own = upper_w.at[y, :, z]
    down_own = down_w.at[y, z]
    upper_z = [
        remote(upper_x, upper_own, uz_send.at[step], uz_recv.at[step], z_peer(step))
        for step in range(1, nf)
    ]
    for hop in range(1, outer):
        arrivals.append(
            remote(upper_x, upper_own, uy_send.at[hop, 0], uy_recv.at[hop, 0], y_peer(hop))
        )
    kept = [keep(0, upper_x, upper_own), keep(1, down_x, down_own), keep(2, cot, back_all.at[0])]
    cot_near = remote(cot, back_all.at[1], row_send.at[0], row_recv.at[0], core_peer)
    cot_far = remote(cot, back_all.at[2], row_send.at[1], row_recv.at[1], x_peer)

    count = tokens.shape[0]
    width = tokens.shape[1]
    chunk = 32

    def norm_rows(index, carry):
        rows = rows_of(index, chunk)
        part = tokens[rows, :].astype(jnp.float32)
        scale = lax.rsqrt(jnp.mean(part * part, -1, keepdims=True) + norm_eps)
        normed[rows, :] = (part * scale * gain_attn[...]).astype(jnp.bfloat16)
        return carry

    lax.fori_loop(0, count // chunk, norm_rows, 0)
    head_tiles = (HQ + KV) * HD // LANES

    def project(index, carry):
        columns = tile_of(index, 2 * LANES)
        raw[:, columns] = jnp.dot(
            normed[...], in_w[:, columns], preferred_element_type=jnp.float32
        )
        return carry

    lax.fori_loop(0, head_tiles // 2, project, 0)
    values[...] = jnp.dot(
        normed[...], in_w[:, pl.ds(head_tiles * LANES, KV * HD)], preferred_element_type=jnp.float32
    ).astype(jnp.bfloat16)
    averages = block_mean()

    def turn(index, carry):
        columns = tile_of(index)
        for row in range(count // length):
            rows = pl.ds(row * length, length)
            part = raw[rows, columns]
            scale = lax.rsqrt(head_mean(part * part, averages) + norm_eps)
            part = part * scale * gain_heads[:, columns]
            part = part * cosine[...] + swap_halves(part) * sine[...]
            heads[rows, columns] = part.astype(jnp.bfloat16)
        return carry

    lax.fori_loop(0, head_tiles, turn, 0)

    def attend(row):
        rows = pl.ds(row * length, length)
        allowed = mask[row] > 0.5

        def pair(tile, carry):
            key_tile = heads[rows, tile_of(HQ * HD // LANES + tile)]
            value_tile = values[rows, tile_of(tile)]
            for own in range(2):
                key = [in_half(key_tile, own, half) for half in range(2)]
                value = [in_half(value_tile, own, half) for half in range(2)]
                for quarter in range(2):
                    columns = tile_of(tile * 4 + own * 2 + quarter)
                    query = heads[rows, columns]
                    total = None
                    for half in range(2):
                        weights = probabilities(query, key[half], allowed).astype(jnp.bfloat16)
                        term = jnp.dot(weights, value[half], preferred_element_type=jnp.float32)
                        total = term if total is None else total + term
                    mixed[rows, columns] = total.astype(jnp.bfloat16)
            return carry

        lax.fori_loop(0, KV * HD // LANES, pair, 0)

    for row in range(count // length):
        attend(row)

    def project_out(index, carry):
        columns = tile_of(index, 2 * LANES)
        hidden_in[:, columns] = tokens[:, columns].astype(jnp.float32) + jnp.dot(
            mixed[...], out_w[:, columns], preferred_element_type=jnp.float32
        )
        return carry

    lax.fori_loop(0, width // (2 * LANES), project_out, 0)

    def norm_hidden(index, carry):
        rows = rows_of(index, chunk)
        part = hidden_in[rows, :]
        scale = lax.rsqrt(jnp.mean(part * part, -1, keepdims=True) + norm_eps)
        ffn_in[rows, :] = (part * scale * gain_ffn[...]).astype(jnp.bfloat16)
        return carry

    lax.fori_loop(0, count // chunk, norm_hidden, 0)
    ffn_far = remote(ffn_in, ffn_all.at[2], row_send.at[3], row_recv.at[3], x_peer)
    ffn_near = remote(ffn_in, ffn_all.at[1], row_send.at[4], row_recv.at[4], core_peer)
    kept.append(keep(3, ffn_in, ffn_all.at[0]))

    cot_far.wait_recv()
    cot_cross = remote(back_all.at[2], back_all.at[3], row_send.at[2], row_recv.at[2], core_peer)
    for step in range(1, nf):
        upper_z[step - 1].wait_recv()
        piece = upper_w.at[y, :, from_z(step)]
        for hop in range(1, outer):
            arrivals.append(
                remote(piece, piece, uy_send.at[hop, step], uy_recv.at[hop, step], y_peer(hop))
            )
    down_z = [
        remote(down_x, down_own, dz_send.at[step], dz_recv.at[step], z_peer(step))
        for step in range(1, nf)
    ]
    for hop in range(1, outer):
        arrivals.append(
            remote(down_x, down_own, dy_send.at[hop, 0], dy_recv.at[hop, 0], y_peer(hop))
        )
    ffn_far.wait_recv()
    ffn_cross = remote(ffn_all.at[2], ffn_all.at[3], row_send.at[5], row_recv.at[5], core_peer)
    for step in range(1, nf):
        down_z[step - 1].wait_recv()
        piece = down_w.at[y, from_z(step)]
        for hop in range(1, outer):
            arrivals.append(
                remote(piece, piece, dy_send.at[hop, step], dy_recv.at[hop, step], y_peer(hop))
            )
    for copy in arrivals + [cot_near, cot_cross, ffn_near, ffn_cross]:
        copy.wait_recv()
    for copy in sent:
        copy.wait_send()
    for copy in kept:
        copy.wait()


def attend(nd, nf, length, tokens, in_w, out_w, small, cot, gate_w, upper_x, down_x):
    outer = nd // MEMBERS
    count, width = tokens.shape
    lo, hi = jnp.bfloat16, jnp.float32
    dma = pltpu.SemaphoreType.DMA
    moves = [(outer, nf), (nf,), (outer, nf), (nf,), (outer, nf), (6,)]
    shapes = [
        (gate_w.shape, lo),
        (gate_w.shape, lo),
        ((outer, nf) + down_x.shape, lo),
        ((MEMBERS, count, width), lo),
        ((MEMBERS, count, width), lo),
        ((count, (HQ + KV) * HD), hi),
        ((count, (HQ + KV) * HD), lo),
        ((count, KV * HD), lo),
        ((count, HQ * HD), lo),
        ((count, width), hi),
    ]
    return pl.pallas_call(
        functools.partial(attend_kernel, nd, nf, length),
        name="attend",
        out_shape=tuple(jax.ShapeDtypeStruct(*item) for item in shapes),
        in_specs=[ON_CHIP] * 9 + [ANYWHERE] * 4,
        out_specs=(ANYWHERE,) * 5 + (ON_CHIP,) * 5,
        input_output_aliases={10: 0},
        scratch_shapes=[pltpu.VMEM((count, width), lo), pltpu.VMEM((count, width), lo)]
        + [dma(shape) for shape in moves for _ in range(2)]
        + [dma((4,))],
        compiler_params=pltpu.CompilerParams(
            collective_id=2, has_side_effects=True, vmem_limit_bytes=40 * 2**20
        ),
    )(tokens, in_w, out_w, *small, cot, gate_w, upper_x, down_x)


def backward_kernel(
    nd,
    nf,
    length,
    ffn_near,
    ffn_far,
    out_near,
    out_far,
    down_terms,
    gate_terms,
    upper_terms,
    tokens,
    cot,
    hidden_in,
    raw,
    heads,
    values,
    mixed,
    in_w,
    out_w,
    gain_attn,
    gain_ffn,
    gain_heads,
    cosine,
    sine,
    mask,
    out_core,
    out_x,
    gate_parts,
    upper_parts,
    input_grad,
    in_sum,
    out_sum,
    down_sum,
    sum_attn,
    sum_ffn,
    sum_heads,
    mine_ref,
    pass_ref,
    core_near,
    core_far,
    from_x,
    out_pass,
    out_core_far,
    normed,
    branch,
    grad_mixed,
    grad_hidden,
    grad_raw,
    wide,
    in_terms,
    out_terms,
    in_core,
    out_core_terms,
    in_x,
    out_x_terms,
    in_y,
    out_y_terms,
    in_total,
    out_total,
    in_zs,
    out_zs,
    in_zr,
    out_zr,
    down_own,
    gate_own,
    upper_own,
    down_y,
    gate_y,
    upper_y,
    down_z,
    gate_z,
    upper_z,
    row_send,
    row_recv,
    fy_send,
    fy_recv,
    fz_send,
    fz_recv,
    swap_send,
    swap_recv,
    ac_send,
    ac_recv,
    ax_send,
    ax_recv,
    ay_send,
    ay_recv,
    az_send,
    az_recv,
    load_sem,
    local_sem,
):
    outer = nd // MEMBERS
    dp = lax.axis_index("dp")
    z = lax.axis_index("fsdp")
    y = dp // MEMBERS
    member = dp % MEMBERS
    x = member // 2
    c = member % 2
    lo, hi = jnp.bfloat16, jnp.float32

    def z_to(step):
        return lax.rem(z + step, nf)

    def z_peer(step):
        return (dp, z_to(step))

    def y_to(step):
        return lax.rem(y + step, outer)

    def y_peer(step):
        return (y_to(step) * MEMBERS + member, z)

    def in_group(k):
        return (y * MEMBERS + k, z)

    x_peer = in_group((1 - x) * 2 + c)
    core_peer = in_group(x * 2 + 1 - c)
    barrier = pltpu.get_barrier_semaphore()
    peers = [z_peer(step) for step in range(1, nf)] + [y_peer(step) for step in range(1, outer)]
    peers += [x_peer, core_peer, in_group(MEMBERS - 1 - member)]
    for peer in peers:
        pl.semaphore_signal(barrier, inc=1, device_id=peer, device_id_type=MESH)
    pl.semaphore_wait(barrier, len(peers))
    sent = []

    def remote(source, target, send, recv, device):
        copy = pltpu.make_async_remote_copy(
            src_ref=source,
            dst_ref=target,
            send_sem=send,
            recv_sem=recv,
            device_id=device,
            device_id_type=MESH,
        )
        copy.start()
        sent.append(copy)
        return copy

    def keep(semaphore, source, target):
        copy = pltpu.make_async_copy(source, target, semaphore)
        copy.start()
        return copy

    count, width = tokens.shape
    here, there = pl.ds(0, count), pl.ds(count, count)

    far_copy = remote(ffn_far.at[there], core_far, row_send.at[0], row_recv.at[0], core_peer)
    pass_copy = keep(local_sem.at[0], ffn_far.at[here], pass_ref)
    near_copy = remote(ffn_near.at[there], core_near, row_send.at[1], row_recv.at[1], core_peer)
    mine_copy = keep(local_sem.at[1], ffn_near.at[here], mine_ref)
    out_far_copy = remote(out_far.at[there], out_core_far, row_send.at[2], row_recv.at[2], core_peer)
    out_pass_copy = keep(local_sem.at[2], out_far.at[here], out_pass)
    out_near_copy = remote(out_near.at[there], out_core, row_send.at[3], row_recv.at[3], core_peer)

    terms = (down_terms, gate_terms, upper_terms)
    owns = (down_own, gate_own, upper_own)
    over_y = (down_y, gate_y, upper_y)
    over_z = (down_z, gate_z, upper_z)

    def piece_of(matrix, place, step):
        if matrix == 0:
            return terms[0].at[place, z_to(step)]
        return terms[matrix].at[place, :, z_to(step)]

    order = [(matrix, step) for matrix in range(3) for step in list(range(1, nf)) + [0]]
    y_copies, loads = {}, {}
    for matrix, step in order:
        loads[matrix, step] = keep(
            load_sem.at[matrix, step], piece_of(matrix, y, step), owns[matrix].at[step]
        )
        for hop in range(1, outer):
            y_copies[matrix, step, hop] = remote(
                piece_of(matrix, y_to(hop), step),
                over_y[matrix].at[hop - 1, step],
                fy_send.at[matrix, hop, step],
                fy_recv.at[matrix, hop, step],
                y_peer(hop),
            )
    z_copies = {}
    waiting = list(order)

    def pieces(number):
        for _ in range(min(number, len(waiting))):
            matrix, step = waiting.pop(0)
            loads[matrix, step].wait()
            total = owns[matrix][step].astype(hi)
            for hop in range(1, outer):
                y_copies[matrix, step, hop].wait_recv()
                total = total + over_y[matrix][hop - 1, step].astype(hi)
            owns[matrix][step] = total.astype(lo)
            if step:
                z_copies[matrix, step] = remote(
                    owns[matrix].at[step],
                    over_z[matrix].at[step - 1],
                    fz_send.at[matrix, step],
                    fz_recv.at[matrix, step],
                    z_peer(step),
                )

    def piece_total(matrix):
        total = owns[matrix][0].astype(hi)
        for step in range(1, nf):
            z_copies[matrix, step].wait_recv()
            total = total + over_z[matrix][step - 1].astype(hi)
        return total

    swaps = []

    def trade(matrix, parts):
        owns[matrix][0] = piece_total(matrix).astype(lo)
        for mask_bits in range(1, MEMBERS):
            other = member ^ mask_bits
            swaps.append(
                remote(
                    owns[matrix].at[0, other],
                    parts.at[member],
                    swap_send.at[matrix - 1, mask_bits],
                    swap_recv.at[matrix - 1, mask_bits],
                    in_group(other),
                )
            )
        swaps_local.append(
            keep(local_sem.at[2 + matrix], owns[matrix].at[0, member], parts.at[member])
        )

    swaps_local = []
    chunk = 32

    far_copy.wait_recv()
    pass_copy.wait()

    def add_rows(target, other):
        def step_once(index, carry):
            rows = rows_of(index, chunk)
            target[rows, :] = (target[rows, :].astype(hi) + other[rows, :].astype(hi)).astype(lo)
            return carry

        lax.fori_loop(0, count // chunk, step_once, 0)

    add_rows(pass_ref, core_far)
    x_copy = remote(pass_ref, from_x, row_send.at[4], row_recv.at[4], x_peer)
    out_far_copy.wait_recv()
    out_pass_copy.wait()
    add_rows(out_pass, out_core_far)
    out_x_copy = remote(out_pass, out_x, row_send.at[5], row_recv.at[5], x_peer)

    def norm_rows(index, carry):
        rows = rows_of(index, chunk)
        part = tokens[rows, :].astype(hi)
        scale = lax.rsqrt(jnp.mean(part * part, -1, keepdims=True) + norm_eps)
        normed[rows, :] = (part * scale * gain_attn[...]).astype(lo)
        return carry

    lax.fori_loop(0, count // chunk, norm_rows, 0)
    sum_attn[...] = jnp.zeros_like(sum_attn)
    sum_ffn[...] = jnp.zeros_like(sum_ffn)
    sum_heads[...] = jnp.zeros_like(sum_heads)
    pieces(3)
    near_copy.wait_recv()
    mine_copy.wait()
    x_copy.wait_recv()

    def norm_back(part, gain, grad):
        scale = lax.rsqrt(jnp.mean(part * part, -1, keepdims=True) + norm_eps)
        unit = part * scale
        inner = grad * gain
        back = scale * (inner - unit * jnp.mean(inner * unit, -1, keepdims=True))
        return back, jnp.sum(grad * unit, 0, keepdims=True)

    def ffn_norm_back(index, carry):
        rows = rows_of(index, chunk)
        grad = mine_ref[rows, :].astype(hi) + core_near[rows, :].astype(hi)
        grad = grad + from_x[rows, :].astype(hi)
        back, gain_term = norm_back(hidden_in[rows, :], gain_ffn[...], grad)
        sum_ffn[...] += gain_term
        back = back + cot[rows, :].astype(hi)
        grad_hidden[rows, :] = back
        branch[rows, :] = back.astype(lo)
        return carry

    lax.fori_loop(0, count // chunk, ffn_norm_back, 0)
    pair = 2 * LANES

    def mixed_back(index, carry):
        columns = tile_of(index, pair)
        grad_mixed[:, columns] = dot_last(branch[...], out_w[columns, :]).astype(lo)
        return carry

    lax.fori_loop(0, HQ * HD // pair, mixed_back, 0)

    def outer_product(left, right, target):
        def step_once(index, carry):
            columns = tile_of(index, pair)
            turned = left[:, columns].T
            for part in range(right.shape[1] // (2 * pair)):
                across = pl.ds(part * 2 * pair, 2 * pair)
                target[columns, across] = jnp.dot(
                    turned, right[:, across], preferred_element_type=hi
                ).astype(lo)
            rest = right.shape[1] % (2 * pair)
            if rest:
                across = pl.ds(right.shape[1] - rest, rest)
                target[columns, across] = jnp.dot(
                    turned, right[:, across], preferred_element_type=hi
                ).astype(lo)
            return carry

        lax.fori_loop(0, left.shape[1] // pair, step_once, 0)

    all_terms = (in_terms, out_terms)
    sizes = (in_terms.shape[0] // (nd), out_terms.shape[0] // (nd))
    core_terms = (in_core, out_core_terms)
    x_terms = (in_x, out_x_terms)
    y_terms = (in_y, out_y_terms)
    totals = (in_total, out_total)
    zs = (in_zs, out_zs)
    zr = (in_zr, out_zr)
    hops = list(range(1, outer)) + [0]
    core_copies, ax_copies, ay_copies, az_copies = {}, {}, {}, {}

    def block(a, hop, bx, bc):
        index = (y_to(hop) * 2 + bx) * 2 + bc
        return pl.ds(pl.multiple_of(index * sizes[a], 16), sizes[a])

    def core_out(a):
        for far in (1, 0):
            for hop in hops:
                bx = 1 - x if far else x
                core_copies[a, hop, far] = remote(
                    all_terms[a].at[block(a, hop, bx, 1 - c)],
                    core_terms[a].at[hop, far],
                    ac_send.at[a, hop, far],
                    ac_recv.at[a, hop, far],
                    core_peer,
                )

    def add_block(a, rows, others):
        some = math.gcd(sizes[a], 32)

        def step_once(index, carry):
            base = rows.start + index * some
            place = pl.ds(pl.multiple_of(base, 16), some)
            total = all_terms[a][place, :].astype(hi)
            for other in others:
                total = total + other[rows_of(index, some), :].astype(hi)
            all_terms[a][place, :] = total.astype(lo)
            return carry

        lax.fori_loop(0, sizes[a] // some, step_once, 0)

    def core_in(a):
        for hop in hops:
            core_copies[a, hop, 1].wait_recv()
            rows = block(a, hop, 1 - x, c)
            add_block(a, rows, [core_terms[a].at[hop, 1]])
            ax_copies[a, hop] = remote(
                all_terms[a].at[rows],
                x_terms[a].at[hop],
                ax_send.at[a, hop],
                ax_recv.at[a, hop],
                x_peer,
            )

    def x_in(a):
        for hop in range(1, outer):
            core_copies[a, hop, 0].wait_recv()
            ax_copies[a, hop].wait_recv()
            rows = block(a, hop, x, c)
            add_block(a, rows, [core_terms[a].at[hop, 0], x_terms[a].at[hop]])
            ay_copies[a, hop] = remote(
                all_terms[a].at[rows],
                y_terms[a].at[hop - 1],
                ay_send.at[a, hop],
                ay_recv.at[a, hop],
                y_peer(hop),
            )

    def y_in(a):
        core_copies[a, 0, 0].wait_recv()
        ax_copies[a, 0].wait_recv()
        others = [core_terms[a].at[0, 0], x_terms[a].at[0]]
        for hop in range(1, outer):
            ay_copies[a, hop].wait_recv()
            others.append(y_terms[a].at[hop - 1])
        start = block(a, 0, x, c).start
        some = math.gcd(sizes[a], 32)

        def step_once(index, carry):
            place = rows_of(index, some)
            own = pl.ds(pl.multiple_of(start + index * some, 16), some)
            total = all_terms[a][own, :].astype(hi)
            for other in others:
                total = total + other[place, :].astype(hi)
            totals[a][place, :] = total
            return carry

        lax.fori_loop(0, sizes[a] // some, step_once, 0)
        rows = sizes[a] // nf
        for place in range(nf):
            zs[a][place] = totals[a][place * rows : (place + 1) * rows, :].astype(lo)
        for step in range(1, nf):
            az_copies[a, step] = remote(
                zs[a].at[z_to(step)],
                zr[a].at[step - 1],
                az_send.at[a, step],
                az_recv.at[a, step],
                z_peer(step),
            )

    def z_in(a, target):
        total = zs[a][z].astype(hi)
        for step in range(1, nf):
            az_copies[a, step].wait_recv()
            total = total + zr[a][step - 1].astype(hi)
        target[...] = total

    outer_product(mixed, branch, out_terms)
    core_out(1)
    pieces(2)
    query_tiles = HQ * HD // LANES
    head_tiles = (HQ + KV) * HD // LANES
    key_tiles = KV * HD // LANES

    def over_rows(left, right):
        return lax.dot_general(left, right, (((0,), (0,)), ((), ())), preferred_element_type=hi)

    def attend_back(row):
        rows = pl.ds(row * length, length)
        allowed = mask[row] > 0.5

        def pair_back(tile, carry):
            key_tile = heads[rows, tile_of(query_tiles + tile)]
            value_tile = values[rows, tile_of(tile)]
            grad_key = None
            grad_value = None
            for own in range(2):
                key = [in_half(key_tile, own, half) for half in range(2)]
                value = [in_half(value_tile, own, half) for half in range(2)]
                for half in range(2):
                    key_total, value_total = None, None
                    for quarter in range(2):
                        columns = tile_of(tile * 4 + own * 2 + quarter)
                        query = heads[rows, columns]
                        grad = grad_mixed[rows, columns]
                        weights = probabilities(query, key[half], allowed)
                        slope = dot_last(grad, value[half])
                        inner = jnp.sum(weights * slope, -1, keepdims=True)
                        score = (weights * (slope - inner)).astype(lo)
                        back = jnp.dot(score, key[half], preferred_element_type=hi) * HD**-0.5
                        if half == 0:
                            wide[rows, columns] = back
                        else:
                            wide[rows, columns] += back
                        key_term = over_rows(score, query)
                        value_term = over_rows(weights.astype(lo), grad)
                        key_total = key_term if key_total is None else key_total + key_term
                        value_total = value_term if value_total is None else value_total + value_term
                    key_term = in_half(key_total, half, own)
                    value_term = in_half(value_total, half, own)
                    grad_key = key_term if grad_key is None else grad_key + key_term
                    grad_value = value_term if grad_value is None else grad_value + value_term
            wide[rows, tile_of(query_tiles + tile)] = grad_key * HD**-0.5
            grad_raw[rows, tile_of(head_tiles + tile)] = grad_value.astype(lo)
            return carry

        lax.fori_loop(0, key_tiles, pair_back, 0)

    batch = count // length
    for row in range(batch):
        attend_back(row)
        pieces(2)
        if row == 0:
            core_in(1)
    averages = block_mean()

    def turn_back(index, carry):
        columns = tile_of(index)
        gain = gain_heads[:, columns]
        for row in range(batch):
            rows = pl.ds(row * length, length)
            grad = wide[rows, columns]
            grad = grad * cosine[...] - swap_halves(grad) * sine[...]
            part = raw[rows, columns]
            scale = lax.rsqrt(head_mean(part * part, averages) + norm_eps)
            unit = part * scale
            sum_heads[:, columns] += jnp.sum(grad * unit, 0, keepdims=True)
            inner = grad * gain
            back = scale * (inner - unit * head_mean(inner * unit, averages))
            grad_raw[rows, columns] = back.astype(lo)
        return carry

    lax.fori_loop(0, head_tiles, turn_back, 0)
    outer_product(normed, grad_raw, in_terms)
    core_out(0)
    pieces(1)
    x_in(1)

    def normed_back(index, carry):
        columns = tile_of(index, pair)
        wide[:, columns] = dot_last(grad_raw[...], in_w[columns, :])
        return carry

    core_in(0)
    lax.fori_loop(0, width // pair, normed_back, 0)

    def attn_norm_back(index, carry):
        rows = rows_of(index, chunk)
        back, gain_term = norm_back(tokens[rows, :].astype(hi), gain_attn[...], wide[rows, :])
        sum_attn[...] += gain_term
        input_grad[rows, :] = (back + grad_hidden[rows, :]).astype(lo)
        return carry

    lax.fori_loop(0, count // chunk, attn_norm_back, 0)
    down_sum[...] = piece_total(0)
    pieces(2)
    x_in(0)
    y_in(1)
    pieces(2 * nf)
    trade(1, gate_parts)
    y_in(0)
    z_in(1, out_sum)
    trade(2, upper_parts)
    z_in(0, in_sum)
    for copy in swaps + [out_near_copy, out_x_copy]:
        copy.wait_recv()
    for copy in sent:
        copy.wait_send()
    for copy in swaps_local:
        copy.wait()


def backward(nd, nf, length, halves, terms, rows, weights, small):
    outer = nd // MEMBERS
    count, width = rows[0].shape
    in_w, out_w = weights
    down_terms, gate_terms, _ = terms
    lo, hi = jnp.bfloat16, jnp.float32
    dma = pltpu.SemaphoreType.DMA
    in_rows, in_cols = in_w.shape[0] // (nd * nf), in_w.shape[1]
    out_rows, out_cols = out_w.shape[0] // (nd * nf), out_w.shape[1]
    inner = (MEMBERS,) + gate_terms.shape[3:]
    down = down_terms.shape[2:]
    shapes = [
        ((count, width), lo),
        ((count, width), lo),
        (inner, lo),
        (inner, lo),
        ((count, width), lo),
        ((in_rows, in_cols), hi),
        ((out_rows, out_cols), hi),
        (down, hi),
        ((1, width), hi),
        ((1, width), hi),
        ((1, (HQ + KV) * HD), hi),
    ]
    in_block, out_block = (nf * in_rows, in_cols), (nf * out_rows, out_cols)
    scratch = [((count, width), lo)] * 7
    scratch += [
        ((count, width), lo),
        ((count, width), lo),
        ((count, HQ * HD), lo),
        ((count, width), hi),
        ((count, in_cols), lo),
        ((count, width), hi),
        (in_w.shape, lo),
        (out_w.shape, lo),
        ((outer, 2) + in_block, lo),
        ((outer, 2) + out_block, lo),
        ((outer,) + in_block, lo),
        ((outer,) + out_block, lo),
        ((outer - 1,) + in_block, lo),
        ((outer - 1,) + out_block, lo),
        (in_block, hi),
        (out_block, hi),
        ((nf, in_rows, in_cols), lo),
        ((nf, out_rows, out_cols), lo),
        ((nf - 1, in_rows, in_cols), lo),
        ((nf - 1, out_rows, out_cols), lo),
        ((nf,) + down, lo),
        ((nf,) + inner, lo),
        ((nf,) + inner, lo),
        ((outer - 1, nf) + down, lo),
        ((outer - 1, nf) + inner, lo),
        ((outer - 1, nf) + inner, lo),
        ((nf - 1,) + down, lo),
        ((nf - 1,) + inner, lo),
        ((nf - 1,) + inner, lo),
    ]
    moves = [(6,), (3, outer, nf), (3, nf), (2, MEMBERS), (2, outer, 2), (2, outer), (2, outer)]
    moves += [(2, nf)]
    return pl.pallas_call(
        functools.partial(backward_kernel, nd, nf, length),
        name="backward",
        out_shape=tuple(jax.ShapeDtypeStruct(*item) for item in shapes),
        in_specs=[ANYWHERE] * 7 + [ON_CHIP] * 15,
        out_specs=(ANYWHERE,) * 4 + (ON_CHIP,) * 7,
        scratch_shapes=[pltpu.VMEM(*item) for item in scratch]
        + [dma(shape) for shape in moves for _ in range(2)]
        + [dma((3, nf)), dma((5,))],
        compiler_params=pltpu.CompilerParams(
            collective_id=3, has_side_effects=True, vmem_limit_bytes=58 * 2**20
        ),
    )(*halves, *terms, *rows, *weights, *small)


def after(value, *others):
    return lax.optimization_barrier((value,) + others)[0]


def low(value):
    return value.astype(jnp.bfloat16)


def shards(
    nd,
    nf,
    tokens,
    cotangent,
    segment_ids,
    w_query,
    w_key,
    w_value,
    w_out,
    w_gate,
    w_up,
    w_down,
    m_query,
    m_key,
    m_value,
    m_out,
    m_gate,
    m_up,
    m_down,
    v_query,
    v_key,
    v_value,
    v_out,
    v_gate,
    v_up,
    v_down,
    gains,
    gain_first,
    gain_second,
):
    masters = (w_query, w_key, w_value, w_out, w_gate, w_up, w_down)
    firsts = (m_query, m_key, m_value, m_out, m_gate, m_up, m_down)
    seconds = (v_query, v_key, v_value, v_out, v_gate, v_up, v_down)
    outer = nd // MEMBERS
    dp = lax.axis_index("dp")
    ring_z = Ring(nf, lax.axis_index("fsdp"), lambda d, f, s: (d, (f + s) % nf), nd, nf)
    ring_y = Ring(
        outer,
        dp // MEMBERS,
        lambda d, f, s: ((d // MEMBERS + s) % outer * MEMBERS + d % MEMBERS, f),
        nd,
        nf,
    )
    ring_x = Ring(2, dp // 2 % 2, lambda d, f, s: (d ^ 2, f), nd, nf)
    ring_core = Ring(2, dp % 2, lambda d, f, s: (d ^ 1, f), nd, nf)
    member = dp % MEMBERS

    def trade(block, mask):
        return Ring(2, dp % 2, lambda d, f, s: (d ^ mask, f), nd, nf).move(block, 1)

    def swap(blocks):
        full = put(jnp.zeros_like(blocks), pick(blocks, 0, member), 0, member)
        for mask in range(1, MEMBERS):
            full = put(full, trade(pick(blocks, 0, member ^ mask), mask), 0, member ^ mask)
        return full

    def spread(rows):
        far = ring_x.move(rows, 1)
        near = jnp.concatenate([rows, ring_core.move(rows, 1)], 0)
        return near, jnp.concatenate([far, ring_core.move(far, 1)], 0)

    def collapse(near, far):
        rows = near.shape[0] // 2
        got = ring_core.move(far[rows:], 1).astype(jnp.float32)
        got = ring_x.move(low(far[:rows].astype(jnp.float32) + got), 1)
        total = near[:rows].astype(jnp.float32)
        total = total + ring_core.move(near[rows:], 1).astype(jnp.float32)
        return total + got.astype(jnp.float32)

    batch, length, width = tokens.shape
    count = batch * length
    hidden_rows = w_down.shape[0]
    hidden_all = w_gate.shape[1]
    span = nf * hidden_rows
    mine = outer * span
    in_rows = w_query.shape[0]
    out_rows = w_out.shape[0]
    attn_cols = (HQ + 2 * KV) * HD

    shard_in = jnp.concatenate([low(w_query), low(w_key), low(w_value)], 1)
    shard_out = low(w_out)

    def member_columns(weight):
        cut = low(weight).reshape(in_rows, outer, MEMBERS, span).transpose(2, 0, 1, 3)
        return cut.reshape(MEMBERS, in_rows, mine)

    columns = jnp.stack([member_columns(w_gate), member_columns(w_up)])
    in_w, out_w, gate_w, upper_x = gather_weights(nd, nf, shard_in, shard_out, columns)
    in_w = in_w.reshape(D, attn_cols)
    out_w = out_w.reshape(HQ * HD, D)

    gain_attn = gains[:D]
    gain_ffn = gains[D : 2 * D]
    gain_query = gains[2 * D : 2 * D + HD]
    gain_key = gains[2 * D + HD :]
    positions = jnp.arange(length)
    causal = positions[None, :] <= positions[:, None]
    allowed = causal[None] & (segment_ids[:, :, None] == segment_ids[:, None, :])
    cosine, sine = rotary_tables(length, HD)
    scale = HD ** (-0.5)
    group_size = HQ // KV
    small = (
        gain_attn[None],
        gain_ffn[None],
        jnp.concatenate([jnp.tile(gain_query, HQ), jnp.tile(gain_key, KV)])[None],
        jnp.tile(cosine, (1, 2 * LANES // HD)),
        jnp.tile(jnp.concatenate([-sine, sine], 1), (1, LANES // HD)),
        allowed.astype(jnp.float32),
    )
    back_in = cotangent.reshape(count, width)
    token_rows = tokens.reshape(count, width)
    (
        gate_w,
        upper_w,
        down_w,
        back_all,
        ffn_all,
        raw,
        heads,
        values,
        mixed,
        hidden_in,
    ) = attend(
        nd, nf, length, token_rows, in_w, out_w, small, back_in, gate_w, upper_x, low(w_down)
    )
    gate_w = gate_w.reshape(D, mine)
    upper_w = upper_w.reshape(D, mine)
    down_w = down_w.reshape(mine, D)
    back_all = back_all.reshape(MEMBERS * count, width)
    ffn_all = ffn_all.reshape(MEMBERS * count, width)
    back_halves = (back_all[: 2 * count], back_all[2 * count :])
    ffn_halves = (ffn_all[: 2 * count], ffn_all[2 * count :])
    gates = [forward_product(half, gate_w) for half in ffn_halves]
    uppers = [forward_product(half, upper_w) for half in ffn_halves]
    hiddens = [low(swiglu(gate, upper)) for gate, upper in zip(gates, uppers)]
    down_terms = low(weight_product(jnp.concatenate(hiddens, 0), back_all))

    def inner_grads(half):
        grad_hidden = back_product(back_halves[half], down_w)
        _, pull = jax.vjp(swiglu, gates[half], uppers[half])
        grad_gate, grad_upper = pull(grad_hidden)
        grad_gate, grad_upper = low(grad_gate), low(grad_upper)
        back = back_product(grad_gate, gate_w) + back_product(grad_upper, upper_w)
        return grad_gate, grad_upper, low(back)

    far_gate, far_upper, far_ffn = inner_grads(1)
    near_gate, near_upper, near_ffn = inner_grads(0)
    gate_terms = low(weight_product(ffn_all, jnp.concatenate([near_gate, far_gate], 0)))
    upper_terms = low(weight_product(ffn_all, jnp.concatenate([near_upper, far_upper], 0)))
    near_out, far_out = [low(forward_product(half, down_w)) for half in hiddens]
    inner_shape = (outer, MEMBERS, nf, in_rows, mine)
    (
        out_core,
        out_x,
        gate_parts,
        upper_parts,
        input_grad,
        in_sum,
        out_sum,
        down_sum,
        grad_gain_attn,
        grad_gain_ffn,
        grad_gain_heads,
    ) = backward(
        nd,
        nf,
        length,
        (near_ffn, far_ffn, near_out, far_out),
        (
            down_terms.reshape(outer, nf, hidden_rows, width),
            gate_terms.reshape(inner_shape),
            upper_terms.reshape(inner_shape),
        ),
        (token_rows, back_in, hidden_in, raw, heads, values, mixed),
        (in_w, out_w),
        small,
    )
    output = hidden_in + near_out[:count].astype(jnp.float32)
    output = low(output + out_core.astype(jnp.float32) + out_x.astype(jnp.float32))

    def all_columns(parts):
        parts = parts.astype(jnp.float32).reshape(MEMBERS, in_rows, outer, span)
        return parts.transpose(1, 2, 0, 3).reshape(in_rows, hidden_all)

    gate_sum = all_columns(gate_parts)
    upper_sum = all_columns(upper_parts)
    head_sums = grad_gain_heads.reshape(HQ + KV, HD)
    gain_terms = jnp.concatenate(
        [
            grad_gain_attn[0],
            grad_gain_ffn[0],
            jnp.sum(head_sums[:HQ], 0),
            jnp.sum(head_sums[HQ:], 0),
        ]
    )

    reduced = (
        in_sum[:, : HQ * HD],
        in_sum[:, HQ * HD : (HQ + KV) * HD],
        in_sum[:, (HQ + KV) * HD :],
        out_sum,
        gate_sum,
        upper_sum,
        down_sum,
    )
    local_squares = (
        jnp.sum(in_sum * in_sum)
        + jnp.sum(out_sum * out_sum)
        + jnp.sum(gate_sum * gate_sum)
        + jnp.sum(upper_sum * upper_sum)
        + jnp.sum(down_sum * down_sum)
    )
    gain_size = gains.shape[0]
    share = -(-gain_size // (nd * nf))
    gain_terms = jnp.pad(gain_terms, (0, share * nd * nf - gain_size)).reshape(nd * nf, share)
    gain_terms = jnp.pad(gain_terms, ((0, 0), (0, LANES - share)))
    gain_total, square_total = all_totals(nd, nf, gain_terms, local_squares)
    gain_total = gain_total[:, :share].reshape(-1)[:gain_size]
    total_norm = jnp.sqrt(square_total + jnp.sum(gain_total * gain_total))
    factor = jnp.minimum(1.0, clip_limit / (total_norm + 1e-06))
    clipped = tuple((share * factor for share in reduced))
    gain_clipped = gain_total * factor
    weight_rate = 2.0 * D ** (-0.5)
    updates = [
        adam_update(
            masters[index], firsts[index], seconds[index], clipped[index], weight_rate, decay_rate
        )
        for index in range(7)
    ]
    new_masters = tuple((item[0] for item in updates))
    new_seconds = tuple((item[1] for item in updates))
    new_gains, gain_seconds = adam_update(
        gains, gain_first, gain_second, gain_clipped, gain_rate, 0.0
    )
    copies = tuple((low(item) for item in new_masters))
    return (
        (output.reshape(tokens.shape), input_grad.reshape(tokens.shape))
        + clipped
        + (gain_clipped, total_norm)
        + new_masters
        + (new_gains,)
        + copies
        + new_seconds
        + (gain_seconds,)
    )


def solution(mesh):
    rows3 = P(AXES, None, None)
    rows2 = P(AXES, None)
    whole = P()
    return jax.shard_map(
        functools.partial(shards, mesh.shape["dp"], mesh.shape["fsdp"]),
        mesh=mesh,
        in_specs=(rows3, rows3) + (rows2,) * 22 + (whole,) * 3,
        out_specs=(rows3, rows3)
        + (rows2,) * 7
        + (whole, whole)
        + (rows2,) * 7
        + (whole,)
        + (rows2,) * 14
        + (whole,),
        check_vma=False,
    )
```

```python
import functools
import math

import jax
import jax.numpy as jnp
import numpy as np
from jax import lax
from jax.experimental import pallas as pl
from jax.experimental.pallas import tpu as pltpu
from jax.sharding import PartitionSpec as P

D = 1280
HQ = 16
KV = 4
HD = 64
STEP = 10
MEMBERS = 4

norm_eps = 1e-05
rope_base = 10000.0
beta_one = 0.9
beta_two = 0.95
adam_eps = 1e-08
decay_rate = 0.1
clip_limit = 1.0
gain_rate = 0.4
masked_score = -1e30

AXES = ("dp", "fsdp")
LANES = 128
MESH = pl.DeviceIdType.MESH
ANYWHERE = pl.BlockSpec(memory_space=pl.ANY)
ON_CHIP = pl.BlockSpec(memory_space=pltpu.VMEM)
VMEM_MOST = 58 * 2**20


def rms_scale(values, gain):
    return values * lax.rsqrt(jnp.mean(values * values, -1, keepdims=True) + norm_eps) * gain


def rotary_tables(length):
    half = HD // 2
    frequency = rope_base ** (-np.arange(half, dtype=np.float64) * 2.0 / HD)
    angles = np.arange(length, dtype=np.float64)[:, None] * frequency[None, :]
    cosine, sine = np.cos(angles), np.sin(angles)
    cosine = np.tile(cosine, (1, LANES // half))
    sine = np.tile(np.concatenate([-sine, sine], 1), (1, LANES // HD))
    return jnp.asarray(cosine, jnp.float32), jnp.asarray(sine, jnp.float32)


def swiglu(gate, upper):
    return jax.nn.silu(gate) * upper


def forward_product(left, right):
    return jnp.dot(left, right, preferred_element_type=jnp.float32)


def weight_product(left, right):
    return lax.dot_general(
        left, right, (((0,), (0,)), ((), ())), preferred_element_type=jnp.float32
    )


def back_product(left, right):
    return lax.dot_general(
        left, right, (((1,), (1,)), ((), ())), preferred_element_type=jnp.float32
    )


def adam_update(master, first, second, grad, rate, decay):
    first_new = beta_one * first + (1.0 - beta_one) * grad
    second_new = beta_two * second + (1.0 - beta_two) * grad * grad
    first_hat = first_new / (1.0 - beta_one**STEP)
    second_hat = second_new / (1.0 - beta_two**STEP)
    master_new = master - rate * (first_hat / (jnp.sqrt(second_hat) + adam_eps) + decay * master)
    return (master_new, second_new)


def put(buffer, block, axis, index):
    return lax.dynamic_update_index_in_dim(buffer, block, index, axis)


def pick(array, axis, index):
    return lax.dynamic_index_in_dim(array, index, axis, keepdims=False)


class Ring:
    def __init__(self, extent, place, target, nd, nf):
        self.extent = extent
        self.place = place
        self.target = target
        self.nd = nd
        self.nf = nf

    def move(self, block, step):
        pairs = []
        for d in range(self.nd):
            for f in range(self.nf):
                d2, f2 = self.target(d, f, step)
                pairs.append((d * self.nf + f, d2 * self.nf + f2))
        return lax.ppermute(block, AXES, pairs)

    def source(self, step):
        return lax.rem(self.place - step + self.extent, self.extent)

    def dest(self, step):
        return lax.rem(self.place + step, self.extent)

    def gather(self, block, axis):
        shape = block.shape[:axis] + (self.extent,) + block.shape[axis:]
        full = put(jnp.zeros(shape, block.dtype), block, axis, self.place)
        for step in range(1, self.extent):
            full = put(full, self.move(block, step), axis, self.source(step))
        return full

    def reduce(self, terms, axis):
        total = pick(terms, axis, self.place).astype(jnp.float32)
        for step in range(1, self.extent):
            got = self.move(pick(terms, axis, self.dest(step)), step)
            total = total + got.astype(jnp.float32)
        return total


def start_all(copies):
    for copy in copies:
        copy.start()
    return copies


def weights_kernel(
    nd,
    nf,
    query_full,
    key_full,
    value_full,
    out_full,
    gate_full,
    up_full,
    in_w,
    out_w,
    gate_w,
    upper_w,
    w_query,
    w_key,
    w_value,
    w_out,
    w_gate,
    w_up,
    in_ref,
    out_ref,
    inner_ref,
    z_send,
    z_recv,
    y_send,
    y_recv,
    x_send,
    x_recv,
    hop_send,
    hop_recv,
    core_send,
    core_recv,
    swap_send,
    swap_recv,
    gate_send,
    gate_recv,
    over_send,
    over_recv,
    up_send,
    up_recv,
    local_sem,
    load_sem,
):
    outer = nd // MEMBERS
    dp = lax.axis_index("dp")
    z = lax.axis_index("fsdp")
    y = dp // MEMBERS
    member = dp % MEMBERS
    x = member // 2
    c = member % 2

    def z_peer(step):
        return (dp, lax.rem(z + step, nf))

    def y_peer(step):
        return (lax.rem(y + step, outer) * MEMBERS + member, z)

    def in_group(k):
        return (y * MEMBERS + k, z)

    def from_z(step):
        return lax.rem(z - step + nf, nf)

    def from_y(step):
        return lax.rem(y - step + outer, outer)

    x_peer = in_group((1 - x) * 2 + c)
    core_peer = in_group(x * 2 + 1 - c)
    barrier = pltpu.get_barrier_semaphore()
    peers = [z_peer(step) for step in range(1, nf)] + [y_peer(step) for step in range(1, outer)]
    peers += [x_peer, core_peer, in_group(MEMBERS - 1 - member)]
    for peer in peers:
        pl.semaphore_signal(barrier, inc=1, device_id=peer, device_id_type=MESH)
    fulls = (query_full, key_full, value_full, out_full, gate_full, up_full)
    loads = [
        pltpu.make_async_copy(full, here, load_sem.at[index])
        for index, (full, here) in enumerate(
            zip(fulls, (w_query, w_key, w_value, w_out, w_gate, w_up))
        )
    ]
    start_all(loads)
    for copy in loads:
        copy.wait()
    column = 0
    for weight in (w_query, w_key, w_value):
        in_ref[:, column : column + weight.shape[1]] = weight[...].astype(jnp.bfloat16)
        column += weight.shape[1]
    out_ref[...] = w_out[...].astype(jnp.bfloat16)
    span = inner_ref.shape[3] // outer
    for half, weight in enumerate((w_gate, w_up)):
        for k in range(MEMBERS):
            for part in range(outer):
                column = (part * MEMBERS + k) * span
                inner_ref[half, k, :, part * span : (part + 1) * span] = weight[
                    :, column : column + span
                ].astype(jnp.bfloat16)
    pl.semaphore_wait(barrier, len(peers))

    def remote(source, target, send, recv, device):
        return pltpu.make_async_remote_copy(
            src_ref=source,
            dst_ref=target,
            send_sem=send,
            recv_sem=recv,
            device_id=device,
            device_id_type=MESH,
        )

    shards_here = (in_ref, out_ref)
    wholes = (in_w, out_w)
    sent = []

    def send(copy):
        copy.start()
        sent.append(copy)
        return copy

    local = [
        pltpu.make_async_copy(shards_here[a], wholes[a].at[y, x, c, z], local_sem.at[a])
        for a in range(2)
    ]
    start_all(local)
    z_copies = {}
    for a in range(2):
        for step in range(1, nf):
            z_copies[a, step] = send(
                remote(
                    shards_here[a],
                    wholes[a].at[y, x, c, z],
                    z_send.at[a, step],
                    z_recv.at[a, step],
                    z_peer(step),
                )
            )
    masks = (2, 1, 3)
    trades = {}
    for half, target in ((0, gate_w.at[y, :, z]), (1, upper_w.at[y, :, z])):
        for mask in masks:
            other = member ^ mask
            trades[half, mask] = send(
                remote(
                    inner_ref.at[half, other],
                    target.at[member],
                    swap_send.at[half, mask],
                    swap_recv.at[half, mask],
                    in_group(other),
                )
            )
        kept = pltpu.make_async_copy(
            inner_ref.at[half, member], target.at[member], local_sem.at[2 + half]
        )
        kept.start()
        local.append(kept)

    def block(a, step, oy=None, ox=None):
        return wholes[a].at[y if oy is None else oy, x if ox is None else ox, c, from_z(step)]

    y_copies = {}
    x_copies = {}
    for a in range(2):
        for step in range(nf):
            if step:
                z_copies[a, step].wait_recv()
            source = shards_here[a] if step == 0 else block(a, step)
            for hop in range(1, outer):
                y_copies[a, hop, step] = send(
                    remote(
                        source,
                        block(a, step),
                        y_send.at[a, hop, step],
                        y_recv.at[a, hop, step],
                        y_peer(hop),
                    )
                )
            x_copies[a, step] = send(
                remote(
                    source, block(a, step), x_send.at[a, step], x_recv.at[a, step], x_peer
                )
            )
    for mask in masks:
        trades[0, mask].wait_recv()
    local[2].wait()
    gates = {}
    gate_own = gate_w.at[y, :, z]

    def gate_to_y(step):
        piece = gate_w.at[y, :, from_z(step)]
        for hop in range(1, outer):
            gates[hop, step] = send(
                remote(
                    piece, piece, over_send.at[hop, step], over_recv.at[hop, step], y_peer(hop)
                )
            )

    for step in range(1, nf):
        gates[0, step] = send(
            remote(gate_own, gate_own, gate_send.at[step], gate_recv.at[step], z_peer(step))
        )
    gate_to_y(0)
    for mask in masks:
        trades[1, mask].wait_recv()
    local[3].wait()
    upper_own = upper_w.at[y, :, z]
    uppers = [
        send(remote(upper_own, upper_own, up_send.at[step], up_recv.at[step], z_peer(step)))
        for step in early_steps(nf)
    ]
    hops = {}
    for a in range(2):
        for step in range(nf):
            for hop in range(1, outer):
                y_copies[a, hop, step].wait_recv()
                hops[a, hop, step] = send(
                    remote(
                        block(a, step, oy=from_y(hop)),
                        block(a, step, oy=from_y(hop)),
                        hop_send.at[a, hop, step],
                        hop_recv.at[a, hop, step],
                        x_peer,
                    )
                )
    for step in range(1, nf):
        gates[0, step].wait_recv()
        gate_to_y(step)
    cores = {}

    def to_core(a, hop, far):
        place = wholes[a].at[y if hop == 0 else from_y(hop), 1 - x if far else x, c]
        cores[a, hop, far] = send(
            remote(
                place,
                place,
                core_send.at[a, hop, far],
                core_recv.at[a, hop, far],
                core_peer,
            )
        )

    local[0].wait()
    local[1].wait()
    for a in range(2):
        for hop in range(outer):
            to_core(a, hop, 0)
    for a in range(2):
        for step in range(nf):
            x_copies[a, step].wait_recv()
        to_core(a, 0, 1)
    for a in range(2):
        for hop in range(1, outer):
            for step in range(nf):
                hops[a, hop, step].wait_recv()
            to_core(a, hop, 1)
    for copy in uppers:
        copy.wait_recv()
    for hop in range(1, outer):
        for step in range(nf):
            gates[hop, step].wait_recv()
    for key in cores:
        cores[key].wait_recv()
    for copy in sent:
        copy.wait_send()


def early_steps(nf):
    return sorted({1, nf - 1})


def gather_weights(nd, nf, shards_here):
    outer = nd // MEMBERS
    dma = pltpu.SemaphoreType.DMA
    lead = (outer, 2, 2, nf)
    low_type = jnp.bfloat16
    w_query, w_key, w_value, w_out, w_gate, w_up = shards_here
    in_shape = (w_query.shape[0], w_query.shape[1] + w_key.shape[1] + w_value.shape[1])
    inner = (w_gate.shape[0], w_gate.shape[1] // MEMBERS)
    pairs = [(2, nf), (2, outer, nf), (2, nf), (2, outer, nf), (2, outer, 2), (2, MEMBERS)]
    pairs += [(nf,), (outer, nf), (nf,)]
    return pl.pallas_call(
        functools.partial(weights_kernel, nd, nf),
        name="gather_weights",
        out_shape=(
            jax.ShapeDtypeStruct(lead + in_shape, low_type),
            jax.ShapeDtypeStruct(lead + w_out.shape, low_type),
            jax.ShapeDtypeStruct((outer, MEMBERS, nf) + inner, low_type),
            jax.ShapeDtypeStruct((outer, MEMBERS, nf) + inner, low_type),
        ),
        in_specs=[ANYWHERE] * 6,
        out_specs=(ANYWHERE,) * 4,
        scratch_shapes=[pltpu.VMEM(weight.shape, weight.dtype) for weight in shards_here]
        + [
            pltpu.VMEM(in_shape, low_type),
            pltpu.VMEM(w_out.shape, low_type),
            pltpu.VMEM((2, MEMBERS) + inner, low_type),
        ]
        + [dma(shape) for shape in pairs for _ in range(2)]
        + [dma((4,)), dma((6,))],
        compiler_params=pltpu.CompilerParams(
            collective_id=0, has_side_effects=True, vmem_limit_bytes=VMEM_MOST
        ),
    )(*shards_here)


def block_mean():
    row = lax.broadcasted_iota(jnp.int32, (LANES, LANES), 0) // HD
    column = lax.broadcasted_iota(jnp.int32, (LANES, LANES), 1) // HD
    return jnp.where(row == column, 1.0 / HD, 0.0).astype(jnp.bfloat16)


def head_mean(values, averages):
    high = values.astype(jnp.bfloat16)
    rest = (values - high.astype(jnp.float32)).astype(jnp.bfloat16)
    total = jnp.dot(high, averages, preferred_element_type=jnp.float32)
    return total + jnp.dot(rest, averages, preferred_element_type=jnp.float32)


def swap_halves(values):
    lane = lax.broadcasted_iota(jnp.int32, values.shape, 1) // (HD // 2)
    ahead = pltpu.roll(values, LANES - HD // 2, 1)
    behind = pltpu.roll(values, HD // 2, 1)
    return jnp.where(lane % 2 == 0, ahead, behind)


def in_half(values, source, target):
    lane = lax.broadcasted_iota(jnp.int32, values.shape, 1) // HD
    wide = values.astype(jnp.float32)
    if source != target:
        wide = pltpu.roll(wide, HD, 1)
    return jnp.where(lane == target, wide, 0.0).astype(values.dtype)


def split_gains(gains):
    width = (gains.shape[1] - 2 * HD) // 2
    heads = gains[:, pl.ds(2 * width, 2 * HD)]
    other = pltpu.roll(heads, HD, 1)
    first = lax.broadcasted_iota(jnp.int32, heads.shape, 1) < HD
    query, key = jnp.where(first, heads, other), jnp.where(first, other, heads)

    def of_tile(index):
        return jnp.where(index < HQ * HD // LANES, query, key)

    return gains[:, pl.ds(0, width)], gains[:, pl.ds(width, width)], of_tile


def tile_of(index, width=LANES):
    return pl.ds(pl.multiple_of(index * width, LANES), width)


def rows_of(index, size):
    return pl.ds(pl.multiple_of(index * size, 16), size)


def dot_last(left, right):
    return lax.dot_general(
        left, right, (((1,), (1,)), ((), ())), preferred_element_type=jnp.float32
    )


def probabilities(query, key, keep):
    scores = dot_last(query, key) * HD**-0.5
    scores = jnp.where(keep, scores, masked_score)
    weights = jnp.exp(scores - jnp.max(scores, -1, keepdims=True))
    return weights / jnp.sum(weights, -1, keepdims=True)


def attend_kernel(
    nd,
    nf,
    length,
    gains,
    cosine,
    sine,
    mask,
    tokens_full,
    down_full,
    in_full,
    out_full,
    cot_full,
    upper_in,
    upper_w,
    down_w,
    back_all,
    ffn_all,
    raw,
    heads,
    values,
    mixed,
    hidden_in,
    normed,
    ffn_in,
    tokens,
    w_down,
    in_w,
    out_w,
    down_x,
    cot,
    uz_send,
    uz_recv,
    uy_send,
    uy_recv,
    dz_send,
    dz_recv,
    dy_send,
    dy_recv,
    row_send,
    row_recv,
    local_sem,
):
    outer = nd // MEMBERS
    dp = lax.axis_index("dp")
    z = lax.axis_index("fsdp")
    y = dp // MEMBERS
    member = dp % MEMBERS
    x = member // 2
    c = member % 2

    def z_peer(step):
        return (dp, lax.rem(z + step, nf))

    def y_peer(step):
        return (lax.rem(y + step, outer) * MEMBERS + member, z)

    def from_z(step):
        return lax.rem(z - step + nf, nf)

    x_peer = (y * MEMBERS + (1 - x) * 2 + c, z)
    core_peer = (y * MEMBERS + x * 2 + 1 - c, z)
    barrier = pltpu.get_barrier_semaphore()
    peers = [z_peer(step) for step in range(1, nf)] + [y_peer(step) for step in range(1, outer)]
    peers += [x_peer, core_peer]
    for peer in peers:
        pl.semaphore_signal(barrier, inc=1, device_id=peer, device_id_type=MESH)
    gain_attn, gain_ffn, gain_heads = split_gains(gains)
    weights_here = []
    operands = (
        (down_full, w_down),
        (cot_full, cot),
        (tokens_full, tokens),
        (in_full, in_w),
        (out_full, out_w),
    )
    for index, (source, target) in enumerate(operands):
        copy = pltpu.make_async_copy(source, target, local_sem.at[4 + index])
        copy.start()
        weights_here.append(copy)
    for _ in range(2):
        weights_here.pop(0).wait()
    down_x[...] = w_down[...].astype(jnp.bfloat16)
    pl.semaphore_wait(barrier, len(peers))
    sent = []

    def remote(source, target, send, recv, device):
        copy = pltpu.make_async_remote_copy(
            src_ref=source,
            dst_ref=target,
            send_sem=send,
            recv_sem=recv,
            device_id=device,
            device_id_type=MESH,
        )
        copy.start()
        sent.append(copy)
        return copy

    def keep(index, source, target):
        copy = pltpu.make_async_copy(source, target, local_sem.at[index])
        copy.start()
        return copy

    arrivals = []
    upper_own = upper_w.at[y, :, z]
    down_own = down_w.at[y, z]
    steps_left = [step for step in range(1, nf) if step not in early_steps(nf)]
    upper_z = {
        step: remote(upper_own, upper_own, uz_send.at[step], uz_recv.at[step], z_peer(step))
        for step in steps_left
    }

    def upper_to_y(step):
        if step in upper_z:
            upper_z[step].wait_recv()
        piece = upper_w.at[y, :, from_z(step)]
        for hop in range(1, outer):
            arrivals.append(
                remote(piece, piece, uy_send.at[hop, step], uy_recv.at[hop, step], y_peer(hop))
            )

    for step in [0] + early_steps(nf):
        upper_to_y(step)
    down_z = [
        remote(down_x, down_own, dz_send.at[step], dz_recv.at[step], z_peer(step))
        for step in range(1, nf)
    ]
    kept = [keep(1, down_x, down_own), keep(2, cot, back_all.at[0])]
    cot_near = remote(cot, back_all.at[1], row_send.at[0, 0], row_recv.at[0, 0], core_peer)
    cot_far = remote(cot, back_all.at[2], row_send.at[0, 1], row_recv.at[0, 1], x_peer)

    def down_to_y(step):
        if step:
            down_z[step - 1].wait_recv()
        piece = down_w.at[y, from_z(step)] if step else down_x
        for hop in range(1, outer):
            arrivals.append(
                remote(
                    piece,
                    down_w.at[y, from_z(step)],
                    dy_send.at[hop, step],
                    dy_recv.at[hop, step],
                    y_peer(hop),
                )
            )

    count = tokens.shape[0]
    width = tokens.shape[1]
    chunk = 32

    weights_here.pop(0).wait()

    def norm_rows(index, carry):
        rows = rows_of(index, chunk)
        part = tokens[rows, :].astype(jnp.float32)
        scale = lax.rsqrt(jnp.mean(part * part, -1, keepdims=True) + norm_eps)
        normed[rows, :] = (part * scale * gain_attn).astype(jnp.bfloat16)
        return carry

    lax.fori_loop(0, count // chunk, norm_rows, 0)
    head_tiles = (HQ + KV) * HD // LANES
    for copy in weights_here:
        copy.wait()

    def project(index, carry):
        columns = tile_of(index, 2 * LANES)
        raw[:, columns] = jnp.dot(
            normed[...], in_w[:, columns], preferred_element_type=jnp.float32
        )
        return carry

    lax.fori_loop(0, head_tiles // 2, project, 0)
    values[...] = jnp.dot(
        normed[...], in_w[:, pl.ds(head_tiles * LANES, KV * HD)], preferred_element_type=jnp.float32
    ).astype(jnp.bfloat16)
    averages = block_mean()

    def turn(index, carry):
        columns = tile_of(index)
        for row in range(count // length):
            rows = pl.ds(row * length, length)
            part = raw[rows, columns]
            scale = lax.rsqrt(head_mean(part * part, averages) + norm_eps)
            part = part * scale * gain_heads(index)
            part = part * cosine[...] + swap_halves(part) * sine[...]
            heads[rows, columns] = part.astype(jnp.bfloat16)
        return carry

    lax.fori_loop(0, head_tiles, turn, 0)

    def attend(row):
        rows = pl.ds(row * length, length)
        allowed = mask[row] > 0.5

        def pair(tile, carry):
            key_tile = heads[rows, tile_of(HQ * HD // LANES + tile)]
            value_tile = values[rows, tile_of(tile)]
            for own in range(2):
                key = [in_half(key_tile, own, half) for half in range(2)]
                value = [in_half(value_tile, own, half) for half in range(2)]
                for quarter in range(2):
                    columns = tile_of(tile * 4 + own * 2 + quarter)
                    query = heads[rows, columns]
                    total = None
                    for half in range(2):
                        weights = probabilities(query, key[half], allowed).astype(jnp.bfloat16)
                        term = jnp.dot(weights, value[half], preferred_element_type=jnp.float32)
                        total = term if total is None else total + term
                    mixed[rows, columns] = total.astype(jnp.bfloat16)
            return carry

        lax.fori_loop(0, KV * HD // LANES, pair, 0)

    down_steps = list(range(nf))
    ffn_far, ffn_near = [], []

    def finish(row):
        rows = pl.ds(row * length, length)

        def project_out(index, carry):
            columns = tile_of(index, 2 * LANES)
            hidden_in[rows, columns] = tokens[rows, columns].astype(jnp.float32) + jnp.dot(
                mixed[rows, :], out_w[:, columns], preferred_element_type=jnp.float32
            )
            return carry

        lax.fori_loop(0, width // (2 * LANES), project_out, 0)

        def norm_hidden(index, carry):
            part_rows = pl.ds(pl.multiple_of(row * length + index * chunk, 16), chunk)
            part = hidden_in[part_rows, :]
            scale = lax.rsqrt(jnp.mean(part * part, -1, keepdims=True) + norm_eps)
            ffn_in[part_rows, :] = (part * scale * gain_ffn).astype(jnp.bfloat16)
            return carry

        lax.fori_loop(0, length // chunk, norm_hidden, 0)
        for slot, peer, copies in ((2, x_peer, ffn_far), (1, core_peer, ffn_near)):
            copies.append(
                remote(
                    ffn_in.at[rows],
                    ffn_all.at[slot, rows],
                    row_send.at[slot, row],
                    row_recv.at[slot, row],
                    peer,
                )
            )

    batch = count // length
    for row in range(batch):
        attend(row)
        finish(row)
        if row == 0:
            for step in steps_left:
                upper_to_y(step)
            down_to_y(down_steps.pop(0))
    kept.append(keep(3, ffn_in, ffn_all.at[0]))

    cot_far.wait_recv()
    cot_cross = remote(
        back_all.at[2], back_all.at[3], row_send.at[0, 2], row_recv.at[0, 2], core_peer
    )
    while len(down_steps) > 1:
        down_to_y(down_steps.pop(0))
    for row in range(batch):
        rows = pl.ds(row * length, length)
        ffn_far[row].wait_recv()
        ffn_near.append(
            remote(
                ffn_all.at[2, rows],
                ffn_all.at[3, rows],
                row_send.at[3, row],
                row_recv.at[3, row],
                core_peer,
            )
        )
    down_to_y(nf - 1)
    for copy in arrivals + ffn_near + [cot_near, cot_cross]:
        copy.wait_recv()
    for copy in sent:
        copy.wait_send()
    for copy in kept:
        copy.wait()


def attend(nd, nf, length, small, tokens, w_down, in_w, out_w, cot, upper_w):
    outer = nd // MEMBERS
    count, width = tokens.shape
    lo, hi = jnp.bfloat16, jnp.float32
    dma = pltpu.SemaphoreType.DMA
    moves = [(nf,), (outer, nf), (nf,), (outer, nf), (4, max(3, count // length))]
    shapes = [
        (upper_w.shape, lo),
        ((outer, nf) + w_down.shape, lo),
        ((MEMBERS, count, width), lo),
        ((MEMBERS, count, width), lo),
        ((count, (HQ + KV) * HD), hi),
        ((count, (HQ + KV) * HD), lo),
        ((count, KV * HD), lo),
        ((count, HQ * HD), lo),
        ((count, width), hi),
    ]
    early = [(count, width), (count, width), (count, width)]
    late = [in_w.shape, out_w.shape, w_down.shape, (count, width)]
    return pl.pallas_call(
        functools.partial(attend_kernel, nd, nf, length),
        name="attend",
        out_shape=tuple(jax.ShapeDtypeStruct(*item) for item in shapes),
        in_specs=[ON_CHIP] * 4 + [ANYWHERE] * 6,
        out_specs=(ANYWHERE,) * 4 + (ON_CHIP,) * 5,
        input_output_aliases={9: 0},
        scratch_shapes=[pltpu.VMEM(shape, lo) for shape in early]
        + [pltpu.VMEM(w_down.shape, hi)]
        + [pltpu.VMEM(shape, lo) for shape in late]
        + [dma(shape) for shape in moves for _ in range(2)]
        + [dma((10,))],
        compiler_params=pltpu.CompilerParams(
            collective_id=2, has_side_effects=True, vmem_limit_bytes=VMEM_MOST
        ),
    )(*small, tokens, w_down, in_w, out_w, cot, upper_w)


def backward_kernel(
    nd,
    nf,
    length,
    gains,
    cosine,
    sine,
    mask,
    out_near,
    out_far,
    down_got,
    down_terms,
    gate_terms,
    upper_terms,
    mine_full,
    near_full,
    far_full,
    hidden_full,
    cot_full,
    out_w_full,
    mixed_full,
    heads_full,
    values_full,
    tokens_full,
    raw_full,
    in_w_full,
    out_core,
    out_x,
    gate_parts,
    upper_parts,
    input_grad,
    in_sum,
    out_sum,
    down_sum,
    gain_totals,
    norm,
    sum_attn,
    sum_ffn,
    sum_heads,
    gain_here,
    gain_group,
    gain_got,
    gain_far,
    square_here,
    square_group,
    square_got,
    square_far,
    mine_ref,
    core_near,
    from_x,
    hidden_in,
    cot,
    out_w,
    mixed,
    heads,
    values,
    tokens,
    raw,
    in_w,
    out_pass,
    out_core_far,
    normed,
    branch,
    grad_mixed,
    grad_hidden,
    grad_raw,
    wide,
    in_terms,
    out_terms,
    in_core,
    out_core_terms,
    in_x,
    out_x_terms,
    in_y,
    out_y_terms,
    in_total,
    out_total,
    in_zs,
    out_zs,
    in_zr,
    out_zr,
    down_own,
    gate_own,
    upper_own,
    down_y,
    gate_y,
    upper_y,
    down_z,
    gate_z,
    upper_z,
    row_send,
    row_recv,
    fy_send,
    fy_recv,
    fz_send,
    fz_recv,
    swap_send,
    swap_recv,
    ac_send,
    ac_recv,
    ax_send,
    ax_recv,
    ay_send,
    ay_recv,
    az_send,
    az_recv,
    tg_send,
    tg_recv,
    tf_send,
    tf_recv,
    load_sem,
    got_sem,
    operand_sem,
    local_sem,
):
    outer = nd // MEMBERS
    dp = lax.axis_index("dp")
    z = lax.axis_index("fsdp")
    y = dp // MEMBERS
    member = dp % MEMBERS
    x = member // 2
    c = member % 2
    lo, hi = jnp.bfloat16, jnp.float32

    def z_to(step):
        return lax.rem(z + step, nf)

    def z_peer(step):
        return (dp, z_to(step))

    def y_to(step):
        return lax.rem(y + step, outer)

    def y_peer(step):
        return (y_to(step) * MEMBERS + member, z)

    def in_group(k):
        return (y * MEMBERS + k, z)

    x_peer = in_group((1 - x) * 2 + c)
    core_peer = in_group(x * 2 + 1 - c)
    barrier = pltpu.get_barrier_semaphore()
    peers = [z_peer(step) for step in range(1, nf)] + [y_peer(step) for step in range(1, outer)]
    peers += [x_peer, core_peer, in_group(MEMBERS - 1 - member)]
    crossed = [(hop, step) for hop in range(outer) for step in range(nf) if hop or step]

    def cross_peer(hop, step):
        return (y_to(hop) * MEMBERS + member, z_to(step))

    peers += [cross_peer(hop, step) for hop, step in crossed if hop and step]
    fulls = (mine_full, near_full, far_full, hidden_full, cot_full, out_w_full, mixed_full)
    fulls += (heads_full, values_full, tokens_full, raw_full, in_w_full)
    places = (mine_ref, core_near, from_x, hidden_in, cot, out_w, mixed)
    places += (heads, values, tokens, raw, in_w)
    operands = [
        pltpu.make_async_copy(source, target, operand_sem.at[index])
        for index, (source, target) in enumerate(zip(fulls, places))
    ]
    start_all(operands)

    def ready(number):
        for _ in range(number):
            operands.pop(0).wait()

    for peer in peers:
        pl.semaphore_signal(barrier, inc=1, device_id=peer, device_id_type=MESH)
    pl.semaphore_wait(barrier, len(peers))
    sent = []

    def remote(source, target, send, recv, device):
        copy = pltpu.make_async_remote_copy(
            src_ref=source,
            dst_ref=target,
            send_sem=send,
            recv_sem=recv,
            device_id=device,
            device_id_type=MESH,
        )
        copy.start()
        sent.append(copy)
        return copy

    def keep(semaphore, source, target):
        copy = pltpu.make_async_copy(source, target, semaphore)
        copy.start()
        return copy

    gain_attn, gain_ffn, gain_heads = split_gains(gains)
    count, width = tokens.shape
    here, there = pl.ds(0, count), pl.ds(count, count)

    out_far_copy = remote(out_far.at[there], out_core_far, row_send.at[0], row_recv.at[0], core_peer)
    out_pass_copy = keep(local_sem.at[0], out_far.at[here], out_pass)
    out_near_copy = remote(out_near.at[there], out_core, row_send.at[1], row_recv.at[1], core_peer)

    terms = (down_terms, gate_terms, upper_terms)
    owns = (down_own, gate_own, upper_own)
    over_y = (down_y, gate_y, upper_y)
    over_z = (down_z, gate_z, upper_z)

    def piece_of(matrix, place, step):
        if matrix == 0:
            return terms[0].at[place, z_to(step)]
        return terms[matrix].at[place, :, z_to(step)]

    order = [(matrix, step) for matrix in range(3) for step in list(range(1, nf)) + [0]]
    y_copies, loads = {}, {}
    for matrix, step in order:
        loads[matrix, step] = keep(
            load_sem.at[matrix, step], piece_of(matrix, y, step), owns[matrix].at[step]
        )
        for hop in range(1, outer):
            if matrix == 0:
                y_copies[0, step, hop] = keep(
                    got_sem.at[hop, step], down_got.at[hop - 1, z_to(step)], down_y.at[hop - 1, step]
                )
                continue
            y_copies[matrix, step, hop] = remote(
                piece_of(matrix, y_to(hop), step),
                over_y[matrix].at[hop - 1, step],
                fy_send.at[matrix, hop, step],
                fy_recv.at[matrix, hop, step],
                y_peer(hop),
            )
    z_copies = {}
    waiting = list(order)

    def pieces(number):
        for _ in range(min(number, len(waiting))):
            matrix, step = waiting.pop(0)
            loads[matrix, step].wait()
            total = owns[matrix][step].astype(hi)
            for hop in range(1, outer):
                if matrix:
                    y_copies[matrix, step, hop].wait_recv()
                else:
                    y_copies[0, step, hop].wait()
                total = total + over_y[matrix][hop - 1, step].astype(hi)
            owns[matrix][step] = total.astype(lo)
            if step:
                z_copies[matrix, step] = remote(
                    owns[matrix].at[step],
                    over_z[matrix].at[step - 1],
                    fz_send.at[matrix, step],
                    fz_recv.at[matrix, step],
                    z_peer(step),
                )

    def piece_total(matrix):
        total = owns[matrix][0].astype(hi)
        for step in range(1, nf):
            z_copies[matrix, step].wait_recv()
            total = total + over_z[matrix][step - 1].astype(hi)
        return total

    swaps = []

    squares = []

    def trade(matrix, parts):
        total = piece_total(matrix).astype(lo)
        owns[matrix][0] = total
        total = total.astype(hi)
        squares.append(jnp.sum(total * total))
        for mask_bits in range(1, MEMBERS):
            other = member ^ mask_bits
            swaps.append(
                remote(
                    owns[matrix].at[0, other],
                    parts.at[member],
                    swap_send.at[matrix - 1, mask_bits],
                    swap_recv.at[matrix - 1, mask_bits],
                    in_group(other),
                )
            )
        swaps_local.append(
            keep(local_sem.at[2 + matrix], owns[matrix].at[0, member], parts.at[member])
        )

    swaps_local = []
    chunk = 32

    def to_group(index, source, target):
        target[member] = source[...]
        return [
            remote(
                source,
                target.at[member],
                tg_send.at[index, mask_bits],
                tg_recv.at[index, mask_bits],
                in_group(member ^ mask_bits),
            )
            for mask_bits in range(1, MEMBERS)
        ]

    def to_crossed(index, source, target):
        target[y * nf + z] = source[...]
        return [
            remote(
                source,
                target.at[y * nf + z],
                tf_send.at[index, place],
                tf_recv.at[index, place],
                cross_peer(hop, step),
            )
            for place, (hop, step) in enumerate(crossed)
        ]

    def summed(got, copies):
        for copy in copies:
            copy.wait_recv()
        return jnp.sum(got[...], 0)

    pieces(nf)

    def add_rows(target, other):
        def step_once(index, carry):
            rows = rows_of(index, chunk)
            target[rows, :] = (target[rows, :].astype(hi) + other[rows, :].astype(hi)).astype(lo)
            return carry

        lax.fori_loop(0, count // chunk, step_once, 0)

    def norm_rows(index, carry):
        rows = rows_of(index, chunk)
        part = tokens[rows, :].astype(hi)
        scale = lax.rsqrt(jnp.mean(part * part, -1, keepdims=True) + norm_eps)
        normed[rows, :] = (part * scale * gain_attn).astype(lo)
        return carry

    sum_attn[...] = jnp.zeros_like(sum_attn)
    sum_ffn[...] = jnp.zeros_like(sum_ffn)
    sum_heads[...] = jnp.zeros_like(sum_heads)
    ready(5)

    def norm_back(part, gain, grad):
        scale = lax.rsqrt(jnp.mean(part * part, -1, keepdims=True) + norm_eps)
        unit = part * scale
        inner = grad * gain
        back = scale * (inner - unit * jnp.mean(inner * unit, -1, keepdims=True))
        return back, jnp.sum(grad * unit, 0, keepdims=True)

    def ffn_norm_back(index, carry):
        rows = rows_of(index, chunk)
        grad = mine_ref[rows, :].astype(hi) + core_near[rows, :].astype(hi)
        grad = grad + from_x[rows, :].astype(hi)
        back, gain_term = norm_back(hidden_in[rows, :], gain_ffn, grad)
        sum_ffn[...] += gain_term
        back = back + cot[rows, :].astype(hi)
        grad_hidden[rows, :] = back
        branch[rows, :] = back.astype(lo)
        return carry

    lax.fori_loop(0, count // chunk, ffn_norm_back, 0)
    pair = 2 * LANES
    ready(2)

    def mixed_back(index, carry):
        columns = tile_of(index, pair)
        grad_mixed[:, columns] = dot_last(branch[...], out_w[columns, :]).astype(lo)
        return carry

    lax.fori_loop(0, HQ * HD // pair, mixed_back, 0)

    def outer_product(left, right, target):
        def step_once(index, carry):
            columns = tile_of(index, pair)
            turned = left[:, columns].T
            for part in range(right.shape[1] // (2 * pair)):
                across = pl.ds(part * 2 * pair, 2 * pair)
                target[columns, across] = jnp.dot(
                    turned, right[:, across], preferred_element_type=hi
                ).astype(lo)
            rest = right.shape[1] % (2 * pair)
            if rest:
                across = pl.ds(right.shape[1] - rest, rest)
                target[columns, across] = jnp.dot(
                    turned, right[:, across], preferred_element_type=hi
                ).astype(lo)
            return carry

        lax.fori_loop(0, left.shape[1] // pair, step_once, 0)

    all_terms = (in_terms, out_terms)
    sizes = (in_terms.shape[0] // (nd), out_terms.shape[0] // (nd))
    core_terms = (in_core, out_core_terms)
    x_terms = (in_x, out_x_terms)
    y_terms = (in_y, out_y_terms)
    totals = (in_total, out_total)
    zs = (in_zs, out_zs)
    zr = (in_zr, out_zr)
    hops = list(range(1, outer)) + [0]
    core_copies, ax_copies, ay_copies, az_copies = {}, {}, {}, {}

    def block(a, hop, bx, bc):
        index = (y_to(hop) * 2 + bx) * 2 + bc
        return pl.ds(pl.multiple_of(index * sizes[a], 16), sizes[a])

    def core_out(a):
        for far in (1, 0):
            for hop in hops:
                bx = 1 - x if far else x
                core_copies[a, hop, far] = remote(
                    all_terms[a].at[block(a, hop, bx, 1 - c)],
                    core_terms[a].at[hop, far],
                    ac_send.at[a, hop, far],
                    ac_recv.at[a, hop, far],
                    core_peer,
                )

    def add_block(a, rows, others):
        some = math.gcd(sizes[a], 32)

        def step_once(index, carry):
            base = rows.start + index * some
            place = pl.ds(pl.multiple_of(base, 16), some)
            total = all_terms[a][place, :].astype(hi)
            for other in others:
                total = total + other[rows_of(index, some), :].astype(hi)
            all_terms[a][place, :] = total.astype(lo)
            return carry

        lax.fori_loop(0, sizes[a] // some, step_once, 0)

    def core_in(a):
        for hop in hops:
            core_copies[a, hop, 1].wait_recv()
            rows = block(a, hop, 1 - x, c)
            add_block(a, rows, [core_terms[a].at[hop, 1]])
            ax_copies[a, hop] = remote(
                all_terms[a].at[rows],
                x_terms[a].at[hop],
                ax_send.at[a, hop],
                ax_recv.at[a, hop],
                x_peer,
            )

    def x_in(a):
        for hop in range(1, outer):
            core_copies[a, hop, 0].wait_recv()
            ax_copies[a, hop].wait_recv()
            rows = block(a, hop, x, c)
            add_block(a, rows, [core_terms[a].at[hop, 0], x_terms[a].at[hop]])
            ay_copies[a, hop] = remote(
                all_terms[a].at[rows],
                y_terms[a].at[hop - 1],
                ay_send.at[a, hop],
                ay_recv.at[a, hop],
                y_peer(hop),
            )

    def y_in(a):
        core_copies[a, 0, 0].wait_recv()
        ax_copies[a, 0].wait_recv()
        others = [core_terms[a].at[0, 0], x_terms[a].at[0]]
        for hop in range(1, outer):
            ay_copies[a, hop].wait_recv()
            others.append(y_terms[a].at[hop - 1])
        start = block(a, 0, x, c).start
        some = math.gcd(sizes[a], 32)

        def step_once(index, carry):
            place = rows_of(index, some)
            own = pl.ds(pl.multiple_of(start + index * some, 16), some)
            total = all_terms[a][own, :].astype(hi)
            for other in others:
                total = total + other[place, :].astype(hi)
            totals[a][place, :] = total
            return carry

        lax.fori_loop(0, sizes[a] // some, step_once, 0)
        rows = sizes[a] // nf
        for place in range(nf):
            zs[a][place] = totals[a][place * rows : (place + 1) * rows, :].astype(lo)
        for step in range(1, nf):
            az_copies[a, step] = remote(
                zs[a].at[z_to(step)],
                zr[a].at[step - 1],
                az_send.at[a, step],
                az_recv.at[a, step],
                z_peer(step),
            )

    def z_in(a, target):
        total = zs[a][z].astype(hi)
        for step in range(1, nf):
            az_copies[a, step].wait_recv()
            total = total + zr[a][step - 1].astype(hi)
        target[...] = total

    outer_product(mixed, branch, out_terms)
    core_out(1)
    pieces(2)
    ready(len(operands))
    query_tiles = HQ * HD // LANES
    head_tiles = (HQ + KV) * HD // LANES
    key_tiles = KV * HD // LANES

    def over_rows(left, right):
        return lax.dot_general(left, right, (((0,), (0,)), ((), ())), preferred_element_type=hi)

    def attend_back(row):
        rows = pl.ds(row * length, length)
        allowed = mask[row] > 0.5

        def pair_back(tile, carry):
            key_tile = heads[rows, tile_of(query_tiles + tile)]
            value_tile = values[rows, tile_of(tile)]
            grad_key = None
            grad_value = None
            for own in range(2):
                key = [in_half(key_tile, own, half) for half in range(2)]
                value = [in_half(value_tile, own, half) for half in range(2)]
                for half in range(2):
                    key_total, value_total = None, None
                    for quarter in range(2):
                        columns = tile_of(tile * 4 + own * 2 + quarter)
                        query = heads[rows, columns]
                        grad = grad_mixed[rows, columns]
                        weights = probabilities(query, key[half], allowed)
                        slope = dot_last(grad, value[half])
                        inner = jnp.sum(weights * slope, -1, keepdims=True)
                        score = (weights * (slope - inner)).astype(lo)
                        back = jnp.dot(score, key[half], preferred_element_type=hi) * HD**-0.5
                        if half == 0:
                            wide[rows, columns] = back
                        else:
                            wide[rows, columns] += back
                        key_term = over_rows(score, query)
                        value_term = over_rows(weights.astype(lo), grad)
                        key_total = key_term if key_total is None else key_total + key_term
                        value_total = value_term if value_total is None else value_total + value_term
                    key_term = in_half(key_total, half, own)
                    value_term = in_half(value_total, half, own)
                    grad_key = key_term if grad_key is None else grad_key + key_term
                    grad_value = value_term if grad_value is None else grad_value + value_term
            wide[rows, tile_of(query_tiles + tile)] = grad_key * HD**-0.5
            grad_raw[rows, tile_of(head_tiles + tile)] = grad_value.astype(lo)
            return carry

        lax.fori_loop(0, key_tiles, pair_back, 0)

    batch = count // length
    for row in range(batch):
        attend_back(row)
        if row == 0:
            core_in(1)
        pieces(1)
    averages = block_mean()

    def turn_back(index, carry):
        columns = tile_of(index)
        gain = gain_heads(index)
        for row in range(batch):
            rows = pl.ds(row * length, length)
            grad = wide[rows, columns]
            grad = grad * cosine[...] - swap_halves(grad) * sine[...]
            part = raw[rows, columns]
            scale = lax.rsqrt(head_mean(part * part, averages) + norm_eps)
            unit = part * scale
            sum_heads[:, columns] += jnp.sum(grad * unit, 0, keepdims=True)
            inner = grad * gain
            back = scale * (inner - unit * head_mean(inner * unit, averages))
            grad_raw[rows, columns] = back.astype(lo)
        return carry

    lax.fori_loop(0, head_tiles, turn_back, 0)
    lax.fori_loop(0, count // chunk, norm_rows, 0)
    outer_product(normed, grad_raw, in_terms)
    core_out(0)
    pieces(1)
    x_in(1)

    def normed_back(index, carry):
        columns = tile_of(index, pair)
        wide[:, columns] = dot_last(grad_raw[...], in_w[columns, :])
        return carry

    core_in(0)
    out_far_copy.wait_recv()
    out_pass_copy.wait()
    add_rows(out_pass, out_core_far)
    out_x_copy = remote(out_pass, out_x, row_send.at[2], row_recv.at[2], x_peer)
    lax.fori_loop(0, width // pair, normed_back, 0)

    def attn_norm_back(index, carry):
        rows = rows_of(index, chunk)
        back, gain_term = norm_back(tokens[rows, :].astype(hi), gain_attn, wide[rows, :])
        sum_attn[...] += gain_term
        input_grad[rows, :] = (back + grad_hidden[rows, :]).astype(lo)
        return carry

    lax.fori_loop(0, count // chunk, attn_norm_back, 0)
    gain_here[...] = jnp.zeros_like(gain_here)
    place = 0
    for source in (sum_attn, sum_ffn, sum_heads):
        for tile in range(source.shape[1] // LANES):
            gain_here[pl.ds(place, 1), :] = source[:, tile * LANES : (tile + 1) * LANES]
            place += 1
    gain_copies = to_group(0, gain_here, gain_got)
    pieces(1)
    x_in(0)
    down_sum[...] = piece_total(0)
    y_in(1)
    pieces(2 * nf)
    trade(1, gate_parts)
    y_in(0)
    gain_group[...] = summed(gain_got, gain_copies)
    gain_copies = to_crossed(0, gain_group, gain_far)
    z_in(1, out_sum)
    trade(2, upper_parts)
    z_in(0, in_sum)
    for target in (down_sum, out_sum, in_sum):
        squares.append(jnp.sum(target[...] * target[...]))
    square_here[...] = jnp.full(square_here.shape, sum(squares))
    square_copies = to_group(1, square_here, square_got)
    square_group[...] = summed(square_got, square_copies)
    square_copies = to_crossed(1, square_group, square_far)
    gain_totals[...] = summed(gain_far, gain_copies)
    gain_place = 2 * width // LANES
    gain_squares = gain_totals[:gain_place, :]
    gain_squares = jnp.sum(gain_squares * gain_squares)
    for first, last in ((0, query_tiles), (query_tiles, head_tiles)):
        total = jnp.sum(gain_totals[gain_place + first : gain_place + last, :], 0, keepdims=True)
        total = jnp.broadcast_to(total, (8, LANES))
        total = total + pltpu.roll(total, HD, 1)
        gain_squares += jnp.sum(total * total) / (8 * LANES // HD)
    norm[...] = jnp.sqrt(summed(square_far, square_copies) + gain_squares)
    for copy in swaps + [out_near_copy, out_x_copy]:
        copy.wait_recv()
    for copy in sent:
        copy.wait_send()
    for copy in swaps_local:
        copy.wait()


def backward(nd, nf, length, small, halves, terms, operands):
    outer = nd // MEMBERS
    count, width = operands[0].shape
    out_w, in_w = operands[5], operands[-1]
    _, down_terms, gate_terms, _ = terms
    lo, hi = jnp.bfloat16, jnp.float32
    dma = pltpu.SemaphoreType.DMA
    in_rows, in_cols = in_w.shape[0] // (nd * nf), in_w.shape[1]
    out_rows, out_cols = out_w.shape[0] // (nd * nf), out_w.shape[1]
    inner = (MEMBERS,) + gate_terms.shape[3:]
    down = down_terms.shape[2:]
    tiles = (2 * width + (HQ + KV) * HD) // LANES
    gain_tile = (-(-tiles // 8) * 8, LANES)
    far = outer * nf - 1
    shapes = [
        ((count, width), lo),
        ((count, width), lo),
        (inner, lo),
        (inner, lo),
        ((count, width), lo),
        ((in_rows, in_cols), hi),
        ((out_rows, out_cols), hi),
        (down, hi),
        (gain_tile, hi),
        ((8, LANES), hi),
    ]
    in_block, out_block = (nf * in_rows, in_cols), (nf * out_rows, out_cols)
    scratch = [((1, width), hi), ((1, width), hi), ((1, (HQ + KV) * HD), hi)]
    for tile in (gain_tile, (8, LANES)):
        scratch += [(tile, hi), (tile, hi), ((MEMBERS,) + tile, hi), ((outer * nf,) + tile, hi)]
    scratch += [(operand.shape, operand.dtype) for operand in operands]
    scratch += [((count, width), lo)] * 2
    scratch += [
        ((count, width), lo),
        ((count, width), lo),
        ((count, HQ * HD), lo),
        ((count, width), hi),
        ((count, in_cols), lo),
        ((count, width), hi),
        (in_w.shape, lo),
        (out_w.shape, lo),
        ((outer, 2) + in_block, lo),
        ((outer, 2) + out_block, lo),
        ((outer,) + in_block, lo),
        ((outer,) + out_block, lo),
        ((outer - 1,) + in_block, lo),
        ((outer - 1,) + out_block, lo),
        (in_block, hi),
        (out_block, hi),
        ((nf, in_rows, in_cols), lo),
        ((nf, out_rows, out_cols), lo),
        ((nf - 1, in_rows, in_cols), lo),
        ((nf - 1, out_rows, out_cols), lo),
        ((nf,) + down, lo),
        ((nf,) + inner, lo),
        ((nf,) + inner, lo),
        ((outer - 1, nf) + down, lo),
        ((outer - 1, nf) + inner, lo),
        ((outer - 1, nf) + inner, lo),
        ((nf - 1,) + down, lo),
        ((nf - 1,) + inner, lo),
        ((nf - 1,) + inner, lo),
    ]
    moves = [(3,), (3, outer, nf), (3, nf), (2, MEMBERS), (2, outer, 2), (2, outer), (2, outer)]
    moves += [(2, nf), (2, MEMBERS), (2, far)]
    return pl.pallas_call(
        functools.partial(backward_kernel, nd, nf, length),
        name="backward",
        out_shape=tuple(jax.ShapeDtypeStruct(*item) for item in shapes),
        in_specs=[ON_CHIP] * 4 + [ANYWHERE] * (6 + len(operands)),
        out_specs=(ANYWHERE,) * 4 + (ON_CHIP,) * 6,
        scratch_shapes=[pltpu.VMEM(*item) for item in scratch]
        + [dma(shape) for shape in moves for _ in range(2)]
        + [dma((3, nf)), dma((outer, nf)), dma((len(operands),)), dma((5,))],
        compiler_params=pltpu.CompilerParams(
            collective_id=3, has_side_effects=True, vmem_limit_bytes=VMEM_MOST
        ),
    )(*small, *halves, *terms, *operands)


def adam_kernel(
    span, norm, gain_totals, in_sum, out_sum, gate_parts, upper_parts, down_sum, *rest
):
    count = 8
    row_terms, rest = rest[:4], rest[4:]
    masters, firsts, seconds = rest[:count], rest[count : 2 * count], rest[2 * count : 3 * count]
    rest = rest[3 * count :]
    outs = [rest[index * count : (index + 1) * count] for index in range(3)]
    copies = rest[3 * count : 4 * count - 1]
    output = rest[4 * count - 1]
    rest = rest[4 * count :]
    ins_here = [rest[index * count : (index + 1) * count] for index in range(3)]
    rest = rest[3 * count :]
    outs_here = [rest[index * count : (index + 1) * count] for index in range(3)]
    copies_here = rest[3 * count : 4 * count - 1]
    sums_here = rest[4 * count - 1 : 4 * count + 4]
    terms_here = rest[4 * count + 4 : 4 * count + 8]
    output_here, sum_sem, in_sem, out_sem, term_sem = rest[4 * count + 8 :]
    sums = (in_sum, out_sum, gate_parts, upper_parts, down_sum)
    loads = {}
    for index in (6, 4, 5, 3, 0, 1, 2, 7):
        source = {6: 4, 4: 2, 5: 3, 3: 1, 0: 0}.get(index)
        if source is not None:
            loads[source] = pltpu.make_async_copy(
                sums[source], sums_here[source], sum_sem.at[source]
            )
            loads[source].start()
        for kind, arrays in enumerate((masters, firsts, seconds)):
            loads[index, kind] = pltpu.make_async_copy(
                arrays[index], ins_here[kind][index], in_sem.at[kind, index]
            )
            loads[index, kind].start()
    rows_count = output.shape[0]
    term_loads = []
    for index, (source, target) in enumerate(zip(row_terms, terms_here)):
        copy = pltpu.make_async_copy(
            source.at[pl.ds(0, rows_count)], target, term_sem.at[index]
        )
        copy.start()
        term_loads.append(copy)
    stores = []

    def store(index):
        pairs = [(outs_here[kind][index], outs[kind][index]) for kind in range(3)]
        if index < count - 1:
            pairs.append((copies_here[index], copies[index]))
        for kind, (source, target) in enumerate(pairs):
            copy = pltpu.make_async_copy(source, target, out_sem.at[kind, index])
            copy.start()
            stores.append(copy)

    factor = jnp.minimum(1.0, clip_limit / (norm[0:1, 0:1] + 1e-06))
    weight_rate = 2.0 * D ** (-0.5)

    def update(index, columns, grad, rate, decay):
        grad = grad * factor
        master, first, second = (ins_here[kind][index][:, columns] for kind in range(3))
        new, second_new = adam_update(master, first, second, grad, rate, decay)
        outs_here[0][index][:, columns] = grad
        outs_here[1][index][:, columns] = new
        outs_here[2][index][:, columns] = second_new
        if index < count - 1:
            copies_here[index][:, columns] = new.astype(jnp.bfloat16)

    def arrived(index):
        for kind in range(3):
            loads[index, kind].wait()

    step = 2 * LANES
    loads[4].wait()
    arrived(6)
    for start in range(0, down_sum.shape[1], step):
        columns = slice(start, start + step)
        update(6, columns, sums_here[4][:, columns], weight_rate, decay_rate)
    store(6)
    members, _, mine = gate_parts.shape
    for index in (4, 5):
        loads[index - 2].wait()
        arrived(index)
        place = 0
        for part in range(mine // span):
            for member in range(members):
                grad = sums_here[index - 2][member, :, part * span : (part + 1) * span]
                columns = slice(place, place + span)
                update(index, columns, grad.astype(jnp.float32), weight_rate, decay_rate)
                place += span
        store(index)
    loads[1].wait()
    arrived(3)
    for start in range(0, out_sum.shape[1], step):
        columns = slice(start, start + step)
        update(3, columns, sums_here[1][:, columns], weight_rate, decay_rate)
    store(3)
    loads[0].wait()
    place = 0
    for index in range(3):
        arrived(index)
        for start in range(0, masters[index].shape[1], step):
            grad = sums_here[0][:, place : place + step]
            update(index, slice(start, start + step), grad, weight_rate, decay_rate)
            place += step
        store(index)
    arrived(7)
    norm_rows = 2 * D // LANES
    head_rows = HQ * HD // LANES
    key_rows = KV * HD // LANES
    folded = []
    for first, size in ((norm_rows, head_rows), (norm_rows + head_rows, key_rows)):
        total = jnp.sum(gain_totals[first : first + size, :], 0, keepdims=True)
        folded.append(total + pltpu.roll(jnp.broadcast_to(total, (8, LANES)), HD, 1)[:1])
    lane = lax.broadcasted_iota(jnp.int32, (1, LANES), 1)
    heads = jnp.where(lane < HD, folded[0], folded[1])
    gain_grad = jnp.concatenate([gain_totals[:norm_rows, :], heads], 0)
    update(7, slice(None), gain_grad, gain_rate, 0.0)
    store(7)
    for copy in term_loads:
        copy.wait()

    def add_rows(index, carry):
        rows = rows_of(index, 32)
        total = terms_here[0][rows, :]
        for term in terms_here[1:]:
            total = total + term[rows, :].astype(jnp.float32)
        output_here[rows, :] = total.astype(jnp.bfloat16)
        return carry

    lax.fori_loop(0, rows_count // 32, add_rows, 0)
    copy = pltpu.make_async_copy(output_here, output, term_sem.at[0])
    copy.start()
    stores.append(copy)
    for copy in stores:
        copy.wait()


def adam(span, norm, gain_totals, sums, row_terms, masters, firsts, seconds):
    lo, hi = jnp.bfloat16, jnp.float32
    dma = pltpu.SemaphoreType.DMA
    shapes = [(array.shape, hi) for _ in range(3) for array in masters]
    shapes += [(array.shape, lo) for array in masters[:-1]]
    rows_shape = row_terms[0].shape
    inputs = [(array.shape, hi) for _ in range(3) for array in masters]
    scratch = inputs + shapes + [(array.shape, array.dtype) for array in sums]
    scratch += [(rows_shape, array.dtype) for array in row_terms] + [(rows_shape, lo)]
    shapes += [(rows_shape, lo)]
    return pl.pallas_call(
        functools.partial(adam_kernel, span),
        name="adam",
        out_shape=tuple(jax.ShapeDtypeStruct(*item) for item in shapes),
        in_specs=[ON_CHIP] * 2 + [ANYWHERE] * (9 + len(inputs)),
        out_specs=(ANYWHERE,) * len(shapes),
        scratch_shapes=[pltpu.VMEM(*item) for item in scratch]
        + [dma((5,)), dma((3, len(masters))), dma((4, len(masters))), dma((4,))],
        compiler_params=pltpu.CompilerParams(vmem_limit_bytes=VMEM_MOST),
    )(norm, gain_totals, *sums, *row_terms, *masters, *firsts, *seconds)


def after(value, *others):
    return lax.optimization_barrier((value,) + others)[0]


def low(value):
    return value.astype(jnp.bfloat16)


def shards(
    nd,
    nf,
    tokens,
    cotangent,
    segment_ids,
    w_query,
    w_key,
    w_value,
    w_out,
    w_gate,
    w_up,
    w_down,
    m_query,
    m_key,
    m_value,
    m_out,
    m_gate,
    m_up,
    m_down,
    v_query,
    v_key,
    v_value,
    v_out,
    v_gate,
    v_up,
    v_down,
    gains,
    gain_first,
    gain_second,
):
    masters = (w_query, w_key, w_value, w_out, w_gate, w_up, w_down)
    firsts = (m_query, m_key, m_value, m_out, m_gate, m_up, m_down)
    seconds = (v_query, v_key, v_value, v_out, v_gate, v_up, v_down)
    outer = nd // MEMBERS
    dp = lax.axis_index("dp")
    ring_z = Ring(nf, lax.axis_index("fsdp"), lambda d, f, s: (d, (f + s) % nf), nd, nf)
    ring_y = Ring(
        outer,
        dp // MEMBERS,
        lambda d, f, s: ((d // MEMBERS + s) % outer * MEMBERS + d % MEMBERS, f),
        nd,
        nf,
    )
    ring_x = Ring(2, dp // 2 % 2, lambda d, f, s: (d ^ 2, f), nd, nf)
    ring_core = Ring(2, dp % 2, lambda d, f, s: (d ^ 1, f), nd, nf)
    member = dp % MEMBERS

    def trade(block, mask):
        return Ring(2, dp % 2, lambda d, f, s: (d ^ mask, f), nd, nf).move(block, 1)

    def swap(blocks):
        full = put(jnp.zeros_like(blocks), pick(blocks, 0, member), 0, member)
        for mask in range(1, MEMBERS):
            full = put(full, trade(pick(blocks, 0, member ^ mask), mask), 0, member ^ mask)
        return full

    def spread(rows):
        far = ring_x.move(rows, 1)
        near = jnp.concatenate([rows, ring_core.move(rows, 1)], 0)
        return near, jnp.concatenate([far, ring_core.move(far, 1)], 0)

    def collapse(near, far):
        rows = near.shape[0] // 2
        got = ring_core.move(far[rows:], 1).astype(jnp.float32)
        got = ring_x.move(low(far[:rows].astype(jnp.float32) + got), 1)
        total = near[:rows].astype(jnp.float32)
        total = total + ring_core.move(near[rows:], 1).astype(jnp.float32)
        return total + got.astype(jnp.float32)

    batch, length, width = tokens.shape
    count = batch * length
    hidden_rows = w_down.shape[0]
    span = nf * hidden_rows
    mine = outer * span
    in_rows = w_query.shape[0]
    out_rows = w_out.shape[0]
    attn_cols = (HQ + 2 * KV) * HD

    in_w, out_w, gate_w, upper_w = gather_weights(nd, nf, masters[:6])
    in_w = in_w.reshape(D, attn_cols)
    out_w = out_w.reshape(HQ * HD, D)

    positions = jnp.arange(length)
    causal = positions[None, :] <= positions[:, None]
    allowed = causal[None] & (segment_ids[:, :, None] == segment_ids[:, None, :])
    small = (gains[None], *rotary_tables(length), allowed.astype(jnp.float32))
    back_in = cotangent.reshape(count, width)
    token_rows = tokens.reshape(count, width)
    (
        upper_w,
        down_w,
        back_all,
        ffn_all,
        raw,
        heads,
        values,
        mixed,
        hidden_in,
    ) = attend(
        nd, nf, length, small, token_rows, w_down, in_w, out_w, back_in, upper_w
    )
    gate_w = gate_w.reshape(D, mine)
    upper_w = upper_w.reshape(D, mine)
    down_w = down_w.reshape(mine, D)
    back_all = back_all.reshape(MEMBERS * count, width)
    ffn_all = ffn_all.reshape(MEMBERS * count, width)
    back_halves = (back_all[: 2 * count], back_all[2 * count :])
    ffn_halves = (ffn_all[: 2 * count], ffn_all[2 * count :])
    def inner_grads(back_half, gate, upper):
        grad_hidden = back_product(back_half, down_w)
        _, pull = jax.vjp(swiglu, gate, upper)
        grad_gate, grad_upper = pull(grad_hidden)
        grad_gate, grad_upper = low(grad_gate), low(grad_upper)
        back = back_product(grad_gate, gate_w) + back_product(grad_upper, upper_w)
        return grad_gate, grad_upper, low(back)

    near_half, far_half = ffn_halves
    gate, upper = forward_product(far_half, gate_w), forward_product(far_half, upper_w)
    far_hidden = low(swiglu(gate, upper))
    far_gate, far_upper, far_ffn = inner_grads(back_halves[1], gate, upper)
    far = far_ffn[:count].astype(jnp.float32) + ring_core.move(far_ffn[count:], 1)
    far = low(far)
    ffn_x = ring_x.move(far, 1)
    gate = forward_product(after(near_half, far_ffn), gate_w)
    upper = forward_product(after(near_half, far), upper_w)
    near_hidden = low(swiglu(gate, upper))
    down_terms = low(weight_product(jnp.concatenate([near_hidden, far_hidden], 0), back_all))
    down_terms = down_terms.reshape(outer, nf, hidden_rows, width)
    down_sent = [pick(down_terms, 0, ring_y.dest(hop)) for hop in range(1, outer)]
    down_got = jnp.stack([ring_y.move(part, hop + 1) for hop, part in enumerate(down_sent)])
    near_gate, near_upper, near_ffn = inner_grads(after(back_halves[0], *down_sent), gate, upper)
    ffn_core = ring_core.move(near_ffn[count:], 1)
    ffn_all = after(ffn_all, near_ffn)
    gate_terms = low(weight_product(ffn_all, jnp.concatenate([near_gate, far_gate], 0)))
    upper_terms = low(weight_product(ffn_all, jnp.concatenate([near_upper, far_upper], 0)))
    near_out, far_out = [
        low(forward_product(after(half, near_ffn, ffn_x, down_got), down_w))
        for half in (near_hidden, far_hidden)
    ]
    inner_shape = (outer, MEMBERS, nf, in_rows, mine)
    (
        out_core,
        out_x,
        gate_parts,
        upper_parts,
        input_grad,
        in_sum,
        out_sum,
        down_sum,
        gain_totals,
        norm,
    ) = backward(
        nd,
        nf,
        length,
        small,
        (near_out, far_out),
        (
            down_got,
            down_terms,
            gate_terms.reshape(inner_shape),
            upper_terms.reshape(inner_shape),
        ),
        (
            near_ffn[:count],
            ffn_core,
            ffn_x,
            hidden_in,
            back_in,
            out_w,
            mixed,
            heads,
            values,
            token_rows,
            raw,
            in_w,
        ),
    )
    tiled = [array.reshape(-1, LANES) for array in (gains, gain_first, gain_second)]
    results = adam(
        span,
        norm,
        gain_totals,
        (in_sum, out_sum, gate_parts, upper_parts, down_sum),
        (hidden_in, near_out, out_core, out_x),
        masters + (tiled[0],),
        firsts + (tiled[1],),
        seconds + (tiled[2],),
    )
    clipped, new_masters, new_seconds = results[:7], results[8:15], results[16:23]
    gain_clipped, new_gains, gain_seconds = (results[k].reshape(-1) for k in (7, 15, 23))
    copies, output = tuple(results[24:31]), results[31]
    total_norm = norm[0, 0]
    return (
        (output.reshape(tokens.shape), input_grad.reshape(tokens.shape))
        + clipped
        + (gain_clipped, total_norm)
        + new_masters
        + (new_gains,)
        + copies
        + new_seconds
        + (gain_seconds,)
    )


def solution(mesh):
    rows3 = P(AXES, None, None)
    rows2 = P(AXES, None)
    whole = P()
    return jax.shard_map(
        functools.partial(shards, mesh.shape["dp"], mesh.shape["fsdp"]),
        mesh=mesh,
        in_specs=(rows3, rows3) + (rows2,) * 22 + (whole,) * 3,
        out_specs=(rows3, rows3)
        + (rows2,) * 7
        + (whole, whole)
        + (rows2,) * 7
        + (whole,)
        + (rows2,) * 14
        + (whole,),
        check_vma=False,
    )
```

```python
import functools
import math

import jax
import jax.numpy as jnp
import numpy as np
from jax import lax
from jax.experimental import pallas as pl
from jax.experimental.pallas import tpu as pltpu
from jax.sharding import PartitionSpec as P

D = 1280
HQ = 16
KV = 4
HD = 64
STEP = 10
MEMBERS = 4

norm_eps = 1e-05
rope_base = 10000.0
beta_one = 0.9
beta_two = 0.95
adam_eps = 1e-08
decay_rate = 0.1
clip_limit = 1.0
gain_rate = 0.4
masked_score = -1e30

AXES = ("dp", "fsdp")
LANES = 128
MESH = pl.DeviceIdType.MESH
ANYWHERE = pl.BlockSpec(memory_space=pl.ANY)
ON_CHIP = pl.BlockSpec(memory_space=pltpu.VMEM)
VMEM_MOST = 58 * 2**20


def rms_scale(values, gain):
    return values * lax.rsqrt(jnp.mean(values * values, -1, keepdims=True) + norm_eps) * gain


def rotary_tables(length):
    half = HD // 2
    frequency = rope_base ** (-np.arange(half, dtype=np.float64) * 2.0 / HD)
    angles = np.arange(length, dtype=np.float64)[:, None] * frequency[None, :]
    cosine, sine = np.cos(angles), np.sin(angles)
    cosine = np.tile(cosine, (1, LANES // half))
    sine = np.tile(np.concatenate([-sine, sine], 1), (1, LANES // HD))
    return jnp.asarray(cosine, jnp.float32), jnp.asarray(sine, jnp.float32)


def swiglu(gate, upper):
    return jax.nn.silu(gate) * upper


def forward_product(left, right):
    return jnp.dot(left, right, preferred_element_type=jnp.float32)


def weight_product(left, right):
    return lax.dot_general(
        left, right, (((0,), (0,)), ((), ())), preferred_element_type=jnp.float32
    )


def back_product(left, right):
    return lax.dot_general(
        left, right, (((1,), (1,)), ((), ())), preferred_element_type=jnp.float32
    )


def adam_update(master, first, second, grad, rate, decay):
    first_new = beta_one * first + (1.0 - beta_one) * grad
    second_new = beta_two * second + (1.0 - beta_two) * grad * grad
    first_hat = first_new / (1.0 - beta_one**STEP)
    second_hat = second_new / (1.0 - beta_two**STEP)
    master_new = master - rate * (first_hat / (jnp.sqrt(second_hat) + adam_eps) + decay * master)
    return (master_new, second_new)


def put(buffer, block, axis, index):
    return lax.dynamic_update_index_in_dim(buffer, block, index, axis)


def pick(array, axis, index):
    return lax.dynamic_index_in_dim(array, index, axis, keepdims=False)


class Ring:
    def __init__(self, extent, place, target, nd, nf):
        self.extent = extent
        self.place = place
        self.target = target
        self.nd = nd
        self.nf = nf

    def move(self, block, step):
        pairs = []
        for d in range(self.nd):
            for f in range(self.nf):
                d2, f2 = self.target(d, f, step)
                pairs.append((d * self.nf + f, d2 * self.nf + f2))
        return lax.ppermute(block, AXES, pairs)

    def source(self, step):
        return lax.rem(self.place - step + self.extent, self.extent)

    def dest(self, step):
        return lax.rem(self.place + step, self.extent)

    def gather(self, block, axis):
        shape = block.shape[:axis] + (self.extent,) + block.shape[axis:]
        full = put(jnp.zeros(shape, block.dtype), block, axis, self.place)
        for step in range(1, self.extent):
            full = put(full, self.move(block, step), axis, self.source(step))
        return full

    def reduce(self, terms, axis):
        total = pick(terms, axis, self.place).astype(jnp.float32)
        for step in range(1, self.extent):
            got = self.move(pick(terms, axis, self.dest(step)), step)
            total = total + got.astype(jnp.float32)
        return total


def start_all(copies):
    for copy in copies:
        copy.start()
    return copies


def weights_kernel(
    nd,
    nf,
    query_full,
    key_full,
    value_full,
    out_full,
    gate_full,
    up_full,
    in_w,
    out_w,
    gate_w,
    upper_w,
    w_query,
    w_key,
    w_value,
    w_out,
    w_gate,
    w_up,
    in_ref,
    out_ref,
    inner_ref,
    z_send,
    z_recv,
    y_send,
    y_recv,
    x_send,
    x_recv,
    hop_send,
    hop_recv,
    core_send,
    core_recv,
    swap_send,
    swap_recv,
    gate_send,
    gate_recv,
    over_send,
    over_recv,
    up_send,
    up_recv,
    local_sem,
    load_sem,
):
    outer = nd // MEMBERS
    dp = lax.axis_index("dp")
    z = lax.axis_index("fsdp")
    y = dp // MEMBERS
    member = dp % MEMBERS
    x = member // 2
    c = member % 2

    def z_peer(step):
        return (dp, lax.rem(z + step, nf))

    def y_peer(step):
        return (lax.rem(y + step, outer) * MEMBERS + member, z)

    def in_group(k):
        return (y * MEMBERS + k, z)

    def from_z(step):
        return lax.rem(z - step + nf, nf)

    def from_y(step):
        return lax.rem(y - step + outer, outer)

    x_peer = in_group((1 - x) * 2 + c)
    core_peer = in_group(x * 2 + 1 - c)
    barrier = pltpu.get_barrier_semaphore()
    peers = [z_peer(step) for step in range(1, nf)] + [y_peer(step) for step in range(1, outer)]
    peers += [x_peer, core_peer, in_group(MEMBERS - 1 - member)]
    for peer in peers:
        pl.semaphore_signal(barrier, inc=1, device_id=peer, device_id_type=MESH)
    fulls = (query_full, key_full, value_full, out_full, gate_full, up_full)
    loads = [
        pltpu.make_async_copy(full, here, load_sem.at[index])
        for index, (full, here) in enumerate(
            zip(fulls, (w_query, w_key, w_value, w_out, w_gate, w_up))
        )
    ]
    start_all(loads)
    for copy in loads:
        copy.wait()
    column = 0
    for weight in (w_query, w_key, w_value):
        in_ref[:, column : column + weight.shape[1]] = weight[...].astype(jnp.bfloat16)
        column += weight.shape[1]
    out_ref[...] = w_out[...].astype(jnp.bfloat16)
    span = inner_ref.shape[3] // outer
    for half, weight in enumerate((w_gate, w_up)):
        for k in range(MEMBERS):
            for part in range(outer):
                column = (part * MEMBERS + k) * span
                inner_ref[half, k, :, part * span : (part + 1) * span] = weight[
                    :, column : column + span
                ].astype(jnp.bfloat16)
    pl.semaphore_wait(barrier, len(peers))

    def remote(source, target, send, recv, device):
        return pltpu.make_async_remote_copy(
            src_ref=source,
            dst_ref=target,
            send_sem=send,
            recv_sem=recv,
            device_id=device,
            device_id_type=MESH,
        )

    shards_here = (in_ref, out_ref)
    wholes = (in_w, out_w)
    sent = []

    def send(copy):
        copy.start()
        sent.append(copy)
        return copy

    local = [
        pltpu.make_async_copy(shards_here[a], wholes[a].at[y, x, c, z], local_sem.at[a])
        for a in range(2)
    ]
    start_all(local)
    z_copies = {}
    for a in range(2):
        for step in range(1, nf):
            z_copies[a, step] = send(
                remote(
                    shards_here[a],
                    wholes[a].at[y, x, c, z],
                    z_send.at[a, step],
                    z_recv.at[a, step],
                    z_peer(step),
                )
            )
    masks = (2, 1, 3)
    trades = {}
    for half, target in ((0, gate_w.at[y, :, z]), (1, upper_w.at[y, :, z])):
        for mask in masks:
            other = member ^ mask
            trades[half, mask] = send(
                remote(
                    inner_ref.at[half, other],
                    target.at[member],
                    swap_send.at[half, mask],
                    swap_recv.at[half, mask],
                    in_group(other),
                )
            )
        kept = pltpu.make_async_copy(
            inner_ref.at[half, member], target.at[member], local_sem.at[2 + half]
        )
        kept.start()
        local.append(kept)

    def block(a, step, oy=None, ox=None):
        return wholes[a].at[y if oy is None else oy, x if ox is None else ox, c, from_z(step)]

    y_copies = {}
    x_copies = {}
    for a in range(2):
        for step in range(nf):
            if step:
                z_copies[a, step].wait_recv()
            source = shards_here[a] if step == 0 else block(a, step)
            for hop in range(1, outer):
                y_copies[a, hop, step] = send(
                    remote(
                        source,
                        block(a, step),
                        y_send.at[a, hop, step],
                        y_recv.at[a, hop, step],
                        y_peer(hop),
                    )
                )
            x_copies[a, step] = send(
                remote(
                    source, block(a, step), x_send.at[a, step], x_recv.at[a, step], x_peer
                )
            )
    for mask in masks:
        trades[0, mask].wait_recv()
    local[2].wait()
    gates = {}
    gate_own = gate_w.at[y, :, z]

    def gate_to_y(step):
        piece = gate_w.at[y, :, from_z(step)]
        for hop in range(1, outer):
            gates[hop, step] = send(
                remote(
                    piece, piece, over_send.at[hop, step], over_recv.at[hop, step], y_peer(hop)
                )
            )

    for step in range(1, nf):
        gates[0, step] = send(
            remote(gate_own, gate_own, gate_send.at[step], gate_recv.at[step], z_peer(step))
        )
    gate_to_y(0)
    for mask in masks:
        trades[1, mask].wait_recv()
    local[3].wait()
    upper_own = upper_w.at[y, :, z]
    uppers = [
        send(remote(upper_own, upper_own, up_send.at[step], up_recv.at[step], z_peer(step)))
        for step in early_steps(nf)
    ]
    hops = {}
    for a in range(2):
        for step in range(nf):
            for hop in range(1, outer):
                y_copies[a, hop, step].wait_recv()
                hops[a, hop, step] = send(
                    remote(
                        block(a, step, oy=from_y(hop)),
                        block(a, step, oy=from_y(hop)),
                        hop_send.at[a, hop, step],
                        hop_recv.at[a, hop, step],
                        x_peer,
                    )
                )
    for step in range(1, nf):
        gates[0, step].wait_recv()
        gate_to_y(step)
    cores = {}

    def to_core(a, hop, far):
        place = wholes[a].at[y if hop == 0 else from_y(hop), 1 - x if far else x, c]
        cores[a, hop, far] = send(
            remote(
                place,
                place,
                core_send.at[a, hop, far],
                core_recv.at[a, hop, far],
                core_peer,
            )
        )

    local[0].wait()
    local[1].wait()
    for a in range(2):
        for hop in range(outer):
            to_core(a, hop, 0)
    for a in range(2):
        for step in range(nf):
            x_copies[a, step].wait_recv()
        to_core(a, 0, 1)
    for a in range(2):
        for hop in range(1, outer):
            for step in range(nf):
                hops[a, hop, step].wait_recv()
            to_core(a, hop, 1)
    for copy in uppers:
        copy.wait_recv()
    for hop in range(1, outer):
        for step in range(nf):
            gates[hop, step].wait_recv()
    for key in cores:
        cores[key].wait_recv()
    for copy in sent:
        copy.wait_send()


def early_steps(nf):
    return sorted({1, nf - 1})


def gather_weights(nd, nf, shards_here):
    outer = nd // MEMBERS
    dma = pltpu.SemaphoreType.DMA
    lead = (outer, 2, 2, nf)
    low_type = jnp.bfloat16
    w_query, w_key, w_value, w_out, w_gate, w_up = shards_here
    in_shape = (w_query.shape[0], w_query.shape[1] + w_key.shape[1] + w_value.shape[1])
    inner = (w_gate.shape[0], w_gate.shape[1] // MEMBERS)
    pairs = [(2, nf), (2, outer, nf), (2, nf), (2, outer, nf), (2, outer, 2), (2, MEMBERS)]
    pairs += [(nf,), (outer, nf), (nf,)]
    return pl.pallas_call(
        functools.partial(weights_kernel, nd, nf),
        name="gather_weights",
        out_shape=(
            jax.ShapeDtypeStruct(lead + in_shape, low_type),
            jax.ShapeDtypeStruct(lead + w_out.shape, low_type),
            jax.ShapeDtypeStruct((outer, MEMBERS, nf) + inner, low_type),
            jax.ShapeDtypeStruct((outer, MEMBERS, nf) + inner, low_type),
        ),
        in_specs=[ANYWHERE] * 6,
        out_specs=(ANYWHERE,) * 4,
        scratch_shapes=[pltpu.VMEM(weight.shape, weight.dtype) for weight in shards_here]
        + [
            pltpu.VMEM(in_shape, low_type),
            pltpu.VMEM(w_out.shape, low_type),
            pltpu.VMEM((2, MEMBERS) + inner, low_type),
        ]
        + [dma(shape) for shape in pairs for _ in range(2)]
        + [dma((4,)), dma((6,))],
        compiler_params=pltpu.CompilerParams(
            collective_id=0, has_side_effects=True, vmem_limit_bytes=VMEM_MOST
        ),
    )(*shards_here)


def block_mean():
    row = lax.broadcasted_iota(jnp.int32, (LANES, LANES), 0) // HD
    column = lax.broadcasted_iota(jnp.int32, (LANES, LANES), 1) // HD
    return jnp.where(row == column, 1.0 / HD, 0.0).astype(jnp.bfloat16)


def head_mean(values, averages):
    high = values.astype(jnp.bfloat16)
    rest = (values - high.astype(jnp.float32)).astype(jnp.bfloat16)
    total = jnp.dot(high, averages, preferred_element_type=jnp.float32)
    return total + jnp.dot(rest, averages, preferred_element_type=jnp.float32)


def swap_halves(values):
    lane = lax.broadcasted_iota(jnp.int32, values.shape, 1) // (HD // 2)
    ahead = pltpu.roll(values, LANES - HD // 2, 1)
    behind = pltpu.roll(values, HD // 2, 1)
    return jnp.where(lane % 2 == 0, ahead, behind)


def in_half(values, source, target):
    lane = lax.broadcasted_iota(jnp.int32, values.shape, 1) // HD
    wide = values.astype(jnp.float32)
    if source != target:
        wide = pltpu.roll(wide, HD, 1)
    return jnp.where(lane == target, wide, 0.0).astype(values.dtype)


def split_gains(gains):
    width = (gains.shape[1] - 2 * HD) // 2
    heads = gains[:, pl.ds(2 * width, 2 * HD)]
    other = pltpu.roll(heads, HD, 1)
    first = lax.broadcasted_iota(jnp.int32, heads.shape, 1) < HD
    query, key = jnp.where(first, heads, other), jnp.where(first, other, heads)

    def of_tile(index):
        return jnp.where(index < HQ * HD // LANES, query, key)

    return gains[:, pl.ds(0, width)], gains[:, pl.ds(width, width)], of_tile


def tile_of(index, width=LANES):
    return pl.ds(pl.multiple_of(index * width, LANES), width)


def rows_of(index, size):
    return pl.ds(pl.multiple_of(index * size, 16), size)


def dot_last(left, right):
    return lax.dot_general(
        left, right, (((1,), (1,)), ((), ())), preferred_element_type=jnp.float32
    )


def probabilities(query, key, keep):
    scores = dot_last(query, key) * HD**-0.5
    scores = jnp.where(keep, scores, masked_score)
    weights = jnp.exp(scores - jnp.max(scores, -1, keepdims=True))
    return weights / jnp.sum(weights, -1, keepdims=True)


def outer_product(left, right, target):
    pair, wide = 2 * LANES, 4 * LANES

    def step_once(index, carry):
        columns = tile_of(index, pair)
        turned = left[:, columns].T
        for start in range(0, right.shape[1], wide):
            across = pl.ds(start, min(wide, right.shape[1] - start))
            target[columns, across] = jnp.dot(
                turned, right[:, across], preferred_element_type=jnp.float32
            ).astype(jnp.bfloat16)
        return carry

    lax.fori_loop(0, left.shape[1] // pair, step_once, 0)


def flatten_blocks(blocks, rows, target):
    outer, members, nf, size, _ = blocks.shape

    def step_once(index, carry):
        for place in range(nf):
            rows[place * size : (place + 1) * size, :] = blocks[
                index // members, lax.rem(index, members), place
            ].astype(jnp.float32)
        target[rows_of(index, nf * size), :] = rows[...].astype(jnp.bfloat16)
        return carry

    lax.fori_loop(0, outer * members, step_once, 0)


def attend_kernel(
    nd,
    nf,
    length,
    gains,
    cosine,
    sine,
    mask,
    tokens_full,
    down_full,
    in_full,
    out_full,
    cot_full,
    upper_in,
    gate_w,
    upper_w,
    down_w,
    back_all,
    ffn_all,
    gate_out,
    upper_out,
    hidden_out,
    down_terms,
    raw,
    heads,
    values,
    mixed,
    hidden_in,
    normed,
    ffn_here,
    tokens,
    w_down,
    in_w,
    out_w,
    down_x,
    cot,
    gate_blocks,
    upper_blocks,
    block_rows,
    gate_flat,
    upper_flat,
    gate_here,
    upper_here,
    hidden_here,
    uz_send,
    uz_recv,
    uy_send,
    uy_recv,
    dz_send,
    dz_recv,
    dy_send,
    dy_recv,
    row_send,
    row_recv,
    local_sem,
):
    outer = nd // MEMBERS
    dp = lax.axis_index("dp")
    z = lax.axis_index("fsdp")
    y = dp // MEMBERS
    member = dp % MEMBERS
    x = member // 2
    c = member % 2

    def z_peer(step):
        return (dp, lax.rem(z + step, nf))

    def y_peer(step):
        return (lax.rem(y + step, outer) * MEMBERS + member, z)

    def from_z(step):
        return lax.rem(z - step + nf, nf)

    x_peer = (y * MEMBERS + (1 - x) * 2 + c, z)
    core_peer = (y * MEMBERS + x * 2 + 1 - c, z)
    barrier = pltpu.get_barrier_semaphore()
    peers = [z_peer(step) for step in range(1, nf)] + [y_peer(step) for step in range(1, outer)]
    peers += [x_peer, core_peer]
    for peer in peers:
        pl.semaphore_signal(barrier, inc=1, device_id=peer, device_id_type=MESH)
    gain_attn, gain_ffn, gain_heads = split_gains(gains)
    count = tokens.shape[0]
    width = tokens.shape[1]

    def member_rows(slot):
        return pl.ds(slot * count, count)

    weights_here = []
    operands = (
        (down_full, w_down),
        (cot_full, cot.at[member_rows(0)]),
        (tokens_full, tokens),
        (in_full, in_w),
        (out_full, out_w),
        (gate_w, gate_blocks),
    )
    for index, (source, target) in enumerate(operands):
        copy = pltpu.make_async_copy(source, target, local_sem.at[4 + index])
        copy.start()
        weights_here.append(copy)
    for _ in range(2):
        weights_here.pop(0).wait()
    down_x[...] = w_down[...].astype(jnp.bfloat16)
    pl.semaphore_wait(barrier, len(peers))
    sent = []

    def remote(source, target, send, recv, device):
        copy = pltpu.make_async_remote_copy(
            src_ref=source,
            dst_ref=target,
            send_sem=send,
            recv_sem=recv,
            device_id=device,
            device_id_type=MESH,
        )
        copy.start()
        sent.append(copy)
        return copy

    def keep(index, source, target):
        copy = pltpu.make_async_copy(source, target, local_sem.at[index])
        copy.start()
        return copy

    arrivals = []
    upper_own = upper_w.at[y, :, z]
    down_own = down_w.at[y, z]
    steps_left = [step for step in range(1, nf) if step not in early_steps(nf)]
    upper_z = {
        step: remote(upper_own, upper_own, uz_send.at[step], uz_recv.at[step], z_peer(step))
        for step in steps_left
    }

    def upper_to_y(step):
        if step in upper_z:
            upper_z[step].wait_recv()
        piece = upper_w.at[y, :, from_z(step)]
        for hop in range(1, outer):
            arrivals.append(
                remote(piece, piece, uy_send.at[hop, step], uy_recv.at[hop, step], y_peer(hop))
            )

    for step in [0] + early_steps(nf):
        upper_to_y(step)
    down_z = [
        remote(down_x, down_own, dz_send.at[step], dz_recv.at[step], z_peer(step))
        for step in range(1, nf)
    ]
    kept = [keep(1, down_x, down_own)]
    cot_own = cot.at[member_rows(0)]
    cot_near = remote(
        cot_own, cot.at[member_rows(1)], row_send.at[0, 0], row_recv.at[0, 0], core_peer
    )
    cot_far = remote(
        cot_own, cot.at[member_rows(2)], row_send.at[0, 1], row_recv.at[0, 1], x_peer
    )

    def down_to_y(step):
        if step:
            down_z[step - 1].wait_recv()
        piece = down_w.at[y, from_z(step)] if step else down_x
        for hop in range(1, outer):
            arrivals.append(
                remote(
                    piece,
                    down_w.at[y, from_z(step)],
                    dy_send.at[hop, step],
                    dy_recv.at[hop, step],
                    y_peer(hop),
                )
            )

    chunk = 32

    weights_here.pop(0).wait()

    def norm_rows(index, carry):
        rows = rows_of(index, chunk)
        part = tokens[rows, :].astype(jnp.float32)
        scale = lax.rsqrt(jnp.mean(part * part, -1, keepdims=True) + norm_eps)
        normed[rows, :] = (part * scale * gain_attn).astype(jnp.bfloat16)
        return carry

    lax.fori_loop(0, count // chunk, norm_rows, 0)
    head_tiles = (HQ + KV) * HD // LANES
    for _ in range(2):
        weights_here.pop(0).wait()

    def project(index, carry):
        columns = tile_of(index, 2 * LANES)
        raw[:, columns] = jnp.dot(
            normed[...], in_w[:, columns], preferred_element_type=jnp.float32
        )
        return carry

    lax.fori_loop(0, head_tiles // 2, project, 0)
    values[...] = jnp.dot(
        normed[...], in_w[:, pl.ds(head_tiles * LANES, KV * HD)], preferred_element_type=jnp.float32
    ).astype(jnp.bfloat16)
    averages = block_mean()

    def turn(index, carry):
        columns = tile_of(index)
        for row in range(count // length):
            rows = pl.ds(row * length, length)
            part = raw[rows, columns]
            scale = lax.rsqrt(head_mean(part * part, averages) + norm_eps)
            part = part * scale * gain_heads(index)
            part = part * cosine[...] + swap_halves(part) * sine[...]
            heads[rows, columns] = part.astype(jnp.bfloat16)
        return carry

    lax.fori_loop(0, head_tiles, turn, 0)

    def attend(row):
        rows = pl.ds(row * length, length)
        allowed = mask[row] > 0.5

        def pair(tile, carry):
            key_tile = heads[rows, tile_of(HQ * HD // LANES + tile)]
            value_tile = values[rows, tile_of(tile)]
            for own in range(2):
                key = [in_half(key_tile, own, half) for half in range(2)]
                value = [in_half(value_tile, own, half) for half in range(2)]
                for quarter in range(2):
                    columns = tile_of(tile * 4 + own * 2 + quarter)
                    query = heads[rows, columns]
                    total = None
                    for half in range(2):
                        weights = probabilities(query, key[half], allowed).astype(jnp.bfloat16)
                        term = jnp.dot(weights, value[half], preferred_element_type=jnp.float32)
                        total = term if total is None else total + term
                    mixed[rows, columns] = total.astype(jnp.bfloat16)
            return carry

        lax.fori_loop(0, KV * HD // LANES, pair, 0)

    down_steps = list(range(nf))
    ffn_far, ffn_near = [], []

    def finish(row):
        rows = pl.ds(row * length, length)

        def project_out(index, carry):
            columns = tile_of(index, 2 * LANES)
            hidden_in[rows, columns] = tokens[rows, columns].astype(jnp.float32) + jnp.dot(
                mixed[rows, :], out_w[:, columns], preferred_element_type=jnp.float32
            )
            return carry

        lax.fori_loop(0, width // (2 * LANES), project_out, 0)

        def norm_hidden(index, carry):
            part_rows = pl.ds(pl.multiple_of(row * length + index * chunk, 16), chunk)
            part = hidden_in[part_rows, :]
            scale = lax.rsqrt(jnp.mean(part * part, -1, keepdims=True) + norm_eps)
            ffn_here[part_rows, :] = (part * scale * gain_ffn).astype(jnp.bfloat16)
            return carry

        lax.fori_loop(0, length // chunk, norm_hidden, 0)
        for slot, peer, copies in ((2, x_peer, ffn_far), (1, core_peer, ffn_near)):
            copies.append(
                remote(
                    ffn_here.at[rows],
                    ffn_here.at[pl.ds(slot * count + row * length, length)],
                    row_send.at[slot, row],
                    row_recv.at[slot, row],
                    peer,
                )
            )

    batch = count // length
    for row in range(batch):
        attend(row)
        finish(row)
        if row == 0:
            for step in steps_left:
                upper_to_y(step)
            uppers = list(arrivals)
            arrivals.clear()
            down_to_y(down_steps.pop(0))

    cot_far.wait_recv()
    cot_cross = remote(
        cot.at[member_rows(2)],
        cot.at[member_rows(3)],
        row_send.at[0, 2],
        row_recv.at[0, 2],
        core_peer,
    )
    down_to_y(down_steps.pop(0))
    weights_here.pop(0).wait()
    flatten_blocks(gate_blocks, block_rows, gate_flat)
    for copy in uppers:
        copy.wait_recv()
    kept.pop(0).wait()
    upper_load = keep(0, upper_w, upper_blocks)
    while len(down_steps) > 1:
        down_to_y(down_steps.pop(0))
    upper_load.wait()
    flatten_blocks(upper_blocks, block_rows, upper_flat)

    def ffn_rows(slot):
        rows = member_rows(slot)

        def tile_once(index, carry):
            columns = tile_of(index, 2 * LANES)
            gate = jnp.dot(
                ffn_here[rows, :], gate_flat[:, columns], preferred_element_type=jnp.float32
            )
            upper = jnp.dot(
                ffn_here[rows, :], upper_flat[:, columns], preferred_element_type=jnp.float32
            )
            gate_here[rows, columns] = gate
            upper_here[rows, columns] = upper
            hidden_here[rows, columns] = (gate / (1.0 + jnp.exp(-gate)) * upper).astype(
                jnp.bfloat16
            )
            return carry

        lax.fori_loop(0, gate_flat.shape[1] // (2 * LANES), tile_once, 0)

    ffn_rows(0)
    for copy in ffn_near:
        copy.wait_recv()
    ffn_rows(1)
    crosses = []
    for row in range(batch):
        ffn_far[row].wait_recv()
        crosses.append(
            remote(
                ffn_here.at[pl.ds(2 * count + row * length, length)],
                ffn_here.at[pl.ds(3 * count + row * length, length)],
                row_send.at[3, row],
                row_recv.at[3, row],
                core_peer,
            )
        )
    down_to_y(nf - 1)
    ffn_rows(2)
    for copy in crosses:
        copy.wait_recv()
    kept.append(keep(2, ffn_here, ffn_all))
    ffn_rows(3)
    kept.append(keep(3, gate_here, gate_out))
    kept.append(keep(9, upper_here, upper_out))
    kept.append(keep(10, hidden_here, hidden_out))
    cot_near.wait_recv()
    cot_cross.wait_recv()
    kept.append(keep(11, cot, back_all))
    outer_product(hidden_here, cot, down_terms)
    for copy in arrivals:
        copy.wait_recv()
    for copy in sent:
        copy.wait_send()
    for copy in kept:
        copy.wait()


def attend(nd, nf, length, small, tokens, w_down, in_w, out_w, cot, upper_w, gate_w):
    outer = nd // MEMBERS
    count, width = tokens.shape
    nf_rows, mine = gate_w.shape[2] * gate_w.shape[3], gate_w.shape[4]
    lo, hi = jnp.bfloat16, jnp.float32
    dma = pltpu.SemaphoreType.DMA
    moves = [(nf,), (outer, nf), (nf,), (outer, nf), (4, max(3, count // length))]
    shapes = [
        (upper_w.shape, lo),
        ((outer, nf) + w_down.shape, lo),
        ((MEMBERS * count, width), lo),
        ((MEMBERS * count, width), lo),
        ((MEMBERS * count, mine), hi),
        ((MEMBERS * count, mine), hi),
        ((MEMBERS * count, mine), lo),
        ((mine, width), lo),
        ((count, (HQ + KV) * HD), hi),
        ((count, (HQ + KV) * HD), lo),
        ((count, KV * HD), lo),
        ((count, HQ * HD), lo),
        ((count, width), hi),
    ]
    early = [(count, width), (MEMBERS * count, width), (count, width)]
    late = [in_w.shape, out_w.shape, w_down.shape, (MEMBERS * count, width)]
    late += [gate_w.shape, gate_w.shape]
    flat = (width, mine)
    return pl.pallas_call(
        functools.partial(attend_kernel, nd, nf, length),
        name="attend",
        out_shape=tuple(jax.ShapeDtypeStruct(*item) for item in shapes),
        in_specs=[ON_CHIP] * 4 + [ANYWHERE] * 7,
        out_specs=(ANYWHERE,) * 7 + (ON_CHIP,) * 6,
        input_output_aliases={9: 0},
        scratch_shapes=[pltpu.VMEM(shape, lo) for shape in early]
        + [pltpu.VMEM(w_down.shape, hi)]
        + [pltpu.VMEM(shape, lo) for shape in late]
        + [pltpu.VMEM((nf_rows, mine), hi), pltpu.VMEM(flat, lo), pltpu.VMEM(flat, lo)]
        + [pltpu.VMEM((MEMBERS * count, mine), kind) for kind in (hi, hi, lo)]
        + [dma(shape) for shape in moves for _ in range(2)]
        + [dma((12,))],
        compiler_params=pltpu.CompilerParams(
            collective_id=2, has_side_effects=True, vmem_limit_bytes=VMEM_MOST
        ),
    )(*small, tokens, w_down, in_w, out_w, cot, upper_w, gate_w)


def backward_kernel(
    nd,
    nf,
    length,
    gains,
    cosine,
    sine,
    mask,
    out_near,
    out_far,
    down_got,
    down_terms,
    gate_terms,
    upper_terms,
    mine_full,
    near_full,
    far_full,
    hidden_full,
    cot_full,
    out_w_full,
    mixed_full,
    heads_full,
    values_full,
    tokens_full,
    raw_full,
    in_w_full,
    out_core,
    out_x,
    gate_parts,
    upper_parts,
    input_grad,
    in_sum,
    out_sum,
    down_sum,
    gain_totals,
    norm,
    sum_attn,
    sum_ffn,
    sum_heads,
    gain_here,
    gain_group,
    gain_got,
    gain_far,
    square_here,
    square_group,
    square_got,
    square_far,
    mine_ref,
    core_near,
    from_x,
    hidden_in,
    cot,
    out_w,
    mixed,
    heads,
    values,
    tokens,
    raw,
    in_w,
    out_pass,
    out_core_far,
    normed,
    branch,
    grad_mixed,
    grad_hidden,
    grad_raw,
    wide,
    in_terms,
    out_terms,
    in_core,
    out_core_terms,
    in_x,
    out_x_terms,
    in_y,
    out_y_terms,
    in_total,
    out_total,
    in_zs,
    out_zs,
    in_zr,
    out_zr,
    down_own,
    gate_own,
    upper_own,
    down_y,
    gate_y,
    upper_y,
    down_z,
    gate_z,
    upper_z,
    row_send,
    row_recv,
    fy_send,
    fy_recv,
    fz_send,
    fz_recv,
    swap_send,
    swap_recv,
    ac_send,
    ac_recv,
    ax_send,
    ax_recv,
    ay_send,
    ay_recv,
    az_send,
    az_recv,
    tg_send,
    tg_recv,
    tf_send,
    tf_recv,
    load_sem,
    got_sem,
    operand_sem,
    local_sem,
):
    outer = nd // MEMBERS
    dp = lax.axis_index("dp")
    z = lax.axis_index("fsdp")
    y = dp // MEMBERS
    member = dp % MEMBERS
    x = member // 2
    c = member % 2
    lo, hi = jnp.bfloat16, jnp.float32

    def z_to(step):
        return lax.rem(z + step, nf)

    def z_peer(step):
        return (dp, z_to(step))

    def y_to(step):
        return lax.rem(y + step, outer)

    def y_peer(step):
        return (y_to(step) * MEMBERS + member, z)

    def in_group(k):
        return (y * MEMBERS + k, z)

    x_peer = in_group((1 - x) * 2 + c)
    core_peer = in_group(x * 2 + 1 - c)
    barrier = pltpu.get_barrier_semaphore()
    peers = [z_peer(step) for step in range(1, nf)] + [y_peer(step) for step in range(1, outer)]
    peers += [x_peer, core_peer, in_group(MEMBERS - 1 - member)]
    crossed = [(hop, step) for hop in range(outer) for step in range(nf) if hop or step]

    def cross_peer(hop, step):
        return (y_to(hop) * MEMBERS + member, z_to(step))

    peers += [cross_peer(hop, step) for hop, step in crossed if hop and step]
    fulls = (mine_full, near_full, far_full, hidden_full, cot_full, out_w_full, mixed_full)
    fulls += (heads_full, values_full, tokens_full, raw_full, in_w_full)
    places = (mine_ref, core_near, from_x, hidden_in, cot, out_w, mixed)
    places += (heads, values, tokens, raw, in_w)
    operands = [
        pltpu.make_async_copy(source, target, operand_sem.at[index])
        for index, (source, target) in enumerate(zip(fulls, places))
    ]
    start_all(operands)

    def ready(number):
        for _ in range(number):
            operands.pop(0).wait()

    for peer in peers:
        pl.semaphore_signal(barrier, inc=1, device_id=peer, device_id_type=MESH)
    pl.semaphore_wait(barrier, len(peers))
    sent = []

    def remote(source, target, send, recv, device):
        copy = pltpu.make_async_remote_copy(
            src_ref=source,
            dst_ref=target,
            send_sem=send,
            recv_sem=recv,
            device_id=device,
            device_id_type=MESH,
        )
        copy.start()
        sent.append(copy)
        return copy

    def keep(semaphore, source, target):
        copy = pltpu.make_async_copy(source, target, semaphore)
        copy.start()
        return copy

    gain_attn, gain_ffn, gain_heads = split_gains(gains)
    count, width = tokens.shape
    here, there = pl.ds(0, count), pl.ds(count, count)

    out_far_copy = remote(out_far.at[there], out_core_far, row_send.at[0], row_recv.at[0], core_peer)
    out_pass_copy = keep(local_sem.at[0], out_far.at[here], out_pass)
    out_near_copy = remote(out_near.at[there], out_core, row_send.at[1], row_recv.at[1], core_peer)

    terms = (down_terms, gate_terms, upper_terms)
    owns = (down_own, gate_own, upper_own)
    over_y = (down_y, gate_y, upper_y)
    over_z = (down_z, gate_z, upper_z)

    def piece_of(matrix, place, step):
        if matrix == 0:
            return terms[0].at[place, z_to(step)]
        return terms[matrix].at[place, :, z_to(step)]

    order = [(matrix, step) for matrix in range(3) for step in list(range(1, nf)) + [0]]
    y_copies, loads = {}, {}
    for matrix, step in order:
        loads[matrix, step] = keep(
            load_sem.at[matrix, step], piece_of(matrix, y, step), owns[matrix].at[step]
        )
        for hop in range(1, outer):
            if matrix == 0:
                y_copies[0, step, hop] = keep(
                    got_sem.at[hop, step], down_got.at[hop - 1, z_to(step)], down_y.at[hop - 1, step]
                )
                continue
            y_copies[matrix, step, hop] = remote(
                piece_of(matrix, y_to(hop), step),
                over_y[matrix].at[hop - 1, step],
                fy_send.at[matrix, hop, step],
                fy_recv.at[matrix, hop, step],
                y_peer(hop),
            )
    z_copies = {}
    waiting = list(order)

    def pieces(number):
        for _ in range(min(number, len(waiting))):
            matrix, step = waiting.pop(0)
            loads[matrix, step].wait()
            total = owns[matrix][step].astype(hi)
            for hop in range(1, outer):
                if matrix:
                    y_copies[matrix, step, hop].wait_recv()
                else:
                    y_copies[0, step, hop].wait()
                total = total + over_y[matrix][hop - 1, step].astype(hi)
            owns[matrix][step] = total.astype(lo)
            if step:
                z_copies[matrix, step] = remote(
                    owns[matrix].at[step],
                    over_z[matrix].at[step - 1],
                    fz_send.at[matrix, step],
                    fz_recv.at[matrix, step],
                    z_peer(step),
                )

    def piece_total(matrix):
        total = owns[matrix][0].astype(hi)
        for step in range(1, nf):
            z_copies[matrix, step].wait_recv()
            total = total + over_z[matrix][step - 1].astype(hi)
        return total

    swaps = []

    squares = []

    def trade(matrix, parts):
        total = piece_total(matrix).astype(lo)
        owns[matrix][0] = total
        total = total.astype(hi)
        squares.append(jnp.sum(total * total))
        for mask_bits in range(1, MEMBERS):
            other = member ^ mask_bits
            swaps.append(
                remote(
                    owns[matrix].at[0, other],
                    parts.at[member],
                    swap_send.at[matrix - 1, mask_bits],
                    swap_recv.at[matrix - 1, mask_bits],
                    in_group(other),
                )
            )
        swaps_local.append(
            keep(local_sem.at[2 + matrix], owns[matrix].at[0, member], parts.at[member])
        )

    swaps_local = []
    chunk = 32

    def to_group(index, source, target):
        target[member] = source[...]
        return [
            remote(
                source,
                target.at[member],
                tg_send.at[index, mask_bits],
                tg_recv.at[index, mask_bits],
                in_group(member ^ mask_bits),
            )
            for mask_bits in range(1, MEMBERS)
        ]

    def to_crossed(index, source, target):
        target[y * nf + z] = source[...]
        return [
            remote(
                source,
                target.at[y * nf + z],
                tf_send.at[index, place],
                tf_recv.at[index, place],
                cross_peer(hop, step),
            )
            for place, (hop, step) in enumerate(crossed)
        ]

    def summed(got, copies):
        for copy in copies:
            copy.wait_recv()
        return jnp.sum(got[...], 0)

    pieces(nf)

    def add_rows(target, other):
        def step_once(index, carry):
            rows = rows_of(index, chunk)
            target[rows, :] = (target[rows, :].astype(hi) + other[rows, :].astype(hi)).astype(lo)
            return carry

        lax.fori_loop(0, count // chunk, step_once, 0)

    def norm_rows(index, carry):
        rows = rows_of(index, chunk)
        part = tokens[rows, :].astype(hi)
        scale = lax.rsqrt(jnp.mean(part * part, -1, keepdims=True) + norm_eps)
        normed[rows, :] = (part * scale * gain_attn).astype(lo)
        return carry

    sum_attn[...] = jnp.zeros_like(sum_attn)
    sum_ffn[...] = jnp.zeros_like(sum_ffn)
    sum_heads[...] = jnp.zeros_like(sum_heads)
    ready(5)

    def norm_back(part, gain, grad):
        scale = lax.rsqrt(jnp.mean(part * part, -1, keepdims=True) + norm_eps)
        unit = part * scale
        inner = grad * gain
        back = scale * (inner - unit * jnp.mean(inner * unit, -1, keepdims=True))
        return back, jnp.sum(grad * unit, 0, keepdims=True)

    def ffn_norm_back(index, carry):
        rows = rows_of(index, chunk)
        grad = mine_ref[rows, :].astype(hi) + core_near[rows, :].astype(hi)
        grad = grad + from_x[rows, :].astype(hi)
        back, gain_term = norm_back(hidden_in[rows, :], gain_ffn, grad)
        sum_ffn[...] += gain_term
        back = back + cot[rows, :].astype(hi)
        grad_hidden[rows, :] = back
        branch[rows, :] = back.astype(lo)
        return carry

    lax.fori_loop(0, count // chunk, ffn_norm_back, 0)
    pair = 2 * LANES
    ready(2)

    def mixed_back(index, carry):
        columns = tile_of(index, pair)
        grad_mixed[:, columns] = dot_last(branch[...], out_w[columns, :]).astype(lo)
        return carry

    lax.fori_loop(0, HQ * HD // pair, mixed_back, 0)

    all_terms = (in_terms, out_terms)
    sizes = (in_terms.shape[0] // (nd), out_terms.shape[0] // (nd))
    core_terms = (in_core, out_core_terms)
    x_terms = (in_x, out_x_terms)
    y_terms = (in_y, out_y_terms)
    totals = (in_total, out_total)
    zs = (in_zs, out_zs)
    zr = (in_zr, out_zr)
    hops = list(range(1, outer)) + [0]
    core_copies, ax_copies, ay_copies, az_copies = {}, {}, {}, {}

    def block(a, hop, bx, bc):
        index = (y_to(hop) * 2 + bx) * 2 + bc
        return pl.ds(pl.multiple_of(index * sizes[a], 16), sizes[a])

    def core_out(a):
        for far in (1, 0):
            for hop in hops:
                bx = 1 - x if far else x
                core_copies[a, hop, far] = remote(
                    all_terms[a].at[block(a, hop, bx, 1 - c)],
                    core_terms[a].at[hop, far],
                    ac_send.at[a, hop, far],
                    ac_recv.at[a, hop, far],
                    core_peer,
                )

    def add_block(a, rows, others):
        some = math.gcd(sizes[a], 32)

        def step_once(index, carry):
            base = rows.start + index * some
            place = pl.ds(pl.multiple_of(base, 16), some)
            total = all_terms[a][place, :].astype(hi)
            for other in others:
                total = total + other[rows_of(index, some), :].astype(hi)
            all_terms[a][place, :] = total.astype(lo)
            return carry

        lax.fori_loop(0, sizes[a] // some, step_once, 0)

    def core_in(a):
        for hop in hops:
            core_copies[a, hop, 1].wait_recv()
            rows = block(a, hop, 1 - x, c)
            add_block(a, rows, [core_terms[a].at[hop, 1]])
            ax_copies[a, hop] = remote(
                all_terms[a].at[rows],
                x_terms[a].at[hop],
                ax_send.at[a, hop],
                ax_recv.at[a, hop],
                x_peer,
            )

    def x_in(a):
        for hop in range(1, outer):
            core_copies[a, hop, 0].wait_recv()
            ax_copies[a, hop].wait_recv()
            rows = block(a, hop, x, c)
            add_block(a, rows, [core_terms[a].at[hop, 0], x_terms[a].at[hop]])
            ay_copies[a, hop] = remote(
                all_terms[a].at[rows],
                y_terms[a].at[hop - 1],
                ay_send.at[a, hop],
                ay_recv.at[a, hop],
                y_peer(hop),
            )

    def y_in(a):
        core_copies[a, 0, 0].wait_recv()
        ax_copies[a, 0].wait_recv()
        others = [core_terms[a].at[0, 0], x_terms[a].at[0]]
        for hop in range(1, outer):
            ay_copies[a, hop].wait_recv()
            others.append(y_terms[a].at[hop - 1])
        start = block(a, 0, x, c).start
        some = math.gcd(sizes[a], 32)

        def step_once(index, carry):
            place = rows_of(index, some)
            own = pl.ds(pl.multiple_of(start + index * some, 16), some)
            total = all_terms[a][own, :].astype(hi)
            for other in others:
                total = total + other[place, :].astype(hi)
            totals[a][place, :] = total
            return carry

        lax.fori_loop(0, sizes[a] // some, step_once, 0)
        rows = sizes[a] // nf
        for place in range(nf):
            zs[a][place] = totals[a][place * rows : (place + 1) * rows, :].astype(lo)
        for step in range(1, nf):
            az_copies[a, step] = remote(
                zs[a].at[z_to(step)],
                zr[a].at[step - 1],
                az_send.at[a, step],
                az_recv.at[a, step],
                z_peer(step),
            )

    def z_in(a, target):
        total = zs[a][z].astype(hi)
        for step in range(1, nf):
            az_copies[a, step].wait_recv()
            total = total + zr[a][step - 1].astype(hi)
        target[...] = total

    outer_product(mixed, branch, out_terms)
    core_out(1)
    pieces(2)
    ready(len(operands))
    query_tiles = HQ * HD // LANES
    head_tiles = (HQ + KV) * HD // LANES
    key_tiles = KV * HD // LANES

    def over_rows(left, right):
        return lax.dot_general(left, right, (((0,), (0,)), ((), ())), preferred_element_type=hi)

    def attend_back(row):
        rows = pl.ds(row * length, length)
        allowed = mask[row] > 0.5

        def pair_back(tile, carry):
            key_tile = heads[rows, tile_of(query_tiles + tile)]
            value_tile = values[rows, tile_of(tile)]
            grad_key = None
            grad_value = None
            for own in range(2):
                key = [in_half(key_tile, own, half) for half in range(2)]
                value = [in_half(value_tile, own, half) for half in range(2)]
                for half in range(2):
                    key_total, value_total = None, None
                    for quarter in range(2):
                        columns = tile_of(tile * 4 + own * 2 + quarter)
                        query = heads[rows, columns]
                        grad = grad_mixed[rows, columns]
                        weights = probabilities(query, key[half], allowed)
                        slope = dot_last(grad, value[half])
                        inner = jnp.sum(weights * slope, -1, keepdims=True)
                        score = (weights * (slope - inner)).astype(lo)
                        back = jnp.dot(score, key[half], preferred_element_type=hi) * HD**-0.5
                        if half == 0:
                            wide[rows, columns] = back
                        else:
                            wide[rows, columns] += back
                        key_term = over_rows(score, query)
                        value_term = over_rows(weights.astype(lo), grad)
                        key_total = key_term if key_total is None else key_total + key_term
                        value_total = value_term if value_total is None else value_total + value_term
                    key_term = in_half(key_total, half, own)
                    value_term = in_half(value_total, half, own)
                    grad_key = key_term if grad_key is None else grad_key + key_term
                    grad_value = value_term if grad_value is None else grad_value + value_term
            wide[rows, tile_of(query_tiles + tile)] = grad_key * HD**-0.5
            grad_raw[rows, tile_of(head_tiles + tile)] = grad_value.astype(lo)
            return carry

        lax.fori_loop(0, key_tiles, pair_back, 0)

    batch = count // length
    for row in range(batch):
        attend_back(row)
        if row == 0:
            core_in(1)
        pieces(1)
    averages = block_mean()

    def turn_back(index, carry):
        columns = tile_of(index)
        gain = gain_heads(index)
        for row in range(batch):
            rows = pl.ds(row * length, length)
            grad = wide[rows, columns]
            grad = grad * cosine[...] - swap_halves(grad) * sine[...]
            part = raw[rows, columns]
            scale = lax.rsqrt(head_mean(part * part, averages) + norm_eps)
            unit = part * scale
            sum_heads[:, columns] += jnp.sum(grad * unit, 0, keepdims=True)
            inner = grad * gain
            back = scale * (inner - unit * head_mean(inner * unit, averages))
            grad_raw[rows, columns] = back.astype(lo)
        return carry

    lax.fori_loop(0, head_tiles, turn_back, 0)
    lax.fori_loop(0, count // chunk, norm_rows, 0)
    outer_product(normed, grad_raw, in_terms)
    core_out(0)
    pieces(1)
    x_in(1)

    def normed_back(index, carry):
        columns = tile_of(index, pair)
        wide[:, columns] = dot_last(grad_raw[...], in_w[columns, :])
        return carry

    core_in(0)
    out_far_copy.wait_recv()
    out_pass_copy.wait()
    add_rows(out_pass, out_core_far)
    out_x_copy = remote(out_pass, out_x, row_send.at[2], row_recv.at[2], x_peer)
    lax.fori_loop(0, width // pair, normed_back, 0)

    def attn_norm_back(index, carry):
        rows = rows_of(index, chunk)
        back, gain_term = norm_back(tokens[rows, :].astype(hi), gain_attn, wide[rows, :])
        sum_attn[...] += gain_term
        input_grad[rows, :] = (back + grad_hidden[rows, :]).astype(lo)
        return carry

    lax.fori_loop(0, count // chunk, attn_norm_back, 0)
    gain_here[...] = jnp.zeros_like(gain_here)
    place = 0
    for source in (sum_attn, sum_ffn, sum_heads):
        for tile in range(source.shape[1] // LANES):
            gain_here[pl.ds(place, 1), :] = source[:, tile * LANES : (tile + 1) * LANES]
            place += 1
    gain_copies = to_group(0, gain_here, gain_got)
    pieces(1)
    x_in(0)
    down_sum[...] = piece_total(0)
    y_in(1)
    pieces(2 * nf)
    trade(1, gate_parts)
    y_in(0)
    gain_group[...] = summed(gain_got, gain_copies)
    gain_copies = to_crossed(0, gain_group, gain_far)
    z_in(1, out_sum)
    trade(2, upper_parts)
    z_in(0, in_sum)
    for target in (down_sum, out_sum, in_sum):
        squares.append(jnp.sum(target[...] * target[...]))
    square_here[...] = jnp.full(square_here.shape, sum(squares))
    square_copies = to_group(1, square_here, square_got)
    square_group[...] = summed(square_got, square_copies)
    square_copies = to_crossed(1, square_group, square_far)
    gain_totals[...] = summed(gain_far, gain_copies)
    gain_place = 2 * width // LANES
    gain_squares = gain_totals[:gain_place, :]
    gain_squares = jnp.sum(gain_squares * gain_squares)
    for first, last in ((0, query_tiles), (query_tiles, head_tiles)):
        total = jnp.sum(gain_totals[gain_place + first : gain_place + last, :], 0, keepdims=True)
        total = jnp.broadcast_to(total, (8, LANES))
        total = total + pltpu.roll(total, HD, 1)
        gain_squares += jnp.sum(total * total) / (8 * LANES // HD)
    norm[...] = jnp.sqrt(summed(square_far, square_copies) + gain_squares)
    for copy in swaps + [out_near_copy, out_x_copy]:
        copy.wait_recv()
    for copy in sent:
        copy.wait_send()
    for copy in swaps_local:
        copy.wait()


def backward(nd, nf, length, small, halves, terms, operands):
    outer = nd // MEMBERS
    count, width = operands[0].shape
    out_w, in_w = operands[5], operands[-1]
    _, down_terms, gate_terms, _ = terms
    lo, hi = jnp.bfloat16, jnp.float32
    dma = pltpu.SemaphoreType.DMA
    in_rows, in_cols = in_w.shape[0] // (nd * nf), in_w.shape[1]
    out_rows, out_cols = out_w.shape[0] // (nd * nf), out_w.shape[1]
    inner = (MEMBERS,) + gate_terms.shape[3:]
    down = down_terms.shape[2:]
    tiles = (2 * width + (HQ + KV) * HD) // LANES
    gain_tile = (-(-tiles // 8) * 8, LANES)
    far = outer * nf - 1
    shapes = [
        ((count, width), lo),
        ((count, width), lo),
        (inner, lo),
        (inner, lo),
        ((count, width), lo),
        ((in_rows, in_cols), hi),
        ((out_rows, out_cols), hi),
        (down, hi),
        (gain_tile, hi),
        ((8, LANES), hi),
    ]
    in_block, out_block = (nf * in_rows, in_cols), (nf * out_rows, out_cols)
    scratch = [((1, width), hi), ((1, width), hi), ((1, (HQ + KV) * HD), hi)]
    for tile in (gain_tile, (8, LANES)):
        scratch += [(tile, hi), (tile, hi), ((MEMBERS,) + tile, hi), ((outer * nf,) + tile, hi)]
    scratch += [(operand.shape, operand.dtype) for operand in operands]
    scratch += [((count, width), lo)] * 2
    scratch += [
        ((count, width), lo),
        ((count, width), lo),
        ((count, HQ * HD), lo),
        ((count, width), hi),
        ((count, in_cols), lo),
        ((count, width), hi),
        (in_w.shape, lo),
        (out_w.shape, lo),
        ((outer, 2) + in_block, lo),
        ((outer, 2) + out_block, lo),
        ((outer,) + in_block, lo),
        ((outer,) + out_block, lo),
        ((outer - 1,) + in_block, lo),
        ((outer - 1,) + out_block, lo),
        (in_block, hi),
        (out_block, hi),
        ((nf, in_rows, in_cols), lo),
        ((nf, out_rows, out_cols), lo),
        ((nf - 1, in_rows, in_cols), lo),
        ((nf - 1, out_rows, out_cols), lo),
        ((nf,) + down, lo),
        ((nf,) + inner, lo),
        ((nf,) + inner, lo),
        ((outer - 1, nf) + down, lo),
        ((outer - 1, nf) + inner, lo),
        ((outer - 1, nf) + inner, lo),
        ((nf - 1,) + down, lo),
        ((nf - 1,) + inner, lo),
        ((nf - 1,) + inner, lo),
    ]
    moves = [(3,), (3, outer, nf), (3, nf), (2, MEMBERS), (2, outer, 2), (2, outer), (2, outer)]
    moves += [(2, nf), (2, MEMBERS), (2, far)]
    return pl.pallas_call(
        functools.partial(backward_kernel, nd, nf, length),
        name="backward",
        out_shape=tuple(jax.ShapeDtypeStruct(*item) for item in shapes),
        in_specs=[ON_CHIP] * 4 + [ANYWHERE] * (6 + len(operands)),
        out_specs=(ANYWHERE,) * 4 + (ON_CHIP,) * 6,
        scratch_shapes=[pltpu.VMEM(*item) for item in scratch]
        + [dma(shape) for shape in moves for _ in range(2)]
        + [dma((3, nf)), dma((outer, nf)), dma((len(operands),)), dma((5,))],
        compiler_params=pltpu.CompilerParams(
            collective_id=3, has_side_effects=True, vmem_limit_bytes=VMEM_MOST
        ),
    )(*small, *halves, *terms, *operands)


def adam_kernel(
    span, norm, gain_totals, in_sum, out_sum, gate_parts, upper_parts, down_sum, *rest
):
    count = 8
    row_terms, rest = rest[:4], rest[4:]
    masters, firsts, seconds = rest[:count], rest[count : 2 * count], rest[2 * count : 3 * count]
    rest = rest[3 * count :]
    outs = [rest[index * count : (index + 1) * count] for index in range(3)]
    copies = rest[3 * count : 4 * count - 1]
    output = rest[4 * count - 1]
    rest = rest[4 * count :]
    ins_here = [rest[index * count : (index + 1) * count] for index in range(3)]
    rest = rest[3 * count :]
    outs_here = [rest[index * count : (index + 1) * count] for index in range(3)]
    copies_here = rest[3 * count : 4 * count - 1]
    sums_here = rest[4 * count - 1 : 4 * count + 4]
    terms_here = rest[4 * count + 4 : 4 * count + 8]
    output_here, sum_sem, in_sem, out_sem, term_sem = rest[4 * count + 8 :]
    sums = (in_sum, out_sum, gate_parts, upper_parts, down_sum)
    loads = {}
    for index in (6, 4, 5, 3, 0, 1, 2, 7):
        source = {6: 4, 4: 2, 5: 3, 3: 1, 0: 0}.get(index)
        if source is not None:
            loads[source] = pltpu.make_async_copy(
                sums[source], sums_here[source], sum_sem.at[source]
            )
            loads[source].start()
        for kind, arrays in enumerate((masters, firsts, seconds)):
            loads[index, kind] = pltpu.make_async_copy(
                arrays[index], ins_here[kind][index], in_sem.at[kind, index]
            )
            loads[index, kind].start()
    rows_count = output.shape[0]
    term_loads = []
    for index, (source, target) in enumerate(zip(row_terms, terms_here)):
        copy = pltpu.make_async_copy(
            source.at[pl.ds(0, rows_count)], target, term_sem.at[index]
        )
        copy.start()
        term_loads.append(copy)
    stores = []

    def store(index):
        pairs = [(outs_here[kind][index], outs[kind][index]) for kind in range(3)]
        if index < count - 1:
            pairs.append((copies_here[index], copies[index]))
        for kind, (source, target) in enumerate(pairs):
            copy = pltpu.make_async_copy(source, target, out_sem.at[kind, index])
            copy.start()
            stores.append(copy)

    factor = jnp.minimum(1.0, clip_limit / (norm[0:1, 0:1] + 1e-06))
    weight_rate = 2.0 * D ** (-0.5)

    def update(index, columns, grad, rate, decay):
        grad = grad * factor
        master, first, second = (ins_here[kind][index][:, columns] for kind in range(3))
        new, second_new = adam_update(master, first, second, grad, rate, decay)
        outs_here[0][index][:, columns] = grad
        outs_here[1][index][:, columns] = new
        outs_here[2][index][:, columns] = second_new
        if index < count - 1:
            copies_here[index][:, columns] = new.astype(jnp.bfloat16)

    def arrived(index):
        for kind in range(3):
            loads[index, kind].wait()

    step = 2 * LANES
    loads[4].wait()
    arrived(6)
    for start in range(0, down_sum.shape[1], step):
        columns = slice(start, start + step)
        update(6, columns, sums_here[4][:, columns], weight_rate, decay_rate)
    store(6)
    members, _, mine = gate_parts.shape
    for index in (4, 5):
        loads[index - 2].wait()
        arrived(index)
        place = 0
        for part in range(mine // span):
            for member in range(members):
                grad = sums_here[index - 2][member, :, part * span : (part + 1) * span]
                columns = slice(place, place + span)
                update(index, columns, grad.astype(jnp.float32), weight_rate, decay_rate)
                place += span
        store(index)
    loads[1].wait()
    arrived(3)
    for start in range(0, out_sum.shape[1], step):
        columns = slice(start, start + step)
        update(3, columns, sums_here[1][:, columns], weight_rate, decay_rate)
    store(3)
    loads[0].wait()
    place = 0
    for index in range(3):
        arrived(index)
        for start in range(0, masters[index].shape[1], step):
            grad = sums_here[0][:, place : place + step]
            update(index, slice(start, start + step), grad, weight_rate, decay_rate)
            place += step
        store(index)
    arrived(7)
    norm_rows = 2 * D // LANES
    head_rows = HQ * HD // LANES
    key_rows = KV * HD // LANES
    folded = []
    for first, size in ((norm_rows, head_rows), (norm_rows + head_rows, key_rows)):
        total = jnp.sum(gain_totals[first : first + size, :], 0, keepdims=True)
        folded.append(total + pltpu.roll(jnp.broadcast_to(total, (8, LANES)), HD, 1)[:1])
    lane = lax.broadcasted_iota(jnp.int32, (1, LANES), 1)
    heads = jnp.where(lane < HD, folded[0], folded[1])
    gain_grad = jnp.concatenate([gain_totals[:norm_rows, :], heads], 0)
    update(7, slice(None), gain_grad, gain_rate, 0.0)
    store(7)
    for copy in term_loads:
        copy.wait()

    def add_rows(index, carry):
        rows = rows_of(index, 32)
        total = terms_here[0][rows, :]
        for term in terms_here[1:]:
            total = total + term[rows, :].astype(jnp.float32)
        output_here[rows, :] = total.astype(jnp.bfloat16)
        return carry

    lax.fori_loop(0, rows_count // 32, add_rows, 0)
    copy = pltpu.make_async_copy(output_here, output, term_sem.at[0])
    copy.start()
    stores.append(copy)
    for copy in stores:
        copy.wait()


def adam(span, norm, gain_totals, sums, row_terms, masters, firsts, seconds):
    lo, hi = jnp.bfloat16, jnp.float32
    dma = pltpu.SemaphoreType.DMA
    shapes = [(array.shape, hi) for _ in range(3) for array in masters]
    shapes += [(array.shape, lo) for array in masters[:-1]]
    rows_shape = row_terms[0].shape
    inputs = [(array.shape, hi) for _ in range(3) for array in masters]
    scratch = inputs + shapes + [(array.shape, array.dtype) for array in sums]
    scratch += [(rows_shape, array.dtype) for array in row_terms] + [(rows_shape, lo)]
    shapes += [(rows_shape, lo)]
    return pl.pallas_call(
        functools.partial(adam_kernel, span),
        name="adam",
        out_shape=tuple(jax.ShapeDtypeStruct(*item) for item in shapes),
        in_specs=[ON_CHIP] * 2 + [ANYWHERE] * (9 + len(inputs)),
        out_specs=(ANYWHERE,) * len(shapes),
        scratch_shapes=[pltpu.VMEM(*item) for item in scratch]
        + [dma((5,)), dma((3, len(masters))), dma((4, len(masters))), dma((4,))],
        compiler_params=pltpu.CompilerParams(vmem_limit_bytes=VMEM_MOST),
    )(norm, gain_totals, *sums, *row_terms, *masters, *firsts, *seconds)


def after(value, *others):
    return lax.optimization_barrier((value,) + others)[0]


def low(value):
    return value.astype(jnp.bfloat16)


def shards(
    nd,
    nf,
    tokens,
    cotangent,
    segment_ids,
    w_query,
    w_key,
    w_value,
    w_out,
    w_gate,
    w_up,
    w_down,
    m_query,
    m_key,
    m_value,
    m_out,
    m_gate,
    m_up,
    m_down,
    v_query,
    v_key,
    v_value,
    v_out,
    v_gate,
    v_up,
    v_down,
    gains,
    gain_first,
    gain_second,
):
    masters = (w_query, w_key, w_value, w_out, w_gate, w_up, w_down)
    firsts = (m_query, m_key, m_value, m_out, m_gate, m_up, m_down)
    seconds = (v_query, v_key, v_value, v_out, v_gate, v_up, v_down)
    outer = nd // MEMBERS
    dp = lax.axis_index("dp")
    ring_z = Ring(nf, lax.axis_index("fsdp"), lambda d, f, s: (d, (f + s) % nf), nd, nf)
    ring_y = Ring(
        outer,
        dp // MEMBERS,
        lambda d, f, s: ((d // MEMBERS + s) % outer * MEMBERS + d % MEMBERS, f),
        nd,
        nf,
    )
    ring_x = Ring(2, dp // 2 % 2, lambda d, f, s: (d ^ 2, f), nd, nf)
    ring_core = Ring(2, dp % 2, lambda d, f, s: (d ^ 1, f), nd, nf)
    member = dp % MEMBERS

    def trade(block, mask):
        return Ring(2, dp % 2, lambda d, f, s: (d ^ mask, f), nd, nf).move(block, 1)

    def swap(blocks):
        full = put(jnp.zeros_like(blocks), pick(blocks, 0, member), 0, member)
        for mask in range(1, MEMBERS):
            full = put(full, trade(pick(blocks, 0, member ^ mask), mask), 0, member ^ mask)
        return full

    def spread(rows):
        far = ring_x.move(rows, 1)
        near = jnp.concatenate([rows, ring_core.move(rows, 1)], 0)
        return near, jnp.concatenate([far, ring_core.move(far, 1)], 0)

    def collapse(near, far):
        rows = near.shape[0] // 2
        got = ring_core.move(far[rows:], 1).astype(jnp.float32)
        got = ring_x.move(low(far[:rows].astype(jnp.float32) + got), 1)
        total = near[:rows].astype(jnp.float32)
        total = total + ring_core.move(near[rows:], 1).astype(jnp.float32)
        return total + got.astype(jnp.float32)

    batch, length, width = tokens.shape
    count = batch * length
    hidden_rows = w_down.shape[0]
    span = nf * hidden_rows
    mine = outer * span
    in_rows = w_query.shape[0]
    out_rows = w_out.shape[0]
    attn_cols = (HQ + 2 * KV) * HD

    in_w, out_w, gate_w, upper_w = gather_weights(nd, nf, masters[:6])
    in_w = in_w.reshape(D, attn_cols)
    out_w = out_w.reshape(HQ * HD, D)

    positions = jnp.arange(length)
    causal = positions[None, :] <= positions[:, None]
    allowed = causal[None] & (segment_ids[:, :, None] == segment_ids[:, None, :])
    small = (gains[None], *rotary_tables(length), allowed.astype(jnp.float32))
    back_in = cotangent.reshape(count, width)
    token_rows = tokens.reshape(count, width)
    (
        upper_w,
        down_w,
        back_all,
        ffn_all,
        gate,
        upper,
        hidden,
        down_terms,
        raw,
        heads,
        values,
        mixed,
        hidden_in,
    ) = attend(
        nd, nf, length, small, token_rows, w_down, in_w, out_w, back_in, upper_w, gate_w
    )
    gate_w = gate_w.reshape(D, mine)
    upper_w = upper_w.reshape(D, mine)
    down_w = down_w.reshape(mine, D)
    def inner_grads(back_half, gate, upper):
        grad_hidden = back_product(back_half, down_w)
        _, pull = jax.vjp(swiglu, gate, upper)
        grad_gate, grad_upper = pull(grad_hidden)
        grad_gate, grad_upper = low(grad_gate), low(grad_upper)
        back = back_product(grad_gate, gate_w) + back_product(grad_upper, upper_w)
        return grad_gate, grad_upper, low(back)

    down_terms = down_terms.reshape(outer, nf, hidden_rows, width)
    down_sent = [pick(down_terms, 0, ring_y.dest(hop)) for hop in range(1, outer)]
    down_got = jnp.stack([ring_y.move(part, hop + 1) for hop, part in enumerate(down_sent)])
    half = 2 * count
    far_gate, far_upper, far_ffn = inner_grads(back_all[half:], gate[half:], upper[half:])
    far = far_ffn[:count].astype(jnp.float32) + ring_core.move(far_ffn[count:], 1)
    far = low(far)
    ffn_x = ring_x.move(far, 1)
    near_gate, near_upper, near_ffn = inner_grads(
        after(back_all[:half], far), gate[:half], upper[:half]
    )
    ffn_core = ring_core.move(near_ffn[count:], 1)
    ffn_all = after(ffn_all, near_ffn)
    gate_terms = low(weight_product(ffn_all, jnp.concatenate([near_gate, far_gate], 0)))
    upper_terms = low(weight_product(ffn_all, jnp.concatenate([near_upper, far_upper], 0)))
    near_out, far_out = [
        low(forward_product(after(rows, near_ffn), down_w))
        for rows in (hidden[:half], hidden[half:])
    ]
    inner_shape = (outer, MEMBERS, nf, in_rows, mine)
    (
        out_core,
        out_x,
        gate_parts,
        upper_parts,
        input_grad,
        in_sum,
        out_sum,
        down_sum,
        gain_totals,
        norm,
    ) = backward(
        nd,
        nf,
        length,
        small,
        (near_out, far_out),
        (
            down_got,
            down_terms,
            gate_terms.reshape(inner_shape),
            upper_terms.reshape(inner_shape),
        ),
        (
            near_ffn[:count],
            ffn_core,
            ffn_x,
            hidden_in,
            back_in,
            out_w,
            mixed,
            heads,
            values,
            token_rows,
            raw,
            in_w,
        ),
    )
    tiled = [array.reshape(-1, LANES) for array in (gains, gain_first, gain_second)]
    results = adam(
        span,
        norm,
        gain_totals,
        (in_sum, out_sum, gate_parts, upper_parts, down_sum),
        (hidden_in, near_out, out_core, out_x),
        masters + (tiled[0],),
        firsts + (tiled[1],),
        seconds + (tiled[2],),
    )
    clipped, new_masters, new_seconds = results[:7], results[8:15], results[16:23]
    gain_clipped, new_gains, gain_seconds = (results[k].reshape(-1) for k in (7, 15, 23))
    copies, output = tuple(results[24:31]), results[31]
    total_norm = norm[0, 0]
    return (
        (output.reshape(tokens.shape), input_grad.reshape(tokens.shape))
        + clipped
        + (gain_clipped, total_norm)
        + new_masters
        + (new_gains,)
        + copies
        + new_seconds
        + (gain_seconds,)
    )


def solution(mesh):
    rows3 = P(AXES, None, None)
    rows2 = P(AXES, None)
    whole = P()
    return jax.shard_map(
        functools.partial(shards, mesh.shape["dp"], mesh.shape["fsdp"]),
        mesh=mesh,
        in_specs=(rows3, rows3) + (rows2,) * 22 + (whole,) * 3,
        out_specs=(rows3, rows3)
        + (rows2,) * 7
        + (whole, whole)
        + (rows2,) * 7
        + (whole,)
        + (rows2,) * 14
        + (whole,),
        check_vma=False,
    )
```

```python
import functools
import math

import jax
import jax.numpy as jnp
import numpy as np
from jax import lax
from jax.experimental import pallas as pl
from jax.experimental.pallas import tpu as pltpu
from jax.sharding import PartitionSpec as P

D = 1280
HQ = 16
KV = 4
HD = 64
STEP = 10
MEMBERS = 4

norm_eps = 1e-05
rope_base = 10000.0
beta_one = 0.9
beta_two = 0.95
adam_eps = 1e-08
decay_rate = 0.1
clip_limit = 1.0
gain_rate = 0.4
masked_score = -1e30

AXES = ("dp", "fsdp")
LANES = 128
MESH = pl.DeviceIdType.MESH
ANYWHERE = pl.BlockSpec(memory_space=pl.ANY)
ON_CHIP = pl.BlockSpec(memory_space=pltpu.VMEM)
VMEM_MOST = 58 * 2**20


def rms_scale(values, gain):
    return values * lax.rsqrt(jnp.mean(values * values, -1, keepdims=True) + norm_eps) * gain


def rotary_tables(length):
    half = HD // 2
    frequency = rope_base ** (-np.arange(half, dtype=np.float64) * 2.0 / HD)
    angles = np.arange(length, dtype=np.float64)[:, None] * frequency[None, :]
    cosine, sine = np.cos(angles), np.sin(angles)
    cosine = np.tile(cosine, (1, LANES // half))
    sine = np.tile(np.concatenate([-sine, sine], 1), (1, LANES // HD))
    return jnp.asarray(cosine, jnp.float32), jnp.asarray(sine, jnp.float32)


def swiglu(gate, upper):
    return jax.nn.silu(gate) * upper


def forward_product(left, right):
    return jnp.dot(left, right, preferred_element_type=jnp.float32)


def weight_product(left, right):
    return lax.dot_general(
        left, right, (((0,), (0,)), ((), ())), preferred_element_type=jnp.float32
    )


def back_product(left, right):
    return lax.dot_general(
        left, right, (((1,), (1,)), ((), ())), preferred_element_type=jnp.float32
    )


def adam_update(master, first, second, grad, rate, decay):
    first_new = beta_one * first + (1.0 - beta_one) * grad
    second_new = beta_two * second + (1.0 - beta_two) * grad * grad
    first_hat = first_new / (1.0 - beta_one**STEP)
    second_hat = second_new / (1.0 - beta_two**STEP)
    master_new = master - rate * (first_hat / (jnp.sqrt(second_hat) + adam_eps) + decay * master)
    return (master_new, second_new)


def put(buffer, block, axis, index):
    return lax.dynamic_update_index_in_dim(buffer, block, index, axis)


def pick(array, axis, index):
    return lax.dynamic_index_in_dim(array, index, axis, keepdims=False)


class Ring:
    def __init__(self, extent, place, target, nd, nf):
        self.extent = extent
        self.place = place
        self.target = target
        self.nd = nd
        self.nf = nf

    def move(self, block, step):
        pairs = []
        for d in range(self.nd):
            for f in range(self.nf):
                d2, f2 = self.target(d, f, step)
                pairs.append((d * self.nf + f, d2 * self.nf + f2))
        return lax.ppermute(block, AXES, pairs)

    def source(self, step):
        return lax.rem(self.place - step + self.extent, self.extent)

    def dest(self, step):
        return lax.rem(self.place + step, self.extent)

    def gather(self, block, axis):
        shape = block.shape[:axis] + (self.extent,) + block.shape[axis:]
        full = put(jnp.zeros(shape, block.dtype), block, axis, self.place)
        for step in range(1, self.extent):
            full = put(full, self.move(block, step), axis, self.source(step))
        return full

    def reduce(self, terms, axis):
        total = pick(terms, axis, self.place).astype(jnp.float32)
        for step in range(1, self.extent):
            got = self.move(pick(terms, axis, self.dest(step)), step)
            total = total + got.astype(jnp.float32)
        return total


def start_all(copies):
    for copy in copies:
        copy.start()
    return copies


def weights_kernel(
    nd,
    nf,
    query_full,
    key_full,
    value_full,
    out_full,
    gate_full,
    up_full,
    in_w,
    out_w,
    gate_w,
    upper_w,
    w_query,
    w_key,
    w_value,
    w_out,
    w_gate,
    w_up,
    in_ref,
    out_ref,
    inner_ref,
    z_send,
    z_recv,
    y_send,
    y_recv,
    x_send,
    x_recv,
    hop_send,
    hop_recv,
    core_send,
    core_recv,
    swap_send,
    swap_recv,
    gate_send,
    gate_recv,
    over_send,
    over_recv,
    up_send,
    up_recv,
    local_sem,
    load_sem,
):
    outer = nd // MEMBERS
    dp = lax.axis_index("dp")
    z = lax.axis_index("fsdp")
    y = dp // MEMBERS
    member = dp % MEMBERS
    x = member // 2
    c = member % 2

    def z_peer(step):
        return (dp, lax.rem(z + step, nf))

    def y_peer(step):
        return (lax.rem(y + step, outer) * MEMBERS + member, z)

    def in_group(k):
        return (y * MEMBERS + k, z)

    def from_z(step):
        return lax.rem(z - step + nf, nf)

    def from_y(step):
        return lax.rem(y - step + outer, outer)

    x_peer = in_group((1 - x) * 2 + c)
    core_peer = in_group(x * 2 + 1 - c)
    barrier = pltpu.get_barrier_semaphore()
    peers = [z_peer(step) for step in range(1, nf)] + [y_peer(step) for step in range(1, outer)]
    peers += [x_peer, core_peer, in_group(MEMBERS - 1 - member)]
    for peer in peers:
        pl.semaphore_signal(barrier, inc=1, device_id=peer, device_id_type=MESH)
    fulls = (query_full, key_full, value_full, out_full, gate_full, up_full)
    loads = [
        pltpu.make_async_copy(full, here, load_sem.at[index])
        for index, (full, here) in enumerate(
            zip(fulls, (w_query, w_key, w_value, w_out, w_gate, w_up))
        )
    ]
    start_all(loads)
    for copy in loads:
        copy.wait()
    column = 0
    for weight in (w_query, w_key, w_value):
        in_ref[:, column : column + weight.shape[1]] = weight[...].astype(jnp.bfloat16)
        column += weight.shape[1]
    out_ref[...] = w_out[...].astype(jnp.bfloat16)
    span = inner_ref.shape[3] // outer
    for half, weight in enumerate((w_gate, w_up)):
        for k in range(MEMBERS):
            for part in range(outer):
                column = (part * MEMBERS + k) * span
                inner_ref[half, k, :, part * span : (part + 1) * span] = weight[
                    :, column : column + span
                ].astype(jnp.bfloat16)
    pl.semaphore_wait(barrier, len(peers))

    def remote(source, target, send, recv, device):
        return pltpu.make_async_remote_copy(
            src_ref=source,
            dst_ref=target,
            send_sem=send,
            recv_sem=recv,
            device_id=device,
            device_id_type=MESH,
        )

    shards_here = (in_ref, out_ref)
    wholes = (in_w, out_w)
    sent = []

    def send(copy):
        copy.start()
        sent.append(copy)
        return copy

    local = [
        pltpu.make_async_copy(shards_here[a], wholes[a].at[y, x, c, z], local_sem.at[a])
        for a in range(2)
    ]
    start_all(local)
    z_copies = {}
    for a in range(2):
        for step in range(1, nf):
            z_copies[a, step] = send(
                remote(
                    shards_here[a],
                    wholes[a].at[y, x, c, z],
                    z_send.at[a, step],
                    z_recv.at[a, step],
                    z_peer(step),
                )
            )
    masks = (2, 1, 3)
    trades = {}
    for half, target in ((0, gate_w.at[y, :, z]), (1, upper_w.at[y, :, z])):
        for mask in masks:
            other = member ^ mask
            trades[half, mask] = send(
                remote(
                    inner_ref.at[half, other],
                    target.at[member],
                    swap_send.at[half, mask],
                    swap_recv.at[half, mask],
                    in_group(other),
                )
            )
        kept = pltpu.make_async_copy(
            inner_ref.at[half, member], target.at[member], local_sem.at[2 + half]
        )
        kept.start()
        local.append(kept)

    def block(a, step, oy=None, ox=None):
        return wholes[a].at[y if oy is None else oy, x if ox is None else ox, c, from_z(step)]

    y_copies = {}
    x_copies = {}
    for a in range(2):
        for step in range(nf):
            if step:
                z_copies[a, step].wait_recv()
            source = shards_here[a] if step == 0 else block(a, step)
            for hop in range(1, outer):
                y_copies[a, hop, step] = send(
                    remote(
                        source,
                        block(a, step),
                        y_send.at[a, hop, step],
                        y_recv.at[a, hop, step],
                        y_peer(hop),
                    )
                )
            x_copies[a, step] = send(
                remote(
                    source, block(a, step), x_send.at[a, step], x_recv.at[a, step], x_peer
                )
            )
    for mask in masks:
        trades[0, mask].wait_recv()
    local[2].wait()
    gates = {}
    gate_own = gate_w.at[y, :, z]

    def gate_to_y(step):
        piece = gate_w.at[y, :, from_z(step)]
        for hop in range(1, outer):
            gates[hop, step] = send(
                remote(
                    piece, piece, over_send.at[hop, step], over_recv.at[hop, step], y_peer(hop)
                )
            )

    for step in range(1, nf):
        gates[0, step] = send(
            remote(gate_own, gate_own, gate_send.at[step], gate_recv.at[step], z_peer(step))
        )
    gate_to_y(0)
    for mask in masks:
        trades[1, mask].wait_recv()
    local[3].wait()
    upper_own = upper_w.at[y, :, z]
    uppers = [
        send(remote(upper_own, upper_own, up_send.at[step], up_recv.at[step], z_peer(step)))
        for step in early_steps(nf)
    ]
    hops = {}
    for a in range(2):
        for step in range(nf):
            for hop in range(1, outer):
                y_copies[a, hop, step].wait_recv()
                hops[a, hop, step] = send(
                    remote(
                        block(a, step, oy=from_y(hop)),
                        block(a, step, oy=from_y(hop)),
                        hop_send.at[a, hop, step],
                        hop_recv.at[a, hop, step],
                        x_peer,
                    )
                )
    for step in range(1, nf):
        gates[0, step].wait_recv()
        gate_to_y(step)
    cores = {}

    def to_core(a, hop, far):
        place = wholes[a].at[y if hop == 0 else from_y(hop), 1 - x if far else x, c]
        cores[a, hop, far] = send(
            remote(
                place,
                place,
                core_send.at[a, hop, far],
                core_recv.at[a, hop, far],
                core_peer,
            )
        )

    local[0].wait()
    local[1].wait()
    for a in range(2):
        for hop in range(outer):
            to_core(a, hop, 0)
    for a in range(2):
        for step in range(nf):
            x_copies[a, step].wait_recv()
        to_core(a, 0, 1)
    for a in range(2):
        for hop in range(1, outer):
            for step in range(nf):
                hops[a, hop, step].wait_recv()
            to_core(a, hop, 1)
    for copy in uppers:
        copy.wait_recv()
    for hop in range(1, outer):
        for step in range(nf):
            gates[hop, step].wait_recv()
    for key in cores:
        cores[key].wait_recv()
    for copy in sent:
        copy.wait_send()


def early_steps(nf):
    return sorted({1, nf - 1})


def gather_weights(nd, nf, shards_here):
    outer = nd // MEMBERS
    dma = pltpu.SemaphoreType.DMA
    lead = (outer, 2, 2, nf)
    low_type = jnp.bfloat16
    w_query, w_key, w_value, w_out, w_gate, w_up = shards_here
    in_shape = (w_query.shape[0], w_query.shape[1] + w_key.shape[1] + w_value.shape[1])
    inner = (w_gate.shape[0], w_gate.shape[1] // MEMBERS)
    pairs = [(2, nf), (2, outer, nf), (2, nf), (2, outer, nf), (2, outer, 2), (2, MEMBERS)]
    pairs += [(nf,), (outer, nf), (nf,)]
    return pl.pallas_call(
        functools.partial(weights_kernel, nd, nf),
        name="gather_weights",
        out_shape=(
            jax.ShapeDtypeStruct(lead + in_shape, low_type),
            jax.ShapeDtypeStruct(lead + w_out.shape, low_type),
            jax.ShapeDtypeStruct((outer, MEMBERS, nf) + inner, low_type),
            jax.ShapeDtypeStruct((outer, MEMBERS, nf) + inner, low_type),
        ),
        in_specs=[ANYWHERE] * 6,
        out_specs=(ANYWHERE,) * 4,
        scratch_shapes=[pltpu.VMEM(weight.shape, weight.dtype) for weight in shards_here]
        + [
            pltpu.VMEM(in_shape, low_type),
            pltpu.VMEM(w_out.shape, low_type),
            pltpu.VMEM((2, MEMBERS) + inner, low_type),
        ]
        + [dma(shape) for shape in pairs for _ in range(2)]
        + [dma((4,)), dma((6,))],
        compiler_params=pltpu.CompilerParams(
            collective_id=0, has_side_effects=True, vmem_limit_bytes=VMEM_MOST
        ),
    )(*shards_here)


def block_mean():
    row = lax.broadcasted_iota(jnp.int32, (LANES, LANES), 0) // HD
    column = lax.broadcasted_iota(jnp.int32, (LANES, LANES), 1) // HD
    return jnp.where(row == column, 1.0 / HD, 0.0).astype(jnp.bfloat16)


def head_mean(values, averages):
    high = values.astype(jnp.bfloat16)
    rest = (values - high.astype(jnp.float32)).astype(jnp.bfloat16)
    total = jnp.dot(high, averages, preferred_element_type=jnp.float32)
    return total + jnp.dot(rest, averages, preferred_element_type=jnp.float32)


def swap_halves(values):
    lane = lax.broadcasted_iota(jnp.int32, values.shape, 1) // (HD // 2)
    ahead = pltpu.roll(values, LANES - HD // 2, 1)
    behind = pltpu.roll(values, HD // 2, 1)
    return jnp.where(lane % 2 == 0, ahead, behind)


def in_half(values, source, target):
    lane = lax.broadcasted_iota(jnp.int32, values.shape, 1) // HD
    wide = values.astype(jnp.float32)
    if source != target:
        wide = pltpu.roll(wide, HD, 1)
    return jnp.where(lane == target, wide, 0.0).astype(values.dtype)


def split_gains(gains):
    rows = (gains.shape[0] - 1) // 2

    def joined(first):
        return jnp.concatenate([gains[first + row : first + row + 1, :] for row in range(rows)], 1)

    heads = gains[2 * rows : 2 * rows + 1, :]
    other = pltpu.roll(jnp.broadcast_to(heads, (8, LANES)), HD, 1)[:1]
    first = lax.broadcasted_iota(jnp.int32, heads.shape, 1) < HD
    query, key = jnp.where(first, heads, other), jnp.where(first, other, heads)

    def of_tile(index):
        return jnp.where(index < HQ * HD // LANES, query, key)

    return joined(0), joined(rows), of_tile


def may_attend(ids, row):
    length = ids.shape[1]
    across = ids[row : row + 1, :].astype(jnp.float32)
    place = lax.broadcasted_iota(jnp.int32, (length, length), 0)
    other = lax.broadcasted_iota(jnp.int32, (length, length), 1)
    down = jnp.sum(jnp.where(place == other, across, 0.0), 1, keepdims=True)
    return (other <= place) & (down == across)


def tile_of(index, width=LANES):
    return pl.ds(pl.multiple_of(index * width, LANES), width)


def rows_of(index, size):
    return pl.ds(pl.multiple_of(index * size, 16), size)


def dot_last(left, right):
    return lax.dot_general(
        left, right, (((1,), (1,)), ((), ())), preferred_element_type=jnp.float32
    )


def probabilities(query, key, keep):
    scores = dot_last(query, key) * HD**-0.5
    scores = jnp.where(keep, scores, masked_score)
    weights = jnp.exp(scores - jnp.max(scores, -1, keepdims=True))
    return weights / jnp.sum(weights, -1, keepdims=True)


def outer_product(left, right, target):
    pair, wide = 2 * LANES, 4 * LANES

    def step_once(index, carry):
        columns = tile_of(index, pair)
        turned = left[:, columns].T
        for start in range(0, right.shape[1], wide):
            across = pl.ds(start, min(wide, right.shape[1] - start))
            target[columns, across] = jnp.dot(
                turned, right[:, across], preferred_element_type=jnp.float32
            ).astype(jnp.bfloat16)
        return carry

    lax.fori_loop(0, left.shape[1] // pair, step_once, 0)


def flatten_blocks(blocks, rows, target):
    outer, members, nf, size, _ = blocks.shape

    def step_once(index, carry):
        for place in range(nf):
            rows[place * size : (place + 1) * size, :] = blocks[
                index // members, lax.rem(index, members), place
            ].astype(jnp.float32)
        target[rows_of(index, nf * size), :] = rows[...].astype(jnp.bfloat16)
        return carry

    lax.fori_loop(0, outer * members, step_once, 0)


def attend_kernel(
    nd,
    nf,
    length,
    gains,
    cosine,
    sine,
    segments,
    tokens_full,
    down_full,
    in_full,
    out_full,
    cot_full,
    upper_in,
    gate_w,
    upper_w,
    down_w,
    back_all,
    ffn_all,
    gate_near,
    upper_near,
    hidden_near,
    gate_far,
    upper_far,
    hidden_far,
    down_terms,
    raw,
    heads,
    values,
    mixed,
    hidden_in,
    normed,
    ffn_here,
    tokens,
    w_down,
    in_w,
    out_w,
    down_x,
    cot,
    gate_blocks,
    upper_blocks,
    block_rows,
    gate_flat,
    upper_flat,
    gate_here,
    upper_here,
    hidden_here,
    uz_send,
    uz_recv,
    uy_send,
    uy_recv,
    dz_send,
    dz_recv,
    dy_send,
    dy_recv,
    row_send,
    row_recv,
    local_sem,
):
    outer = nd // MEMBERS
    dp = lax.axis_index("dp")
    z = lax.axis_index("fsdp")
    y = dp // MEMBERS
    member = dp % MEMBERS
    x = member // 2
    c = member % 2

    def z_peer(step):
        return (dp, lax.rem(z + step, nf))

    def y_peer(step):
        return (lax.rem(y + step, outer) * MEMBERS + member, z)

    def from_z(step):
        return lax.rem(z - step + nf, nf)

    x_peer = (y * MEMBERS + (1 - x) * 2 + c, z)
    core_peer = (y * MEMBERS + x * 2 + 1 - c, z)
    barrier = pltpu.get_barrier_semaphore()
    peers = [z_peer(step) for step in range(1, nf)] + [y_peer(step) for step in range(1, outer)]
    peers += [x_peer, core_peer]
    for peer in peers:
        pl.semaphore_signal(barrier, inc=1, device_id=peer, device_id_type=MESH)
    gain_attn, gain_ffn, gain_heads = split_gains(gains)
    count = tokens.shape[0]
    width = tokens.shape[1]

    def member_rows(slot):
        return pl.ds(slot * count, count)

    weights_here = []
    operands = (
        (down_full, w_down),
        (cot_full, cot.at[member_rows(0)]),
        (tokens_full, tokens),
        (in_full, in_w),
        (out_full, out_w),
        (gate_w, gate_blocks),
    )
    for index, (source, target) in enumerate(operands):
        copy = pltpu.make_async_copy(source, target, local_sem.at[4 + index])
        copy.start()
        weights_here.append(copy)
    for _ in range(2):
        weights_here.pop(0).wait()
    down_x[...] = w_down[...].astype(jnp.bfloat16)
    pl.semaphore_wait(barrier, len(peers))
    sent = []

    def remote(source, target, send, recv, device):
        copy = pltpu.make_async_remote_copy(
            src_ref=source,
            dst_ref=target,
            send_sem=send,
            recv_sem=recv,
            device_id=device,
            device_id_type=MESH,
        )
        copy.start()
        sent.append(copy)
        return copy

    def keep(index, source, target):
        copy = pltpu.make_async_copy(source, target, local_sem.at[index])
        copy.start()
        return copy

    arrivals = []
    upper_own = upper_w.at[y, :, z]
    down_own = down_w.at[y, z]
    steps_left = [step for step in range(1, nf) if step not in early_steps(nf)]
    upper_z = {
        step: remote(upper_own, upper_own, uz_send.at[step], uz_recv.at[step], z_peer(step))
        for step in steps_left
    }

    def upper_to_y(step):
        if step in upper_z:
            upper_z[step].wait_recv()
        piece = upper_w.at[y, :, from_z(step)]
        for hop in range(1, outer):
            arrivals.append(
                remote(piece, piece, uy_send.at[hop, step], uy_recv.at[hop, step], y_peer(hop))
            )

    for step in [0] + early_steps(nf):
        upper_to_y(step)
    down_z = [
        remote(down_x, down_own, dz_send.at[step], dz_recv.at[step], z_peer(step))
        for step in range(1, nf)
    ]
    kept = [keep(1, down_x, down_own)]
    cot_own = cot.at[member_rows(0)]
    cot_near = remote(
        cot_own, cot.at[member_rows(1)], row_send.at[0, 0], row_recv.at[0, 0], core_peer
    )
    cot_far = remote(
        cot_own, cot.at[member_rows(2)], row_send.at[0, 1], row_recv.at[0, 1], x_peer
    )

    def down_to_y(step):
        if step:
            down_z[step - 1].wait_recv()
        piece = down_w.at[y, from_z(step)] if step else down_x
        for hop in range(1, outer):
            arrivals.append(
                remote(
                    piece,
                    down_w.at[y, from_z(step)],
                    dy_send.at[hop, step],
                    dy_recv.at[hop, step],
                    y_peer(hop),
                )
            )

    chunk = 32

    weights_here.pop(0).wait()

    def norm_rows(index, carry):
        rows = rows_of(index, chunk)
        part = tokens[rows, :].astype(jnp.float32)
        scale = lax.rsqrt(jnp.mean(part * part, -1, keepdims=True) + norm_eps)
        normed[rows, :] = (part * scale * gain_attn).astype(jnp.bfloat16)
        return carry

    lax.fori_loop(0, count // chunk, norm_rows, 0)
    head_tiles = (HQ + KV) * HD // LANES
    for _ in range(2):
        weights_here.pop(0).wait()

    def project(index, carry):
        columns = tile_of(index, 2 * LANES)
        raw[:, columns] = jnp.dot(
            normed[...], in_w[:, columns], preferred_element_type=jnp.float32
        )
        return carry

    lax.fori_loop(0, head_tiles // 2, project, 0)
    values[...] = jnp.dot(
        normed[...], in_w[:, pl.ds(head_tiles * LANES, KV * HD)], preferred_element_type=jnp.float32
    ).astype(jnp.bfloat16)
    averages = block_mean()

    def turn(index, carry):
        columns = tile_of(index)
        for row in range(count // length):
            rows = pl.ds(row * length, length)
            part = raw[rows, columns]
            scale = lax.rsqrt(head_mean(part * part, averages) + norm_eps)
            part = part * scale * gain_heads(index)
            part = part * cosine[...] + swap_halves(part) * sine[...]
            heads[rows, columns] = part.astype(jnp.bfloat16)
        return carry

    lax.fori_loop(0, head_tiles, turn, 0)

    def attend(row):
        rows = pl.ds(row * length, length)
        allowed = may_attend(segments, row)

        def pair(tile, carry):
            key_tile = heads[rows, tile_of(HQ * HD // LANES + tile)]
            value_tile = values[rows, tile_of(tile)]
            for own in range(2):
                key = [in_half(key_tile, own, half) for half in range(2)]
                value = [in_half(value_tile, own, half) for half in range(2)]
                for quarter in range(2):
                    columns = tile_of(tile * 4 + own * 2 + quarter)
                    query = heads[rows, columns]
                    total = None
                    for half in range(2):
                        weights = probabilities(query, key[half], allowed).astype(jnp.bfloat16)
                        term = jnp.dot(weights, value[half], preferred_element_type=jnp.float32)
                        total = term if total is None else total + term
                    mixed[rows, columns] = total.astype(jnp.bfloat16)
            return carry

        lax.fori_loop(0, KV * HD // LANES, pair, 0)

    down_steps = list(range(nf))
    ffn_far, ffn_near = [], []

    def finish(row):
        rows = pl.ds(row * length, length)

        def project_out(index, carry):
            columns = tile_of(index, 2 * LANES)
            hidden_in[rows, columns] = tokens[rows, columns].astype(jnp.float32) + jnp.dot(
                mixed[rows, :], out_w[:, columns], preferred_element_type=jnp.float32
            )
            return carry

        lax.fori_loop(0, width // (2 * LANES), project_out, 0)

        def norm_hidden(index, carry):
            part_rows = pl.ds(pl.multiple_of(row * length + index * chunk, 16), chunk)
            part = hidden_in[part_rows, :]
            scale = lax.rsqrt(jnp.mean(part * part, -1, keepdims=True) + norm_eps)
            ffn_here[part_rows, :] = (part * scale * gain_ffn).astype(jnp.bfloat16)
            return carry

        lax.fori_loop(0, length // chunk, norm_hidden, 0)
        for slot, peer, copies in ((2, x_peer, ffn_far), (1, core_peer, ffn_near)):
            copies.append(
                remote(
                    ffn_here.at[rows],
                    ffn_here.at[pl.ds(slot * count + row * length, length)],
                    row_send.at[slot, row],
                    row_recv.at[slot, row],
                    peer,
                )
            )

    batch = count // length
    for row in range(batch):
        attend(row)
        finish(row)
        if row == 0:
            for step in steps_left:
                upper_to_y(step)
            uppers = list(arrivals)
            arrivals.clear()
            down_to_y(down_steps.pop(0))

    cot_far.wait_recv()
    cot_cross = remote(
        cot.at[member_rows(2)],
        cot.at[member_rows(3)],
        row_send.at[0, 2],
        row_recv.at[0, 2],
        core_peer,
    )
    down_to_y(down_steps.pop(0))
    weights_here.pop(0).wait()
    flatten_blocks(gate_blocks, block_rows, gate_flat)
    for copy in uppers:
        copy.wait_recv()
    kept.pop(0).wait()
    upper_load = keep(0, upper_w, upper_blocks)
    while len(down_steps) > 1:
        down_to_y(down_steps.pop(0))
    upper_load.wait()
    flatten_blocks(upper_blocks, block_rows, upper_flat)

    def ffn_rows(slot):
        rows = member_rows(slot)

        def tile_once(index, carry):
            columns = tile_of(index, 2 * LANES)
            gate = jnp.dot(
                ffn_here[rows, :], gate_flat[:, columns], preferred_element_type=jnp.float32
            )
            upper = jnp.dot(
                ffn_here[rows, :], upper_flat[:, columns], preferred_element_type=jnp.float32
            )
            gate_here[rows, columns] = gate
            upper_here[rows, columns] = upper
            hidden_here[rows, columns] = (gate / (1.0 + jnp.exp(-gate)) * upper).astype(
                jnp.bfloat16
            )
            return carry

        lax.fori_loop(0, gate_flat.shape[1] // (2 * LANES), tile_once, 0)

    ffn_rows(0)
    for copy in ffn_near:
        copy.wait_recv()
    ffn_rows(1)
    crosses = []
    for row in range(batch):
        ffn_far[row].wait_recv()
        crosses.append(
            remote(
                ffn_here.at[pl.ds(2 * count + row * length, length)],
                ffn_here.at[pl.ds(3 * count + row * length, length)],
                row_send.at[3, row],
                row_recv.at[3, row],
                core_peer,
            )
        )
    down_to_y(nf - 1)
    ffn_rows(2)
    for copy in crosses:
        copy.wait_recv()
    kept.append(keep(2, ffn_here, ffn_all))
    ffn_rows(3)
    halves = (
        (gate_near, upper_near, hidden_near),
        (gate_far, upper_far, hidden_far),
    )
    for far, targets in enumerate(halves):
        rows = pl.ds(far * 2 * count, 2 * count)
        for index, source in enumerate((gate_here, upper_here, hidden_here)):
            kept.append(keep(9 + 3 * far + index, source.at[rows], targets[index]))
    cot_near.wait_recv()
    cot_cross.wait_recv()
    kept.append(keep(3, cot, back_all))
    outer_product(hidden_here, cot, down_terms)
    for copy in arrivals:
        copy.wait_recv()
    for copy in sent:
        copy.wait_send()
    for copy in kept:
        copy.wait()


def attend(nd, nf, length, small, tokens, w_down, in_w, out_w, cot, upper_w, gate_w):
    outer = nd // MEMBERS
    count, width = tokens.shape
    nf_rows, mine = gate_w.shape[2] * gate_w.shape[3], gate_w.shape[4]
    lo, hi = jnp.bfloat16, jnp.float32
    dma = pltpu.SemaphoreType.DMA
    moves = [(nf,), (outer, nf), (nf,), (outer, nf), (4, max(3, count // length))]
    shapes = [
        (upper_w.shape, lo),
        ((outer, nf) + w_down.shape, lo),
        ((MEMBERS * count, width), lo),
        ((MEMBERS * count, width), lo),
        *[((2 * count, mine), kind) for kind in (hi, hi, lo)] * 2,
        ((mine, width), lo),
        ((count, (HQ + KV) * HD), hi),
        ((count, (HQ + KV) * HD), lo),
        ((count, KV * HD), lo),
        ((count, HQ * HD), lo),
        ((count, width), hi),
    ]
    early = [(count, width), (MEMBERS * count, width), (count, width)]
    late = [in_w.shape, out_w.shape, w_down.shape, (MEMBERS * count, width)]
    late += [gate_w.shape, gate_w.shape]
    flat = (width, mine)
    return pl.pallas_call(
        functools.partial(attend_kernel, nd, nf, length),
        name="attend",
        out_shape=tuple(jax.ShapeDtypeStruct(*item) for item in shapes),
        in_specs=[ON_CHIP] * 4 + [ANYWHERE] * 7,
        out_specs=(ANYWHERE,) * 10 + (ON_CHIP,) * 6,
        input_output_aliases={9: 0},
        scratch_shapes=[pltpu.VMEM(shape, lo) for shape in early]
        + [pltpu.VMEM(w_down.shape, hi)]
        + [pltpu.VMEM(shape, lo) for shape in late]
        + [pltpu.VMEM((nf_rows, mine), hi), pltpu.VMEM(flat, lo), pltpu.VMEM(flat, lo)]
        + [pltpu.VMEM((MEMBERS * count, mine), kind) for kind in (hi, hi, lo)]
        + [dma(shape) for shape in moves for _ in range(2)]
        + [dma((15,))],
        compiler_params=pltpu.CompilerParams(
            collective_id=2, has_side_effects=True, vmem_limit_bytes=VMEM_MOST
        ),
    )(*small, tokens, w_down, in_w, out_w, cot, upper_w, gate_w)


def backward_kernel(
    nd,
    nf,
    length,
    gains,
    cosine,
    sine,
    segments,
    hidden_near,
    hidden_far,
    down_got,
    down_terms,
    gate_terms,
    upper_terms,
    tokens_full,
    mine_full,
    near_full,
    far_full,
    hidden_full,
    cot_full,
    out_w_full,
    mixed_full,
    heads_full,
    values_full,
    raw_full,
    in_w_full,
    down_full,
    out_mine,
    out_core,
    out_x,
    gate_parts,
    upper_parts,
    input_grad,
    in_sum,
    out_sum,
    down_sum,
    gain_totals,
    norm,
    sum_attn,
    sum_ffn,
    sum_heads,
    gain_here,
    gain_group,
    gain_got,
    gain_far,
    square_here,
    square_group,
    square_got,
    square_far,
    tokens,
    mine_ref,
    core_near,
    from_x,
    hidden_in,
    cot,
    out_w,
    mixed,
    heads,
    values,
    raw,
    in_w,
    down_w,
    near_here,
    far_here,
    out_near,
    out_far,
    out_core_far,
    normed,
    branch,
    grad_mixed,
    grad_hidden,
    grad_raw,
    wide,
    in_terms,
    out_terms,
    in_core,
    out_core_terms,
    in_x,
    out_x_terms,
    in_y,
    out_y_terms,
    in_total,
    out_total,
    in_zs,
    out_zs,
    in_zr,
    out_zr,
    down_own,
    gate_own,
    upper_own,
    down_y,
    gate_y,
    upper_y,
    down_z,
    gate_z,
    upper_z,
    row_send,
    row_recv,
    fy_send,
    fy_recv,
    fz_send,
    fz_recv,
    swap_send,
    swap_recv,
    ac_send,
    ac_recv,
    ax_send,
    ax_recv,
    ay_send,
    ay_recv,
    az_send,
    az_recv,
    tg_send,
    tg_recv,
    tf_send,
    tf_recv,
    load_sem,
    got_sem,
    operand_sem,
    local_sem,
):
    outer = nd // MEMBERS
    dp = lax.axis_index("dp")
    z = lax.axis_index("fsdp")
    y = dp // MEMBERS
    member = dp % MEMBERS
    x = member // 2
    c = member % 2
    lo, hi = jnp.bfloat16, jnp.float32

    def z_to(step):
        return lax.rem(z + step, nf)

    def z_peer(step):
        return (dp, z_to(step))

    def y_to(step):
        return lax.rem(y + step, outer)

    def y_peer(step):
        return (y_to(step) * MEMBERS + member, z)

    def in_group(k):
        return (y * MEMBERS + k, z)

    x_peer = in_group((1 - x) * 2 + c)
    core_peer = in_group(x * 2 + 1 - c)
    barrier = pltpu.get_barrier_semaphore()
    peers = [z_peer(step) for step in range(1, nf)] + [y_peer(step) for step in range(1, outer)]
    peers += [x_peer, core_peer, in_group(MEMBERS - 1 - member)]
    crossed = [(hop, step) for hop in range(outer) for step in range(nf) if hop or step]

    def cross_peer(hop, step):
        return (y_to(hop) * MEMBERS + member, z_to(step))

    peers += [cross_peer(hop, step) for hop, step in crossed if hop and step]
    fulls = (tokens_full, mine_full, near_full, far_full, hidden_full, cot_full, out_w_full, mixed_full)
    fulls += (heads_full, values_full, raw_full, in_w_full)
    fulls += (down_full, hidden_near, hidden_far)
    places = (tokens, mine_ref, core_near, from_x, hidden_in, cot, out_w, mixed)
    places += (heads, values, raw, in_w, down_w, near_here, far_here)
    operands = [
        pltpu.make_async_copy(source, target, operand_sem.at[index])
        for index, (source, target) in enumerate(zip(fulls, places))
    ]
    start_all(operands)

    def ready(number):
        for _ in range(number):
            operands.pop(0).wait()

    for peer in peers:
        pl.semaphore_signal(barrier, inc=1, device_id=peer, device_id_type=MESH)
    pl.semaphore_wait(barrier, len(peers))
    sent = []

    def remote(source, target, send, recv, device):
        copy = pltpu.make_async_remote_copy(
            src_ref=source,
            dst_ref=target,
            send_sem=send,
            recv_sem=recv,
            device_id=device,
            device_id_type=MESH,
        )
        copy.start()
        sent.append(copy)
        return copy

    def keep(semaphore, source, target):
        copy = pltpu.make_async_copy(source, target, semaphore)
        copy.start()
        return copy

    gain_attn, gain_ffn, gain_heads = split_gains(gains)
    count, width = tokens.shape
    here, there = pl.ds(0, count), pl.ds(count, count)

    terms = (down_terms, gate_terms, upper_terms)
    owns = (down_own, gate_own, upper_own)
    over_y = (down_y, gate_y, upper_y)
    over_z = (down_z, gate_z, upper_z)

    def piece_of(matrix, place, step):
        if matrix == 0:
            return terms[0].at[place, z_to(step)]
        return terms[matrix].at[place, :, z_to(step)]

    order = [(matrix, step) for matrix in range(3) for step in list(range(1, nf)) + [0]]
    y_copies, loads = {}, {}
    for matrix, step in order:
        loads[matrix, step] = keep(
            load_sem.at[matrix, step], piece_of(matrix, y, step), owns[matrix].at[step]
        )
        for hop in range(1, outer):
            if matrix == 0:
                y_copies[0, step, hop] = keep(
                    got_sem.at[hop, step], down_got.at[hop - 1, z_to(step)], down_y.at[hop - 1, step]
                )
                continue
            y_copies[matrix, step, hop] = remote(
                piece_of(matrix, y_to(hop), step),
                over_y[matrix].at[hop - 1, step],
                fy_send.at[matrix, hop, step],
                fy_recv.at[matrix, hop, step],
                y_peer(hop),
            )
    z_copies = {}
    waiting = list(order)

    def pieces(number):
        for _ in range(min(number, len(waiting))):
            matrix, step = waiting.pop(0)
            loads[matrix, step].wait()
            total = owns[matrix][step].astype(hi)
            for hop in range(1, outer):
                if matrix:
                    y_copies[matrix, step, hop].wait_recv()
                else:
                    y_copies[0, step, hop].wait()
                total = total + over_y[matrix][hop - 1, step].astype(hi)
            owns[matrix][step] = total.astype(lo)
            if step:
                z_copies[matrix, step] = remote(
                    owns[matrix].at[step],
                    over_z[matrix].at[step - 1],
                    fz_send.at[matrix, step],
                    fz_recv.at[matrix, step],
                    z_peer(step),
                )

    def piece_total(matrix):
        total = owns[matrix][0].astype(hi)
        for step in range(1, nf):
            z_copies[matrix, step].wait_recv()
            total = total + over_z[matrix][step - 1].astype(hi)
        return total

    swaps = []

    squares = []

    def trade(matrix, parts):
        total = piece_total(matrix).astype(lo)
        owns[matrix][0] = total
        total = total.astype(hi)
        squares.append(jnp.sum(total * total))
        for mask_bits in range(1, MEMBERS):
            other = member ^ mask_bits
            swaps.append(
                remote(
                    owns[matrix].at[0, other],
                    parts.at[member],
                    swap_send.at[matrix - 1, mask_bits],
                    swap_recv.at[matrix - 1, mask_bits],
                    in_group(other),
                )
            )
        swaps_local.append(
            keep(local_sem.at[2 + matrix], owns[matrix].at[0, member], parts.at[member])
        )

    swaps_local = []
    chunk = 32

    def to_group(index, source, target):
        target[member] = source[...]
        return [
            remote(
                source,
                target.at[member],
                tg_send.at[index, mask_bits],
                tg_recv.at[index, mask_bits],
                in_group(member ^ mask_bits),
            )
            for mask_bits in range(1, MEMBERS)
        ]

    def to_crossed(index, source, target):
        target[y * nf + z] = source[...]
        return [
            remote(
                source,
                target.at[y * nf + z],
                tf_send.at[index, place],
                tf_recv.at[index, place],
                cross_peer(hop, step),
            )
            for place, (hop, step) in enumerate(crossed)
        ]

    def summed(got, copies):
        for copy in copies:
            copy.wait_recv()
        return jnp.sum(got[...], 0)

    ready(1)
    def add_rows(target, other):
        def step_once(index, carry):
            rows = rows_of(index, chunk)
            target[rows, :] = (target[rows, :].astype(hi) + other[rows, :].astype(hi)).astype(lo)
            return carry

        lax.fori_loop(0, count // chunk, step_once, 0)

    def norm_rows(index, carry):
        rows = rows_of(index, chunk)
        part = tokens[rows, :].astype(hi)
        scale = lax.rsqrt(jnp.mean(part * part, -1, keepdims=True) + norm_eps)
        normed[rows, :] = (part * scale * gain_attn).astype(lo)
        return carry

    lax.fori_loop(0, count // chunk, norm_rows, 0)
    sum_attn[...] = jnp.zeros_like(sum_attn)
    sum_ffn[...] = jnp.zeros_like(sum_ffn)
    sum_heads[...] = jnp.zeros_like(sum_heads)
    pieces(nf)
    ready(5)

    def norm_back(part, gain, grad):
        scale = lax.rsqrt(jnp.mean(part * part, -1, keepdims=True) + norm_eps)
        unit = part * scale
        inner = grad * gain
        back = scale * (inner - unit * jnp.mean(inner * unit, -1, keepdims=True))
        return back, jnp.sum(grad * unit, 0, keepdims=True)

    def ffn_norm_back(index, carry):
        rows = rows_of(index, chunk)
        grad = mine_ref[rows, :].astype(hi) + core_near[rows, :].astype(hi)
        grad = grad + from_x[rows, :].astype(hi)
        back, gain_term = norm_back(hidden_in[rows, :], gain_ffn, grad)
        sum_ffn[...] += gain_term
        back = back + cot[rows, :].astype(hi)
        grad_hidden[rows, :] = back
        branch[rows, :] = back.astype(lo)
        return carry

    lax.fori_loop(0, count // chunk, ffn_norm_back, 0)
    pair = 2 * LANES
    ready(2)

    def mixed_back(index, carry):
        columns = tile_of(index, pair)
        grad_mixed[:, columns] = dot_last(branch[...], out_w[columns, :]).astype(lo)
        return carry

    lax.fori_loop(0, HQ * HD // pair, mixed_back, 0)

    all_terms = (in_terms, out_terms)
    sizes = (in_terms.shape[0] // (nd), out_terms.shape[0] // (nd))
    core_terms = (in_core, out_core_terms)
    x_terms = (in_x, out_x_terms)
    y_terms = (in_y, out_y_terms)
    totals = (in_total, out_total)
    zs = (in_zs, out_zs)
    zr = (in_zr, out_zr)
    hops = list(range(1, outer)) + [0]
    core_copies, ax_copies, ay_copies, az_copies = {}, {}, {}, {}

    def block(a, hop, bx, bc):
        index = (y_to(hop) * 2 + bx) * 2 + bc
        return pl.ds(pl.multiple_of(index * sizes[a], 16), sizes[a])

    def core_out(a):
        for far in (1, 0):
            for hop in hops:
                bx = 1 - x if far else x
                core_copies[a, hop, far] = remote(
                    all_terms[a].at[block(a, hop, bx, 1 - c)],
                    core_terms[a].at[hop, far],
                    ac_send.at[a, hop, far],
                    ac_recv.at[a, hop, far],
                    core_peer,
                )

    def add_block(a, rows, others):
        some = math.gcd(sizes[a], 32)

        def step_once(index, carry):
            base = rows.start + index * some
            place = pl.ds(pl.multiple_of(base, 16), some)
            total = all_terms[a][place, :].astype(hi)
            for other in others:
                total = total + other[rows_of(index, some), :].astype(hi)
            all_terms[a][place, :] = total.astype(lo)
            return carry

        lax.fori_loop(0, sizes[a] // some, step_once, 0)

    def core_in(a):
        for hop in hops:
            core_copies[a, hop, 1].wait_recv()
            rows = block(a, hop, 1 - x, c)
            add_block(a, rows, [core_terms[a].at[hop, 1]])
            ax_copies[a, hop] = remote(
                all_terms[a].at[rows],
                x_terms[a].at[hop],
                ax_send.at[a, hop],
                ax_recv.at[a, hop],
                x_peer,
            )

    def x_in(a):
        for hop in range(1, outer):
            core_copies[a, hop, 0].wait_recv()
            ax_copies[a, hop].wait_recv()
            rows = block(a, hop, x, c)
            add_block(a, rows, [core_terms[a].at[hop, 0], x_terms[a].at[hop]])
            ay_copies[a, hop] = remote(
                all_terms[a].at[rows],
                y_terms[a].at[hop - 1],
                ay_send.at[a, hop],
                ay_recv.at[a, hop],
                y_peer(hop),
            )

    def y_in(a):
        core_copies[a, 0, 0].wait_recv()
        ax_copies[a, 0].wait_recv()
        others = [core_terms[a].at[0, 0], x_terms[a].at[0]]
        for hop in range(1, outer):
            ay_copies[a, hop].wait_recv()
            others.append(y_terms[a].at[hop - 1])
        start = block(a, 0, x, c).start
        some = math.gcd(sizes[a], 32)

        def step_once(index, carry):
            place = rows_of(index, some)
            own = pl.ds(pl.multiple_of(start + index * some, 16), some)
            total = all_terms[a][own, :].astype(hi)
            for other in others:
                total = total + other[place, :].astype(hi)
            totals[a][place, :] = total
            return carry

        lax.fori_loop(0, sizes[a] // some, step_once, 0)
        rows = sizes[a] // nf
        for place in range(nf):
            zs[a][place] = totals[a][place * rows : (place + 1) * rows, :].astype(lo)
        for step in range(1, nf):
            az_copies[a, step] = remote(
                zs[a].at[z_to(step)],
                zr[a].at[step - 1],
                az_send.at[a, step],
                az_recv.at[a, step],
                z_peer(step),
            )

    def z_in(a, target):
        total = zs[a][z].astype(hi)
        for step in range(1, nf):
            az_copies[a, step].wait_recv()
            total = total + zr[a][step - 1].astype(hi)
        target[...] = total

    outer_product(mixed, branch, out_terms)
    core_out(1)
    pieces(2)
    ready(len(operands))
    query_tiles = HQ * HD // LANES
    head_tiles = (HQ + KV) * HD // LANES
    key_tiles = KV * HD // LANES

    def over_rows(left, right):
        return lax.dot_general(left, right, (((0,), (0,)), ((), ())), preferred_element_type=hi)

    def attend_back(row):
        rows = pl.ds(row * length, length)
        allowed = may_attend(segments, row)

        def pair_back(tile, carry):
            key_tile = heads[rows, tile_of(query_tiles + tile)]
            value_tile = values[rows, tile_of(tile)]
            grad_key = None
            grad_value = None
            for own in range(2):
                key = [in_half(key_tile, own, half) for half in range(2)]
                value = [in_half(value_tile, own, half) for half in range(2)]
                for half in range(2):
                    key_total, value_total = None, None
                    for quarter in range(2):
                        columns = tile_of(tile * 4 + own * 2 + quarter)
                        query = heads[rows, columns]
                        grad = grad_mixed[rows, columns]
                        weights = probabilities(query, key[half], allowed)
                        slope = dot_last(grad, value[half])
                        inner = jnp.sum(weights * slope, -1, keepdims=True)
                        score = (weights * (slope - inner)).astype(lo)
                        back = jnp.dot(score, key[half], preferred_element_type=hi) * HD**-0.5
                        if half == 0:
                            wide[rows, columns] = back
                        else:
                            wide[rows, columns] += back
                        key_term = over_rows(score, query)
                        value_term = over_rows(weights.astype(lo), grad)
                        key_total = key_term if key_total is None else key_total + key_term
                        value_total = value_term if value_total is None else value_total + value_term
                    key_term = in_half(key_total, half, own)
                    value_term = in_half(value_total, half, own)
                    grad_key = key_term if grad_key is None else grad_key + key_term
                    grad_value = value_term if grad_value is None else grad_value + value_term
            wide[rows, tile_of(query_tiles + tile)] = grad_key * HD**-0.5
            grad_raw[rows, tile_of(head_tiles + tile)] = grad_value.astype(lo)
            return carry

        lax.fori_loop(0, key_tiles, pair_back, 0)

    batch = count // length
    for row in range(batch):
        attend_back(row)
        if row == 0:
            core_in(1)
        pieces(1)
    averages = block_mean()

    def turn_back(index, carry):
        columns = tile_of(index)
        gain = gain_heads(index)
        for row in range(batch):
            rows = pl.ds(row * length, length)
            grad = wide[rows, columns]
            grad = grad * cosine[...] - swap_halves(grad) * sine[...]
            part = raw[rows, columns]
            scale = lax.rsqrt(head_mean(part * part, averages) + norm_eps)
            unit = part * scale
            sum_heads[:, columns] += jnp.sum(grad * unit, 0, keepdims=True)
            inner = grad * gain
            back = scale * (inner - unit * head_mean(inner * unit, averages))
            grad_raw[rows, columns] = back.astype(lo)
        return carry

    lax.fori_loop(0, head_tiles, turn_back, 0)
    outer_product(normed, grad_raw, in_terms)
    core_out(0)
    pieces(1)
    x_in(1)

    def normed_back(index, carry):
        columns = tile_of(index, pair)
        wide[:, columns] = dot_last(grad_raw[...], in_w[columns, :])
        return carry

    core_in(0)

    def down_product(left, target):
        def step_once(index, carry):
            columns = tile_of(index, pair)
            target[:, columns] = jnp.dot(
                left[...], down_w[:, columns], preferred_element_type=hi
            ).astype(lo)
            return carry

        lax.fori_loop(0, width // pair, step_once, 0)

    down_product(far_here, out_far)
    out_far_copy = remote(out_far.at[there], out_core_far, row_send.at[0], row_recv.at[0], core_peer)
    down_product(near_here, out_near)
    out_near_copy = remote(out_near.at[there], out_core, row_send.at[1], row_recv.at[1], core_peer)
    mine_copy = keep(local_sem.at[0], out_near.at[here], out_mine)
    out_far_copy.wait_recv()
    add_rows(out_far, out_core_far)
    out_x_copy = remote(out_far.at[here], out_x, row_send.at[2], row_recv.at[2], x_peer)
    lax.fori_loop(0, width // pair, normed_back, 0)

    def attn_norm_back(index, carry):
        rows = rows_of(index, chunk)
        back, gain_term = norm_back(tokens[rows, :].astype(hi), gain_attn, wide[rows, :])
        sum_attn[...] += gain_term
        input_grad[rows, :] = (back + grad_hidden[rows, :]).astype(lo)
        return carry

    lax.fori_loop(0, count // chunk, attn_norm_back, 0)
    gain_here[...] = jnp.zeros_like(gain_here)
    place = 0
    for source in (sum_attn, sum_ffn, sum_heads):
        for tile in range(source.shape[1] // LANES):
            gain_here[pl.ds(place, 1), :] = source[:, tile * LANES : (tile + 1) * LANES]
            place += 1
    gain_copies = to_group(0, gain_here, gain_got)
    pieces(1)
    x_in(0)
    down_sum[...] = piece_total(0)
    y_in(1)
    pieces(2 * nf)
    trade(1, gate_parts)
    y_in(0)
    gain_group[...] = summed(gain_got, gain_copies)
    gain_copies = to_crossed(0, gain_group, gain_far)
    z_in(1, out_sum)
    trade(2, upper_parts)
    z_in(0, in_sum)
    for target in (down_sum, out_sum, in_sum):
        squares.append(jnp.sum(target[...] * target[...]))
    square_here[...] = jnp.full(square_here.shape, sum(squares))
    square_copies = to_group(1, square_here, square_got)
    square_group[...] = summed(square_got, square_copies)
    square_copies = to_crossed(1, square_group, square_far)
    gain_totals[...] = summed(gain_far, gain_copies)
    gain_place = 2 * width // LANES
    gain_squares = gain_totals[:gain_place, :]
    gain_squares = jnp.sum(gain_squares * gain_squares)
    for first, last in ((0, query_tiles), (query_tiles, head_tiles)):
        total = jnp.sum(gain_totals[gain_place + first : gain_place + last, :], 0, keepdims=True)
        total = jnp.broadcast_to(total, (8, LANES))
        total = total + pltpu.roll(total, HD, 1)
        gain_squares += jnp.sum(total * total) / (8 * LANES // HD)
    norm[...] = jnp.sqrt(summed(square_far, square_copies) + gain_squares)
    for copy in swaps + [out_near_copy, out_x_copy]:
        copy.wait_recv()
    for copy in sent:
        copy.wait_send()
    for copy in swaps_local + [mine_copy]:
        copy.wait()


def backward(nd, nf, length, small, halves, terms, operands):
    outer = nd // MEMBERS
    count, width = operands[0].shape
    out_w, in_w = operands[6], operands[-2]
    _, down_terms, gate_terms, _ = terms
    lo, hi = jnp.bfloat16, jnp.float32
    dma = pltpu.SemaphoreType.DMA
    in_rows, in_cols = in_w.shape[0] // (nd * nf), in_w.shape[1]
    out_rows, out_cols = out_w.shape[0] // (nd * nf), out_w.shape[1]
    inner = (MEMBERS,) + gate_terms.shape[3:]
    down = down_terms.shape[2:]
    tiles = (2 * width + (HQ + KV) * HD) // LANES
    gain_tile = (-(-tiles // 8) * 8, LANES)
    far = outer * nf - 1
    shapes = [
        ((count, width), lo),
        ((count, width), lo),
        ((count, width), lo),
        (inner, lo),
        (inner, lo),
        ((count, width), lo),
        ((in_rows, in_cols), hi),
        ((out_rows, out_cols), hi),
        (down, hi),
        (gain_tile, hi),
        ((8, LANES), hi),
    ]
    in_block, out_block = (nf * in_rows, in_cols), (nf * out_rows, out_cols)
    scratch = [((1, width), hi), ((1, width), hi), ((1, (HQ + KV) * HD), hi)]
    for tile in (gain_tile, (8, LANES)):
        scratch += [(tile, hi), (tile, hi), ((MEMBERS,) + tile, hi), ((outer * nf,) + tile, hi)]
    scratch += [(operand.shape, operand.dtype) for operand in operands]
    scratch += [(array.shape, lo) for array in halves]
    scratch += [((2 * count, width), lo)] * 2 + [((count, width), lo)]
    scratch += [
        ((count, width), lo),
        ((count, width), lo),
        ((count, HQ * HD), lo),
        ((count, width), hi),
        ((count, in_cols), lo),
        ((count, width), hi),
        (in_w.shape, lo),
        (out_w.shape, lo),
        ((outer, 2) + in_block, lo),
        ((outer, 2) + out_block, lo),
        ((outer,) + in_block, lo),
        ((outer,) + out_block, lo),
        ((outer - 1,) + in_block, lo),
        ((outer - 1,) + out_block, lo),
        (in_block, hi),
        (out_block, hi),
        ((nf, in_rows, in_cols), lo),
        ((nf, out_rows, out_cols), lo),
        ((nf - 1, in_rows, in_cols), lo),
        ((nf - 1, out_rows, out_cols), lo),
        ((nf,) + down, lo),
        ((nf,) + inner, lo),
        ((nf,) + inner, lo),
        ((outer - 1, nf) + down, lo),
        ((outer - 1, nf) + inner, lo),
        ((outer - 1, nf) + inner, lo),
        ((nf - 1,) + down, lo),
        ((nf - 1,) + inner, lo),
        ((nf - 1,) + inner, lo),
    ]
    moves = [(3,), (3, outer, nf), (3, nf), (2, MEMBERS), (2, outer, 2), (2, outer), (2, outer)]
    moves += [(2, nf), (2, MEMBERS), (2, far)]
    return pl.pallas_call(
        functools.partial(backward_kernel, nd, nf, length),
        name="backward",
        out_shape=tuple(jax.ShapeDtypeStruct(*item) for item in shapes),
        in_specs=[ON_CHIP] * 4 + [ANYWHERE] * (6 + len(operands)),
        out_specs=(ANYWHERE,) * 5 + (ON_CHIP,) * 6,
        scratch_shapes=[pltpu.VMEM(*item) for item in scratch]
        + [dma(shape) for shape in moves for _ in range(2)]
        + [dma((3, nf)), dma((outer, nf)), dma((len(operands) + 2,)), dma((5,))],
        compiler_params=pltpu.CompilerParams(
            collective_id=3, has_side_effects=True, vmem_limit_bytes=VMEM_MOST
        ),
    )(*small, *halves, *terms, *operands)


def adam_kernel(
    span, norm, gain_totals, in_sum, out_sum, gate_parts, upper_parts, down_sum, *rest
):
    count = 8
    row_terms, rest = rest[:5], rest[5:]
    masters, firsts, seconds = rest[:count], rest[count : 2 * count], rest[2 * count : 3 * count]
    rest = rest[3 * count :]
    outs = [rest[index * count : (index + 1) * count] for index in range(3)]
    copies = rest[3 * count : 4 * count - 1]
    output, rows_out, norm_out = rest[4 * count - 1 : 4 * count + 2]
    rest = rest[4 * count + 2 :]
    norm_out[...] = norm[0:1, 0:1]
    ins_here = [rest[index * count : (index + 1) * count] for index in range(3)]
    rest = rest[3 * count :]
    outs_here = [rest[index * count : (index + 1) * count] for index in range(3)]
    copies_here = rest[3 * count : 4 * count - 1]
    sums_here = rest[4 * count - 1 : 4 * count + 4]
    terms_here = rest[4 * count + 4 : 4 * count + 9]
    output_here, sum_sem, in_sem, out_sem, term_sem = rest[4 * count + 9 :]
    sums = (in_sum, out_sum, gate_parts, upper_parts, down_sum)
    loads = {}
    for index in (6, 4, 5, 3, 0, 1, 2, 7):
        source = {6: 4, 4: 2, 5: 3, 3: 1, 0: 0}.get(index)
        if source is not None:
            loads[source] = pltpu.make_async_copy(
                sums[source], sums_here[source], sum_sem.at[source]
            )
            loads[source].start()
        for kind, arrays in enumerate((masters, firsts, seconds)):
            loads[index, kind] = pltpu.make_async_copy(
                arrays[index], ins_here[kind][index], in_sem.at[kind, index]
            )
            loads[index, kind].start()
    rows_count = output.shape[0]
    term_loads = []
    for index, (source, target) in enumerate(zip(row_terms, terms_here)):
        copy = pltpu.make_async_copy(
            source.at[pl.ds(0, rows_count)], target, term_sem.at[index]
        )
        copy.start()
        term_loads.append(copy)
    stores = []

    def store(index):
        pairs = [(outs_here[kind][index], outs[kind][index]) for kind in range(3)]
        if index < count - 1:
            pairs.append((copies_here[index], copies[index]))
        for kind, (source, target) in enumerate(pairs):
            copy = pltpu.make_async_copy(source, target, out_sem.at[kind, index])
            copy.start()
            stores.append(copy)

    factor = jnp.minimum(1.0, clip_limit / (norm[0:1, 0:1] + 1e-06))
    weight_rate = 2.0 * D ** (-0.5)

    def update(index, columns, grad, rate, decay):
        grad = grad * factor
        master, first, second = (ins_here[kind][index][:, columns] for kind in range(3))
        new, second_new = adam_update(master, first, second, grad, rate, decay)
        outs_here[0][index][:, columns] = grad
        outs_here[1][index][:, columns] = new
        outs_here[2][index][:, columns] = second_new
        if index < count - 1:
            copies_here[index][:, columns] = new.astype(jnp.bfloat16)

    def arrived(index):
        for kind in range(3):
            loads[index, kind].wait()

    step = 2 * LANES
    loads[4].wait()
    arrived(6)
    for start in range(0, down_sum.shape[1], step):
        columns = slice(start, start + step)
        update(6, columns, sums_here[4][:, columns], weight_rate, decay_rate)
    store(6)
    members, _, mine = gate_parts.shape
    for index in (4, 5):
        loads[index - 2].wait()
        arrived(index)
        place = 0
        for part in range(mine // span):
            for member in range(members):
                grad = sums_here[index - 2][member, :, part * span : (part + 1) * span]
                columns = slice(place, place + span)
                update(index, columns, grad.astype(jnp.float32), weight_rate, decay_rate)
                place += span
        store(index)
    loads[1].wait()
    arrived(3)
    for start in range(0, out_sum.shape[1], step):
        columns = slice(start, start + step)
        update(3, columns, sums_here[1][:, columns], weight_rate, decay_rate)
    store(3)
    loads[0].wait()
    place = 0
    for index in range(3):
        arrived(index)
        for start in range(0, masters[index].shape[1], step):
            grad = sums_here[0][:, place : place + step]
            update(index, slice(start, start + step), grad, weight_rate, decay_rate)
            place += step
        store(index)
    arrived(7)
    norm_rows = 2 * D // LANES
    head_rows = HQ * HD // LANES
    key_rows = KV * HD // LANES
    folded = []
    for first, size in ((norm_rows, head_rows), (norm_rows + head_rows, key_rows)):
        total = jnp.sum(gain_totals[first : first + size, :], 0, keepdims=True)
        folded.append(total + pltpu.roll(jnp.broadcast_to(total, (8, LANES)), HD, 1)[:1])
    lane = lax.broadcasted_iota(jnp.int32, (1, LANES), 1)
    heads = jnp.where(lane < HD, folded[0], folded[1])
    gain_grad = jnp.concatenate([gain_totals[:norm_rows, :], heads], 0)
    update(7, slice(None), gain_grad, gain_rate, 0.0)
    store(7)
    for copy in term_loads:
        copy.wait()

    def add_rows(index, carry):
        rows = rows_of(index, 32)
        total = terms_here[0][rows, :]
        for term in terms_here[1:4]:
            total = total + term[rows, :].astype(jnp.float32)
        output_here[rows, :] = total.astype(jnp.bfloat16)
        return carry

    copy = pltpu.make_async_copy(terms_here[4], rows_out, term_sem.at[4])
    copy.start()
    stores.append(copy)
    lax.fori_loop(0, rows_count // 32, add_rows, 0)
    copy = pltpu.make_async_copy(output_here, output, term_sem.at[0])
    copy.start()
    stores.append(copy)
    for copy in stores:
        copy.wait()


def adam(span, norm, gain_totals, sums, row_terms, masters, firsts, seconds):
    lo, hi = jnp.bfloat16, jnp.float32
    dma = pltpu.SemaphoreType.DMA
    shapes = [(array.shape, hi) for _ in range(3) for array in masters]
    shapes += [(array.shape, lo) for array in masters[:-1]]
    rows_shape = row_terms[0].shape
    inputs = [(array.shape, hi) for _ in range(3) for array in masters]
    scratch = inputs + shapes + [(array.shape, array.dtype) for array in sums]
    scratch += [(rows_shape, array.dtype) for array in row_terms] + [(rows_shape, lo)]
    shapes += [(rows_shape, lo), (rows_shape, lo), ((1, 1), hi)]
    return pl.pallas_call(
        functools.partial(adam_kernel, span),
        name="adam",
        out_shape=tuple(jax.ShapeDtypeStruct(*item) for item in shapes),
        in_specs=[ON_CHIP] * 2 + [ANYWHERE] * (10 + len(inputs)),
        out_specs=(ANYWHERE,) * (len(shapes) - 1) + (ON_CHIP,),
        scratch_shapes=[pltpu.VMEM(*item) for item in scratch]
        + [dma((5,)), dma((3, len(masters))), dma((4, len(masters))), dma((5,))],
        compiler_params=pltpu.CompilerParams(vmem_limit_bytes=VMEM_MOST),
    )(norm, gain_totals, *sums, *row_terms, *masters, *firsts, *seconds)


def after(value, *others):
    return lax.optimization_barrier((value,) + others)[0]


def low(value):
    return value.astype(jnp.bfloat16)


def shards(
    nd,
    nf,
    tokens,
    cotangent,
    segment_ids,
    w_query,
    w_key,
    w_value,
    w_out,
    w_gate,
    w_up,
    w_down,
    m_query,
    m_key,
    m_value,
    m_out,
    m_gate,
    m_up,
    m_down,
    v_query,
    v_key,
    v_value,
    v_out,
    v_gate,
    v_up,
    v_down,
    gains,
    gain_first,
    gain_second,
):
    masters = (w_query, w_key, w_value, w_out, w_gate, w_up, w_down)
    firsts = (m_query, m_key, m_value, m_out, m_gate, m_up, m_down)
    seconds = (v_query, v_key, v_value, v_out, v_gate, v_up, v_down)
    outer = nd // MEMBERS
    dp = lax.axis_index("dp")
    ring_z = Ring(nf, lax.axis_index("fsdp"), lambda d, f, s: (d, (f + s) % nf), nd, nf)
    ring_y = Ring(
        outer,
        dp // MEMBERS,
        lambda d, f, s: ((d // MEMBERS + s) % outer * MEMBERS + d % MEMBERS, f),
        nd,
        nf,
    )
    ring_x = Ring(2, dp // 2 % 2, lambda d, f, s: (d ^ 2, f), nd, nf)
    ring_core = Ring(2, dp % 2, lambda d, f, s: (d ^ 1, f), nd, nf)
    member = dp % MEMBERS

    def trade(block, mask):
        return Ring(2, dp % 2, lambda d, f, s: (d ^ mask, f), nd, nf).move(block, 1)

    def swap(blocks):
        full = put(jnp.zeros_like(blocks), pick(blocks, 0, member), 0, member)
        for mask in range(1, MEMBERS):
            full = put(full, trade(pick(blocks, 0, member ^ mask), mask), 0, member ^ mask)
        return full

    def spread(rows):
        far = ring_x.move(rows, 1)
        near = jnp.concatenate([rows, ring_core.move(rows, 1)], 0)
        return near, jnp.concatenate([far, ring_core.move(far, 1)], 0)

    def collapse(near, far):
        rows = near.shape[0] // 2
        got = ring_core.move(far[rows:], 1).astype(jnp.float32)
        got = ring_x.move(low(far[:rows].astype(jnp.float32) + got), 1)
        total = near[:rows].astype(jnp.float32)
        total = total + ring_core.move(near[rows:], 1).astype(jnp.float32)
        return total + got.astype(jnp.float32)

    batch, length, width = tokens.shape
    count = batch * length
    hidden_rows = w_down.shape[0]
    span = nf * hidden_rows
    mine = outer * span
    in_rows = w_query.shape[0]
    out_rows = w_out.shape[0]
    attn_cols = (HQ + 2 * KV) * HD

    in_w, out_w, gate_w, upper_w = gather_weights(nd, nf, masters[:6])
    in_w = in_w.reshape(D, attn_cols)
    out_w = out_w.reshape(HQ * HD, D)

    tiled = [array.reshape(-1, LANES) for array in (gains, gain_first, gain_second)]
    small = (tiled[0], *rotary_tables(length), segment_ids)
    back_in = cotangent.reshape(count, width)
    token_rows = tokens.reshape(count, width)
    (
        upper_w,
        down_w,
        back_all,
        ffn_all,
        gate_near,
        upper_near,
        hidden_near,
        gate_far,
        upper_far,
        hidden_far,
        down_terms,
        raw,
        heads,
        values,
        mixed,
        hidden_in,
    ) = attend(
        nd, nf, length, small, token_rows, w_down, in_w, out_w, back_in, upper_w, gate_w
    )
    gate_w = gate_w.reshape(D, mine)
    upper_w = upper_w.reshape(D, mine)
    down_w = down_w.reshape(mine, D)
    def inner_grads(back_half, gate, upper):
        grad_hidden = back_product(back_half, down_w)
        _, pull = jax.vjp(swiglu, gate, upper)
        grad_gate, grad_upper = pull(grad_hidden)
        grad_gate, grad_upper = low(grad_gate), low(grad_upper)
        back = back_product(grad_gate, gate_w) + back_product(grad_upper, upper_w)
        return grad_gate, grad_upper, low(back)

    down_terms = down_terms.reshape(outer, nf, hidden_rows, width)
    down_sent = [pick(down_terms, 0, ring_y.dest(hop)) for hop in range(1, outer)]
    down_got = jnp.stack([ring_y.move(part, hop + 1) for hop, part in enumerate(down_sent)])
    half = 2 * count
    far_gate, far_upper, far_ffn = inner_grads(back_all[half:], gate_far, upper_far)
    far = far_ffn[:count].astype(jnp.float32) + ring_core.move(far_ffn[count:], 1)
    far = low(far)
    ffn_x = ring_x.move(far, 1)
    near_gate, near_upper, near_ffn = inner_grads(
        after(back_all[:half], far), gate_near, upper_near
    )
    ffn_core = ring_core.move(near_ffn[count:], 1)
    ffn_all = after(ffn_all, near_ffn)
    gate_terms = low(weight_product(ffn_all, jnp.concatenate([near_gate, far_gate], 0)))
    upper_terms = low(weight_product(ffn_all, jnp.concatenate([near_upper, far_upper], 0)))
    inner_shape = (outer, MEMBERS, nf, in_rows, mine)
    (
        out_mine,
        out_core,
        out_x,
        gate_parts,
        upper_parts,
        input_grad,
        in_sum,
        out_sum,
        down_sum,
        gain_totals,
        norm,
    ) = backward(
        nd,
        nf,
        length,
        small,
        (hidden_near, hidden_far),
        (
            down_got,
            down_terms,
            gate_terms.reshape(inner_shape),
            upper_terms.reshape(inner_shape),
        ),
        (
            token_rows,
            near_ffn[:count],
            ffn_core,
            ffn_x,
            hidden_in,
            back_in,
            out_w,
            mixed,
            heads,
            values,
            raw,
            in_w,
            down_w,
        ),
    )
    results = adam(
        span,
        norm,
        gain_totals,
        (in_sum, out_sum, gate_parts, upper_parts, down_sum),
        (hidden_in, out_mine, out_core, out_x, input_grad),
        masters + (tiled[0],),
        firsts + (tiled[1],),
        seconds + (tiled[2],),
    )
    clipped, new_masters, new_seconds = results[:7], results[8:15], results[16:23]
    gain_clipped, new_gains, gain_seconds = (results[k].reshape(-1) for k in (7, 15, 23))
    copies, output, input_grad = tuple(results[24:31]), results[31], results[32]
    total_norm = results[33].reshape(())
    return (
        (output.reshape(tokens.shape), input_grad.reshape(tokens.shape))
        + clipped
        + (gain_clipped, total_norm)
        + new_masters
        + (new_gains,)
        + copies
        + new_seconds
        + (gain_seconds,)
    )


def solution(mesh):
    rows3 = P(AXES, None, None)
    rows2 = P(AXES, None)
    whole = P()
    return jax.shard_map(
        functools.partial(shards, mesh.shape["dp"], mesh.shape["fsdp"]),
        mesh=mesh,
        in_specs=(rows3, rows3) + (rows2,) * 22 + (whole,) * 3,
        out_specs=(rows3, rows3)
        + (rows2,) * 7
        + (whole, whole)
        + (rows2,) * 7
        + (whole,)
        + (rows2,) * 14
        + (whole,),
        check_vma=False,
    )
```

```python
import functools
import math

import jax
import jax.numpy as jnp
import numpy as np
from jax import lax
from jax.experimental import pallas as pl
from jax.experimental.pallas import tpu as pltpu
from jax.sharding import PartitionSpec as P

D = 1280
HQ = 16
KV = 4
HD = 64
STEP = 10
MEMBERS = 4

norm_eps = 1e-05
rope_base = 10000.0
beta_one = 0.9
beta_two = 0.95
adam_eps = 1e-08
decay_rate = 0.1
clip_limit = 1.0
gain_rate = 0.4
masked_score = -1e30

AXES = ("dp", "fsdp")
LANES = 128
MESH = pl.DeviceIdType.MESH
ANYWHERE = pl.BlockSpec(memory_space=pl.ANY)
ON_CHIP = pl.BlockSpec(memory_space=pltpu.VMEM)
VMEM_MOST = 58 * 2**20


def rms_scale(values, gain):
    return values * lax.rsqrt(jnp.mean(values * values, -1, keepdims=True) + norm_eps) * gain


def rotary_tables(length):
    half = HD // 2
    frequency = rope_base ** (-np.arange(half, dtype=np.float64) * 2.0 / HD)
    angles = np.arange(length, dtype=np.float64)[:, None] * frequency[None, :]
    cosine, sine = np.cos(angles), np.sin(angles)
    cosine = np.tile(cosine, (1, LANES // half))
    sine = np.tile(np.concatenate([-sine, sine], 1), (1, LANES // HD))
    return jnp.asarray(cosine, jnp.float32), jnp.asarray(sine, jnp.float32)


def swiglu(gate, upper):
    return jax.nn.silu(gate) * upper


def forward_product(left, right):
    return jnp.dot(left, right, preferred_element_type=jnp.float32)


def weight_product(left, right):
    return lax.dot_general(
        left, right, (((0,), (0,)), ((), ())), preferred_element_type=jnp.float32
    )


def back_product(left, right):
    return lax.dot_general(
        left, right, (((1,), (1,)), ((), ())), preferred_element_type=jnp.float32
    )


def adam_update(master, first, second, grad, rate, decay):
    first_new = beta_one * first + (1.0 - beta_one) * grad
    second_new = beta_two * second + (1.0 - beta_two) * grad * grad
    first_hat = first_new / (1.0 - beta_one**STEP)
    second_hat = second_new / (1.0 - beta_two**STEP)
    master_new = master - rate * (first_hat / (jnp.sqrt(second_hat) + adam_eps) + decay * master)
    return (master_new, second_new)


def put(buffer, block, axis, index):
    return lax.dynamic_update_index_in_dim(buffer, block, index, axis)


def pick(array, axis, index):
    return lax.dynamic_index_in_dim(array, index, axis, keepdims=False)


class Ring:
    def __init__(self, extent, place, target, nd, nf):
        self.extent = extent
        self.place = place
        self.target = target
        self.nd = nd
        self.nf = nf

    def move(self, block, step):
        pairs = []
        for d in range(self.nd):
            for f in range(self.nf):
                d2, f2 = self.target(d, f, step)
                pairs.append((d * self.nf + f, d2 * self.nf + f2))
        return lax.ppermute(block, AXES, pairs)

    def source(self, step):
        return lax.rem(self.place - step + self.extent, self.extent)

    def dest(self, step):
        return lax.rem(self.place + step, self.extent)

    def gather(self, block, axis):
        shape = block.shape[:axis] + (self.extent,) + block.shape[axis:]
        full = put(jnp.zeros(shape, block.dtype), block, axis, self.place)
        for step in range(1, self.extent):
            full = put(full, self.move(block, step), axis, self.source(step))
        return full

    def reduce(self, terms, axis):
        total = pick(terms, axis, self.place).astype(jnp.float32)
        for step in range(1, self.extent):
            got = self.move(pick(terms, axis, self.dest(step)), step)
            total = total + got.astype(jnp.float32)
        return total


def start_all(copies):
    for copy in copies:
        copy.start()
    return copies


def weights_kernel(
    nd,
    nf,
    query_full,
    key_full,
    value_full,
    out_full,
    gate_full,
    up_full,
    in_w,
    out_w,
    gate_w,
    upper_w,
    w_query,
    w_key,
    w_value,
    w_out,
    w_gate,
    w_up,
    in_ref,
    out_ref,
    inner_ref,
    z_send,
    z_recv,
    y_send,
    y_recv,
    x_send,
    x_recv,
    hop_send,
    hop_recv,
    core_send,
    core_recv,
    swap_send,
    swap_recv,
    gate_send,
    gate_recv,
    over_send,
    over_recv,
    up_send,
    up_recv,
    local_sem,
    load_sem,
):
    outer = nd // MEMBERS
    dp = lax.axis_index("dp")
    z = lax.axis_index("fsdp")
    y = dp // MEMBERS
    member = dp % MEMBERS
    x = member // 2
    c = member % 2

    def z_peer(step):
        return (dp, lax.rem(z + step, nf))

    def y_peer(step):
        return (lax.rem(y + step, outer) * MEMBERS + member, z)

    def in_group(k):
        return (y * MEMBERS + k, z)

    def from_z(step):
        return lax.rem(z - step + nf, nf)

    def from_y(step):
        return lax.rem(y - step + outer, outer)

    x_peer = in_group((1 - x) * 2 + c)
    core_peer = in_group(x * 2 + 1 - c)
    barrier = pltpu.get_barrier_semaphore()
    peers = [z_peer(step) for step in range(1, nf)] + [y_peer(step) for step in range(1, outer)]
    peers += [x_peer, core_peer, in_group(MEMBERS - 1 - member)]
    for peer in peers:
        pl.semaphore_signal(barrier, inc=1, device_id=peer, device_id_type=MESH)
    fulls = (query_full, key_full, value_full, out_full, gate_full, up_full)
    loads = [
        pltpu.make_async_copy(full, here, load_sem.at[index])
        for index, (full, here) in enumerate(
            zip(fulls, (w_query, w_key, w_value, w_out, w_gate, w_up))
        )
    ]
    start_all(loads)
    column = 0
    for index, weight in enumerate((w_query, w_key, w_value)):
        loads[index].wait()
        in_ref[:, column : column + weight.shape[1]] = weight[...].astype(jnp.bfloat16)
        column += weight.shape[1]
    pl.semaphore_wait(barrier, len(peers))

    def remote(source, target, send, recv, device):
        return pltpu.make_async_remote_copy(
            src_ref=source,
            dst_ref=target,
            send_sem=send,
            recv_sem=recv,
            device_id=device,
            device_id_type=MESH,
        )

    shards_here = (in_ref, out_ref)
    wholes = (in_w, out_w)
    sent = []

    def send(copy):
        copy.start()
        sent.append(copy)
        return copy

    local = []
    z_copies = {}

    def start_shard(a):
        kept = pltpu.make_async_copy(shards_here[a], wholes[a].at[y, x, c, z], local_sem.at[a])
        kept.start()
        local.append(kept)
        for step in range(1, nf):
            z_copies[a, step] = send(
                remote(
                    shards_here[a],
                    wholes[a].at[y, x, c, z],
                    z_send.at[a, step],
                    z_recv.at[a, step],
                    z_peer(step),
                )
            )

    def block(a, step, oy=None, ox=None):
        return wholes[a].at[y if oy is None else oy, x if ox is None else ox, c, from_z(step)]

    y_copies = {}
    x_copies = {}

    def to_plane(a, step):
        source = shards_here[a] if step == 0 else block(a, step)
        for hop in range(1, outer):
            y_copies[a, hop, step] = send(
                remote(
                    source,
                    block(a, step),
                    y_send.at[a, hop, step],
                    y_recv.at[a, hop, step],
                    y_peer(hop),
                )
            )
        x_copies[a, step] = send(
            remote(source, block(a, step), x_send.at[a, step], x_recv.at[a, step], x_peer)
        )

    start_shard(0)
    to_plane(0, 0)
    loads[3].wait()
    out_ref[...] = w_out[...].astype(jnp.bfloat16)
    start_shard(1)
    to_plane(1, 0)
    span = inner_ref.shape[3] // outer
    for half, weight in enumerate((w_gate, w_up)):
        loads[4 + half].wait()
        for k in range(MEMBERS):
            for part in range(outer):
                column = (part * MEMBERS + k) * span
                inner_ref[half, k, :, part * span : (part + 1) * span] = weight[
                    :, column : column + span
                ].astype(jnp.bfloat16)
    masks = (2, 1, 3)
    trades = {}
    for half, target in ((0, gate_w.at[y, :, z]), (1, upper_w.at[y, :, z])):
        for mask in masks:
            other = member ^ mask
            trades[half, mask] = send(
                remote(
                    inner_ref.at[half, other],
                    target.at[member],
                    swap_send.at[half, mask],
                    swap_recv.at[half, mask],
                    in_group(other),
                )
            )
        kept = pltpu.make_async_copy(
            inner_ref.at[half, member], target.at[member], local_sem.at[2 + half]
        )
        kept.start()
        local.append(kept)

    for a in range(2):
        for step in range(1, nf):
            z_copies[a, step].wait_recv()
            to_plane(a, step)
    for mask in masks:
        trades[0, mask].wait_recv()
    local[2].wait()
    gates = {}
    gate_own = gate_w.at[y, :, z]

    def gate_to_y(step):
        piece = gate_w.at[y, :, from_z(step)]
        for hop in range(1, outer):
            gates[hop, step] = send(
                remote(
                    piece, piece, over_send.at[hop, step], over_recv.at[hop, step], y_peer(hop)
                )
            )

    for step in range(1, nf):
        gates[0, step] = send(
            remote(gate_own, gate_own, gate_send.at[step], gate_recv.at[step], z_peer(step))
        )
    gate_to_y(0)
    for mask in masks:
        trades[1, mask].wait_recv()
    local[3].wait()
    upper_own = upper_w.at[y, :, z]
    uppers = [
        send(remote(upper_own, upper_own, up_send.at[step], up_recv.at[step], z_peer(step)))
        for step in early_steps(nf)
    ]
    hops = {}
    for a in range(2):
        for step in range(nf):
            for hop in range(1, outer):
                y_copies[a, hop, step].wait_recv()
                hops[a, hop, step] = send(
                    remote(
                        block(a, step, oy=from_y(hop)),
                        block(a, step, oy=from_y(hop)),
                        hop_send.at[a, hop, step],
                        hop_recv.at[a, hop, step],
                        x_peer,
                    )
                )
    for step in range(1, nf):
        gates[0, step].wait_recv()
        gate_to_y(step)
    cores = {}

    def to_core(a, hop, far):
        place = wholes[a].at[y if hop == 0 else from_y(hop), 1 - x if far else x, c]
        cores[a, hop, far] = send(
            remote(
                place,
                place,
                core_send.at[a, hop, far],
                core_recv.at[a, hop, far],
                core_peer,
            )
        )

    local[0].wait()
    local[1].wait()
    for a in range(2):
        for hop in range(outer):
            to_core(a, hop, 0)
    for a in range(2):
        for step in range(nf):
            x_copies[a, step].wait_recv()
        to_core(a, 0, 1)
    for a in range(2):
        for hop in range(1, outer):
            for step in range(nf):
                hops[a, hop, step].wait_recv()
            to_core(a, hop, 1)
    for copy in uppers:
        copy.wait_recv()
    for hop in range(1, outer):
        for step in range(nf):
            gates[hop, step].wait_recv()
    for key in cores:
        cores[key].wait_recv()
    for copy in sent:
        copy.wait_send()


def early_steps(nf):
    return sorted({1, nf - 1})


def gather_weights(nd, nf, shards_here):
    outer = nd // MEMBERS
    dma = pltpu.SemaphoreType.DMA
    lead = (outer, 2, 2, nf)
    low_type = jnp.bfloat16
    w_query, w_key, w_value, w_out, w_gate, w_up = shards_here
    in_shape = (w_query.shape[0], w_query.shape[1] + w_key.shape[1] + w_value.shape[1])
    inner = (w_gate.shape[0], w_gate.shape[1] // MEMBERS)
    pairs = [(2, nf), (2, outer, nf), (2, nf), (2, outer, nf), (2, outer, 2), (2, MEMBERS)]
    pairs += [(nf,), (outer, nf), (nf,)]
    return pl.pallas_call(
        functools.partial(weights_kernel, nd, nf),
        name="gather_weights",
        out_shape=(
            jax.ShapeDtypeStruct(lead + in_shape, low_type),
            jax.ShapeDtypeStruct(lead + w_out.shape, low_type),
            jax.ShapeDtypeStruct((outer, MEMBERS, nf) + inner, low_type),
            jax.ShapeDtypeStruct((outer, MEMBERS, nf) + inner, low_type),
        ),
        in_specs=[ANYWHERE] * 6,
        out_specs=(ANYWHERE,) * 4,
        scratch_shapes=[pltpu.VMEM(weight.shape, weight.dtype) for weight in shards_here]
        + [
            pltpu.VMEM(in_shape, low_type),
            pltpu.VMEM(w_out.shape, low_type),
            pltpu.VMEM((2, MEMBERS) + inner, low_type),
        ]
        + [dma(shape) for shape in pairs for _ in range(2)]
        + [dma((4,)), dma((6,))],
        compiler_params=pltpu.CompilerParams(
            collective_id=0, has_side_effects=True, vmem_limit_bytes=VMEM_MOST
        ),
    )(*shards_here)


def block_mean():
    row = lax.broadcasted_iota(jnp.int32, (LANES, LANES), 0) // HD
    column = lax.broadcasted_iota(jnp.int32, (LANES, LANES), 1) // HD
    return jnp.where(row == column, 1.0 / HD, 0.0).astype(jnp.bfloat16)


def head_mean(values, averages):
    high = values.astype(jnp.bfloat16)
    rest = (values - high.astype(jnp.float32)).astype(jnp.bfloat16)
    total = jnp.dot(high, averages, preferred_element_type=jnp.float32)
    return total + jnp.dot(rest, averages, preferred_element_type=jnp.float32)


def swap_halves(values):
    lane = lax.broadcasted_iota(jnp.int32, values.shape, 1) // (HD // 2)
    ahead = pltpu.roll(values, LANES - HD // 2, 1)
    behind = pltpu.roll(values, HD // 2, 1)
    return jnp.where(lane % 2 == 0, ahead, behind)


def in_half(values, source, target):
    lane = lax.broadcasted_iota(jnp.int32, values.shape, 1) // HD
    wide = values.astype(jnp.float32)
    if source != target:
        wide = pltpu.roll(wide, HD, 1)
    return jnp.where(lane == target, wide, 0.0).astype(values.dtype)


def split_gains(gains):
    rows = (gains.shape[0] - 1) // 2

    def joined(first):
        return jnp.concatenate([gains[first + row : first + row + 1, :] for row in range(rows)], 1)

    heads = gains[2 * rows : 2 * rows + 1, :]
    other = pltpu.roll(jnp.broadcast_to(heads, (8, LANES)), HD, 1)[:1]
    first = lax.broadcasted_iota(jnp.int32, heads.shape, 1) < HD
    query, key = jnp.where(first, heads, other), jnp.where(first, other, heads)

    def of_tile(index):
        return jnp.where(index < HQ * HD // LANES, query, key)

    return joined(0), joined(rows), of_tile


def may_attend(ids, row):
    length = ids.shape[1]
    across = ids[row : row + 1, :].astype(jnp.float32)
    place = lax.broadcasted_iota(jnp.int32, (length, length), 0)
    other = lax.broadcasted_iota(jnp.int32, (length, length), 1)
    down = jnp.sum(jnp.where(place == other, across, 0.0), 1, keepdims=True)
    return (other <= place) & (down == across)


def tile_of(index, width=LANES):
    return pl.ds(pl.multiple_of(index * width, LANES), width)


def rows_of(index, size):
    return pl.ds(pl.multiple_of(index * size, 16), size)


def dot_last(left, right):
    return lax.dot_general(
        left, right, (((1,), (1,)), ((), ())), preferred_element_type=jnp.float32
    )


def probabilities(query, key, keep):
    scores = dot_last(query, key) * HD**-0.5
    scores = jnp.where(keep, scores, masked_score)
    weights = jnp.exp(scores - jnp.max(scores, -1, keepdims=True))
    return weights / jnp.sum(weights, -1, keepdims=True)


def outer_product(left, right, target):
    pair, wide = 2 * LANES, 4 * LANES

    def step_once(index, carry):
        columns = tile_of(index, pair)
        turned = left[:, columns].T
        for start in range(0, right.shape[1], wide):
            across = pl.ds(start, min(wide, right.shape[1] - start))
            target[columns, across] = jnp.dot(
                turned, right[:, across], preferred_element_type=jnp.float32
            ).astype(jnp.bfloat16)
        return carry

    lax.fori_loop(0, left.shape[1] // pair, step_once, 0)


def flatten_blocks(blocks, rows, target):
    outer, members, nf, size, _ = blocks.shape

    def step_once(index, carry):
        for place in range(nf):
            rows[place * size : (place + 1) * size, :] = blocks[
                index // members, lax.rem(index, members), place
            ].astype(jnp.float32)
        target[rows_of(index, nf * size), :] = rows[...].astype(jnp.bfloat16)
        return carry

    lax.fori_loop(0, outer * members, step_once, 0)


def attend_kernel(
    nd,
    nf,
    length,
    gains,
    cosine,
    sine,
    segments,
    tokens_full,
    down_full,
    in_full,
    out_full,
    cot_full,
    upper_in,
    gate_w,
    upper_w,
    down_w,
    back_near,
    back_far,
    ffn_all,
    gate_near,
    upper_near,
    hidden_near,
    gate_far,
    upper_far,
    hidden_far,
    down_terms,
    raw,
    heads,
    values,
    mixed,
    hidden_in,
    normed,
    ffn_here,
    tokens,
    w_down,
    in_w,
    out_w,
    down_x,
    cot,
    gate_blocks,
    upper_blocks,
    block_rows,
    gate_flat,
    upper_flat,
    gate_here,
    upper_here,
    hidden_here,
    uz_send,
    uz_recv,
    uy_send,
    uy_recv,
    dz_send,
    dz_recv,
    dy_send,
    dy_recv,
    row_send,
    row_recv,
    local_sem,
):
    outer = nd // MEMBERS
    dp = lax.axis_index("dp")
    z = lax.axis_index("fsdp")
    y = dp // MEMBERS
    member = dp % MEMBERS
    x = member // 2
    c = member % 2

    def z_peer(step):
        return (dp, lax.rem(z + step, nf))

    def y_peer(step):
        return (lax.rem(y + step, outer) * MEMBERS + member, z)

    def from_z(step):
        return lax.rem(z - step + nf, nf)

    x_peer = (y * MEMBERS + (1 - x) * 2 + c, z)
    core_peer = (y * MEMBERS + x * 2 + 1 - c, z)
    barrier = pltpu.get_barrier_semaphore()
    peers = [z_peer(step) for step in range(1, nf)] + [y_peer(step) for step in range(1, outer)]
    peers += [x_peer, core_peer]
    for peer in peers:
        pl.semaphore_signal(barrier, inc=1, device_id=peer, device_id_type=MESH)
    gain_attn, gain_ffn, gain_heads = split_gains(gains)
    count = tokens.shape[0]
    width = tokens.shape[1]

    def member_rows(slot):
        return pl.ds(slot * count, count)

    weights_here = []
    operands = (
        (down_full, w_down),
        (cot_full, cot.at[member_rows(0)]),
        (tokens_full, tokens),
        (in_full, in_w),
        (out_full, out_w),
        (gate_w, gate_blocks),
    )
    for index, (source, target) in enumerate(operands):
        copy = pltpu.make_async_copy(source, target, local_sem.at[4 + index])
        copy.start()
        weights_here.append(copy)
    pl.semaphore_wait(barrier, len(peers))
    sent = []

    def remote(source, target, send, recv, device):
        copy = pltpu.make_async_remote_copy(
            src_ref=source,
            dst_ref=target,
            send_sem=send,
            recv_sem=recv,
            device_id=device,
            device_id_type=MESH,
        )
        copy.start()
        sent.append(copy)
        return copy

    def keep(index, source, target):
        copy = pltpu.make_async_copy(source, target, local_sem.at[index])
        copy.start()
        return copy

    arrivals = []
    upper_own = upper_w.at[y, :, z]
    down_own = down_w.at[y, z]
    steps_left = [step for step in range(1, nf) if step not in early_steps(nf)]
    upper_z = {
        step: remote(upper_own, upper_own, uz_send.at[step], uz_recv.at[step], z_peer(step))
        for step in steps_left
    }

    def upper_to_y(step):
        if step in upper_z:
            upper_z[step].wait_recv()
        piece = upper_w.at[y, :, from_z(step)]
        for hop in range(1, outer):
            arrivals.append(
                remote(piece, piece, uy_send.at[hop, step], uy_recv.at[hop, step], y_peer(hop))
            )

    for step in [0] + early_steps(nf):
        upper_to_y(step)
    for _ in range(2):
        weights_here.pop(0).wait()
    down_x[...] = w_down[...].astype(jnp.bfloat16)
    down_z = [
        remote(down_x, down_own, dz_send.at[step], dz_recv.at[step], z_peer(step))
        for step in range(1, nf)
    ]
    kept = [keep(1, down_x, down_own)]
    cot_own = cot.at[member_rows(0)]
    cot_near = remote(
        cot_own, cot.at[member_rows(1)], row_send.at[0, 0], row_recv.at[0, 0], core_peer
    )
    cot_far = remote(
        cot_own, cot.at[member_rows(2)], row_send.at[0, 1], row_recv.at[0, 1], x_peer
    )

    def down_to_y(step):
        if step:
            down_z[step - 1].wait_recv()
        piece = down_w.at[y, from_z(step)] if step else down_x
        for hop in range(1, outer):
            arrivals.append(
                remote(
                    piece,
                    down_w.at[y, from_z(step)],
                    dy_send.at[hop, step],
                    dy_recv.at[hop, step],
                    y_peer(hop),
                )
            )

    chunk = 32

    weights_here.pop(0).wait()

    def norm_rows(index, carry):
        rows = rows_of(index, chunk)
        part = tokens[rows, :].astype(jnp.float32)
        scale = lax.rsqrt(jnp.mean(part * part, -1, keepdims=True) + norm_eps)
        normed[rows, :] = (part * scale * gain_attn).astype(jnp.bfloat16)
        return carry

    lax.fori_loop(0, count // chunk, norm_rows, 0)
    head_tiles = (HQ + KV) * HD // LANES
    for _ in range(2):
        weights_here.pop(0).wait()

    def project(index, carry):
        columns = tile_of(index, 2 * LANES)
        raw[:, columns] = jnp.dot(
            normed[...], in_w[:, columns], preferred_element_type=jnp.float32
        )
        return carry

    lax.fori_loop(0, head_tiles // 2, project, 0)
    values[...] = jnp.dot(
        normed[...], in_w[:, pl.ds(head_tiles * LANES, KV * HD)], preferred_element_type=jnp.float32
    ).astype(jnp.bfloat16)
    averages = block_mean()

    def turn(index, carry):
        columns = tile_of(index)
        for row in range(count // length):
            rows = pl.ds(row * length, length)
            part = raw[rows, columns]
            scale = lax.rsqrt(head_mean(part * part, averages) + norm_eps)
            part = part * scale * gain_heads(index)
            part = part * cosine[...] + swap_halves(part) * sine[...]
            heads[rows, columns] = part.astype(jnp.bfloat16)
        return carry

    lax.fori_loop(0, head_tiles, turn, 0)

    def attend(row):
        rows = pl.ds(row * length, length)
        allowed = may_attend(segments, row)

        def pair(tile, carry):
            key_tile = heads[rows, tile_of(HQ * HD // LANES + tile)]
            value_tile = values[rows, tile_of(tile)]
            for own in range(2):
                key = [in_half(key_tile, own, half) for half in range(2)]
                value = [in_half(value_tile, own, half) for half in range(2)]
                for quarter in range(2):
                    columns = tile_of(tile * 4 + own * 2 + quarter)
                    query = heads[rows, columns]
                    total = None
                    for half in range(2):
                        weights = probabilities(query, key[half], allowed).astype(jnp.bfloat16)
                        term = jnp.dot(weights, value[half], preferred_element_type=jnp.float32)
                        total = term if total is None else total + term
                    mixed[rows, columns] = total.astype(jnp.bfloat16)
            return carry

        lax.fori_loop(0, KV * HD // LANES, pair, 0)

    down_steps = list(range(nf))
    ffn_far, ffn_near = [], []

    def finish(row):
        rows = pl.ds(row * length, length)

        def project_out(index, carry):
            columns = tile_of(index, 2 * LANES)
            hidden_in[rows, columns] = tokens[rows, columns].astype(jnp.float32) + jnp.dot(
                mixed[rows, :], out_w[:, columns], preferred_element_type=jnp.float32
            )
            return carry

        lax.fori_loop(0, width // (2 * LANES), project_out, 0)

        def norm_hidden(index, carry):
            part_rows = pl.ds(pl.multiple_of(row * length + index * chunk, 16), chunk)
            part = hidden_in[part_rows, :]
            scale = lax.rsqrt(jnp.mean(part * part, -1, keepdims=True) + norm_eps)
            ffn_here[part_rows, :] = (part * scale * gain_ffn).astype(jnp.bfloat16)
            return carry

        lax.fori_loop(0, length // chunk, norm_hidden, 0)
        for slot, peer, copies in ((2, x_peer, ffn_far), (1, core_peer, ffn_near)):
            copies.append(
                remote(
                    ffn_here.at[rows],
                    ffn_here.at[pl.ds(slot * count + row * length, length)],
                    row_send.at[slot, row],
                    row_recv.at[slot, row],
                    peer,
                )
            )

    batch = count // length
    for row in range(batch):
        attend(row)
        finish(row)
        if row == 0:
            for step in steps_left:
                upper_to_y(step)
            uppers = list(arrivals)
            arrivals.clear()
            down_to_y(down_steps.pop(0))

    cot_far.wait_recv()
    cot_cross = remote(
        cot.at[member_rows(2)],
        cot.at[member_rows(3)],
        row_send.at[0, 2],
        row_recv.at[0, 2],
        core_peer,
    )
    down_to_y(down_steps.pop(0))
    weights_here.pop(0).wait()
    flatten_blocks(gate_blocks, block_rows, gate_flat)
    for copy in uppers:
        copy.wait_recv()
    kept.pop(0).wait()
    upper_load = keep(0, upper_w, upper_blocks)
    while len(down_steps) > 1:
        down_to_y(down_steps.pop(0))
    upper_load.wait()
    flatten_blocks(upper_blocks, block_rows, upper_flat)

    def ffn_rows(slot):
        rows = member_rows(slot)

        def tile_once(index, carry):
            columns = tile_of(index, 2 * LANES)
            gate = jnp.dot(
                ffn_here[rows, :], gate_flat[:, columns], preferred_element_type=jnp.float32
            )
            upper = jnp.dot(
                ffn_here[rows, :], upper_flat[:, columns], preferred_element_type=jnp.float32
            )
            gate_here[rows, columns] = gate
            upper_here[rows, columns] = upper
            hidden_here[rows, columns] = (gate / (1.0 + jnp.exp(-gate)) * upper).astype(
                jnp.bfloat16
            )
            return carry

        lax.fori_loop(0, gate_flat.shape[1] // (2 * LANES), tile_once, 0)

    ffn_rows(0)
    for copy in ffn_near:
        copy.wait_recv()
    ffn_rows(1)
    crosses = []
    for row in range(batch):
        ffn_far[row].wait_recv()
        crosses.append(
            remote(
                ffn_here.at[pl.ds(2 * count + row * length, length)],
                ffn_here.at[pl.ds(3 * count + row * length, length)],
                row_send.at[3, row],
                row_recv.at[3, row],
                core_peer,
            )
        )
    down_to_y(nf - 1)
    ffn_rows(2)
    for copy in crosses:
        copy.wait_recv()
    kept.append(keep(2, ffn_here, ffn_all))
    ffn_rows(3)
    halves = (
        (gate_near, upper_near, hidden_near),
        (gate_far, upper_far, hidden_far),
    )
    for far, targets in enumerate(halves):
        rows = pl.ds(far * 2 * count, 2 * count)
        for index, source in enumerate((gate_here, upper_here, hidden_here)):
            kept.append(keep(9 + 3 * far + index, source.at[rows], targets[index]))
    cot_near.wait_recv()
    cot_cross.wait_recv()
    for far, target in enumerate((back_near, back_far)):
        rows = pl.ds(far * 2 * count, 2 * count)
        kept.append(keep(15 if far else 3, cot.at[rows], target))
    outer_product(hidden_here, cot, down_terms)
    for copy in arrivals:
        copy.wait_recv()
    for copy in sent:
        copy.wait_send()
    for copy in kept:
        copy.wait()


def attend(nd, nf, length, small, tokens, w_down, in_w, out_w, cot, upper_w, gate_w):
    outer = nd // MEMBERS
    count, width = tokens.shape
    nf_rows, mine = gate_w.shape[2] * gate_w.shape[3], gate_w.shape[4]
    lo, hi = jnp.bfloat16, jnp.float32
    dma = pltpu.SemaphoreType.DMA
    moves = [(nf,), (outer, nf), (nf,), (outer, nf), (4, max(3, count // length))]
    shapes = [
        (upper_w.shape, lo),
        ((outer, nf) + w_down.shape, lo),
        ((2 * count, width), lo),
        ((2 * count, width), lo),
        ((MEMBERS * count, width), lo),
        *[((2 * count, mine), kind) for kind in (hi, hi, lo)] * 2,
        ((mine, width), lo),
        ((count, (HQ + KV) * HD), hi),
        ((count, (HQ + KV) * HD), lo),
        ((count, KV * HD), lo),
        ((count, HQ * HD), lo),
        ((count, width), hi),
    ]
    early = [(count, width), (MEMBERS * count, width), (count, width)]
    late = [in_w.shape, out_w.shape, w_down.shape, (MEMBERS * count, width)]
    late += [gate_w.shape, gate_w.shape]
    flat = (width, mine)
    return pl.pallas_call(
        functools.partial(attend_kernel, nd, nf, length),
        name="attend",
        out_shape=tuple(jax.ShapeDtypeStruct(*item) for item in shapes),
        in_specs=[ON_CHIP] * 4 + [ANYWHERE] * 7,
        out_specs=(ANYWHERE,) * 11 + (ON_CHIP,) * 6,
        input_output_aliases={9: 0},
        scratch_shapes=[pltpu.VMEM(shape, lo) for shape in early]
        + [pltpu.VMEM(w_down.shape, hi)]
        + [pltpu.VMEM(shape, lo) for shape in late]
        + [pltpu.VMEM((nf_rows, mine), hi), pltpu.VMEM(flat, lo), pltpu.VMEM(flat, lo)]
        + [pltpu.VMEM((MEMBERS * count, mine), kind) for kind in (hi, hi, lo)]
        + [dma(shape) for shape in moves for _ in range(2)]
        + [dma((16,))],
        compiler_params=pltpu.CompilerParams(
            collective_id=2, has_side_effects=True, vmem_limit_bytes=VMEM_MOST
        ),
    )(*small, tokens, w_down, in_w, out_w, cot, upper_w, gate_w)


def ahead_steps(nf):
    return list(range(1, nf))


def backward_kernel(
    nd,
    nf,
    length,
    gains,
    cosine,
    sine,
    segments,
    hidden_near,
    hidden_far,
    down_got,
    down_terms,
    gate_terms,
    upper_terms,
    tokens_full,
    mine_full,
    near_full,
    far_full,
    hidden_full,
    cot_full,
    out_w_full,
    mixed_full,
    heads_full,
    values_full,
    raw_full,
    in_w_full,
    down_full,
    out_mine,
    out_core,
    out_x,
    gate_parts,
    upper_parts,
    input_grad,
    in_sum,
    out_sum,
    down_sum,
    gain_totals,
    norm,
    sum_attn,
    sum_ffn,
    sum_heads,
    gain_here,
    gain_group,
    gain_got,
    gain_far,
    square_here,
    square_group,
    square_got,
    square_far,
    tokens,
    mine_ref,
    core_near,
    from_x,
    hidden_in,
    cot,
    out_w,
    mixed,
    heads,
    values,
    raw,
    in_w,
    down_w,
    near_here,
    far_here,
    out_near,
    out_far,
    out_core_far,
    normed,
    branch,
    grad_mixed,
    grad_hidden,
    grad_raw,
    wide,
    in_terms,
    out_terms,
    in_core,
    out_core_terms,
    in_x,
    out_x_terms,
    in_y,
    out_y_terms,
    in_total,
    out_total,
    in_zs,
    out_zs,
    in_zr,
    out_zr,
    down_own,
    gate_own,
    upper_own,
    down_y,
    gate_y,
    upper_y,
    down_z,
    gate_z,
    upper_z,
    row_send,
    row_recv,
    fy_send,
    fy_recv,
    fz_send,
    fz_recv,
    swap_send,
    swap_recv,
    ac_send,
    ac_recv,
    ax_send,
    ax_recv,
    ay_send,
    ay_recv,
    az_send,
    az_recv,
    tg_send,
    tg_recv,
    tf_send,
    tf_recv,
    load_sem,
    got_sem,
    operand_sem,
    local_sem,
):
    outer = nd // MEMBERS
    dp = lax.axis_index("dp")
    z = lax.axis_index("fsdp")
    y = dp // MEMBERS
    member = dp % MEMBERS
    x = member // 2
    c = member % 2
    lo, hi = jnp.bfloat16, jnp.float32

    def z_to(step):
        return lax.rem(z + step, nf)

    def z_peer(step):
        return (dp, z_to(step))

    def y_to(step):
        return lax.rem(y + step, outer)

    def y_peer(step):
        return (y_to(step) * MEMBERS + member, z)

    def in_group(k):
        return (y * MEMBERS + k, z)

    x_peer = in_group((1 - x) * 2 + c)
    core_peer = in_group(x * 2 + 1 - c)
    barrier = pltpu.get_barrier_semaphore()
    peers = [z_peer(step) for step in range(1, nf)] + [y_peer(step) for step in range(1, outer)]
    peers += [x_peer, core_peer, in_group(MEMBERS - 1 - member)]
    crossed = [(hop, step) for hop in range(outer) for step in range(nf) if hop or step]

    def cross_peer(hop, step):
        return (y_to(hop) * MEMBERS + member, z_to(step))

    peers += [cross_peer(hop, step) for hop, step in crossed if hop and step]
    fulls = (tokens_full, mine_full, near_full, far_full, hidden_full, cot_full, out_w_full, mixed_full)
    fulls += (heads_full, values_full, raw_full, in_w_full)
    fulls += (down_full, hidden_near, hidden_far)
    places = (tokens, mine_ref, core_near, from_x, hidden_in, cot, out_w, mixed)
    places += (heads, values, raw, in_w, down_w, near_here, far_here)
    operands = [
        pltpu.make_async_copy(source, target, operand_sem.at[index])
        for index, (source, target) in enumerate(zip(fulls, places))
    ]
    start_all(operands)

    def ready(number):
        for _ in range(number):
            operands.pop(0).wait()

    for peer in peers:
        pl.semaphore_signal(barrier, inc=1, device_id=peer, device_id_type=MESH)
    pl.semaphore_wait(barrier, len(peers))
    sent = []

    def remote(source, target, send, recv, device):
        copy = pltpu.make_async_remote_copy(
            src_ref=source,
            dst_ref=target,
            send_sem=send,
            recv_sem=recv,
            device_id=device,
            device_id_type=MESH,
        )
        copy.start()
        sent.append(copy)
        return copy

    def keep(semaphore, source, target):
        copy = pltpu.make_async_copy(source, target, semaphore)
        copy.start()
        return copy

    gain_attn, gain_ffn, gain_heads = split_gains(gains)
    count, width = tokens.shape
    here, there = pl.ds(0, count), pl.ds(count, count)

    terms = (down_terms, gate_terms, upper_terms)
    owns = (down_own, gate_own, upper_own)
    over_y = (down_y, gate_y, upper_y)
    over_z = (down_z, gate_z, upper_z)

    def piece_of(matrix, place, step):
        if matrix == 0:
            return terms[0].at[place, z_to(step)]
        return terms[matrix].at[place, :, z_to(step)]

    ahead = ahead_steps(nf)
    steps = list(range(1, nf)) + [0]
    order = [(0, step) for step in ahead] + [(1, step) for step in steps]
    order += [(0, step) for step in steps if step not in ahead] + [(2, step) for step in steps]
    y_copies, loads = {}, {}
    for matrix, step in order:
        loads[matrix, step] = keep(
            load_sem.at[matrix, step], piece_of(matrix, y, step), owns[matrix].at[step]
        )
        for hop in range(1, outer):
            if matrix == 0 and step in ahead:
                y_copies[0, step, hop] = keep(
                    got_sem.at[hop, step],
                    down_got.at[hop - 1, ahead.index(step)],
                    down_y.at[hop - 1, step],
                )
                continue
            y_copies[matrix, step, hop] = remote(
                piece_of(matrix, y_to(hop), step),
                over_y[matrix].at[hop - 1, step],
                fy_send.at[matrix, hop, step],
                fy_recv.at[matrix, hop, step],
                y_peer(hop),
            )
    z_copies = {}
    waiting = list(order)

    def pieces(number):
        for _ in range(min(number, len(waiting))):
            matrix, step = waiting.pop(0)
            loads[matrix, step].wait()
            total = owns[matrix][step].astype(hi)
            for hop in range(1, outer):
                if matrix == 0 and step in ahead:
                    y_copies[0, step, hop].wait()
                else:
                    y_copies[matrix, step, hop].wait_recv()
                total = total + over_y[matrix][hop - 1, step].astype(hi)
            owns[matrix][step] = total.astype(lo)
            if step:
                z_copies[matrix, step] = remote(
                    owns[matrix].at[step],
                    over_z[matrix].at[step - 1],
                    fz_send.at[matrix, step],
                    fz_recv.at[matrix, step],
                    z_peer(step),
                )

    def piece_total(matrix):
        total = owns[matrix][0].astype(hi)
        for step in range(1, nf):
            z_copies[matrix, step].wait_recv()
            total = total + over_z[matrix][step - 1].astype(hi)
        return total

    swaps = []

    squares = []

    def trade(matrix, parts):
        total = piece_total(matrix).astype(lo)
        owns[matrix][0] = total
        total = total.astype(hi)
        squares.append(jnp.sum(total * total))
        for mask_bits in range(1, MEMBERS):
            other = member ^ mask_bits
            swaps.append(
                remote(
                    owns[matrix].at[0, other],
                    parts.at[member],
                    swap_send.at[matrix - 1, mask_bits],
                    swap_recv.at[matrix - 1, mask_bits],
                    in_group(other),
                )
            )
        swaps_local.append(
            keep(local_sem.at[2 + matrix], owns[matrix].at[0, member], parts.at[member])
        )

    swaps_local = []
    chunk = 32

    def to_group(index, source, target):
        target[member] = source[...]
        return [
            remote(
                source,
                target.at[member],
                tg_send.at[index, mask_bits],
                tg_recv.at[index, mask_bits],
                in_group(member ^ mask_bits),
            )
            for mask_bits in range(1, MEMBERS)
        ]

    def to_crossed(index, source, target):
        target[y * nf + z] = source[...]
        return [
            remote(
                source,
                target.at[y * nf + z],
                tf_send.at[index, place],
                tf_recv.at[index, place],
                cross_peer(hop, step),
            )
            for place, (hop, step) in enumerate(crossed)
        ]

    def summed(got, copies):
        for copy in copies:
            copy.wait_recv()
        return jnp.sum(got[...], 0)

    ready(1)
    def add_rows(target, other):
        def step_once(index, carry):
            rows = rows_of(index, chunk)
            target[rows, :] = (target[rows, :].astype(hi) + other[rows, :].astype(hi)).astype(lo)
            return carry

        lax.fori_loop(0, count // chunk, step_once, 0)

    def norm_rows(index, carry):
        rows = rows_of(index, chunk)
        part = tokens[rows, :].astype(hi)
        scale = lax.rsqrt(jnp.mean(part * part, -1, keepdims=True) + norm_eps)
        normed[rows, :] = (part * scale * gain_attn).astype(lo)
        return carry

    lax.fori_loop(0, count // chunk, norm_rows, 0)
    sum_attn[...] = jnp.zeros_like(sum_attn)
    sum_ffn[...] = jnp.zeros_like(sum_ffn)
    sum_heads[...] = jnp.zeros_like(sum_heads)
    pieces(len(ahead))
    ready(5)

    def norm_back(part, gain, grad):
        scale = lax.rsqrt(jnp.mean(part * part, -1, keepdims=True) + norm_eps)
        unit = part * scale
        inner = grad * gain
        back = scale * (inner - unit * jnp.mean(inner * unit, -1, keepdims=True))
        return back, jnp.sum(grad * unit, 0, keepdims=True)

    def ffn_norm_back(index, carry):
        rows = rows_of(index, chunk)
        grad = mine_ref[rows, :].astype(hi) + core_near[rows, :].astype(hi)
        grad = grad + from_x[rows, :].astype(hi)
        back, gain_term = norm_back(hidden_in[rows, :], gain_ffn, grad)
        sum_ffn[...] += gain_term
        back = back + cot[rows, :].astype(hi)
        grad_hidden[rows, :] = back
        branch[rows, :] = back.astype(lo)
        return carry

    lax.fori_loop(0, count // chunk, ffn_norm_back, 0)
    pair = 2 * LANES
    ready(2)

    def mixed_back(index, carry):
        columns = tile_of(index, pair)
        grad_mixed[:, columns] = dot_last(branch[...], out_w[columns, :]).astype(lo)
        return carry

    lax.fori_loop(0, HQ * HD // pair, mixed_back, 0)

    all_terms = (in_terms, out_terms)
    sizes = (in_terms.shape[0] // (nd), out_terms.shape[0] // (nd))
    core_terms = (in_core, out_core_terms)
    x_terms = (in_x, out_x_terms)
    y_terms = (in_y, out_y_terms)
    totals = (in_total, out_total)
    zs = (in_zs, out_zs)
    zr = (in_zr, out_zr)
    hops = list(range(1, outer)) + [0]
    core_copies, ax_copies, ay_copies, az_copies = {}, {}, {}, {}

    def block(a, hop, bx, bc):
        index = (y_to(hop) * 2 + bx) * 2 + bc
        return pl.ds(pl.multiple_of(index * sizes[a], 16), sizes[a])

    def core_out(a):
        for far in (1, 0):
            for hop in hops:
                bx = 1 - x if far else x
                core_copies[a, hop, far] = remote(
                    all_terms[a].at[block(a, hop, bx, 1 - c)],
                    core_terms[a].at[hop, far],
                    ac_send.at[a, hop, far],
                    ac_recv.at[a, hop, far],
                    core_peer,
                )

    def add_block(a, rows, others):
        some = math.gcd(sizes[a], 32)

        def step_once(index, carry):
            base = rows.start + index * some
            place = pl.ds(pl.multiple_of(base, 16), some)
            total = all_terms[a][place, :].astype(hi)
            for other in others:
                total = total + other[rows_of(index, some), :].astype(hi)
            all_terms[a][place, :] = total.astype(lo)
            return carry

        lax.fori_loop(0, sizes[a] // some, step_once, 0)

    def core_in(a):
        for hop in hops:
            core_copies[a, hop, 1].wait_recv()
            rows = block(a, hop, 1 - x, c)
            add_block(a, rows, [core_terms[a].at[hop, 1]])
            ax_copies[a, hop] = remote(
                all_terms[a].at[rows],
                x_terms[a].at[hop],
                ax_send.at[a, hop],
                ax_recv.at[a, hop],
                x_peer,
            )

    def x_in(a):
        for hop in range(1, outer):
            core_copies[a, hop, 0].wait_recv()
            ax_copies[a, hop].wait_recv()
            rows = block(a, hop, x, c)
            add_block(a, rows, [core_terms[a].at[hop, 0], x_terms[a].at[hop]])
            ay_copies[a, hop] = remote(
                all_terms[a].at[rows],
                y_terms[a].at[hop - 1],
                ay_send.at[a, hop],
                ay_recv.at[a, hop],
                y_peer(hop),
            )

    def y_in(a):
        core_copies[a, 0, 0].wait_recv()
        ax_copies[a, 0].wait_recv()
        others = [core_terms[a].at[0, 0], x_terms[a].at[0]]
        for hop in range(1, outer):
            ay_copies[a, hop].wait_recv()
            others.append(y_terms[a].at[hop - 1])
        start = block(a, 0, x, c).start
        some = math.gcd(sizes[a], 32)

        def step_once(index, carry):
            place = rows_of(index, some)
            own = pl.ds(pl.multiple_of(start + index * some, 16), some)
            total = all_terms[a][own, :].astype(hi)
            for other in others:
                total = total + other[place, :].astype(hi)
            totals[a][place, :] = total
            return carry

        lax.fori_loop(0, sizes[a] // some, step_once, 0)
        rows = sizes[a] // nf
        for place in range(nf):
            zs[a][place] = totals[a][place * rows : (place + 1) * rows, :].astype(lo)
        for step in range(1, nf):
            az_copies[a, step] = remote(
                zs[a].at[z_to(step)],
                zr[a].at[step - 1],
                az_send.at[a, step],
                az_recv.at[a, step],
                z_peer(step),
            )

    def z_in(a, target):
        total = zs[a][z].astype(hi)
        for step in range(1, nf):
            az_copies[a, step].wait_recv()
            total = total + zr[a][step - 1].astype(hi)
        target[...] = total

    outer_product(mixed, branch, out_terms)
    core_out(1)
    pieces(2)
    ready(len(operands))
    query_tiles = HQ * HD // LANES
    head_tiles = (HQ + KV) * HD // LANES
    key_tiles = KV * HD // LANES

    def over_rows(left, right):
        return lax.dot_general(left, right, (((0,), (0,)), ((), ())), preferred_element_type=hi)

    def attend_back(row):
        rows = pl.ds(row * length, length)
        allowed = may_attend(segments, row)

        def pair_back(tile, carry):
            key_tile = heads[rows, tile_of(query_tiles + tile)]
            value_tile = values[rows, tile_of(tile)]
            grad_key = None
            grad_value = None
            for own in range(2):
                key = [in_half(key_tile, own, half) for half in range(2)]
                value = [in_half(value_tile, own, half) for half in range(2)]
                for half in range(2):
                    key_total, value_total = None, None
                    for quarter in range(2):
                        columns = tile_of(tile * 4 + own * 2 + quarter)
                        query = heads[rows, columns]
                        grad = grad_mixed[rows, columns]
                        weights = probabilities(query, key[half], allowed)
                        slope = dot_last(grad, value[half])
                        inner = jnp.sum(weights * slope, -1, keepdims=True)
                        score = (weights * (slope - inner)).astype(lo)
                        back = jnp.dot(score, key[half], preferred_element_type=hi) * HD**-0.5
                        if half == 0:
                            wide[rows, columns] = back
                        else:
                            wide[rows, columns] += back
                        key_term = over_rows(score, query)
                        value_term = over_rows(weights.astype(lo), grad)
                        key_total = key_term if key_total is None else key_total + key_term
                        value_total = value_term if value_total is None else value_total + value_term
                    key_term = in_half(key_total, half, own)
                    value_term = in_half(value_total, half, own)
                    grad_key = key_term if grad_key is None else grad_key + key_term
                    grad_value = value_term if grad_value is None else grad_value + value_term
            wide[rows, tile_of(query_tiles + tile)] = grad_key * HD**-0.5
            grad_raw[rows, tile_of(head_tiles + tile)] = grad_value.astype(lo)
            return carry

        lax.fori_loop(0, key_tiles, pair_back, 0)

    batch = count // length
    for row in range(batch):
        attend_back(row)
        if row == 0:
            core_in(1)
        pieces(1 if row else 2)
    averages = block_mean()

    def turn_back(index, carry):
        columns = tile_of(index)
        gain = gain_heads(index)
        for row in range(batch):
            rows = pl.ds(row * length, length)
            grad = wide[rows, columns]
            grad = grad * cosine[...] - swap_halves(grad) * sine[...]
            part = raw[rows, columns]
            scale = lax.rsqrt(head_mean(part * part, averages) + norm_eps)
            unit = part * scale
            sum_heads[:, columns] += jnp.sum(grad * unit, 0, keepdims=True)
            inner = grad * gain
            back = scale * (inner - unit * head_mean(inner * unit, averages))
            grad_raw[rows, columns] = back.astype(lo)
        return carry

    lax.fori_loop(0, head_tiles, turn_back, 0)
    outer_product(normed, grad_raw, in_terms)
    core_out(0)
    pieces(1)
    x_in(1)

    def normed_back(index, carry):
        columns = tile_of(index, pair)
        wide[:, columns] = dot_last(grad_raw[...], in_w[columns, :])
        return carry

    core_in(0)

    def down_product(left, target):
        def step_once(index, carry):
            columns = tile_of(index, pair)
            target[:, columns] = jnp.dot(
                left[...], down_w[:, columns], preferred_element_type=hi
            ).astype(lo)
            return carry

        lax.fori_loop(0, width // pair, step_once, 0)

    down_product(far_here, out_far)
    out_far_copy = remote(out_far.at[there], out_core_far, row_send.at[0], row_recv.at[0], core_peer)
    down_product(near_here, out_near)
    out_near_copy = remote(out_near.at[there], out_core, row_send.at[1], row_recv.at[1], core_peer)
    mine_copy = keep(local_sem.at[0], out_near.at[here], out_mine)
    out_far_copy.wait_recv()
    add_rows(out_far, out_core_far)
    out_x_copy = remote(out_far.at[here], out_x, row_send.at[2], row_recv.at[2], x_peer)
    pieces(2)
    lax.fori_loop(0, width // pair, normed_back, 0)

    def attn_norm_back(index, carry):
        rows = rows_of(index, chunk)
        back, gain_term = norm_back(tokens[rows, :].astype(hi), gain_attn, wide[rows, :])
        sum_attn[...] += gain_term
        input_grad[rows, :] = (back + grad_hidden[rows, :]).astype(lo)
        return carry

    lax.fori_loop(0, count // chunk, attn_norm_back, 0)
    gain_here[...] = jnp.zeros_like(gain_here)
    place = 0
    for source in (sum_attn, sum_ffn, sum_heads):
        for tile in range(source.shape[1] // LANES):
            gain_here[pl.ds(place, 1), :] = source[:, tile * LANES : (tile + 1) * LANES]
            place += 1
    gain_copies = to_group(0, gain_here, gain_got)
    pieces(1)
    x_in(0)
    down_sum[...] = piece_total(0)
    y_in(1)
    pieces(2 * nf)
    trade(1, gate_parts)
    y_in(0)
    gain_group[...] = summed(gain_got, gain_copies)
    gain_copies = to_crossed(0, gain_group, gain_far)
    z_in(1, out_sum)
    trade(2, upper_parts)
    z_in(0, in_sum)
    for target in (down_sum, out_sum, in_sum):
        squares.append(jnp.sum(target[...] * target[...]))
    square_here[...] = jnp.full(square_here.shape, sum(squares))
    square_copies = to_group(1, square_here, square_got)
    square_group[...] = summed(square_got, square_copies)
    square_copies = to_crossed(1, square_group, square_far)
    gain_totals[...] = summed(gain_far, gain_copies)
    gain_place = 2 * width // LANES
    gain_squares = gain_totals[:gain_place, :]
    gain_squares = jnp.sum(gain_squares * gain_squares)
    for first, last in ((0, query_tiles), (query_tiles, head_tiles)):
        total = jnp.sum(gain_totals[gain_place + first : gain_place + last, :], 0, keepdims=True)
        total = jnp.broadcast_to(total, (8, LANES))
        total = total + pltpu.roll(total, HD, 1)
        gain_squares += jnp.sum(total * total) / (8 * LANES // HD)
    norm[...] = jnp.sqrt(summed(square_far, square_copies) + gain_squares)
    for copy in swaps + [out_near_copy, out_x_copy]:
        copy.wait_recv()
    for copy in sent:
        copy.wait_send()
    for copy in swaps_local + [mine_copy]:
        copy.wait()


def backward(nd, nf, length, small, halves, terms, operands):
    outer = nd // MEMBERS
    count, width = operands[0].shape
    out_w, in_w = operands[6], operands[-2]
    _, down_terms, gate_terms, _ = terms
    lo, hi = jnp.bfloat16, jnp.float32
    dma = pltpu.SemaphoreType.DMA
    in_rows, in_cols = in_w.shape[0] // (nd * nf), in_w.shape[1]
    out_rows, out_cols = out_w.shape[0] // (nd * nf), out_w.shape[1]
    inner = (MEMBERS,) + gate_terms.shape[3:]
    down = down_terms.shape[2:]
    tiles = (2 * width + (HQ + KV) * HD) // LANES
    gain_tile = (-(-tiles // 8) * 8, LANES)
    far = outer * nf - 1
    shapes = [
        ((count, width), lo),
        ((count, width), lo),
        ((count, width), lo),
        (inner, lo),
        (inner, lo),
        ((count, width), lo),
        ((in_rows, in_cols), hi),
        ((out_rows, out_cols), hi),
        (down, hi),
        (gain_tile, hi),
        ((8, LANES), hi),
    ]
    in_block, out_block = (nf * in_rows, in_cols), (nf * out_rows, out_cols)
    scratch = [((1, width), hi), ((1, width), hi), ((1, (HQ + KV) * HD), hi)]
    for tile in (gain_tile, (8, LANES)):
        scratch += [(tile, hi), (tile, hi), ((MEMBERS,) + tile, hi), ((outer * nf,) + tile, hi)]
    scratch += [(operand.shape, operand.dtype) for operand in operands]
    scratch += [(array.shape, lo) for array in halves]
    scratch += [((2 * count, width), lo)] * 2 + [((count, width), lo)]
    scratch += [
        ((count, width), lo),
        ((count, width), lo),
        ((count, HQ * HD), lo),
        ((count, width), hi),
        ((count, in_cols), lo),
        ((count, width), hi),
        (in_w.shape, lo),
        (out_w.shape, lo),
        ((outer, 2) + in_block, lo),
        ((outer, 2) + out_block, lo),
        ((outer,) + in_block, lo),
        ((outer,) + out_block, lo),
        ((outer - 1,) + in_block, lo),
        ((outer - 1,) + out_block, lo),
        (in_block, hi),
        (out_block, hi),
        ((nf, in_rows, in_cols), lo),
        ((nf, out_rows, out_cols), lo),
        ((nf - 1, in_rows, in_cols), lo),
        ((nf - 1, out_rows, out_cols), lo),
        ((nf,) + down, lo),
        ((nf,) + inner, lo),
        ((nf,) + inner, lo),
        ((outer - 1, nf) + down, lo),
        ((outer - 1, nf) + inner, lo),
        ((outer - 1, nf) + inner, lo),
        ((nf - 1,) + down, lo),
        ((nf - 1,) + inner, lo),
        ((nf - 1,) + inner, lo),
    ]
    moves = [(3,), (3, outer, nf), (3, nf), (2, MEMBERS), (2, outer, 2), (2, outer), (2, outer)]
    moves += [(2, nf), (2, MEMBERS), (2, far)]
    return pl.pallas_call(
        functools.partial(backward_kernel, nd, nf, length),
        name="backward",
        out_shape=tuple(jax.ShapeDtypeStruct(*item) for item in shapes),
        in_specs=[ON_CHIP] * 4 + [ANYWHERE] * (6 + len(operands)),
        out_specs=(ANYWHERE,) * 5 + (ON_CHIP,) * 6,
        scratch_shapes=[pltpu.VMEM(*item) for item in scratch]
        + [dma(shape) for shape in moves for _ in range(2)]
        + [dma((3, nf)), dma((outer, nf)), dma((len(operands) + 2,)), dma((5,))],
        compiler_params=pltpu.CompilerParams(
            collective_id=3, has_side_effects=True, vmem_limit_bytes=VMEM_MOST
        ),
    )(*small, *halves, *terms, *operands)


def adam_kernel(
    span, norm, gain_totals, in_sum, out_sum, gate_parts, upper_parts, down_sum, *rest
):
    count = 8
    row_terms, rest = rest[:5], rest[5:]
    masters, firsts, seconds = rest[:count], rest[count : 2 * count], rest[2 * count : 3 * count]
    rest = rest[3 * count :]
    outs = [rest[index * count : (index + 1) * count] for index in range(3)]
    copies = rest[3 * count : 4 * count - 1]
    output, rows_out, norm_out = rest[4 * count - 1 : 4 * count + 2]
    rest = rest[4 * count + 2 :]
    norm_out[...] = norm[0:1, 0:1]
    ins_here = [rest[index * count : (index + 1) * count] for index in range(3)]
    rest = rest[3 * count :]
    outs_here = [rest[index * count : (index + 1) * count] for index in range(3)]
    copies_here = rest[3 * count : 4 * count - 1]
    sums_here = rest[4 * count - 1 : 4 * count + 4]
    terms_here = rest[4 * count + 4 : 4 * count + 9]
    output_here, sum_sem, in_sem, out_sem, term_sem = rest[4 * count + 9 :]
    sums = (in_sum, out_sum, gate_parts, upper_parts, down_sum)
    loads = {}
    for index in (6, 4, 5, 3, 0, 1, 2, 7):
        source = {6: 4, 4: 2, 5: 3, 3: 1, 0: 0}.get(index)
        if source is not None:
            loads[source] = pltpu.make_async_copy(
                sums[source], sums_here[source], sum_sem.at[source]
            )
            loads[source].start()
        for kind, arrays in enumerate((masters, firsts, seconds)):
            loads[index, kind] = pltpu.make_async_copy(
                arrays[index], ins_here[kind][index], in_sem.at[kind, index]
            )
            loads[index, kind].start()
    rows_count = output.shape[0]
    term_loads = []
    for index, (source, target) in enumerate(zip(row_terms, terms_here)):
        copy = pltpu.make_async_copy(
            source.at[pl.ds(0, rows_count)], target, term_sem.at[index]
        )
        copy.start()
        term_loads.append(copy)
    stores = []

    def store(index):
        pairs = [(outs_here[kind][index], outs[kind][index]) for kind in range(3)]
        if index < count - 1:
            pairs.append((copies_here[index], copies[index]))
        for kind, (source, target) in enumerate(pairs):
            copy = pltpu.make_async_copy(source, target, out_sem.at[kind, index])
            copy.start()
            stores.append(copy)

    factor = jnp.minimum(1.0, clip_limit / (norm[0:1, 0:1] + 1e-06))
    weight_rate = 2.0 * D ** (-0.5)

    def update(index, columns, grad, rate, decay):
        grad = grad * factor
        master, first, second = (ins_here[kind][index][:, columns] for kind in range(3))
        new, second_new = adam_update(master, first, second, grad, rate, decay)
        outs_here[0][index][:, columns] = grad
        outs_here[1][index][:, columns] = new
        outs_here[2][index][:, columns] = second_new
        if index < count - 1:
            copies_here[index][:, columns] = new.astype(jnp.bfloat16)

    def arrived(index):
        for kind in range(3):
            loads[index, kind].wait()

    step = 2 * LANES
    loads[4].wait()
    arrived(6)
    for start in range(0, down_sum.shape[1], step):
        columns = slice(start, start + step)
        update(6, columns, sums_here[4][:, columns], weight_rate, decay_rate)
    store(6)
    members, _, mine = gate_parts.shape
    for index in (4, 5):
        loads[index - 2].wait()
        arrived(index)
        place = 0
        for part in range(mine // span):
            for member in range(members):
                grad = sums_here[index - 2][member, :, part * span : (part + 1) * span]
                columns = slice(place, place + span)
                update(index, columns, grad.astype(jnp.float32), weight_rate, decay_rate)
                place += span
        store(index)
    loads[1].wait()
    arrived(3)
    for start in range(0, out_sum.shape[1], step):
        columns = slice(start, start + step)
        update(3, columns, sums_here[1][:, columns], weight_rate, decay_rate)
    store(3)
    loads[0].wait()
    place = 0
    for index in range(3):
        arrived(index)
        for start in range(0, masters[index].shape[1], step):
            grad = sums_here[0][:, place : place + step]
            update(index, slice(start, start + step), grad, weight_rate, decay_rate)
            place += step
        store(index)
    arrived(7)
    norm_rows = 2 * D // LANES
    head_rows = HQ * HD // LANES
    key_rows = KV * HD // LANES
    folded = []
    for first, size in ((norm_rows, head_rows), (norm_rows + head_rows, key_rows)):
        total = jnp.sum(gain_totals[first : first + size, :], 0, keepdims=True)
        folded.append(total + pltpu.roll(jnp.broadcast_to(total, (8, LANES)), HD, 1)[:1])
    lane = lax.broadcasted_iota(jnp.int32, (1, LANES), 1)
    heads = jnp.where(lane < HD, folded[0], folded[1])
    gain_grad = jnp.concatenate([gain_totals[:norm_rows, :], heads], 0)
    update(7, slice(None), gain_grad, gain_rate, 0.0)
    store(7)
    for copy in term_loads:
        copy.wait()

    def add_rows(index, carry):
        rows = rows_of(index, 32)
        total = terms_here[0][rows, :]
        for term in terms_here[1:4]:
            total = total + term[rows, :].astype(jnp.float32)
        output_here[rows, :] = total.astype(jnp.bfloat16)
        return carry

    copy = pltpu.make_async_copy(terms_here[4], rows_out, term_sem.at[4])
    copy.start()
    stores.append(copy)
    lax.fori_loop(0, rows_count // 32, add_rows, 0)
    copy = pltpu.make_async_copy(output_here, output, term_sem.at[0])
    copy.start()
    stores.append(copy)
    for copy in stores:
        copy.wait()


def adam(span, norm, gain_totals, sums, row_terms, masters, firsts, seconds):
    lo, hi = jnp.bfloat16, jnp.float32
    dma = pltpu.SemaphoreType.DMA
    shapes = [(array.shape, hi) for _ in range(3) for array in masters]
    shapes += [(array.shape, lo) for array in masters[:-1]]
    rows_shape = row_terms[0].shape
    inputs = [(array.shape, hi) for _ in range(3) for array in masters]
    scratch = inputs + shapes + [(array.shape, array.dtype) for array in sums]
    scratch += [(rows_shape, array.dtype) for array in row_terms] + [(rows_shape, lo)]
    shapes += [(rows_shape, lo), (rows_shape, lo), ((1, 1), hi)]
    return pl.pallas_call(
        functools.partial(adam_kernel, span),
        name="adam",
        out_shape=tuple(jax.ShapeDtypeStruct(*item) for item in shapes),
        in_specs=[ON_CHIP] * 2 + [ANYWHERE] * (10 + len(inputs)),
        out_specs=(ANYWHERE,) * (len(shapes) - 1) + (ON_CHIP,),
        scratch_shapes=[pltpu.VMEM(*item) for item in scratch]
        + [dma((5,)), dma((3, len(masters))), dma((4, len(masters))), dma((5,))],
        compiler_params=pltpu.CompilerParams(vmem_limit_bytes=VMEM_MOST),
    )(norm, gain_totals, *sums, *row_terms, *masters, *firsts, *seconds)


def after(value, *others):
    return lax.optimization_barrier((value,) + others)[0]


def low(value):
    return value.astype(jnp.bfloat16)


def shards(
    nd,
    nf,
    tokens,
    cotangent,
    segment_ids,
    w_query,
    w_key,
    w_value,
    w_out,
    w_gate,
    w_up,
    w_down,
    m_query,
    m_key,
    m_value,
    m_out,
    m_gate,
    m_up,
    m_down,
    v_query,
    v_key,
    v_value,
    v_out,
    v_gate,
    v_up,
    v_down,
    gains,
    gain_first,
    gain_second,
):
    masters = (w_query, w_key, w_value, w_out, w_gate, w_up, w_down)
    firsts = (m_query, m_key, m_value, m_out, m_gate, m_up, m_down)
    seconds = (v_query, v_key, v_value, v_out, v_gate, v_up, v_down)
    outer = nd // MEMBERS
    dp = lax.axis_index("dp")
    ring_z = Ring(nf, lax.axis_index("fsdp"), lambda d, f, s: (d, (f + s) % nf), nd, nf)
    ring_y = Ring(
        outer,
        dp // MEMBERS,
        lambda d, f, s: ((d // MEMBERS + s) % outer * MEMBERS + d % MEMBERS, f),
        nd,
        nf,
    )
    ring_x = Ring(2, dp // 2 % 2, lambda d, f, s: (d ^ 2, f), nd, nf)
    ring_core = Ring(2, dp % 2, lambda d, f, s: (d ^ 1, f), nd, nf)
    member = dp % MEMBERS

    def trade(block, mask):
        return Ring(2, dp % 2, lambda d, f, s: (d ^ mask, f), nd, nf).move(block, 1)

    def swap(blocks):
        full = put(jnp.zeros_like(blocks), pick(blocks, 0, member), 0, member)
        for mask in range(1, MEMBERS):
            full = put(full, trade(pick(blocks, 0, member ^ mask), mask), 0, member ^ mask)
        return full

    def spread(rows):
        far = ring_x.move(rows, 1)
        near = jnp.concatenate([rows, ring_core.move(rows, 1)], 0)
        return near, jnp.concatenate([far, ring_core.move(far, 1)], 0)

    def collapse(near, far):
        rows = near.shape[0] // 2
        got = ring_core.move(far[rows:], 1).astype(jnp.float32)
        got = ring_x.move(low(far[:rows].astype(jnp.float32) + got), 1)
        total = near[:rows].astype(jnp.float32)
        total = total + ring_core.move(near[rows:], 1).astype(jnp.float32)
        return total + got.astype(jnp.float32)

    batch, length, width = tokens.shape
    count = batch * length
    hidden_rows = w_down.shape[0]
    span = nf * hidden_rows
    mine = outer * span
    in_rows = w_query.shape[0]
    out_rows = w_out.shape[0]
    attn_cols = (HQ + 2 * KV) * HD

    in_w, out_w, gate_w, upper_w = gather_weights(nd, nf, masters[:6])
    in_w = in_w.reshape(D, attn_cols)
    out_w = out_w.reshape(HQ * HD, D)

    tiled = [array.reshape(-1, LANES) for array in (gains, gain_first, gain_second)]
    small = (tiled[0], *rotary_tables(length), segment_ids)
    back_in = cotangent.reshape(count, width)
    token_rows = tokens.reshape(count, width)
    (
        upper_w,
        down_w,
        back_near,
        back_far,
        ffn_all,
        gate_near,
        upper_near,
        hidden_near,
        gate_far,
        upper_far,
        hidden_far,
        down_terms,
        raw,
        heads,
        values,
        mixed,
        hidden_in,
    ) = attend(
        nd, nf, length, small, token_rows, w_down, in_w, out_w, back_in, upper_w, gate_w
    )
    gate_w = gate_w.reshape(D, mine)
    upper_w = upper_w.reshape(D, mine)
    down_w = down_w.reshape(mine, D)
    def inner_grads(back_half, gate, upper):
        grad_hidden = back_product(back_half, down_w)
        _, pull = jax.vjp(swiglu, gate, upper)
        grad_gate, grad_upper = pull(grad_hidden)
        grad_gate, grad_upper = low(grad_gate), low(grad_upper)
        back = back_product(grad_gate, gate_w) + back_product(grad_upper, upper_w)
        return grad_gate, grad_upper, low(back)

    down_terms = down_terms.reshape(outer, nf, hidden_rows, width)
    down_got = []
    for hop in range(1, outer):
        parts = pick(down_terms, 0, ring_y.dest(hop))
        parts = jnp.stack([pick(parts, 0, ring_z.dest(step)) for step in ahead_steps(nf)])
        down_got.append(ring_y.move(parts, hop))
    down_got = jnp.stack(down_got)
    far_gate, far_upper, far_ffn = inner_grads(back_far, gate_far, upper_far)
    far = far_ffn[:count].astype(jnp.float32) + ring_core.move(far_ffn[count:], 1)
    far = low(far)
    ffn_x = ring_x.move(far, 1)
    near_gate, near_upper, near_ffn = inner_grads(
        after(back_near, far), gate_near, upper_near
    )
    ffn_core = ring_core.move(near_ffn[count:], 1)
    ffn_all = after(ffn_all, near_ffn)
    gate_terms = low(weight_product(ffn_all, jnp.concatenate([near_gate, far_gate], 0)))
    upper_terms = low(weight_product(ffn_all, jnp.concatenate([near_upper, far_upper], 0)))
    inner_shape = (outer, MEMBERS, nf, in_rows, mine)
    (
        out_mine,
        out_core,
        out_x,
        gate_parts,
        upper_parts,
        input_grad,
        in_sum,
        out_sum,
        down_sum,
        gain_totals,
        norm,
    ) = backward(
        nd,
        nf,
        length,
        small,
        (hidden_near, hidden_far),
        (
            down_got,
            down_terms,
            gate_terms.reshape(inner_shape),
            upper_terms.reshape(inner_shape),
        ),
        (
            token_rows,
            near_ffn[:count],
            ffn_core,
            ffn_x,
            hidden_in,
            back_in,
            out_w,
            mixed,
            heads,
            values,
            raw,
            in_w,
            down_w,
        ),
    )
    results = adam(
        span,
        norm,
        gain_totals,
        (in_sum, out_sum, gate_parts, upper_parts, down_sum),
        (hidden_in, out_mine, out_core, out_x, input_grad),
        masters + (tiled[0],),
        firsts + (tiled[1],),
        seconds + (tiled[2],),
    )
    clipped, new_masters, new_seconds = results[:7], results[8:15], results[16:23]
    gain_clipped, new_gains, gain_seconds = (results[k].reshape(-1) for k in (7, 15, 23))
    copies, output, input_grad = tuple(results[24:31]), results[31], results[32]
    total_norm = results[33].reshape(())
    return (
        (output.reshape(tokens.shape), input_grad.reshape(tokens.shape))
        + clipped
        + (gain_clipped, total_norm)
        + new_masters
        + (new_gains,)
        + copies
        + new_seconds
        + (gain_seconds,)
    )


def solution(mesh):
    rows3 = P(AXES, None, None)
    rows2 = P(AXES, None)
    whole = P()
    return jax.shard_map(
        functools.partial(shards, mesh.shape["dp"], mesh.shape["fsdp"]),
        mesh=mesh,
        in_specs=(rows3, rows3) + (rows2,) * 22 + (whole,) * 3,
        out_specs=(rows3, rows3)
        + (rows2,) * 7
        + (whole, whole)
        + (rows2,) * 7
        + (whole,)
        + (rows2,) * 14
        + (whole,),
        check_vma=False,
    )
```
